128 devices in a mesh: mp: 16 (over x, y_hi, core), wide: 8 (over z, y_lo).
Axes of the slice: x: 4, y: 4 (y_hi: 2, y_lo: 2; y = y_hi * 2 + y_lo), z: 4, core: 2. Of those that a mesh axis runs over, the one named last changes fastest.
Arguments:
- tokens: bfloat16 [2048, 16384], P('wide', 'mp'), may hold values from -6 to 6
- grad_out: bfloat16 [2048, 16384], P('wide', 'mp'), may hold values from -1536 to 1536
- keep: int32 [2048], P('wide'), may hold values 0 or 1
- count: int32 [1], replicated, may hold values from 1024 to 2048
- w_gate: bfloat16 [16384, 4096], P('mp', 'wide'), may hold values from -0.046875 to 0.046875
- w_up: bfloat16 [16384, 4096], P('mp', 'wide'), may hold values from -0.046875 to 0.046875
- w_down: bfloat16 [4096, 16384], P('wide', 'mp'), may hold values from -0.09375 to 0.09375
Outputs:
- grad_tokens: bfloat16 [2048, 16384], P('wide', 'mp')
- grad_gate: float32 [16384, 4096], P('mp', 'wide')
- grad_up: float32 [16384, 4096], P('mp', 'wide')
- grad_down: float32 [4096, 16384], P('wide', 'mp')
The draws below stay inside these ranges and needn't reach their ends.
All inputs are finite; a program needn't handle non-finite values. No bound on the sum of `keep` on one device may be relied on, other than what follows from the above.
Results may differ from the reference program's by a relative error of at most 0.0058.
Values may be sent and summed in bfloat16 or wider, within the bound.
A program may use at most 128 MiB of HBM per device.

```python
import jax
import jax.numpy as jnp
from jax import lax

D = 16384
UNITS = 4096
TOKENS = 2048


def plant(values, rng, least, high):
    longest = values.shape.index(max(values.shape))
    spots = []
    for shift in (0, 1):
        where = [jax.random.randint(jax.random.fold_in(rng, axis), (), 0, length) for axis, length in enumerate(values.shape)]
        where[longest] = (where[longest] + shift) % values.shape[longest]
        spots.append(tuple(where))
    return values.at[spots[0]].set(least).at[spots[1]].set(high)


def shard_levels(stream_key, shape, pieces, least, top_value):
    loudness = 1.0
    for dim, blocks in pieces:
        steps = jax.random.uniform(jax.random.fold_in(jax.random.fold_in(stream_key, 6), dim), (blocks,), jnp.float32, least / len(pieces), top_value / len(pieces))
        loudness = loudness * jnp.repeat(jnp.exp(steps), shape[dim] // blocks).reshape((-1,) + (1,) * (len(shape) - 1 - dim))
    return loudness


def scatter_about(rng, dims, spread, bound, cuts=(), dtype=jnp.bfloat16):
    drawn = jax.random.normal(rng, dims, jnp.float32) * spread
    if len(cuts) > 0:
        drawn = shard_levels(rng, dims, cuts, -0.22, 0.18) * drawn
    return jnp.clip(drawn, min=-bound, max=bound).astype(dtype)


def setup_inputs(seed: int = 0) -> dict:
    key_of = jax.random.split(jax.random.key(seed), 8)
    return {
        "tokens": scatter_about(key_of[0], (TOKENS, D), 1.0, 6.0, ((0, 8), (1, 16))),
        "grad_out": scatter_about(key_of[1], (TOKENS, D), (TOKENS // 8), 1536.0, ((0, 8), (1, 16))),
        "keep": plant((jax.random.randint(key_of[2], (TOKENS,), 0, 4) < 3).astype(jnp.int32), jax.random.fold_in(key_of[2], 1), 0, 1),
        "count": jax.random.randint(key_of[3], (1,), TOKENS // 2, TOKENS + 1).astype(jnp.int32),
        "w_gate": scatter_about(key_of[4], (D, UNITS), D ** -0.5, 0.046875, ((0, 16), (1, 8))),
        "w_up": scatter_about(key_of[5], (D, UNITS), D ** -0.5, 0.046875, ((0, 16), (1, 8))),
        "w_down": scatter_about(key_of[6], (UNITS, D), UNITS ** -0.5, 0.09375, ((0, 8), (1, 16))),
    }


def reference(tokens, grad_out, keep, count, w_gate, w_up, w_down):
    factor = keep.astype(jnp.float32) / count[0].astype(jnp.float32)
    scaled = (grad_out.astype(jnp.float32) * factor[:, None]).astype(jnp.bfloat16)
    gate = jnp.dot(tokens, w_gate, preferred_element_type=jnp.float32)
    up = jnp.dot(tokens, w_up, preferred_element_type=jnp.float32)
    back = lax.dot_general(scaled, w_down, (((1,), (1,)), ((), ())), preferred_element_type=jnp.float32)
    sigma = jax.nn.sigmoid(gate)
    silu = gate * sigma
    hidden = (silu * up).astype(jnp.bfloat16)
    d_up = (back * silu).astype(jnp.bfloat16)
    d_gate = (back * up * sigma * (1.0 + gate * (1.0 - sigma))).astype(jnp.bfloat16)
    grad_down = lax.dot_general(hidden, scaled, (((0,), (0,)), ((), ())), preferred_element_type=jnp.float32)
    grad_gate = lax.dot_general(tokens, d_gate, (((0,), (0,)), ((), ())), preferred_element_type=jnp.float32)
    grad_up = lax.dot_general(tokens, d_up, (((0,), (0,)), ((), ())), preferred_element_type=jnp.float32)
    total = lax.dot_general(d_gate, w_gate, (((1,), (1,)), ((), ())), preferred_element_type=jnp.float32)
    total = total + lax.dot_general(d_up, w_up, (((1,), (1,)), ((), ())), preferred_element_type=jnp.float32)
    return total.astype(jnp.bfloat16), grad_gate, grad_up, grad_down
```

```python
import jax
import jax.numpy as jnp
from jax import lax
from jax.experimental import pallas as pl
from jax.experimental.pallas import tpu as pltpu
from jax.sharding import PartitionSpec as P

BF = jnp.bfloat16
F32 = jnp.float32
ROWS = 256
HALF = 128
DM = 1024
U = 512
U3 = 3 * U
CHUNKS = 8
OWN, ZP, ZM, ZF, YF, YP, YM, YO = range(CHUNKS)
B0, X1P, X1M, X2P, X2M, YB, C1, C2P, C2M, C3P, C3M, C4 = range(12)


def dot(a, b):
    return lax.dot_general(a, b, (((1,), (0,)), ((), ())), preferred_element_type=F32)


def kernel(
    tokens, grad_out, factor, w_gate, w_up, w_down,
    out_tok, out_gate, out_up, out_down,
    tg, wcat, wdt, part, b0_r, x1_s, x1_r, x2_s, x2_r, yb_s, yb_r, own16, hid,
    to, dy_s, dy_r, zf_s, zf_r, dz_s, dz_r,
    c_ss, c_rs, a_ss, a_rs, d_ss, d_rs,
):
    mp, wide = lax.axis_index("mp"), lax.axis_index("wide")
    x, yh, c = mp // 4, (mp // 2) % 2, mp % 2
    z = wide // 2
    core = (mp + 1 - 2 * c, wide)
    xp = ((mp + 4) % 16, wide)
    xm = ((mp + 12) % 16, wide)
    yhp = (mp + 2 - 4 * yh, wide)
    ylp = (mp, wide + 1 - 2 * (wide % 2))
    zp = (mp, (wide + 2) % 8)
    zm = (mp, (wide + 6) % 8)

    def remote(src, dst, ssem, rsem, dev):
        return pltpu.make_async_remote_copy(
            src_ref=src, dst_ref=dst, send_sem=ssem, recv_sem=rsem,
            device_id=dev, device_id_type=pl.DeviceIdType.MESH,
        )

    barrier = pltpu.get_barrier_semaphore()
    for dev in (core, xp, xm, yhp, ylp, zp, zm):
        pl.semaphore_signal(barrier, inc=1, device_id=dev, device_id_type=pl.DeviceIdType.MESH)

    tg[OWN, 0] = tokens[...]
    tg[OWN, 1] = (grad_out[...].astype(F32) * factor[...]).astype(BF)
    pl.semaphore_wait(barrier, 7)

    def gather(src, dst, h, dev):
        rows = pl.ds(h * HALF, HALF)
        return remote(
            tg.at[src, :, rows], tg.at[dst, :, rows], a_ss.at[dst, h], a_rs.at[dst, h], dev
        )

    def arrived(dst, h):
        gather(OWN, dst, h, zp).wait_recv()

    gather(OWN, ZM, 0, zp).start()
    gather(OWN, ZP, 1, zm).start()
    gather(OWN, YO, 0, ylp).start()
    gather(OWN, YO, 1, ylp).start()
    gather(OWN, ZM, 1, zp).start()
    gather(OWN, ZP, 0, zm).start()

    for n in range(0, U, 256):
        wcat[n : n + 256, :] = w_gate[:, n : n + 256].T
        wcat[U + n : U + n + 256, :] = w_up[:, n : n + 256].T
        wdt[:, n : n + 256] = w_down[n : n + 256, :].T
    out_gate[...] = jnp.zeros_like(out_gate)
    out_up[...] = jnp.zeros_like(out_up)
    out_down[...] = jnp.zeros_like(out_down)

    def b0(i):
        rows = pl.ds(pl.multiple_of((1 - c) * HALF, HALF), HALF)
        return remote(part.at[i % 2, rows], b0_r.at[i], c_ss.at[B0, i], c_rs.at[B0, i], core)

    def x1(i, k):
        return remote(
            x1_s.at[i, k], x1_r.at[i, k], c_ss.at[X1P + k, i], c_rs.at[X1P + k, i], (xp, xm)[k]
        )

    def x2(i, k):
        return remote(
            x2_s.at[i, k], x2_r.at[i, k], c_ss.at[X2P + k, i], c_rs.at[X2P + k, i], (xp, xm)[k]
        )

    def yb(i):
        return remote(yb_s.at[i], yb_r.at[i], c_ss.at[YB, i], c_rs.at[YB, i], yhp)

    def same(i, first, count, sem, dev):
        rows = pl.ds(pl.multiple_of(first, 16), count)
        return remote(hid.at[i, rows], hid.at[i, rows], c_ss.at[sem, i], c_rs.at[sem, i], dev)

    mine = c * HALF + x * 32
    left = c * HALF + ((x + 3) % 4) * 32
    right = c * HALF + ((x + 1) % 4) * 32

    def c1(i):
        return same(i, mine + yh * 16, 16, C1, yhp)

    def c2(i, k):
        return same(i, mine, 32, C2P + k, (xp, xm)[k])

    def c3(i, k):
        return same(i, (left, right + 16)[k], 16, C3P + k, (xp, xm)[k])

    def c4(i):
        return same(i, c * HALF, HALF, C4, core)

    def summed(i, xd, h):
        at = xd * 32 + h * 16
        a = part[i % 2, pl.ds(pl.multiple_of(c * HALF + at, 16), 16), :]
        return a + b0_r[i, pl.ds(pl.multiple_of(at, 16), 16), :]

    def partial(i):
        s = i % 2
        for n in range(0, U, 256):
            part[s, :, n : n + 256] = dot(tg[i, 0], w_gate[:, n : n + 256])
        for n in range(0, U, 256):
            part[s, :, U + n : U + n + 256] = dot(tg[i, 0], w_up[:, n : n + 256])
        for n in range(0, U, 256):
            part[s, :, 2 * U + n : 2 * U + n + 256] = dot(tg[i, 1], wdt[:, n : n + 256])
        b0(i).start()

    def send_x1(i):
        b0(i).wait()
        x1_s[i, 0] = summed(i, (x + 2) % 4, 0).astype(BF)
        x1(i, 0).start()
        x1_s[i, 1] = summed(i, (x + 2) % 4, 1).astype(BF)
        x1(i, 1).start()

    def send_x2(i):
        x1(i, 0).wait_recv()
        x2_s[i, 0, :16] = (summed(i, (x + 1) % 4, 0) + x1_r[i, 0].astype(F32)).astype(BF)
        x2_s[i, 0, 16:] = summed(i, (x + 1) % 4, 1).astype(BF)
        x2(i, 0).start()
        x1(i, 1).wait_recv()
        x2_s[i, 1, :16] = summed(i, (x + 3) % 4, 0).astype(BF)
        x2_s[i, 1, 16:] = (summed(i, (x + 3) % 4, 1) + x1_r[i, 1].astype(F32)).astype(BF)
        x2(i, 1).start()

    def send_yb(i):
        x2(i, 0).wait_recv()
        x2(i, 1).wait_recv()

        def total(h):
            at = pl.ds(pl.multiple_of(h * 16, 16), 16)
            return summed(i, x, h) + x2_r[i, 0, at].astype(F32) + x2_r[i, 1, at].astype(F32)

        yb_s[i] = total(1 - yh).astype(BF)
        yb(i).start()
        own16[i % 2] = total(yh)

    def send_c1(i):
        yb(i).wait_recv()
        full = own16[i % 2] + yb_r[i].astype(F32)
        gate, up, back = full[:, :U], full[:, U : 2 * U], full[:, 2 * U :]
        sigma = 1.0 / (1.0 + jnp.exp(-gate))
        silu = gate * sigma
        rows = pl.ds(pl.multiple_of(mine + yh * 16, 16), 16)
        hid[i, rows, :U] = (silu * up).astype(BF)
        hid[i, rows, U : 2 * U] = (back * up * sigma * (1.0 + gate * (1.0 - sigma))).astype(BF)
        hid[i, rows, 2 * U :] = (back * silu).astype(BF)
        c1(i).start()

    def send_c2(i):
        c1(i).wait_recv()
        c2(i, 0).start()
        c2(i, 1).start()

    def send_c3(i):
        c2(i, 0).wait_recv()
        c3(i, 0).start()
        c2(i, 1).wait_recv()
        c3(i, 1).start()

    def send_c4(i):
        c3(i, 0).wait_recv()
        c3(i, 1).wait_recv()
        c4(i).start()

    def grads_in(g, first):
        for d in (first, first + 256):
            turned = tg[g, 0, :, d : d + 256].T
            for n in range(0, U, 256):
                out_gate[d : d + 256, n : n + 256] += dot(turned, hid[g, :, U + n : U + n + 256])
                out_up[d : d + 256, n : n + 256] += dot(
                    turned, hid[g, :, 2 * U + n : 2 * U + n + 256]
                )

    def grads_down(g):
        for u in range(0, U, 256):
            turned = hid[g, :, u : u + 256].T
            for n in range(0, DM, 256):
                out_down[u : u + 256, n : n + 256] += dot(turned, tg[g, 1, :, n : n + 256])

    def dy(k, h):
        rows = pl.ds(h * HALF, HALF)
        return remote(dy_s.at[k, rows], dy_r.at[k, rows], d_ss.at[k, h], d_rs.at[k, h], ylp)

    def zf(k):
        return remote(zf_s.at[k], zf_r.at[k], d_ss.at[4, k], d_rs.at[4, k], (zp, zm)[k])

    def dz(k, h):
        rows = pl.ds(h * HALF, HALF)
        return remote(
            dz_s.at[k, rows], dz_r.at[k, rows], d_ss.at[5 + k, h], d_rs.at[5 + k, h], (zp, zm)[k]
        )

    def send_zf():
        for k in (0, 1):
            dy(0, k).wait_recv()
            rows = pl.ds(k * HALF, HALF)
            zf_s[k] = (to[ZF, rows] + dy_r[0, rows].astype(F32)).astype(BF)
            zf(k).start()

    def send_dz(k):
        for h in (1 - k, k):
            dy(1 + k, h).wait_recv()
            rows = pl.ds(h * HALF, HALF)
            total = to[ZP + k, rows] + dy_r[1 + k, rows].astype(F32)
            if h == k:
                zf(k).wait_recv()
                total = total + zf_r[k].astype(F32)
            dz_s[k, rows] = total.astype(BF)
            dz(k, h).start()

    def term(j):
        c4(j).wait_recv()

        @pl.when(j < YF)
        def _():
            for n in range(0, DM, 256):
                to[j, :, n : n + 256] = dot(hid[j, :, U:], wcat[:, n : n + 256])

        @pl.when(j >= YF)
        def _():
            k = j - YF
            for h in (0, 1):
                rows = pl.ds(h * HALF, HALF)
                for n in range(0, DM, 256):
                    dy_s[k, rows, n : n + 256] = dot(
                        hid[j, rows, U:], wcat[:, n : n + 256]
                    ).astype(BF)
                dy(k, h).start()

    def tick(t, carry):
        i, j, g = t, t - 1, t - 2

        @pl.when(t < CHUNKS)
        def _():
            @pl.when(t == ZP)
            def _():
                arrived(ZM, 0)
                gather(ZM, ZF, 0, zp).start()
                arrived(ZP, 1)
                gather(ZP, ZF, 1, zm).start()
                arrived(YO, 0)
                gather(YO, YM, 0, zp).start()
                arrived(YO, 1)
                gather(YO, YP, 1, zm).start()
                gather(YO, YM, 1, zp).start()
                gather(YO, YP, 0, zm).start()
                arrived(ZP, 0)

            @pl.when(t == ZM)
            def _():
                arrived(ZM, 1)

            @pl.when(t == ZF)
            def _():
                arrived(ZF, 0)
                arrived(ZF, 1)

            @pl.when(t == YF)
            def _():
                arrived(YF, 0)
                arrived(YF, 1)

            @pl.when(t == YP)
            def _():
                arrived(YP, 0)

            @pl.when(t == YM)
            def _():
                arrived(YM, 1)

            partial(i)

        @pl.when(t >= 1)
        def _():
            send_c1(j)

        @pl.when(t < CHUNKS)
        def _():
            send_x1(i)

        @pl.when(t >= 2)
        def _():
            grads_in(g, 0)

        @pl.when(t >= 1)
        def _():
            send_c2(j)

        @pl.when(t < CHUNKS)
        def _():
            send_x2(i)

        @pl.when(t >= 2)
        def _():
            grads_in(g, 512)

        @pl.when(t >= 1)
        def _():
            send_c3(j)

        @pl.when(t < CHUNKS)
        def _():
            send_yb(i)

        @pl.when(t == ZF)
        def _():
            arrived(YM, 0)
            gather(YM, YF, 0, zp).start()
            arrived(YP, 1)
            gather(YP, YF, 1, zm).start()

        @pl.when(t >= 2)
        def _():
            grads_down(g)

        @pl.when(t >= 1)
        def _():
            send_c4(j)

        @pl.when(t == 6)
        def _():
            send_zf()

        @pl.when(t == 7)
        def _():
            send_dz(0)

        @pl.when(t == 8)
        def _():
            send_dz(1)

        @pl.when(t >= 1)
        def _():
            term(j)

        return carry

    lax.fori_loop(0, CHUNKS + 1, tick, 0)

    grads_in(CHUNKS - 1, 0)
    grads_in(CHUNKS - 1, 512)
    grads_down(CHUNKS - 1)
    for h in (0, 1):
        rows = pl.ds(h * HALF, HALF)
        dy(3, h).wait_recv()
        dz(0, h).wait_recv()
        dz(1, h).wait_recv()
        out_tok[rows] = (
            to[OWN, rows]
            + dy_r[3, rows].astype(F32)
            + (dz_r[0, rows].astype(F32) + dz_r[1, rows].astype(F32))
        ).astype(BF)

    def left_all(i, carry):
        for k in (0, 1):
            x1(i, k).wait_send()
            x2(i, k).wait_send()
            c2(i, k).wait_send()
            c3(i, k).wait_send()
        yb(i).wait_send()
        c1(i).wait_send()
        c4(i).wait_send()
        return carry

    lax.fori_loop(0, CHUNKS, left_all, 0)
    for dst in range(1, CHUNKS):
        for h in (0, 1):
            gather(OWN, dst, h, zp).wait_send()
    for h in (0, 1):
        for k in range(4):
            dy(k, h).wait_send()
        dz(0, h).wait_send()
        dz(1, h).wait_send()
        zf(h).wait_send()


def local(tokens, grad_out, keep, count, w_gate, w_up, w_down):
    factor = (keep.astype(F32) / count[0].astype(F32))[:, None]
    vmem = pl.BlockSpec(memory_space=pltpu.VMEM)
    dma = pltpu.SemaphoreType.DMA
    return pl.pallas_call(
        kernel,
        out_shape=(
            jax.ShapeDtypeStruct((ROWS, DM), BF),
            jax.ShapeDtypeStruct((DM, U), F32),
            jax.ShapeDtypeStruct((DM, U), F32),
            jax.ShapeDtypeStruct((U, DM), F32),
        ),
        in_specs=[vmem] * 6,
        out_specs=[vmem] * 4,
        scratch_shapes=[
            pltpu.VMEM((CHUNKS, 2, ROWS, DM), BF),
            pltpu.VMEM((2 * U, DM), BF),
            pltpu.VMEM((DM, U), BF),
            pltpu.VMEM((2, ROWS, U3), F32),
            pltpu.VMEM((CHUNKS, HALF, U3), F32),
            pltpu.VMEM((CHUNKS, 2, 16, U3), BF),
            pltpu.VMEM((CHUNKS, 2, 16, U3), BF),
            pltpu.VMEM((CHUNKS, 2, 32, U3), BF),
            pltpu.VMEM((CHUNKS, 2, 32, U3), BF),
            pltpu.VMEM((CHUNKS, 16, U3), BF),
            pltpu.VMEM((CHUNKS, 16, U3), BF),
            pltpu.VMEM((2, 16, U3), F32),
            pltpu.VMEM((CHUNKS, ROWS, U3), BF),
            pltpu.VMEM((4, ROWS, DM), F32),
            pltpu.VMEM((4, ROWS, DM), BF),
            pltpu.VMEM((4, ROWS, DM), BF),
            pltpu.VMEM((2, HALF, DM), BF),
            pltpu.VMEM((2, HALF, DM), BF),
            pltpu.VMEM((2, ROWS, DM), BF),
            pltpu.VMEM((2, ROWS, DM), BF),
            dma((12, CHUNKS)),
            dma((12, CHUNKS)),
            dma((CHUNKS, 2)),
            dma((CHUNKS, 2)),
            dma((7, 2)),
            dma((7, 2)),
        ],
        compiler_params=pltpu.CompilerParams(
            collective_id=0, has_side_effects=True, vmem_limit_bytes=62 * 1024 * 1024
        ),
        cost_estimate=pl.CostEstimate(
            flops=16 * 2048 * DM * U, bytes_accessed=16 << 20, transcendentals=0
        ),
    )(tokens, grad_out, factor, w_gate, w_up, w_down)


def solution(mesh):
    placed = (
        P("wide", "mp"),
        P("wide", "mp"),
        P("wide"),
        P(),
        P("mp", "wide"),
        P("mp", "wide"),
        P("wide", "mp"),
    )
    return jax.shard_map(
        local,
        mesh=mesh,
        in_specs=placed,
        out_specs=(P("wide", "mp"), P("mp", "wide"), P("mp", "wide"), P("wide", "mp")),
        check_vma=False,
    )
```

```python
import jax
import jax.numpy as jnp
from jax import lax
from jax.experimental import pallas as pl
from jax.experimental.pallas import tpu as pltpu
from jax.sharding import PartitionSpec as P

BF = jnp.bfloat16
F32 = jnp.float32
ROWS = 256
HALF = 128
DM = 1024
U = 512
U3 = 3 * U
CHUNKS = 8
OWN, C1, C2, YO, F, Y1, YF, Y2 = range(CHUNKS)
B0, X1P, X1M, X2P, X2M, YB, H1, H2P, H2M, H3P, H3M, H4 = range(12)


def dot(a, b):
    return lax.dot_general(a, b, (((1,), (0,)), ((), ())), preferred_element_type=F32)


def kernel(
    tokens, grad_out, factor, w_gate, w_up, w_down,
    out_tok, out_gate, out_up, out_down,
    tg, wcat, wdt, part, b0_r, x1_s, x1_r, x2_s, x2_r, yb_s, yb_r, own16, hid, turned,
    to, dy_s, dy_r, zf_s, zf_r, dz_s, dz_r,
    c_ss, c_rs, a_ss, a_rs, d_ss, d_rs,
):
    mp, wide = lax.axis_index("mp"), lax.axis_index("wide")
    x, yh, c = mp // 4, (mp // 2) % 2, mp % 2
    z = wide // 2
    core = (mp + 1 - 2 * c, wide)
    xp = ((mp + 4) % 16, wide)
    xm = ((mp + 12) % 16, wide)
    yhp = (mp + 2 - 4 * yh, wide)
    ylp = (mp, wide + 1 - 2 * (wide % 2))
    zp = (mp, (wide + 2) % 8)
    zm = (mp, (wide + 6) % 8)

    def remote(src, dst, ssem, rsem, dev):
        return pltpu.make_async_remote_copy(
            src_ref=src, dst_ref=dst, send_sem=ssem, recv_sem=rsem,
            device_id=dev, device_id_type=pl.DeviceIdType.MESH,
        )

    barrier = pltpu.get_barrier_semaphore()
    for dev in (core, xp, xm, yhp, ylp, zp, zm):
        pl.semaphore_signal(barrier, inc=1, device_id=dev, device_id_type=pl.DeviceIdType.MESH)

    tg[OWN, 0] = tokens[...]
    tg[OWN, 1] = (grad_out[...].astype(F32) * factor[...]).astype(BF)
    pl.semaphore_wait(barrier, 7)

    def gather(src, dst, h, dev):
        rows = pl.ds(h * HALF, HALF)
        return remote(
            tg.at[src, :, rows], tg.at[dst, :, rows], a_ss.at[dst, h], a_rs.at[dst, h], dev
        )

    def arrived(dst, h):
        gather(OWN, dst, h, zp).wait_recv()

    gather(OWN, C1, 0, zp).start()
    gather(OWN, C1, 1, zm).start()
    gather(OWN, YO, 0, ylp).start()
    gather(OWN, YO, 1, ylp).start()
    gather(OWN, C2, 1, zp).start()
    gather(OWN, C2, 0, zm).start()

    for n in range(0, U, 256):
        wcat[n : n + 256, :] = w_gate[:, n : n + 256].T
        wcat[U + n : U + n + 256, :] = w_up[:, n : n + 256].T
        wdt[:, n : n + 256] = w_down[n : n + 256, :].T
    out_gate[...] = jnp.zeros_like(out_gate)
    out_up[...] = jnp.zeros_like(out_up)
    out_down[...] = jnp.zeros_like(out_down)

    def b0(i):
        rows = pl.ds(pl.multiple_of((1 - c) * HALF, HALF), HALF)
        return remote(part.at[i % 2, rows], b0_r.at[i], c_ss.at[B0, i], c_rs.at[B0, i], core)

    def x1(i, k):
        return remote(
            x1_s.at[i, k], x1_r.at[i, k], c_ss.at[X1P + k, i], c_rs.at[X1P + k, i], (xp, xm)[k]
        )

    def x2(i, k):
        return remote(
            x2_s.at[i, k], x2_r.at[i, k], c_ss.at[X2P + k, i], c_rs.at[X2P + k, i], (xp, xm)[k]
        )

    def yb(i):
        return remote(yb_s.at[i], yb_r.at[i], c_ss.at[YB, i], c_rs.at[YB, i], yhp)

    def same(i, first, count, sem, dev):
        rows = pl.ds(pl.multiple_of(first, 16), count)
        return remote(hid.at[i, rows], hid.at[i, rows], c_ss.at[sem, i], c_rs.at[sem, i], dev)

    mine = c * HALF + x * 32
    left = c * HALF + ((x + 3) % 4) * 32
    right = c * HALF + ((x + 1) % 4) * 32

    def h1(i):
        return same(i, mine + yh * 16, 16, H1, yhp)

    def h2(i, k):
        return same(i, mine, 32, H2P + k, (xp, xm)[k])

    def h3(i, k):
        return same(i, (left, right + 16)[k], 16, H3P + k, (xp, xm)[k])

    def h4(i):
        return same(i, c * HALF, HALF, H4, core)

    def summed(i, xd, h):
        at = xd * 32 + h * 16
        a = part[i % 2, pl.ds(pl.multiple_of(c * HALF + at, 16), 16), :]
        return a + b0_r[i, pl.ds(pl.multiple_of(at, 16), 16), :]

    def partial(i):
        s = i % 2
        for n in range(0, U, 256):
            part[s, :, n : n + 256] = dot(tg[i, 0], w_gate[:, n : n + 256])
        for n in range(0, U, 256):
            part[s, :, U + n : U + n + 256] = dot(tg[i, 0], w_up[:, n : n + 256])
        for n in range(0, U, 256):
            part[s, :, 2 * U + n : 2 * U + n + 256] = dot(tg[i, 1], wdt[:, n : n + 256])
        b0(i).start()

    def send_x1(i):
        b0(i).wait()
        x1_s[i, 0] = summed(i, (x + 2) % 4, 0).astype(BF)
        x1(i, 0).start()
        x1_s[i, 1] = summed(i, (x + 2) % 4, 1).astype(BF)
        x1(i, 1).start()

    def send_x2(i):
        x1(i, 0).wait_recv()
        x2_s[i, 0, :16] = (summed(i, (x + 1) % 4, 0) + x1_r[i, 0].astype(F32)).astype(BF)
        x2_s[i, 0, 16:] = summed(i, (x + 1) % 4, 1).astype(BF)
        x2(i, 0).start()
        x1(i, 1).wait_recv()
        x2_s[i, 1, :16] = summed(i, (x + 3) % 4, 0).astype(BF)
        x2_s[i, 1, 16:] = (summed(i, (x + 3) % 4, 1) + x1_r[i, 1].astype(F32)).astype(BF)
        x2(i, 1).start()

    def send_yb(i):
        x2(i, 0).wait_recv()
        x2(i, 1).wait_recv()

        def total(h):
            at = pl.ds(pl.multiple_of(h * 16, 16), 16)
            return summed(i, x, h) + x2_r[i, 0, at].astype(F32) + x2_r[i, 1, at].astype(F32)

        yb_s[i] = total(1 - yh).astype(BF)
        yb(i).start()
        own16[i % 2] = total(yh)

    def send_h1(i):
        yb(i).wait_recv()
        full = own16[i % 2] + yb_r[i].astype(F32)
        gate, up, back = full[:, :U], full[:, U : 2 * U], full[:, 2 * U :]
        sigma = 1.0 / (1.0 + jnp.exp(-gate))
        silu = gate * sigma
        rows = pl.ds(pl.multiple_of(mine + yh * 16, 16), 16)
        hid[i, rows, :U] = (silu * up).astype(BF)
        hid[i, rows, U : 2 * U] = (back * up * sigma * (1.0 + gate * (1.0 - sigma))).astype(BF)
        hid[i, rows, 2 * U :] = (back * silu).astype(BF)
        h1(i).start()

    def send_h2(i):
        h1(i).wait_recv()
        h2(i, 0).start()
        h2(i, 1).start()

    def send_h3(i):
        h2(i, 0).wait_recv()
        h3(i, 0).start()
        h2(i, 1).wait_recv()
        h3(i, 1).start()

    def send_h4(i):
        h3(i, 0).wait_recv()
        h3(i, 1).wait_recv()
        h4(i).start()

    def grads(g):
        for d in range(0, DM, 256):
            turned[d : d + 256, :] = tg[g, 0, :, d : d + 256].T
        for n in range(0, U, 256):
            out_gate[:, n : n + 256] += dot(turned[...], hid[g, :, U + n : U + n + 256])
        for n in range(0, U, 256):
            out_up[:, n : n + 256] += dot(turned[...], hid[g, :, 2 * U + n : 2 * U + n + 256])
        for u in range(0, U, 256):
            turned[u : u + 256, :] = hid[g, :, u : u + 256].T
        for n in range(0, DM, 256):
            out_down[:, n : n + 256] += dot(turned[:U], tg[g, 1, :, n : n + 256])

    def dy(k, h):
        rows = pl.ds(h * HALF, HALF)
        return remote(dy_s.at[k, rows], dy_r.at[k, rows], d_ss.at[k, h], d_rs.at[k, h], ylp)

    def zf(h):
        return remote(zf_s.at[h], zf_r.at[h], d_ss.at[4, h], d_rs.at[4, h], (zp, zm)[h])

    def dz(k, h):
        rows = pl.ds(h * HALF, HALF)
        return remote(
            dz_s.at[k, rows], dz_r.at[k, rows], d_ss.at[5 + k, h], d_rs.at[5 + k, h],
            (zp, zm)[(h + 1 + k) % 2],
        )

    def send_zf():
        for h in (0, 1):
            dy(2, h).wait_recv()
            rows = pl.ds(h * HALF, HALF)
            zf_s[h] = (to[3, rows] + dy_r[2, rows].astype(F32)).astype(BF)
            zf(h).start()

    def send_dz(k):
        for h in (0, 1):
            rows = pl.ds(h * HALF, HALF)
            dy(1 + 2 * k, h).wait_recv()
            total = to[1 + k, rows] + dy_r[1 + 2 * k, rows].astype(F32)
            if k == 1:
                zf(h).wait_recv()
                total = total + zf_r[h].astype(F32)
            dz_s[k, rows] = total.astype(BF)
            dz(k, h).start()

    def term(j):
        h4(j).wait_recv()
        kept = (j < YO) | (j == F)

        @pl.when(kept)
        def _():
            for n in range(0, DM, 256):
                to[j - j // F, :, n : n + 256] = dot(hid[j, :, U:], wcat[:, n : n + 256])

        @pl.when(jnp.logical_not(kept))
        def _():
            k = j - YO - j // Y1
            for h in (0, 1):
                rows = pl.ds(h * HALF, HALF)
                for n in range(0, DM, 256):
                    dy_s[k, rows, n : n + 256] = dot(
                        hid[j, rows, U:], wcat[:, n : n + 256]
                    ).astype(BF)
                dy(k, h).start()

    def arrivals(t):
        @pl.when(t == C1)
        def _():
            arrived(C1, 0)
            gather(C1, F, 0, zp).start()
            arrived(C1, 1)
            gather(C1, F, 1, zm).start()

        @pl.when(t == C2)
        def _():
            arrived(C2, 0)
            arrived(C2, 1)
            arrived(YO, 0)
            gather(YO, Y1, 0, zp).start()
            arrived(YO, 1)
            gather(YO, Y1, 1, zm).start()
            gather(YO, Y2, 1, zp).start()
            gather(YO, Y2, 0, zm).start()

        @pl.when(t == F)
        def _():
            arrived(F, 0)
            arrived(F, 1)

        @pl.when(t == Y1)
        def _():
            arrived(Y1, 0)
            gather(Y1, YF, 0, zp).start()
            arrived(Y1, 1)
            gather(Y1, YF, 1, zm).start()

        @pl.when(t == YF)
        def _():
            arrived(YF, 0)
            arrived(YF, 1)

        @pl.when(t == Y2)
        def _():
            arrived(Y2, 0)
            arrived(Y2, 1)

    def tick(t, carry):
        def stage(step, lag):
            pl.when((t >= lag) & (t < CHUNKS + lag))(lambda: step(t - lag))

        stage(send_x2, 1)
        stage(send_h1, 2)
        stage(send_h3, 3)
        arrivals(t)
        stage(partial, 0)
        stage(term, 4)

        stage(send_yb, 1)
        stage(send_h2, 2)
        stage(send_h4, 3)
        stage(send_x1, 0)

        @pl.when(t == Y1 + 5)
        def _():
            send_dz(0)

        @pl.when(t == YF + 5)
        def _():
            send_zf()

        stage(grads, 4)
        return carry

    lax.fori_loop(0, CHUNKS + 4, tick, 0)

    send_dz(1)
    for h in (0, 1):
        rows = pl.ds(h * HALF, HALF)
        dy(0, h).wait_recv()
        dz(0, h).wait_recv()
        dz(1, h).wait_recv()
        out_tok[rows] = (
            to[OWN, rows]
            + dy_r[0, rows].astype(F32)
            + (dz_r[0, rows].astype(F32) + dz_r[1, rows].astype(F32))
        ).astype(BF)

    def left_all(i, carry):
        for k in (0, 1):
            x1(i, k).wait_send()
            x2(i, k).wait_send()
            h2(i, k).wait_send()
            h3(i, k).wait_send()
        yb(i).wait_send()
        h1(i).wait_send()
        h4(i).wait_send()
        return carry

    lax.fori_loop(0, CHUNKS, left_all, 0)
    for dst in range(1, CHUNKS):
        for h in (0, 1):
            gather(OWN, dst, h, zp).wait_send()
    for h in (0, 1):
        for k in range(4):
            dy(k, h).wait_send()
        dz(0, h).wait_send()
        dz(1, h).wait_send()
        zf(h).wait_send()


def local(tokens, grad_out, keep, count, w_gate, w_up, w_down):
    factor = (keep.astype(F32) / count[0].astype(F32))[:, None]
    vmem = pl.BlockSpec(memory_space=pltpu.VMEM)
    dma = pltpu.SemaphoreType.DMA
    return pl.pallas_call(
        kernel,
        out_shape=(
            jax.ShapeDtypeStruct((ROWS, DM), BF),
            jax.ShapeDtypeStruct((DM, U), F32),
            jax.ShapeDtypeStruct((DM, U), F32),
            jax.ShapeDtypeStruct((U, DM), F32),
        ),
        in_specs=[vmem] * 6,
        out_specs=[vmem] * 4,
        scratch_shapes=[
            pltpu.VMEM((CHUNKS, 2, ROWS, DM), BF),
            pltpu.VMEM((2 * U, DM), BF),
            pltpu.VMEM((DM, U), BF),
            pltpu.VMEM((2, ROWS, U3), F32),
            pltpu.VMEM((CHUNKS, HALF, U3), F32),
            pltpu.VMEM((CHUNKS, 2, 16, U3), BF),
            pltpu.VMEM((CHUNKS, 2, 16, U3), BF),
            pltpu.VMEM((CHUNKS, 2, 32, U3), BF),
            pltpu.VMEM((CHUNKS, 2, 32, U3), BF),
            pltpu.VMEM((CHUNKS, 16, U3), BF),
            pltpu.VMEM((CHUNKS, 16, U3), BF),
            pltpu.VMEM((2, 16, U3), F32),
            pltpu.VMEM((CHUNKS, ROWS, U3), BF),
            pltpu.VMEM((DM, ROWS), BF),
            pltpu.VMEM((4, ROWS, DM), F32),
            pltpu.VMEM((4, ROWS, DM), BF),
            pltpu.VMEM((4, ROWS, DM), BF),
            pltpu.VMEM((2, HALF, DM), BF),
            pltpu.VMEM((2, HALF, DM), BF),
            pltpu.VMEM((2, ROWS, DM), BF),
            pltpu.VMEM((2, ROWS, DM), BF),
            dma((12, CHUNKS)),
            dma((12, CHUNKS)),
            dma((CHUNKS, 2)),
            dma((CHUNKS, 2)),
            dma((7, 2)),
            dma((7, 2)),
        ],
        compiler_params=pltpu.CompilerParams(
            collective_id=0, has_side_effects=True, vmem_limit_bytes=62 * 1024 * 1024
        ),
        cost_estimate=pl.CostEstimate(
            flops=16 * 2048 * DM * U, bytes_accessed=16 << 20, transcendentals=0
        ),
    )(tokens, grad_out, factor, w_gate, w_up, w_down)


def solution(mesh):
    placed = (
        P("wide", "mp"),
        P("wide", "mp"),
        P("wide"),
        P(),
        P("mp", "wide"),
        P("mp", "wide"),
        P("wide", "mp"),
    )
    return jax.shard_map(
        local,
        mesh=mesh,
        in_specs=placed,
        out_specs=(P("wide", "mp"), P("mp", "wide"), P("mp", "wide"), P("wide", "mp")),
        check_vma=False,
    )
```

```python
import jax
import jax.numpy as jnp
from jax import lax
from jax.experimental import pallas as pl
from jax.experimental.pallas import tpu as pltpu
from jax.sharding import PartitionSpec as P

BF = jnp.bfloat16
F32 = jnp.float32
ROWS = 256
HALF = 128
DM = 1024
U = 512
U3 = 3 * U
CHUNKS = 8
PIECES = 4
OWN, C1, YO, F, Y1, YF, Y2, C2 = range(CHUNKS)
B0, X1P, X1M, X2P, X2M, YB, H1, H2P, H2M, H3P, H3M, H4 = range(12)


def dot(a, b):
    return lax.dot_general(a, b, (((1,), (0,)), ((), ())), preferred_element_type=F32)


def kernel(
    tokens, grad_out, factor, w_gate, w_up, w_down,
    out_tok, out_gate, out_up, out_down,
    sum_gate, sum_up, sum_down, tg, wcat, wdt, part, b0_r, x1_s, x1_r, x2_s, x2_r, yb_s, yb_r, own16, hid, turned,
    to, dy_s, dy_r, zf_s, zf_r, dz_s, dz_r,
    c_ss, c_rs, a_ss, a_rs, d_ss, d_rs, o_s,
):
    mp, wide = lax.axis_index("mp"), lax.axis_index("wide")
    x, yh, c = mp // 4, (mp // 2) % 2, mp % 2
    z = wide // 2
    core = (mp + 1 - 2 * c, wide)
    xp = ((mp + 4) % 16, wide)
    xm = ((mp + 12) % 16, wide)
    yhp = (mp + 2 - 4 * yh, wide)
    ylp = (mp, wide + 1 - 2 * (wide % 2))
    zp = (mp, (wide + 2) % 8)
    zm = (mp, (wide + 6) % 8)

    def remote(src, dst, ssem, rsem, dev):
        return pltpu.make_async_remote_copy(
            src_ref=src, dst_ref=dst, send_sem=ssem, recv_sem=rsem,
            device_id=dev, device_id_type=pl.DeviceIdType.MESH,
        )

    barrier = pltpu.get_barrier_semaphore()
    for dev in (core, xp, xm, yhp, ylp, zp, zm):
        pl.semaphore_signal(barrier, inc=1, device_id=dev, device_id_type=pl.DeviceIdType.MESH)

    tg[OWN, 0] = tokens[...]
    tg[OWN, 1] = (grad_out[...].astype(F32) * factor[...]).astype(BF)
    pl.semaphore_wait(barrier, 7)

    def gather(src, dst, h, dev):
        rows = pl.ds(h * HALF, HALF)
        return remote(
            tg.at[src, :, rows], tg.at[dst, :, rows], a_ss.at[dst, h], a_rs.at[dst, h], dev
        )

    def arrived(dst, h):
        gather(OWN, dst, h, zp).wait_recv()

    gather(OWN, C1, 0, zp).start()
    gather(OWN, C1, 1, zm).start()
    gather(OWN, YO, 0, ylp).start()
    gather(OWN, YO, 1, ylp).start()
    gather(OWN, C2, 1, zp).start()
    gather(OWN, C2, 0, zm).start()

    for n in range(0, U, 256):
        wcat[n : n + 256, :] = w_gate[:, n : n + 256].T
        wcat[U + n : U + n + 256, :] = w_up[:, n : n + 256].T
        wdt[:, n : n + 256] = w_down[n : n + 256, :].T
    sum_gate[...] = jnp.zeros_like(sum_gate)
    sum_up[...] = jnp.zeros_like(sum_up)
    sum_down[...] = jnp.zeros_like(sum_down)

    def b0(i):
        rows = pl.ds(pl.multiple_of((1 - c) * HALF, HALF), HALF)
        return remote(part.at[i % 2, rows], b0_r.at[i], c_ss.at[B0, i], c_rs.at[B0, i], core)

    def x1(i, k):
        return remote(
            x1_s.at[i, k], x1_r.at[i, k], c_ss.at[X1P + k, i], c_rs.at[X1P + k, i], (xp, xm)[k]
        )

    def x2(i, k):
        return remote(
            x2_s.at[i, k], x2_r.at[i, k], c_ss.at[X2P + k, i], c_rs.at[X2P + k, i], (xp, xm)[k]
        )

    def yb(i):
        return remote(yb_s.at[i], yb_r.at[i], c_ss.at[YB, i], c_rs.at[YB, i], yhp)

    def same(i, first, count, sem, dev):
        rows = pl.ds(pl.multiple_of(first, 16), count)
        return remote(hid.at[i, rows], hid.at[i, rows], c_ss.at[sem, i], c_rs.at[sem, i], dev)

    mine = c * HALF + x * 32
    left = c * HALF + ((x + 3) % 4) * 32
    right = c * HALF + ((x + 1) % 4) * 32

    def h1(i):
        return same(i, mine + yh * 16, 16, H1, yhp)

    def h2(i, k):
        return same(i, mine, 32, H2P + k, (xp, xm)[k])

    def h3(i, k):
        return same(i, (left, right + 16)[k], 16, H3P + k, (xp, xm)[k])

    def h4(i):
        return same(i, c * HALF, HALF, H4, core)

    def summed(i, xd, h):
        at = xd * 32 + h * 16
        a = part[i % 2, pl.ds(pl.multiple_of(c * HALF + at, 16), 16), :]
        return a + b0_r[i, pl.ds(pl.multiple_of(at, 16), 16), :]

    def partial(i):
        s = i % 2
        for n in range(0, U, 256):
            part[s, :, n : n + 256] = dot(tg[i, 0], w_gate[:, n : n + 256])
        for n in range(0, U, 256):
            part[s, :, U + n : U + n + 256] = dot(tg[i, 0], w_up[:, n : n + 256])
        for n in range(0, U, 256):
            part[s, :, 2 * U + n : 2 * U + n + 256] = dot(tg[i, 1], wdt[:, n : n + 256])
        b0(i).start()

    def send_x1(i):
        b0(i).wait()
        x1_s[i, 0] = summed(i, (x + 2) % 4, 0).astype(BF)
        x1(i, 0).start()
        x1_s[i, 1] = summed(i, (x + 2) % 4, 1).astype(BF)
        x1(i, 1).start()

    def send_x2(i):
        x1(i, 0).wait_recv()
        x2_s[i, 0, :16] = (summed(i, (x + 1) % 4, 0) + x1_r[i, 0].astype(F32)).astype(BF)
        x2_s[i, 0, 16:] = summed(i, (x + 1) % 4, 1).astype(BF)
        x2(i, 0).start()
        x1(i, 1).wait_recv()
        x2_s[i, 1, :16] = summed(i, (x + 3) % 4, 0).astype(BF)
        x2_s[i, 1, 16:] = (summed(i, (x + 3) % 4, 1) + x1_r[i, 1].astype(F32)).astype(BF)
        x2(i, 1).start()

    def send_yb(i):
        x2(i, 0).wait_recv()
        x2(i, 1).wait_recv()

        def total(h):
            at = pl.ds(pl.multiple_of(h * 16, 16), 16)
            return summed(i, x, h) + x2_r[i, 0, at].astype(F32) + x2_r[i, 1, at].astype(F32)

        yb_s[i] = total(1 - yh).astype(BF)
        yb(i).start()
        own16[i % 2] = total(yh)

    def send_h1(i):
        yb(i).wait_recv()
        full = own16[i % 2] + yb_r[i].astype(F32)
        gate, up, back = full[:, :U], full[:, U : 2 * U], full[:, 2 * U :]
        sigma = 1.0 / (1.0 + jnp.exp(-gate))
        silu = gate * sigma
        rows = pl.ds(pl.multiple_of(mine + yh * 16, 16), 16)
        hid[i, rows, :U] = (silu * up).astype(BF)
        hid[i, rows, U : 2 * U] = (back * up * sigma * (1.0 + gate * (1.0 - sigma))).astype(BF)
        hid[i, rows, 2 * U :] = (back * silu).astype(BF)
        h1(i).start()

    def send_h2(i):
        h1(i).wait_recv()
        h2(i, 0).start()
        h2(i, 1).start()

    def send_h3(i):
        h2(i, 0).wait_recv()
        h3(i, 0).start()
        h2(i, 1).wait_recv()
        h3(i, 1).start()

    def send_h4(i):
        h3(i, 0).wait_recv()
        h3(i, 1).wait_recv()
        h4(i).start()

    def grads(g):
        for d in range(0, DM, 256):
            turned[d : d + 256, :] = tg[g, 0, :, d : d + 256].T
        for n in range(0, U, 256):
            sum_gate[:, n : n + 256] += dot(turned[...], hid[g, :, U + n : U + n + 256])
        for n in range(0, U, 256):
            sum_up[:, n : n + 256] += dot(turned[...], hid[g, :, 2 * U + n : 2 * U + n + 256])
        for u in range(0, U, 256):
            turned[u : u + 256, :] = hid[g, :, u : u + 256].T
        for n in range(0, DM, 256):
            sum_down[:, n : n + 256] += dot(turned[:U], tg[g, 1, :, n : n + 256])

    def dy(k, h):
        rows = pl.ds(h * HALF, HALF)
        return remote(dy_s.at[k, rows], dy_r.at[k, rows], d_ss.at[k, h], d_rs.at[k, h], ylp)

    def zf(h):
        return remote(zf_s.at[h], zf_r.at[h], d_ss.at[4, h], d_rs.at[4, h], (zm, zp)[h])

    def dz(k, h):
        rows = pl.ds(h * HALF, HALF)
        return remote(
            dz_s.at[k, rows], dz_r.at[k, rows], d_ss.at[5 + k, h], d_rs.at[5 + k, h],
            (zp, zm)[(h + 1 + k) % 2],
        )

    def send_zf():
        for h in (0, 1):
            dy(2, h).wait_recv()
            rows = pl.ds(h * HALF, HALF)
            zf_s[h] = (to[2, rows] + dy_r[2, rows].astype(F32)).astype(BF)
            zf(h).start()

    def send_dz(k):
        for h in (0, 1):
            rows = pl.ds(h * HALF, HALF)
            dy(1 + 2 * k, h).wait_recv()
            total = to[1 + 2 * k, rows] + dy_r[1 + 2 * k, rows].astype(F32)
            if k == 0:
                zf(h).wait_recv()
                total = total + zf_r[h].astype(F32)
            dz_s[k, rows] = total.astype(BF)
            dz(k, h).start()

    def term(j):
        h4(j).wait_recv()
        kept = (j < YO) | (j == F) | (j == C2)

        @pl.when(kept)
        def _():
            for n in range(0, DM, 256):
                to[j - j // F - 2 * (j // C2), :, n : n + 256] = dot(hid[j, :, U:], wcat[:, n : n + 256])

        @pl.when(jnp.logical_not(kept))
        def _():
            k = j - YO - j // Y1
            for h in (0, 1):
                rows = pl.ds(h * HALF, HALF)
                for n in range(0, DM, 256):
                    dy_s[k, rows, n : n + 256] = dot(
                        hid[j, rows, U:], wcat[:, n : n + 256]
                    ).astype(BF)
                dy(k, h).start()

    def arrivals(t):
        @pl.when(t == C1)
        def _():
            arrived(C1, 0)
            gather(C1, F, 0, zp).start()
            arrived(C1, 1)
            gather(C1, F, 1, zm).start()

        @pl.when(t == YO)
        def _():
            arrived(YO, 0)
            gather(YO, Y1, 0, zp).start()
            arrived(YO, 1)
            gather(YO, Y1, 1, zm).start()

        @pl.when(t == F)
        def _():
            arrived(F, 0)
            arrived(F, 1)

        @pl.when(t == Y1)
        def _():
            arrived(Y1, 0)
            gather(Y1, YF, 0, zp).start()
            arrived(Y1, 1)
            gather(Y1, YF, 1, zm).start()

        @pl.when(t == YF)
        def _():
            arrived(YF, 0)
            arrived(YF, 1)

        @pl.when(t == Y2)
        def _():
            arrived(Y2, 0)
            arrived(Y2, 1)

    def tick(t, carry):
        def stage(step, lag):
            pl.when((t >= lag) & (t < CHUNKS + lag))(lambda: step(t - lag))

        stage(send_x2, 1)
        stage(send_h1, 2)
        stage(send_h3, 3)
        arrivals(t)
        stage(partial, 0)
        stage(term, 4)

        @pl.when(t == YO)
        def _():
            arrived(C2, 0)
            gather(C2, Y2, 0, ylp).start()
            arrived(C2, 1)
            gather(C2, Y2, 1, ylp).start()

        stage(send_yb, 1)
        stage(send_h2, 2)
        stage(send_h4, 3)
        stage(send_x1, 0)

        @pl.when(t == YF + 5)
        def _():
            send_zf()

        @pl.when(t == YF + 6)
        def _():
            send_dz(0)

        stage(grads, 4)
        return carry

    lax.fori_loop(0, CHUNKS + 4, tick, 0)

    sums = ((sum_gate, out_gate), (sum_up, out_up), (sum_down, out_down))
    stores = [pltpu.make_async_copy(a, b, o_s.at[k]) for k, (a, b) in enumerate(sums)]
    for store in stores:
        store.start()
    send_dz(1)
    for h in (0, 1):
        rows = pl.ds(h * HALF, HALF)
        dy(0, h).wait_recv()
        dz(0, h).wait_recv()
        dz(1, h).wait_recv()
        out_tok[rows] = (
            to[OWN, rows]
            + dy_r[0, rows].astype(F32)
            + (dz_r[0, rows].astype(F32) + dz_r[1, rows].astype(F32))
        ).astype(BF)

    for store in stores:
        store.wait()

    def left_all(i, carry):
        for k in (0, 1):
            x1(i, k).wait_send()
            x2(i, k).wait_send()
            h2(i, k).wait_send()
            h3(i, k).wait_send()
        yb(i).wait_send()
        h1(i).wait_send()
        h4(i).wait_send()
        return carry

    lax.fori_loop(0, CHUNKS, left_all, 0)
    for dst in range(1, CHUNKS):
        for h in (0, 1):
            gather(OWN, dst, h, zp).wait_send()
    for h in (0, 1):
        for k in range(4):
            dy(k, h).wait_send()
        dz(0, h).wait_send()
        dz(1, h).wait_send()
        zf(h).wait_send()


def place(*refs):
    ins, outs, sems = refs[:4], refs[4:8], refs[8]
    copies = []
    for k, (a, b) in enumerate(zip(ins, outs)):
        count = a.shape[0] // PIECES
        for p in range(PIECES):
            rows = pl.ds(p * count, count)
            copies.append(pltpu.make_async_copy(a.at[rows], b.at[rows], sems.at[k, p]))
    for copy in copies:
        copy.start()
    for copy in copies:
        copy.wait()


def local(tokens, grad_out, keep, count, w_gate, w_up, w_down):
    factor = (keep.astype(F32) / count[0].astype(F32))[:, None]
    vmem = pl.BlockSpec(memory_space=pltpu.VMEM)
    dma = pltpu.SemaphoreType.DMA
    outs = pl.pallas_call(
        kernel,
        out_shape=(
            jax.ShapeDtypeStruct((ROWS, DM), BF),
            jax.ShapeDtypeStruct((DM, U), F32),
            jax.ShapeDtypeStruct((DM, U), F32),
            jax.ShapeDtypeStruct((U, DM), F32),
        ),
        in_specs=[vmem] * 6,
        out_specs=[vmem] + [pl.BlockSpec(memory_space=pl.ANY)] * 3,
        scratch_shapes=[
            pltpu.VMEM((DM, U), F32),
            pltpu.VMEM((DM, U), F32),
            pltpu.VMEM((U, DM), F32),
            pltpu.VMEM((CHUNKS, 2, ROWS, DM), BF),
            pltpu.VMEM((2 * U, DM), BF),
            pltpu.VMEM((DM, U), BF),
            pltpu.VMEM((2, ROWS, U3), F32),
            pltpu.VMEM((CHUNKS, HALF, U3), F32),
            pltpu.VMEM((CHUNKS, 2, 16, U3), BF),
            pltpu.VMEM((CHUNKS, 2, 16, U3), BF),
            pltpu.VMEM((CHUNKS, 2, 32, U3), BF),
            pltpu.VMEM((CHUNKS, 2, 32, U3), BF),
            pltpu.VMEM((CHUNKS, 16, U3), BF),
            pltpu.VMEM((CHUNKS, 16, U3), BF),
            pltpu.VMEM((2, 16, U3), F32),
            pltpu.VMEM((CHUNKS, ROWS, U3), BF),
            pltpu.VMEM((DM, ROWS), BF),
            pltpu.VMEM((4, ROWS, DM), F32),
            pltpu.VMEM((4, ROWS, DM), BF),
            pltpu.VMEM((4, ROWS, DM), BF),
            pltpu.VMEM((2, HALF, DM), BF),
            pltpu.VMEM((2, HALF, DM), BF),
            pltpu.VMEM((2, ROWS, DM), BF),
            pltpu.VMEM((2, ROWS, DM), BF),
            dma((12, CHUNKS)),
            dma((12, CHUNKS)),
            dma((CHUNKS, 2)),
            dma((CHUNKS, 2)),
            dma((7, 2)),
            dma((7, 2)),
            dma((3,)),
        ],
        compiler_params=pltpu.CompilerParams(
            collective_id=0, has_side_effects=True, vmem_limit_bytes=62 * 1024 * 1024
        ),
        cost_estimate=pl.CostEstimate(
            flops=16 * 2048 * DM * U, bytes_accessed=16 << 20, transcendentals=0
        ),
    )(tokens, grad_out, factor, w_gate, w_up, w_down)
    hbm = pl.BlockSpec(memory_space=pltpu.HBM)
    return pl.pallas_call(
        place,
        out_shape=tuple(jax.ShapeDtypeStruct(o.shape, o.dtype) for o in outs),
        in_specs=[hbm] * 4,
        out_specs=[hbm] * 4,
        scratch_shapes=[dma((4, PIECES))],
        compiler_params=pltpu.CompilerParams(vmem_limit_bytes=62 * 1024 * 1024),
    )(*outs)


def solution(mesh):
    placed = (
        P("wide", "mp"),
        P("wide", "mp"),
        P("wide"),
        P(),
        P("mp", "wide"),
        P("mp", "wide"),
        P("wide", "mp"),
    )
    return jax.shard_map(
        local,
        mesh=mesh,
        in_specs=placed,
        out_specs=(P("wide", "mp"), P("mp", "wide"), P("mp", "wide"), P("wide", "mp")),
        check_vma=False,
    )
```

```python
import jax
import jax.numpy as jnp
from jax import lax
from jax.experimental import pallas as pl
from jax.experimental.pallas import tpu as pltpu
from jax.sharding import PartitionSpec as P

BF = jnp.bfloat16
F32 = jnp.float32
ROWS = 256
HALF = 128
DM = 1024
U = 512
U3 = 3 * U
CHUNKS = 8
PIECES = 8
OWN, C1, C2, F, Y1, YF, Y2, YO = range(CHUNKS)
B0, X1P, X1M, X2P, X2M, YB, H1, H2P, H2M, H3P, H3M, H4 = range(12)


def dot(a, b):
    return lax.dot_general(a, b, (((1,), (0,)), ((), ())), preferred_element_type=F32)


def kernel(
    tokens, grad_out, factor, w_gate, w_up, w_down,
    out_tok, out_gate, out_up, out_down,
    sum_gate, sum_up, sum_down, tg, wcat, wdt, part, b0_r, x1_s, x1_r, x2_s, x2_r, yb_s, yb_r, own16, hid, turned,
    to, dy_s, dy_r, zf_s, zf_r, dz_s, dz_r,
    c_ss, c_rs, a_ss, a_rs, d_ss, d_rs, o_s,
):
    mp, wide = lax.axis_index("mp"), lax.axis_index("wide")
    x, yh, c = mp // 4, (mp // 2) % 2, mp % 2
    z = wide // 2
    core = (mp + 1 - 2 * c, wide)
    xp = ((mp + 4) % 16, wide)
    xm = ((mp + 12) % 16, wide)
    yhp = (mp + 2 - 4 * yh, wide)
    ylp = (mp, wide + 1 - 2 * (wide % 2))
    zp = (mp, (wide + 2) % 8)
    zm = (mp, (wide + 6) % 8)

    def remote(src, dst, ssem, rsem, dev):
        return pltpu.make_async_remote_copy(
            src_ref=src, dst_ref=dst, send_sem=ssem, recv_sem=rsem,
            device_id=dev, device_id_type=pl.DeviceIdType.MESH,
        )

    barrier = pltpu.get_barrier_semaphore()
    for dev in (core, xp, xm, yhp, ylp, zp, zm):
        pl.semaphore_signal(barrier, inc=1, device_id=dev, device_id_type=pl.DeviceIdType.MESH)

    tg[0, OWN] = tokens[...]
    tg[1, OWN] = (grad_out[...].astype(F32) * factor[...]).astype(BF)
    pl.semaphore_wait(barrier, 7)

    def gather(src, dst, h, dev):
        rows = pl.ds(h * HALF, HALF)
        return remote(
            tg.at[:, src, rows], tg.at[:, dst, rows], a_ss.at[dst, h], a_rs.at[dst, h], dev
        )

    def arrived(dst, h):
        gather(OWN, dst, h, zp).wait_recv()

    gather(OWN, C1, 0, zp).start()
    gather(OWN, C1, 1, zm).start()
    gather(OWN, YO, 0, ylp).start()
    gather(OWN, YO, 1, ylp).start()
    gather(OWN, C2, 1, zp).start()
    gather(OWN, C2, 0, zm).start()

    for n in range(0, U, 256):
        wcat[n : n + 256, :] = w_gate[:, n : n + 256].T
        wcat[U + n : U + n + 256, :] = w_up[:, n : n + 256].T
        wdt[:, n : n + 256] = w_down[n : n + 256, :].T
    sum_gate[...] = jnp.zeros_like(sum_gate)
    sum_up[...] = jnp.zeros_like(sum_up)
    sum_down[...] = jnp.zeros_like(sum_down)

    def b0(i):
        rows = pl.ds(pl.multiple_of((1 - c) * HALF, HALF), HALF)
        return remote(part.at[i % 2, rows], b0_r.at[i], c_ss.at[B0, i], c_rs.at[B0, i], core)

    def x1(i, k):
        return remote(
            x1_s.at[i, k], x1_r.at[i, k], c_ss.at[X1P + k, i], c_rs.at[X1P + k, i], (xp, xm)[k]
        )

    def x2(i, k):
        return remote(
            x2_s.at[i, k], x2_r.at[i, k], c_ss.at[X2P + k, i], c_rs.at[X2P + k, i], (xp, xm)[k]
        )

    def yb(i):
        return remote(yb_s.at[i], yb_r.at[i], c_ss.at[YB, i], c_rs.at[YB, i], yhp)

    def same(i, first, count, sem, dev):
        rows = pl.ds(pl.multiple_of(first, 16), count)
        return remote(hid.at[i, rows], hid.at[i, rows], c_ss.at[sem, i], c_rs.at[sem, i], dev)

    mine = c * HALF + x * 32
    left = c * HALF + ((x + 3) % 4) * 32
    right = c * HALF + ((x + 1) % 4) * 32

    def h1(i):
        return same(i, mine + yh * 16, 16, H1, yhp)

    def h2(i, k):
        return same(i, mine, 32, H2P + k, (xp, xm)[k])

    def h3(i, k):
        return same(i, (left, right + 16)[k], 16, H3P + k, (xp, xm)[k])

    def h4(i):
        return same(i, c * HALF, HALF, H4, core)

    def summed(i, xd, h):
        at = xd * 32 + h * 16
        a = part[i % 2, pl.ds(pl.multiple_of(c * HALF + at, 16), 16), :]
        return a + b0_r[i, pl.ds(pl.multiple_of(at, 16), 16), :]

    def partial(i):
        s = i % 2
        for n in range(0, U, 256):
            part[s, :, n : n + 256] = dot(tg[0, i], w_gate[:, n : n + 256])
        for n in range(0, U, 256):
            part[s, :, U + n : U + n + 256] = dot(tg[0, i], w_up[:, n : n + 256])
        for n in range(0, U, 256):
            part[s, :, 2 * U + n : 2 * U + n + 256] = dot(tg[1, i], wdt[:, n : n + 256])
        b0(i).start()

    def send_x1(i):
        b0(i).wait()
        x1_s[i, 0] = summed(i, (x + 2) % 4, 0).astype(BF)
        x1(i, 0).start()
        x1_s[i, 1] = summed(i, (x + 2) % 4, 1).astype(BF)
        x1(i, 1).start()

    def send_x2(i):
        x1(i, 0).wait_recv()
        x2_s[i, 0, :16] = (summed(i, (x + 1) % 4, 0) + x1_r[i, 0].astype(F32)).astype(BF)
        x2_s[i, 0, 16:] = summed(i, (x + 1) % 4, 1).astype(BF)
        x2(i, 0).start()
        x1(i, 1).wait_recv()
        x2_s[i, 1, :16] = summed(i, (x + 3) % 4, 0).astype(BF)
        x2_s[i, 1, 16:] = (summed(i, (x + 3) % 4, 1) + x1_r[i, 1].astype(F32)).astype(BF)
        x2(i, 1).start()

    def send_yb(i):
        x2(i, 0).wait_recv()
        x2(i, 1).wait_recv()

        def total(h):
            at = pl.ds(pl.multiple_of(h * 16, 16), 16)
            return summed(i, x, h) + x2_r[i, 0, at].astype(F32) + x2_r[i, 1, at].astype(F32)

        yb_s[i] = total(1 - yh).astype(BF)
        yb(i).start()
        own16[i % 2] = total(yh)

    def send_h1(i):
        yb(i).wait_recv()
        full = own16[i % 2] + yb_r[i].astype(F32)
        gate, up, back = full[:, :U], full[:, U : 2 * U], full[:, 2 * U :]
        sigma = 1.0 / (1.0 + jnp.exp(-gate))
        silu = gate * sigma
        rows = pl.ds(pl.multiple_of(mine + yh * 16, 16), 16)
        hid[i, rows, :U] = (silu * up).astype(BF)
        hid[i, rows, U : 2 * U] = (back * up * sigma * (1.0 + gate * (1.0 - sigma))).astype(BF)
        hid[i, rows, 2 * U :] = (back * silu).astype(BF)
        h1(i).start()

    def send_h2(i):
        h1(i).wait_recv()
        h2(i, 0).start()
        h2(i, 1).start()

    def send_h3(i):
        h2(i, 0).wait_recv()
        h3(i, 0).start()
        h2(i, 1).wait_recv()
        h3(i, 1).start()

    def send_h4(i):
        h3(i, 0).wait_recv()
        h3(i, 1).wait_recv()
        h4(i).start()

    def grads_in(g):
        tok = tg[0, pl.ds(g - 1, 2)].reshape(2 * ROWS, DM)
        for d in range(0, DM, 256):
            turned[d : d + 256, :] = tok[:, d : d + 256].T
        for sums, u in ((sum_gate, U), (sum_up, 2 * U)):
            for n in range(0, U, 256):
                h = hid[pl.ds(g - 1, 2), :, u + n : u + n + 256].reshape(2 * ROWS, 256)
                sums[:, n : n + 256] += dot(turned[...], h)

    def grads_down(g):
        h = hid[pl.ds(g - 1, 2), :, :U].reshape(2 * ROWS, U)
        for u in range(0, U, 256):
            turned[u : u + 256, :] = h[:, u : u + 256].T
        for n in range(0, DM, 256):
            sc = tg[1, pl.ds(g - 1, 2), :, n : n + 256].reshape(2 * ROWS, 256)
            sum_down[:, n : n + 256] += dot(turned[:U], sc)

    def zf(col, h):
        sem = 2 * col
        return remote(
            zf_s.at[col, h], zf_r.at[col, h], d_ss.at[sem, h], d_rs.at[sem, h], (zm, zp)[h]
        )

    def dz(col, k, h):
        rows = pl.ds(h * HALF, HALF)
        sem = 2 * col + 1
        return remote(
            dz_s.at[col, k, rows], dz_r.at[col, k, rows],
            d_ss.at[sem, 2 * k + h], d_rs.at[sem, 2 * k + h], (zp, zm)[(h + 1 + k) % 2],
        )

    def dy(h):
        rows = pl.ds(h * HALF, HALF)
        return remote(dy_s.at[rows], dy_r.at[rows], d_ss.at[4, h], d_rs.at[4, h], ylp)

    def send_zf(col):
        for h in (0, 1):
            zf_s[col, h] = to[(F, YF)[col], pl.ds(h * HALF, HALF)].astype(BF)
            zf(col, h).start()

    def send_dz(col, k):
        for h in (0, 1):
            rows = pl.ds(h * HALF, HALF)
            total = to[((C1, C2), (Y1, Y2))[col][k], rows]
            if k == 0:
                zf(col, h).wait_recv()
                total = total + zf_r[col, h].astype(F32)
            dz_s[col, k, rows] = total.astype(BF)
            dz(col, k, h).start()

    def column(col, h):
        rows = pl.ds(h * HALF, HALF)
        dz(col, 0, h).wait_recv()
        dz(col, 1, h).wait_recv()
        return to[(OWN, YO)[col], rows] + (
            dz_r[col, 0, rows].astype(F32) + dz_r[col, 1, rows].astype(F32)
        )

    def term(j):
        h4(j).wait_recv()
        for n in range(0, DM, 256):
            to[j, :, n : n + 256] = dot(hid[j, :, U:], wcat[:, n : n + 256])

    def arrivals(t):
        @pl.when(t == C1)
        def _():
            arrived(C1, 0)
            gather(C1, F, 0, zp).start()
            arrived(C1, 1)
            gather(C1, F, 1, zm).start()

        @pl.when(t == C2)
        def _():
            arrived(C2, 0)
            arrived(C2, 1)
            arrived(YO, 0)
            gather(YO, Y1, 0, zp).start()
            arrived(YO, 1)
            gather(YO, Y1, 1, zm).start()
            gather(YO, Y2, 1, zp).start()
            gather(YO, Y2, 0, zm).start()

        @pl.when(t == F)
        def _():
            arrived(F, 0)
            arrived(F, 1)

        @pl.when(t == Y1)
        def _():
            arrived(Y1, 0)
            gather(Y1, YF, 0, zp).start()
            arrived(Y1, 1)
            gather(Y1, YF, 1, zm).start()

        @pl.when(t == YF)
        def _():
            arrived(YF, 0)
            arrived(YF, 1)

        @pl.when(t == Y2)
        def _():
            arrived(Y2, 0)
            arrived(Y2, 1)

    def tick(t, carry):
        def stage(step, lag):
            pl.when((t >= lag) & (t < CHUNKS + lag))(lambda: step(t - lag))

        stage(send_x2, 1)
        stage(send_h1, 2)
        stage(send_h3, 3)
        arrivals(t)
        stage(partial, 0)
        stage(term, 4)

        @pl.when(t == YF + 4)
        def _():
            send_zf(1)

        @pl.when(t == Y2 + 4)
        def _():
            send_dz(1, 1)
            send_dz(1, 0)

        stage(send_yb, 1)
        stage(send_h2, 2)
        stage(send_h4, 3)
        stage(send_x1, 0)

        @pl.when(t == 8)
        def _():
            send_zf(0)
            send_dz(0, 1)

        @pl.when(t == 9)
        def _():
            send_dz(0, 0)

        pl.when((t >= 5) & (t % 2 == 1))(lambda: grads_in(t - 4))
        pl.when((t >= 6) & (t % 2 == 0))(lambda: grads_down(t - 5))
        return carry

    lax.fori_loop(0, CHUNKS + 4, tick, 0)

    sums = ((sum_gate, out_gate), (sum_up, out_up), (sum_down, out_down))
    stores = [pltpu.make_async_copy(a, b, o_s.at[k]) for k, (a, b) in enumerate(sums)]
    stores[0].start()
    stores[1].start()
    for h in (0, 1):
        dy_s[pl.ds(h * HALF, HALF)] = column(1, h).astype(BF)
        dy(h).start()
    grads_down(CHUNKS - 1)
    stores[2].start()
    for h in (0, 1):
        rows = pl.ds(h * HALF, HALF)
        total = column(0, h)
        dy(h).wait_recv()
        out_tok[rows] = (total + dy_r[rows].astype(F32)).astype(BF)

    for store in stores:
        store.wait()

    def left_all(i, carry):
        for k in (0, 1):
            x1(i, k).wait_send()
            x2(i, k).wait_send()
            h2(i, k).wait_send()
            h3(i, k).wait_send()
        yb(i).wait_send()
        h1(i).wait_send()
        h4(i).wait_send()
        return carry

    lax.fori_loop(0, CHUNKS, left_all, 0)
    for dst in range(1, CHUNKS):
        for h in (0, 1):
            gather(OWN, dst, h, zp).wait_send()
    for h in (0, 1):
        for col in (0, 1):
            zf(col, h).wait_send()
            dz(col, 0, h).wait_send()
            dz(col, 1, h).wait_send()
        dy(h).wait_send()


def place(*refs):
    for a, b in zip(refs[:4], refs[4:]):
        b[...] = a[...]


def local(tokens, grad_out, keep, count, w_gate, w_up, w_down):
    factor = (keep.astype(F32) / count[0].astype(F32))[:, None]
    vmem = pl.BlockSpec(memory_space=pltpu.VMEM)
    dma = pltpu.SemaphoreType.DMA
    outs = pl.pallas_call(
        kernel,
        out_shape=(
            jax.ShapeDtypeStruct((ROWS, DM), BF),
            jax.ShapeDtypeStruct((DM, U), F32),
            jax.ShapeDtypeStruct((DM, U), F32),
            jax.ShapeDtypeStruct((U, DM), F32),
        ),
        in_specs=[vmem] * 6,
        out_specs=[vmem] + [pl.BlockSpec(memory_space=pl.ANY)] * 3,
        scratch_shapes=[
            pltpu.VMEM((DM, U), F32),
            pltpu.VMEM((DM, U), F32),
            pltpu.VMEM((U, DM), F32),
            pltpu.VMEM((2, CHUNKS, ROWS, DM), BF),
            pltpu.VMEM((2 * U, DM), BF),
            pltpu.VMEM((DM, U), BF),
            pltpu.VMEM((2, ROWS, U3), F32),
            pltpu.VMEM((CHUNKS, HALF, U3), F32),
            pltpu.VMEM((CHUNKS, 2, 16, U3), BF),
            pltpu.VMEM((CHUNKS, 2, 16, U3), BF),
            pltpu.VMEM((CHUNKS, 2, 32, U3), BF),
            pltpu.VMEM((CHUNKS, 2, 32, U3), BF),
            pltpu.VMEM((CHUNKS, 16, U3), BF),
            pltpu.VMEM((CHUNKS, 16, U3), BF),
            pltpu.VMEM((2, 16, U3), F32),
            pltpu.VMEM((CHUNKS, ROWS, U3), BF),
            pltpu.VMEM((DM, 2 * ROWS), BF),
            pltpu.VMEM((CHUNKS, ROWS, DM), F32),
            pltpu.VMEM((ROWS, DM), BF),
            pltpu.VMEM((ROWS, DM), BF),
            pltpu.VMEM((2, 2, HALF, DM), BF),
            pltpu.VMEM((2, 2, HALF, DM), BF),
            pltpu.VMEM((2, 2, ROWS, DM), BF),
            pltpu.VMEM((2, 2, ROWS, DM), BF),
            dma((12, CHUNKS)),
            dma((12, CHUNKS)),
            dma((CHUNKS, 2)),
            dma((CHUNKS, 2)),
            dma((5, 4)),
            dma((5, 4)),
            dma((3,)),
        ],
        compiler_params=pltpu.CompilerParams(
            collective_id=0, has_side_effects=True, vmem_limit_bytes=62 * 1024 * 1024
        ),
        cost_estimate=pl.CostEstimate(
            flops=16 * 2048 * DM * U, bytes_accessed=16 << 20, transcendentals=0
        ),
    )(tokens, grad_out, factor, w_gate, w_up, w_down)
    blocks = [pl.BlockSpec((o.shape[0] // PIECES, o.shape[1]), lambda i: (i, 0)) for o in outs]
    return pl.pallas_call(
        place,
        out_shape=tuple(jax.ShapeDtypeStruct(o.shape, o.dtype) for o in outs),
        grid=(PIECES,),
        in_specs=blocks,
        out_specs=blocks,
        compiler_params=pltpu.CompilerParams(vmem_limit_bytes=62 * 1024 * 1024),
    )(*outs)


def solution(mesh):
    placed = (
        P("wide", "mp"),
        P("wide", "mp"),
        P("wide"),
        P(),
        P("mp", "wide"),
        P("mp", "wide"),
        P("wide", "mp"),
    )
    return jax.shard_map(
        local,
        mesh=mesh,
        in_specs=placed,
        out_specs=(P("wide", "mp"), P("mp", "wide"), P("mp", "wide"), P("wide", "mp")),
        check_vma=False,
    )
```

```python
import jax
import jax.numpy as jnp
from jax import lax
from jax.experimental import pallas as pl
from jax.experimental.pallas import tpu as pltpu
from jax.sharding import PartitionSpec as P

BF = jnp.bfloat16
F32 = jnp.float32
ROWS = 256
HALF = 128
DM = 1024
U = 512
U3 = 3 * U
CHUNKS = 8
PIECES = 4
OWN, C1, F, YO, Y1, YF, Y2, C2 = range(CHUNKS)
B0, X1P, X1M, X2P, X2M, YB, H1, H2P, H2M, H3P, H3M, H4 = range(12)


def dot(a, b):
    return lax.dot_general(a, b, (((1,), (0,)), ((), ())), preferred_element_type=F32)


def kernel(
    tokens, grad_out, factor, w_gate, w_up, w_down,
    out_tok, out_gate, out_up, out_down,
    sum_gate, sum_up, sum_down, tg, wcat, wdt, part, b0_r, x1_s, x1_r, x2_s, x2_r, yb_s, yb_r, own16, hid, turned,
    to, dy_s, dy_r, zf_s, zf_r, dz_s, dz_r,
    c_ss, c_rs, a_ss, a_rs, d_ss, d_rs, o_s,
):
    mp, wide = lax.axis_index("mp"), lax.axis_index("wide")
    x, yh, c = mp // 4, (mp // 2) % 2, mp % 2
    z = wide // 2
    core = (mp + 1 - 2 * c, wide)
    xp = ((mp + 4) % 16, wide)
    xm = ((mp + 12) % 16, wide)
    yhp = (mp + 2 - 4 * yh, wide)
    ylp = (mp, wide + 1 - 2 * (wide % 2))
    zp = (mp, (wide + 2) % 8)
    zm = (mp, (wide + 6) % 8)

    def remote(src, dst, ssem, rsem, dev):
        return pltpu.make_async_remote_copy(
            src_ref=src, dst_ref=dst, send_sem=ssem, recv_sem=rsem,
            device_id=dev, device_id_type=pl.DeviceIdType.MESH,
        )

    barrier = pltpu.get_barrier_semaphore()
    for dev in (core, xp, xm, yhp, ylp, zp, zm):
        pl.semaphore_signal(barrier, inc=1, device_id=dev, device_id_type=pl.DeviceIdType.MESH)

    tg[0, OWN] = tokens[...]
    tg[1, OWN] = (grad_out[...].astype(F32) * factor[...]).astype(BF)
    pl.semaphore_wait(barrier, 7)

    def gather(src, dst, h, dev):
        rows = pl.ds(h * HALF, HALF)
        return remote(
            tg.at[:, src, rows], tg.at[:, dst, rows], a_ss.at[dst, h], a_rs.at[dst, h], dev
        )

    def arrived(dst, h):
        gather(OWN, dst, h, zp).wait_recv()

    gather(OWN, C1, 0, zp).start()
    gather(OWN, C1, 1, zm).start()
    gather(OWN, YO, 0, ylp).start()
    gather(OWN, YO, 1, ylp).start()

    for n in range(0, U, 256):
        wcat[n : n + 256, :] = w_gate[:, n : n + 256].T
        wcat[U + n : U + n + 256, :] = w_up[:, n : n + 256].T
        wdt[:, n : n + 256] = w_down[n : n + 256, :].T
    sum_gate[...] = jnp.zeros_like(sum_gate)
    sum_up[...] = jnp.zeros_like(sum_up)
    sum_down[...] = jnp.zeros_like(sum_down)

    def b0(i):
        rows = pl.ds(pl.multiple_of((1 - c) * HALF, HALF), HALF)
        return remote(part.at[i % 2, rows], b0_r.at[i], c_ss.at[B0, i], c_rs.at[B0, i], core)

    def x1(i, k):
        return remote(
            x1_s.at[i, k], x1_r.at[i, k], c_ss.at[X1P + k, i], c_rs.at[X1P + k, i], (xp, xm)[k]
        )

    def x2(i, k):
        return remote(
            x2_s.at[i, k], x2_r.at[i, k], c_ss.at[X2P + k, i], c_rs.at[X2P + k, i], (xp, xm)[k]
        )

    def yb(i):
        return remote(yb_s.at[i], yb_r.at[i], c_ss.at[YB, i], c_rs.at[YB, i], yhp)

    def same(i, first, count, sem, dev):
        rows = pl.ds(pl.multiple_of(first, 16), count)
        return remote(hid.at[i, rows], hid.at[i, rows], c_ss.at[sem, i], c_rs.at[sem, i], dev)

    mine = c * HALF + x * 32
    left = c * HALF + ((x + 3) % 4) * 32
    right = c * HALF + ((x + 1) % 4) * 32

    def h1(i):
        return same(i, mine + yh * 16, 16, H1, yhp)

    def h2(i, k):
        return same(i, mine, 32, H2P + k, (xp, xm)[k])

    def h3(i, k):
        return same(i, (left, right + 16)[k], 16, H3P + k, (xp, xm)[k])

    def h4(i):
        return same(i, c * HALF, HALF, H4, core)

    def summed(i, xd, h):
        at = xd * 32 + h * 16
        a = part[i % 2, pl.ds(pl.multiple_of(c * HALF + at, 16), 16), :]
        return a + b0_r[i, pl.ds(pl.multiple_of(at, 16), 16), :]

    def partial(i):
        s = i % 2
        for n in range(0, U, 256):
            part[s, :, n : n + 256] = dot(tg[0, i], w_gate[:, n : n + 256])
        for n in range(0, U, 256):
            part[s, :, U + n : U + n + 256] = dot(tg[0, i], w_up[:, n : n + 256])
        for n in range(0, U, 256):
            part[s, :, 2 * U + n : 2 * U + n + 256] = dot(tg[1, i], wdt[:, n : n + 256])
        b0(i).start()

    def send_x1(i):
        b0(i).wait()
        x1_s[i, 0] = summed(i, (x + 2) % 4, 0).astype(BF)
        x1(i, 0).start()
        x1_s[i, 1] = summed(i, (x + 2) % 4, 1).astype(BF)
        x1(i, 1).start()

    def send_x2(i):
        x1(i, 0).wait_recv()
        x2_s[i, 0, :16] = (summed(i, (x + 1) % 4, 0) + x1_r[i, 0].astype(F32)).astype(BF)
        x2_s[i, 0, 16:] = summed(i, (x + 1) % 4, 1).astype(BF)
        x2(i, 0).start()
        x1(i, 1).wait_recv()
        x2_s[i, 1, :16] = summed(i, (x + 3) % 4, 0).astype(BF)
        x2_s[i, 1, 16:] = (summed(i, (x + 3) % 4, 1) + x1_r[i, 1].astype(F32)).astype(BF)
        x2(i, 1).start()

    def send_yb(i):
        x2(i, 0).wait_recv()
        x2(i, 1).wait_recv()

        def total(h):
            at = pl.ds(pl.multiple_of(h * 16, 16), 16)
            return summed(i, x, h) + x2_r[i, 0, at].astype(F32) + x2_r[i, 1, at].astype(F32)

        yb_s[i] = total(1 - yh).astype(BF)
        yb(i).start()
        own16[i % 2] = total(yh)

    def send_h1(i):
        yb(i).wait_recv()
        full = own16[i % 2] + yb_r[i].astype(F32)
        gate, up, back = full[:, :U], full[:, U : 2 * U], full[:, 2 * U :]
        sigma = 1.0 / (1.0 + jnp.exp(-gate))
        silu = gate * sigma
        rows = pl.ds(pl.multiple_of(mine + yh * 16, 16), 16)
        hid[i, rows, :U] = (silu * up).astype(BF)
        hid[i, rows, U : 2 * U] = (back * up * sigma * (1.0 + gate * (1.0 - sigma))).astype(BF)
        hid[i, rows, 2 * U :] = (back * silu).astype(BF)
        h1(i).start()

    def send_h2(i):
        h1(i).wait_recv()
        h2(i, 0).start()
        h2(i, 1).start()

    def send_h3(i):
        h2(i, 0).wait_recv()
        h3(i, 0).start()
        h2(i, 1).wait_recv()
        h3(i, 1).start()

    def send_h4(i):
        h3(i, 0).wait_recv()
        h3(i, 1).wait_recv()
        h4(i).start()

    def grads_in(g):
        tok = tg[0, pl.ds(g - 1, 2)].reshape(2 * ROWS, DM)
        for d in range(0, DM, 256):
            turned[d : d + 256, :] = tok[:, d : d + 256].T
        for sums, u in ((sum_gate, U), (sum_up, 2 * U)):
            for n in range(0, U, 256):
                h = hid[pl.ds(g - 1, 2), :, u + n : u + n + 256].reshape(2 * ROWS, 256)
                sums[:, n : n + 256] += dot(turned[...], h)

    def grads_down(g):
        h = hid[pl.ds(g - 1, 2), :, :U].reshape(2 * ROWS, U)
        for u in range(0, U, 256):
            turned[u : u + 256, :] = h[:, u : u + 256].T
        for n in range(0, DM, 256):
            sc = tg[1, pl.ds(g - 1, 2), :, n : n + 256].reshape(2 * ROWS, 256)
            sum_down[:, n : n + 256] += dot(turned[:U], sc)

    def zf(col, h):
        sem = 2 * col
        return remote(
            zf_s.at[col, h], zf_r.at[col, h], d_ss.at[sem, h], d_rs.at[sem, h], (zm, zp)[h]
        )

    def dz(col, k, h):
        rows = pl.ds(h * HALF, HALF)
        sem = 2 * col + 1
        return remote(
            dz_s.at[col, k, rows], dz_r.at[col, k, rows],
            d_ss.at[sem, 2 * k + h], d_rs.at[sem, 2 * k + h], (zp, zm)[(h + 1 + k) % 2],
        )

    def dy(h):
        rows = pl.ds(h * HALF, HALF)
        return remote(dy_s.at[rows], dy_r.at[rows], d_ss.at[4, h], d_rs.at[4, h], ylp)

    def send_zf(col):
        for h in (0, 1):
            zf_s[col, h] = to[(F, YF)[col], pl.ds(h * HALF, HALF)].astype(BF)
            zf(col, h).start()

    def send_dz(col, k):
        for h in (0, 1):
            rows = pl.ds(h * HALF, HALF)
            total = to[((C1, C2), (Y1, Y2))[col][k], rows]
            if k == 0:
                zf(col, h).wait_recv()
                total = total + zf_r[col, h].astype(F32)
            dz_s[col, k, rows] = total.astype(BF)
            dz(col, k, h).start()

    def column(col, h):
        rows = pl.ds(h * HALF, HALF)
        dz(col, 0, h).wait_recv()
        dz(col, 1, h).wait_recv()
        return to[(OWN, YO)[col], rows] + (
            dz_r[col, 0, rows].astype(F32) + dz_r[col, 1, rows].astype(F32)
        )

    def term(j):
        h4(j).wait_recv()
        for n in range(0, DM, 256):
            to[j, :, n : n + 256] = dot(hid[j, :, U:], wcat[:, n : n + 256])

    def arrivals(t):
        @pl.when(t == C1)
        def _():
            arrived(C1, 0)
            gather(C1, F, 0, zp).start()
            arrived(C1, 1)
            gather(C1, F, 1, zm).start()

        @pl.when(t == F)
        def _():
            arrived(YO, 0)
            gather(YO, Y1, 0, zp).start()
            arrived(YO, 1)
            gather(YO, Y1, 1, zm).start()
            arrived(F, 0)
            arrived(F, 1)

        @pl.when(t == Y1)
        def _():
            arrived(Y1, 0)
            gather(Y1, YF, 0, zp).start()
            arrived(Y1, 1)
            gather(Y1, YF, 1, zm).start()

        @pl.when(t == YF)
        def _():
            arrived(YF, 0)
            arrived(YF, 1)

        @pl.when(t == Y2)
        def _():
            arrived(Y2, 0)
            arrived(Y2, 1)

        @pl.when(t == C2)
        def _():
            arrived(C2, 0)
            arrived(C2, 1)

    def tick(t, carry):
        def stage(step, lag):
            pl.when((t >= lag) & (t < CHUNKS + lag))(lambda: step(t - lag))

        stage(send_yb, 2)
        stage(send_h3, 4)
        arrivals(t)
        stage(partial, 0)

        stage(send_x2, 1)
        stage(send_h2, 3)
        stage(term, 5)

        @pl.when(t == YF + 5)
        def _():
            send_zf(1)

        @pl.when(t == Y2 + 5)
        def _():
            send_dz(1, 1)
            send_dz(1, 0)

        @pl.when(t == C2 + 5)
        def _():
            send_dz(0, 1)
            for h in (0, 1):
                dy_s[pl.ds(h * HALF, HALF)] = column(1, h).astype(BF)
                dy(h).start()

        stage(send_h1, 2)
        stage(send_h4, 4)
        stage(send_x1, 0)

        @pl.when(t == Y1)
        def _():
            gather(YO, Y2, 1, zp).start()
            gather(YO, Y2, 0, zm).start()

        @pl.when(t == YF)
        def _():
            gather(OWN, C2, 1, zp).start()
            gather(OWN, C2, 0, zm).start()

        @pl.when(t == F + 5)
        def _():
            send_zf(0)

        @pl.when(t == F + 6)
        def _():
            send_dz(0, 0)

        pl.when((t >= 6) & (t % 2 == 0))(lambda: grads_in(t - 5))
        pl.when((t >= 7) & (t % 2 == 1))(lambda: grads_down(t - 6))
        return carry

    lax.fori_loop(0, CHUNKS + 5, tick, 0)

    sums = ((sum_gate, out_gate), (sum_up, out_up), (sum_down, out_down))
    stores = [pltpu.make_async_copy(a, b, o_s.at[k]) for k, (a, b) in enumerate(sums)]
    stores[0].start()
    stores[1].start()
    grads_down(CHUNKS - 1)
    stores[2].start()
    for h in (0, 1):
        rows = pl.ds(h * HALF, HALF)
        total = column(0, h)
        dy(h).wait_recv()
        out_tok[rows] = (total + dy_r[rows].astype(F32)).astype(BF)

    for store in stores:
        store.wait()

    def left_all(i, carry):
        for k in (0, 1):
            x1(i, k).wait_send()
            x2(i, k).wait_send()
            h2(i, k).wait_send()
            h3(i, k).wait_send()
        yb(i).wait_send()
        h1(i).wait_send()
        h4(i).wait_send()
        return carry

    lax.fori_loop(0, CHUNKS, left_all, 0)
    for dst in range(1, CHUNKS):
        for h in (0, 1):
            gather(OWN, dst, h, zp).wait_send()
    for h in (0, 1):
        for col in (0, 1):
            zf(col, h).wait_send()
            dz(col, 0, h).wait_send()
            dz(col, 1, h).wait_send()
        dy(h).wait_send()


def place(*refs):
    ins, outs, by_way, sems = refs[:4], refs[4:8], refs[8:12], refs[12]
    reads, writes = [], []
    for k, (a, b, v) in enumerate(zip(ins, outs, by_way)):
        count = a.shape[0] // PIECES
        for p in range(PIECES):
            rows = pl.ds(p * count, count)
            reads.append(pltpu.make_async_copy(a.at[rows], v.at[rows], sems.at[0, k, p]))
            writes.append(pltpu.make_async_copy(v.at[rows], b.at[rows], sems.at[1, k, p]))
    for copy in reads:
        copy.start()
    for read, write in zip(reads, writes):
        read.wait()
        write.start()
    for copy in writes:
        copy.wait()


def local(tokens, grad_out, keep, count, w_gate, w_up, w_down):
    factor = (keep.astype(F32) / count[0].astype(F32))[:, None]
    vmem = pl.BlockSpec(memory_space=pltpu.VMEM)
    dma = pltpu.SemaphoreType.DMA
    outs = pl.pallas_call(
        kernel,
        out_shape=(
            jax.ShapeDtypeStruct((ROWS, DM), BF),
            jax.ShapeDtypeStruct((DM, U), F32),
            jax.ShapeDtypeStruct((DM, U), F32),
            jax.ShapeDtypeStruct((U, DM), F32),
        ),
        in_specs=[vmem] * 6,
        out_specs=[vmem] + [pl.BlockSpec(memory_space=pl.ANY)] * 3,
        scratch_shapes=[
            pltpu.VMEM((DM, U), F32),
            pltpu.VMEM((DM, U), F32),
            pltpu.VMEM((U, DM), F32),
            pltpu.VMEM((2, CHUNKS, ROWS, DM), BF),
            pltpu.VMEM((2 * U, DM), BF),
            pltpu.VMEM((DM, U), BF),
            pltpu.VMEM((2, ROWS, U3), F32),
            pltpu.VMEM((CHUNKS, HALF, U3), F32),
            pltpu.VMEM((CHUNKS, 2, 16, U3), BF),
            pltpu.VMEM((CHUNKS, 2, 16, U3), BF),
            pltpu.VMEM((CHUNKS, 2, 32, U3), BF),
            pltpu.VMEM((CHUNKS, 2, 32, U3), BF),
            pltpu.VMEM((CHUNKS, 16, U3), BF),
            pltpu.VMEM((CHUNKS, 16, U3), BF),
            pltpu.VMEM((2, 16, U3), F32),
            pltpu.VMEM((CHUNKS, ROWS, U3), BF),
            pltpu.VMEM((DM, 2 * ROWS), BF),
            pltpu.VMEM((CHUNKS, ROWS, DM), F32),
            pltpu.VMEM((ROWS, DM), BF),
            pltpu.VMEM((ROWS, DM), BF),
            pltpu.VMEM((2, 2, HALF, DM), BF),
            pltpu.VMEM((2, 2, HALF, DM), BF),
            pltpu.VMEM((2, 2, ROWS, DM), BF),
            pltpu.VMEM((2, 2, ROWS, DM), BF),
            dma((12, CHUNKS)),
            dma((12, CHUNKS)),
            dma((CHUNKS, 2)),
            dma((CHUNKS, 2)),
            dma((5, 4)),
            dma((5, 4)),
            dma((3,)),
        ],
        compiler_params=pltpu.CompilerParams(
            collective_id=0, has_side_effects=True, vmem_limit_bytes=62 * 1024 * 1024
        ),
        cost_estimate=pl.CostEstimate(
            flops=16 * 2048 * DM * U, bytes_accessed=16 << 20, transcendentals=0
        ),
    )(tokens, grad_out, factor, w_gate, w_up, w_down)
    anywhere = pl.BlockSpec(memory_space=pl.ANY)
    return pl.pallas_call(
        place,
        out_shape=tuple(jax.ShapeDtypeStruct(o.shape, o.dtype) for o in outs),
        in_specs=[anywhere] * 4,
        out_specs=[anywhere] * 4,
        scratch_shapes=[pltpu.VMEM(o.shape, o.dtype) for o in outs] + [dma((2, 4, PIECES))],
        compiler_params=pltpu.CompilerParams(vmem_limit_bytes=62 * 1024 * 1024),
    )(*outs)


def solution(mesh):
    placed = (
        P("wide", "mp"),
        P("wide", "mp"),
        P("wide"),
        P(),
        P("mp", "wide"),
        P("mp", "wide"),
        P("wide", "mp"),
    )
    return jax.shard_map(
        local,
        mesh=mesh,
        in_specs=placed,
        out_specs=(P("wide", "mp"), P("mp", "wide"), P("mp", "wide"), P("wide", "mp")),
        check_vma=False,
    )
```

```python
import jax
import jax.numpy as jnp
from jax import lax
from jax.experimental import pallas as pl
from jax.experimental.pallas import tpu as pltpu
from jax.sharding import PartitionSpec as P

BF = jnp.bfloat16
F32 = jnp.float32
ROWS = 256
HALF = 128
DM = 1024
U = 512
U3 = 3 * U
CHUNKS = 8
PIECES = 4
OWN, C1, F, YO, Y1, YF, Y2, C2 = range(CHUNKS)
B0, X1P, X1M, X2P, X2M, YB, H1, H2P, H2M, H3P, H3M, H4 = range(12)


def dot(a, b):
    return lax.dot_general(a, b, (((1,), (0,)), ((), ())), preferred_element_type=F32)


def kernel(
    tokens, grad_out, keep, count, w_gate, w_up, w_down,
    out_tok, out_gate, out_up, out_down,
    sum_gate, sum_up, sum_down, tg, wcat, wdt, part, b0_r, x1_s, x1_r, x2_s, x2_r, yb_s, yb_r, own16, hid, turned,
    to, dy_s, dy_r, zf_s, zf_r, dz_s, dz_r,
    c_ss, c_rs, a_ss, a_rs, d_ss, d_rs, o_s,
):
    mp, wide = lax.axis_index("mp"), lax.axis_index("wide")
    x, yh, c = mp // 4, (mp // 2) % 2, mp % 2
    z = wide // 2
    core = (mp + 1 - 2 * c, wide)
    xp = ((mp + 4) % 16, wide)
    xm = ((mp + 12) % 16, wide)
    yhp = (mp + 2 - 4 * yh, wide)
    ylp = (mp, wide + 1 - 2 * (wide % 2))
    zp = (mp, (wide + 2) % 8)
    zm = (mp, (wide + 6) % 8)

    def remote(src, dst, ssem, rsem, dev):
        return pltpu.make_async_remote_copy(
            src_ref=src, dst_ref=dst, send_sem=ssem, recv_sem=rsem,
            device_id=dev, device_id_type=pl.DeviceIdType.MESH,
        )

    barrier = pltpu.get_barrier_semaphore()
    for dev in (core, xp, xm, yhp, ylp, zp, zm):
        pl.semaphore_signal(barrier, inc=1, device_id=dev, device_id_type=pl.DeviceIdType.MESH)

    tg[0, OWN] = tokens[...]
    for r in range(0, ROWS, 128):
        factor = keep[pl.ds(r, 128)].astype(F32) / count[0].astype(F32)
        factor = jnp.broadcast_to(factor[None, :], (128, 128)).T
        for n in range(0, DM, 128):
            block = grad_out[r : r + 128, n : n + 128].astype(F32) * factor
            tg[1, OWN, r : r + 128, n : n + 128] = block.astype(BF)
    pl.semaphore_wait(barrier, 7)

    def gather(src, dst, h, dev):
        rows = pl.ds(h * HALF, HALF)
        return remote(
            tg.at[:, src, rows], tg.at[:, dst, rows], a_ss.at[dst, h], a_rs.at[dst, h], dev
        )

    def arrived(dst, h):
        gather(OWN, dst, h, zp).wait_recv()

    gather(OWN, C1, 0, zp).start()
    gather(OWN, C1, 1, zm).start()
    gather(OWN, YO, 0, ylp).start()
    gather(OWN, YO, 1, ylp).start()

    for n in range(0, U, 256):
        wcat[n : n + 256, :] = w_gate[:, n : n + 256].T
        wcat[U + n : U + n + 256, :] = w_up[:, n : n + 256].T
        wdt[:, n : n + 256] = w_down[n : n + 256, :].T
    sum_gate[...] = jnp.zeros_like(sum_gate)
    sum_up[...] = jnp.zeros_like(sum_up)
    sum_down[...] = jnp.zeros_like(sum_down)

    def b0(i):
        rows = pl.ds(pl.multiple_of((1 - c) * HALF, HALF), HALF)
        return remote(part.at[i % 2, rows], b0_r.at[i], c_ss.at[B0, i], c_rs.at[B0, i], core)

    def x1(i, k):
        return remote(
            x1_s.at[i, k], x1_r.at[i, k], c_ss.at[X1P + k, i], c_rs.at[X1P + k, i], (xp, xm)[k]
        )

    def x2(i, k):
        return remote(
            x2_s.at[i, k], x2_r.at[i, k], c_ss.at[X2P + k, i], c_rs.at[X2P + k, i], (xp, xm)[k]
        )

    def yb(i):
        return remote(yb_s.at[i], yb_r.at[i], c_ss.at[YB, i], c_rs.at[YB, i], yhp)

    def same(i, first, count, sem, dev):
        rows = pl.ds(pl.multiple_of(first, 16), count)
        return remote(hid.at[i, rows], hid.at[i, rows], c_ss.at[sem, i], c_rs.at[sem, i], dev)

    mine = c * HALF + x * 32
    left = c * HALF + ((x + 3) % 4) * 32
    right = c * HALF + ((x + 1) % 4) * 32

    def h1(i):
        return same(i, mine + yh * 16, 16, H1, yhp)

    def h2(i, k):
        return same(i, mine, 32, H2P + k, (xp, xm)[k])

    def h3(i, k):
        return same(i, (left, right + 16)[k], 16, H3P + k, (xp, xm)[k])

    def h4(i):
        return same(i, c * HALF, HALF, H4, core)

    def summed(i, xd, h):
        at = xd * 32 + h * 16
        a = part[i % 2, pl.ds(pl.multiple_of(c * HALF + at, 16), 16), :]
        return a + b0_r[i, pl.ds(pl.multiple_of(at, 16), 16), :]

    def partial(i):
        s = i % 2
        for n in range(0, U, 256):
            part[s, :, n : n + 256] = dot(tg[0, i], w_gate[:, n : n + 256])
        for n in range(0, U, 256):
            part[s, :, U + n : U + n + 256] = dot(tg[0, i], w_up[:, n : n + 256])
        for n in range(0, U, 256):
            part[s, :, 2 * U + n : 2 * U + n + 256] = dot(tg[1, i], wdt[:, n : n + 256])
        b0(i).start()

    def send_x1(i):
        b0(i).wait()
        x1_s[i, 0] = summed(i, (x + 2) % 4, 0).astype(BF)
        x1(i, 0).start()
        x1_s[i, 1] = summed(i, (x + 2) % 4, 1).astype(BF)
        x1(i, 1).start()

    def send_x2(i):
        x1(i, 0).wait_recv()
        x2_s[i, 0, :16] = (summed(i, (x + 1) % 4, 0) + x1_r[i, 0].astype(F32)).astype(BF)
        x2_s[i, 0, 16:] = summed(i, (x + 1) % 4, 1).astype(BF)
        x2(i, 0).start()
        x1(i, 1).wait_recv()
        x2_s[i, 1, :16] = summed(i, (x + 3) % 4, 0).astype(BF)
        x2_s[i, 1, 16:] = (summed(i, (x + 3) % 4, 1) + x1_r[i, 1].astype(F32)).astype(BF)
        x2(i, 1).start()

    def send_yb(i):
        x2(i, 0).wait_recv()
        x2(i, 1).wait_recv()

        def total(h):
            at = pl.ds(pl.multiple_of(h * 16, 16), 16)
            return summed(i, x, h) + x2_r[i, 0, at].astype(F32) + x2_r[i, 1, at].astype(F32)

        yb_s[i] = total(1 - yh).astype(BF)
        yb(i).start()
        own16[i % 2] = total(yh)

    def send_h1(i):
        yb(i).wait_recv()
        full = own16[i % 2] + yb_r[i].astype(F32)
        gate, up, back = full[:, :U], full[:, U : 2 * U], full[:, 2 * U :]
        sigma = 1.0 / (1.0 + jnp.exp(-gate))
        silu = gate * sigma
        rows = pl.ds(pl.multiple_of(mine + yh * 16, 16), 16)
        hid[i, rows, :U] = (silu * up).astype(BF)
        hid[i, rows, U : 2 * U] = (back * up * sigma * (1.0 + gate * (1.0 - sigma))).astype(BF)
        hid[i, rows, 2 * U :] = (back * silu).astype(BF)
        h1(i).start()

    def send_h2(i):
        h1(i).wait_recv()
        h2(i, 0).start()
        h2(i, 1).start()

    def send_h3(i):
        h2(i, 0).wait_recv()
        h3(i, 0).start()
        h2(i, 1).wait_recv()
        h3(i, 1).start()

    def send_h4(i):
        h3(i, 0).wait_recv()
        h3(i, 1).wait_recv()
        h4(i).start()

    def grads_in(g):
        tok = tg[0, pl.ds(g - 1, 2)].reshape(2 * ROWS, DM)
        for d in range(0, DM, 256):
            turned[d : d + 256, :] = tok[:, d : d + 256].T
        for sums, u in ((sum_gate, U), (sum_up, 2 * U)):
            for n in range(0, U, 256):
                h = hid[pl.ds(g - 1, 2), :, u + n : u + n + 256].reshape(2 * ROWS, 256)
                sums[:, n : n + 256] += dot(turned[...], h)

    def grads_down(g):
        h = hid[pl.ds(g - 1, 2), :, :U].reshape(2 * ROWS, U)
        for u in range(0, U, 256):
            turned[u : u + 256, :] = h[:, u : u + 256].T
        for n in range(0, DM, 256):
            sc = tg[1, pl.ds(g - 1, 2), :, n : n + 256].reshape(2 * ROWS, 256)
            sum_down[:, n : n + 256] += dot(turned[:U], sc)

    def zf(col, h):
        sem = 2 * col
        return remote(
            zf_s.at[col, h], zf_r.at[col, h], d_ss.at[sem, h], d_rs.at[sem, h], (zm, zp)[h]
        )

    def dz(col, k, h):
        rows = pl.ds(h * HALF, HALF)
        sem = 2 * col + 1
        return remote(
            dz_s.at[col, k, rows], dz_r.at[col, k, rows],
            d_ss.at[sem, 2 * k + h], d_rs.at[sem, 2 * k + h], (zp, zm)[(h + 1 + k) % 2],
        )

    def dy(h):
        rows = pl.ds(h * HALF, HALF)
        return remote(dy_s.at[rows], dy_r.at[rows], d_ss.at[4, h], d_rs.at[4, h], ylp)

    def send_zf(col):
        for h in (0, 1):
            zf_s[col, h] = to[(F, YF)[col], pl.ds(h * HALF, HALF)].astype(BF)
            zf(col, h).start()

    def send_dz(col, k):
        for h in (0, 1):
            rows = pl.ds(h * HALF, HALF)
            total = to[((C1, C2), (Y1, Y2))[col][k], rows]
            if k == 0:
                zf(col, h).wait_recv()
                total = total + zf_r[col, h].astype(F32)
            dz_s[col, k, rows] = total.astype(BF)
            dz(col, k, h).start()

    def column(col, h):
        rows = pl.ds(h * HALF, HALF)
        dz(col, 0, h).wait_recv()
        dz(col, 1, h).wait_recv()
        return to[(OWN, YO)[col], rows] + (
            dz_r[col, 0, rows].astype(F32) + dz_r[col, 1, rows].astype(F32)
        )

    def term(j):
        h4(j).wait_recv()
        for n in range(0, DM, 256):
            to[j, :, n : n + 256] = dot(hid[j, :, U:], wcat[:, n : n + 256])

    def arrivals(t):
        @pl.when(t == C1)
        def _():
            arrived(C1, 0)
            gather(C1, F, 0, zp).start()
            arrived(C1, 1)
            gather(C1, F, 1, zm).start()

        @pl.when(t == F)
        def _():
            arrived(YO, 0)
            gather(YO, Y1, 0, zp).start()
            arrived(YO, 1)
            gather(YO, Y1, 1, zm).start()
            arrived(F, 0)
            gather(F, YF, 0, ylp).start()
            arrived(F, 1)

        @pl.when(t == YO)
        def _():
            gather(F, YF, 1, ylp).start()

        @pl.when(t == Y1)
        def _():
            arrived(Y1, 0)
            arrived(Y1, 1)

        @pl.when(t == YF)
        def _():
            arrived(YF, 0)
            arrived(YF, 1)

        @pl.when(t == Y2)
        def _():
            arrived(Y2, 0)
            arrived(Y2, 1)

        @pl.when(t == C2)
        def _():
            arrived(C2, 0)
            arrived(C2, 1)

    def tick(t, carry):
        def stage(step, lag):
            pl.when((t >= lag) & (t < CHUNKS + lag))(lambda: step(t - lag))

        stage(send_yb, 2)
        stage(send_h3, 4)
        arrivals(t)
        stage(partial, 0)

        stage(send_x2, 1)
        stage(send_h2, 3)
        stage(term, 5)

        @pl.when(t == YO)
        def _():
            gather(YO, Y2, 1, zp).start()
            gather(YO, Y2, 0, zm).start()

        @pl.when(t == Y1)
        def _():
            gather(OWN, C2, 1, zp).start()
            gather(OWN, C2, 0, zm).start()

        @pl.when(t == YF + 5)
        def _():
            send_zf(1)

        @pl.when(t == Y2 + 5)
        def _():
            send_dz(1, 1)
            send_dz(1, 0)

        @pl.when(t == C2 + 5)
        def _():
            send_dz(0, 1)
            for h in (0, 1):
                dy_s[pl.ds(h * HALF, HALF)] = column(1, h).astype(BF)
                dy(h).start()

        stage(send_h1, 2)
        stage(send_h4, 4)
        stage(send_x1, 0)

        @pl.when(t == F + 5)
        def _():
            send_zf(0)

        @pl.when(t == F + 6)
        def _():
            send_dz(0, 0)

        pl.when((t >= 6) & (t % 2 == 0))(lambda: grads_in(t - 5))
        pl.when((t >= 7) & (t % 2 == 1))(lambda: grads_down(t - 6))
        return carry

    lax.fori_loop(0, CHUNKS + 5, tick, 0)

    sums = ((sum_gate, out_gate), (sum_up, out_up), (sum_down, out_down))
    stores = [pltpu.make_async_copy(a, b, o_s.at[k]) for k, (a, b) in enumerate(sums)]
    stores[0].start()
    stores[1].start()
    grads_down(CHUNKS - 1)
    stores[2].start()
    for h in (0, 1):
        rows = pl.ds(h * HALF, HALF)
        total = column(0, h)
        dy(h).wait_recv()
        out_tok[rows] = (total + dy_r[rows].astype(F32)).astype(BF)

    for store in stores:
        store.wait()

    def left_all(i, carry):
        for k in (0, 1):
            x1(i, k).wait_send()
            x2(i, k).wait_send()
            h2(i, k).wait_send()
            h3(i, k).wait_send()
        yb(i).wait_send()
        h1(i).wait_send()
        h4(i).wait_send()
        return carry

    lax.fori_loop(0, CHUNKS, left_all, 0)
    for dst in range(1, CHUNKS):
        for h in (0, 1):
            gather(OWN, dst, h, zp).wait_send()
    for h in (0, 1):
        for col in (0, 1):
            zf(col, h).wait_send()
            dz(col, 0, h).wait_send()
            dz(col, 1, h).wait_send()
        dy(h).wait_send()


def place(*refs):
    ins, outs, by_way, sems = refs[:4], refs[4:8], refs[8:12], refs[12]
    reads, writes = [], []
    for k, (a, b, v) in enumerate(zip(ins, outs, by_way)):
        count = a.shape[0] // PIECES
        for p in range(PIECES):
            rows = pl.ds(p * count, count)
            reads.append(pltpu.make_async_copy(a.at[rows], v.at[rows], sems.at[0, k, p]))
            writes.append(pltpu.make_async_copy(v.at[rows], b.at[rows], sems.at[1, k, p]))
    for copy in reads:
        copy.start()
    for read, write in zip(reads, writes):
        read.wait()
        write.start()
    for copy in writes:
        copy.wait()


def local(tokens, grad_out, keep, count, w_gate, w_up, w_down):
    vmem = pl.BlockSpec(memory_space=pltpu.VMEM)
    dma = pltpu.SemaphoreType.DMA
    outs = pl.pallas_call(
        kernel,
        out_shape=(
            jax.ShapeDtypeStruct((ROWS, DM), BF),
            jax.ShapeDtypeStruct((DM, U), F32),
            jax.ShapeDtypeStruct((DM, U), F32),
            jax.ShapeDtypeStruct((U, DM), F32),
        ),
        in_specs=[vmem] * 3 + [pl.BlockSpec(memory_space=pltpu.SMEM)] + [vmem] * 3,
        out_specs=[vmem] + [pl.BlockSpec(memory_space=pl.ANY)] * 3,
        scratch_shapes=[
            pltpu.VMEM((DM, U), F32),
            pltpu.VMEM((DM, U), F32),
            pltpu.VMEM((U, DM), F32),
            pltpu.VMEM((2, CHUNKS, ROWS, DM), BF),
            pltpu.VMEM((2 * U, DM), BF),
            pltpu.VMEM((DM, U), BF),
            pltpu.VMEM((2, ROWS, U3), F32),
            pltpu.VMEM((CHUNKS, HALF, U3), F32),
            pltpu.VMEM((CHUNKS, 2, 16, U3), BF),
            pltpu.VMEM((CHUNKS, 2, 16, U3), BF),
            pltpu.VMEM((CHUNKS, 2, 32, U3), BF),
            pltpu.VMEM((CHUNKS, 2, 32, U3), BF),
            pltpu.VMEM((CHUNKS, 16, U3), BF),
            pltpu.VMEM((CHUNKS, 16, U3), BF),
            pltpu.VMEM((2, 16, U3), F32),
            pltpu.VMEM((CHUNKS, ROWS, U3), BF),
            pltpu.VMEM((DM, 2 * ROWS), BF),
            pltpu.VMEM((CHUNKS, ROWS, DM), F32),
            pltpu.VMEM((ROWS, DM), BF),
            pltpu.VMEM((ROWS, DM), BF),
            pltpu.VMEM((2, 2, HALF, DM), BF),
            pltpu.VMEM((2, 2, HALF, DM), BF),
            pltpu.VMEM((2, 2, ROWS, DM), BF),
            pltpu.VMEM((2, 2, ROWS, DM), BF),
            dma((12, CHUNKS)),
            dma((12, CHUNKS)),
            dma((CHUNKS, 2)),
            dma((CHUNKS, 2)),
            dma((5, 4)),
            dma((5, 4)),
            dma((3,)),
        ],
        compiler_params=pltpu.CompilerParams(
            collective_id=0, has_side_effects=True, vmem_limit_bytes=62 * 1024 * 1024
        ),
        cost_estimate=pl.CostEstimate(
            flops=16 * 2048 * DM * U, bytes_accessed=16 << 20, transcendentals=0
        ),
    )(tokens, grad_out, keep, count, w_gate, w_up, w_down)
    anywhere = pl.BlockSpec(memory_space=pl.ANY)
    return pl.pallas_call(
        place,
        out_shape=tuple(jax.ShapeDtypeStruct(o.shape, o.dtype) for o in outs),
        in_specs=[anywhere] * 4,
        out_specs=[anywhere] * 4,
        scratch_shapes=[pltpu.VMEM(o.shape, o.dtype) for o in outs] + [dma((2, 4, PIECES))],
        compiler_params=pltpu.CompilerParams(vmem_limit_bytes=62 * 1024 * 1024),
    )(*outs)


def solution(mesh):
    placed = (
        P("wide", "mp"),
        P("wide", "mp"),
        P("wide"),
        P(),
        P("mp", "wide"),
        P("mp", "wide"),
        P("wide", "mp"),
    )
    return jax.shard_map(
        local,
        mesh=mesh,
        in_specs=placed,
        out_specs=(P("wide", "mp"), P("mp", "wide"), P("mp", "wide"), P("wide", "mp")),
        check_vma=False,
    )
```

```python
import functools

import jax
import jax.numpy as jnp
from jax import lax
from jax.experimental import pallas as pl
from jax.experimental.pallas import tpu as pltpu
from jax.sharding import PartitionSpec as P

BF = jnp.bfloat16
F32 = jnp.float32
ROWS = 256
HALF = 128
DM = 1024
U = 512
U3 = 3 * U
LEFT, RIGHT = 512, 512
CHUNKS = 8
PIECES = 4
OWN, C1, F, YO, Y1, YF, Y2, C2 = range(CHUNKS)
B0, X1P, X1M, X2P, X2M, YB, H1, H2P, H2M, H3P, H3M, H4 = range(12)


def dot(a, b):
    return lax.dot_general(a, b, (((1,), (0,)), ((), ())), preferred_element_type=F32)


def kernel(
    tokens, grad_out, keep, count, in_gate, in_up, in_down,
    out_tok, out_gate, out_up, out_down,
    w_gate, w_up, w_down, sum_gate, sum_up, sum_down, tg, wcat, wdt, part, b0_r, x1_s, x1_r, x2_s, x2_r, yb_s, yb_r, own16, hid, turned,
    to, dy_s, dy_r, zf_s, zf_r, dz_s, dz_r, dv_s, dv_r, zg_s, zg_r, dw_s, dw_r,
    c_ss, c_rs, a_ss, a_rs, d_ss, d_rs, o_s, i_s,
):
    mp, wide = lax.axis_index("mp"), lax.axis_index("wide")
    x, yh, c = mp // 4, (mp // 2) % 2, mp % 2
    z = wide // 2
    core = (mp + 1 - 2 * c, wide)
    xp = ((mp + 4) % 16, wide)
    xm = ((mp + 12) % 16, wide)
    yhp = (mp + 2 - 4 * yh, wide)
    ylp = (mp, wide + 1 - 2 * (wide % 2))
    zp = (mp, (wide + 2) % 8)
    zm = (mp, (wide + 6) % 8)

    def remote(src, dst, ssem, rsem, dev):
        return pltpu.make_async_remote_copy(
            src_ref=src, dst_ref=dst, send_sem=ssem, recv_sem=rsem,
            device_id=dev, device_id_type=pl.DeviceIdType.MESH,
        )

    loads = [
        pltpu.make_async_copy(a, b, i_s.at[k])
        for k, (a, b) in enumerate(
            ((tokens, tg.at[0, OWN]), (in_gate, w_gate), (in_up, w_up), (in_down, w_down))
        )
    ]
    for load in loads:
        load.start()

    barrier = pltpu.get_barrier_semaphore()
    for dev in (core, xp, xm, yhp, ylp, zp, zm):
        pl.semaphore_signal(barrier, inc=1, device_id=dev, device_id_type=pl.DeviceIdType.MESH)

    for r in range(0, ROWS, 128):
        factor = keep[pl.ds(r, 128)].astype(F32) / count[0].astype(F32)
        factor = jnp.broadcast_to(factor[None, :], (128, 128)).T
        for n in range(0, DM, 128):
            block = grad_out[r : r + 128, n : n + 128].astype(F32) * factor
            tg[1, OWN, r : r + 128, n : n + 128] = block.astype(BF)
    loads[0].wait()
    pl.semaphore_wait(barrier, 7)

    def gather(src, dst, h, dev):
        rows = pl.ds(h * HALF, HALF)
        return remote(
            tg.at[:, src, rows], tg.at[:, dst, rows], a_ss.at[dst, h], a_rs.at[dst, h], dev
        )

    def arrived(dst, h):
        gather(OWN, dst, h, zp).wait_recv()

    gather(OWN, C1, 0, zp).start()
    gather(OWN, C1, 1, zm).start()
    gather(OWN, YO, 0, ylp).start()
    gather(OWN, YO, 1, ylp).start()

    for load in loads[1:]:
        load.wait()
    for n in range(0, U, 256):
        wcat[n : n + 256, :] = w_gate[:, n : n + 256].T
        wcat[U + n : U + n + 256, :] = w_up[:, n : n + 256].T
        wdt[:, n : n + 256] = w_down[n : n + 256, :].T
    sum_gate[...] = jnp.zeros_like(sum_gate)
    sum_up[...] = jnp.zeros_like(sum_up)
    sum_down[...] = jnp.zeros_like(sum_down)

    def b0(i):
        rows = pl.ds(pl.multiple_of((1 - c) * HALF, HALF), HALF)
        return remote(part.at[i % 2, rows], b0_r.at[i], c_ss.at[B0, i], c_rs.at[B0, i], core)

    def x1(i, k):
        return remote(
            x1_s.at[i, k], x1_r.at[i, k], c_ss.at[X1P + k, i], c_rs.at[X1P + k, i], (xp, xm)[k]
        )

    def x2(i, k):
        return remote(
            x2_s.at[i, k], x2_r.at[i, k], c_ss.at[X2P + k, i], c_rs.at[X2P + k, i], (xp, xm)[k]
        )

    def yb(i):
        return remote(yb_s.at[i], yb_r.at[i], c_ss.at[YB, i], c_rs.at[YB, i], yhp)

    def same(i, first, count, sem, dev):
        rows = pl.ds(pl.multiple_of(first, 16), count)
        return remote(hid.at[i, rows], hid.at[i, rows], c_ss.at[sem, i], c_rs.at[sem, i], dev)

    mine = c * HALF + x * 32
    left = c * HALF + ((x + 3) % 4) * 32
    right = c * HALF + ((x + 1) % 4) * 32

    def h1(i):
        return same(i, mine + yh * 16, 16, H1, yhp)

    def h2(i, k):
        return same(i, mine, 32, H2P + k, (xp, xm)[k])

    def h3(i, k):
        return same(i, (left, right + 16)[k], 16, H3P + k, (xp, xm)[k])

    def h4(i):
        return same(i, c * HALF, HALF, H4, core)

    def summed(i, xd, h):
        at = xd * 32 + h * 16
        a = part[i % 2, pl.ds(pl.multiple_of(c * HALF + at, 16), 16), :]
        return a + b0_r[i, pl.ds(pl.multiple_of(at, 16), 16), :]

    def partial(i):
        s = i % 2
        for n in range(0, U, 256):
            part[s, :, n : n + 256] = dot(tg[0, i], w_gate[:, n : n + 256])
        for n in range(0, U, 256):
            part[s, :, U + n : U + n + 256] = dot(tg[0, i], w_up[:, n : n + 256])
        for n in range(0, U, 256):
            part[s, :, 2 * U + n : 2 * U + n + 256] = dot(tg[1, i], wdt[:, n : n + 256])
        b0(i).start()

    def send_x1(i):
        b0(i).wait()
        x1_s[i, 0] = summed(i, (x + 2) % 4, 0).astype(BF)
        x1(i, 0).start()
        x1_s[i, 1] = summed(i, (x + 2) % 4, 1).astype(BF)
        x1(i, 1).start()

    def send_x2(i):
        x1(i, 0).wait_recv()
        x2_s[i, 0, :16] = (summed(i, (x + 1) % 4, 0) + x1_r[i, 0].astype(F32)).astype(BF)
        x2_s[i, 0, 16:] = summed(i, (x + 1) % 4, 1).astype(BF)
        x2(i, 0).start()
        x1(i, 1).wait_recv()
        x2_s[i, 1, :16] = summed(i, (x + 3) % 4, 0).astype(BF)
        x2_s[i, 1, 16:] = (summed(i, (x + 3) % 4, 1) + x1_r[i, 1].astype(F32)).astype(BF)
        x2(i, 1).start()

    def send_yb(i):
        x2(i, 0).wait_recv()
        x2(i, 1).wait_recv()

        def total(h):
            at = pl.ds(pl.multiple_of(h * 16, 16), 16)
            return summed(i, x, h) + x2_r[i, 0, at].astype(F32) + x2_r[i, 1, at].astype(F32)

        yb_s[i] = total(1 - yh).astype(BF)
        yb(i).start()
        own16[i % 2] = total(yh)

    def send_h1(i):
        yb(i).wait_recv()
        full = own16[i % 2] + yb_r[i].astype(F32)
        gate, up, back = full[:, :U], full[:, U : 2 * U], full[:, 2 * U :]
        sigma = 1.0 / (1.0 + jnp.exp(-gate))
        silu = gate * sigma
        rows = pl.ds(pl.multiple_of(mine + yh * 16, 16), 16)
        hid[i, rows, :U] = (silu * up).astype(BF)
        hid[i, rows, U : 2 * U] = (back * up * sigma * (1.0 + gate * (1.0 - sigma))).astype(BF)
        hid[i, rows, 2 * U :] = (back * silu).astype(BF)
        h1(i).start()

    def send_h2(i):
        h1(i).wait_recv()
        h2(i, 0).start()
        h2(i, 1).start()

    def send_h3(i):
        h2(i, 0).wait_recv()
        h3(i, 0).start()
        h2(i, 1).wait_recv()
        h3(i, 1).start()

    def send_h4(i):
        h3(i, 0).wait_recv()
        h3(i, 1).wait_recv()
        h4(i).start()

    def grads_in(g):
        tok = tg[0, pl.ds(g - 1, 2)].reshape(2 * ROWS, DM)
        for d in range(0, DM, 256):
            turned[d : d + 256, :] = tok[:, d : d + 256].T
        for sums, u in ((sum_gate, U), (sum_up, 2 * U)):
            for n in range(0, U, 256):
                h = hid[pl.ds(g - 1, 2), :, u + n : u + n + 256].reshape(2 * ROWS, 256)
                sums[:, n : n + 256] += dot(turned[...], h)

    def grads_down(g):
        h = hid[pl.ds(g - 1, 2), :, :U].reshape(2 * ROWS, U)
        for u in range(0, U, 256):
            turned[u : u + 256, :] = h[:, u : u + 256].T
        for n in range(0, DM, 256):
            sc = tg[1, pl.ds(g - 1, 2), :, n : n + 256].reshape(2 * ROWS, 256)
            sum_down[:, n : n + 256] += dot(turned[:U], sc)

    def zf(col, h):
        return remote(
            zf_s.at[col, h], zf_r.at[col, h], d_ss.at[2 * col, h], d_rs.at[2 * col, h], (zm, zp)[h]
        )

    def zf_right(h):
        return remote(zg_s.at[h], zg_r.at[h], d_ss.at[0, 2 + h], d_rs.at[0, 2 + h], (zm, zp)[h])

    def dz(col, k, h):
        rows = pl.ds(h * HALF, HALF)
        sem = 2 * col + 1
        return remote(
            dz_s.at[col, k, rows], dz_r.at[col, k, rows],
            d_ss.at[sem, 2 * k + h], d_rs.at[sem, 2 * k + h], (zp, zm)[(h + 1 + k) % 2],
        )

    def dz_right(k, h):
        rows = pl.ds(h * HALF, HALF)
        return remote(
            dw_s.at[k, rows], dw_r.at[k, rows],
            d_ss.at[4, 2 * k + h], d_rs.at[4, 2 * k + h], (zp, zm)[(h + 1 + k) % 2],
        )

    def dy(h):
        rows = pl.ds(h * HALF, HALF)
        return remote(dy_s.at[rows], dy_r.at[rows], d_ss.at[2, 2 + h], d_rs.at[2, 2 + h], ylp)

    def dy_right(k, h):
        rows = pl.ds(h * HALF, HALF)
        return remote(
            dv_s.at[k, rows], dv_r.at[k, rows], d_ss.at[5 + h, k], d_rs.at[5 + h, k], ylp
        )

    def send_zf(col):
        for h in (0, 1):
            zf_s[col, h] = to[(F, YF)[col], pl.ds(h * HALF, HALF), :LEFT].astype(BF)
            zf(col, h).start()

    def send_dz(col, k):
        for h in (0, 1):
            rows = pl.ds(h * HALF, HALF)
            total = to[((C1, C2), (Y1, Y2))[col][k], rows, :LEFT]
            if k == 0:
                zf(col, h).wait_recv()
                total = total + zf_r[col, h].astype(F32)
            dz_s[col, k, rows] = total.astype(BF)
            dz(col, k, h).start()

    def column(col, h):
        rows = pl.ds(h * HALF, HALF)
        dz(col, 0, h).wait_recv()
        dz(col, 1, h).wait_recv()
        return to[(OWN, YO)[col], rows, :LEFT] + (
            dz_r[col, 0, rows].astype(F32) + dz_r[col, 1, rows].astype(F32)
        )

    def send_dy_right(k):
        for h in (0, 1):
            rows = pl.ds(h * HALF, HALF)
            dv_s[k, rows] = to[(YO, Y1, YF, Y2)[k], rows, LEFT:].astype(BF)
            dy_right(k, h).start()

    def both_right(j, k, h):
        rows = pl.ds(h * HALF, HALF)
        dy_right(k, h).wait_recv()
        return to[j, rows, LEFT:] + dv_r[k, rows].astype(F32)

    def send_zf_right():
        for h in (0, 1):
            zg_s[h] = both_right(F, 2, h).astype(BF)
            zf_right(h).start()

    def send_dz_right(k):
        for h in (0, 1):
            total = both_right((C1, C2)[k], 1 + 2 * k, h)
            if k == 0:
                zf_right(h).wait_recv()
                total = total + zg_r[h].astype(F32)
            dw_s[k, pl.ds(h * HALF, HALF)] = total.astype(BF)
            dz_right(k, h).start()

    def term(j):
        h4(j).wait_recv()
        for n in range(0, DM, 256):
            to[j, :, n : n + 256] = dot(hid[j, :, U:], wcat[:, n : n + 256])

    def arrivals(t):
        @pl.when(t == C1)
        def _():
            arrived(C1, 0)
            gather(C1, F, 0, zp).start()
            arrived(C1, 1)
            gather(C1, F, 1, zm).start()

        @pl.when(t == F)
        def _():
            arrived(YO, 0)
            gather(YO, Y1, 0, zp).start()
            arrived(YO, 1)
            gather(YO, Y1, 1, zm).start()
            arrived(F, 0)
            gather(F, YF, 0, ylp).start()
            arrived(F, 1)

        @pl.when(t == YO)
        def _():
            gather(F, YF, 1, ylp).start()

        @pl.when(t == Y1)
        def _():
            arrived(Y1, 0)
            arrived(Y1, 1)

        @pl.when(t == YF)
        def _():
            arrived(YF, 0)
            arrived(YF, 1)

        @pl.when(t == Y2)
        def _():
            arrived(Y2, 0)
            arrived(Y2, 1)

        @pl.when(t == C2)
        def _():
            arrived(C2, 0)
            arrived(C2, 1)

    def tick(t, carry):
        def stage(step, lag):
            pl.when((t >= lag) & (t < CHUNKS + lag))(lambda: step(t - lag))

        stage(send_yb, 2)
        stage(send_h3, 4)
        arrivals(t)
        stage(partial, 0)

        stage(send_x2, 1)
        stage(send_h2, 3)
        stage(term, 5)

        @pl.when(t == YO)
        def _():
            gather(YO, Y2, 1, zp).start()
            gather(YO, Y2, 0, zm).start()

        @pl.when(t == Y1)
        def _():
            gather(OWN, C2, 1, zp).start()
            gather(OWN, C2, 0, zm).start()

        for k, chunk in enumerate((YO, Y1, YF, Y2)):
            pl.when(t == chunk + 5)(functools.partial(send_dy_right, k))

        @pl.when(t == YF + 5)
        def _():
            send_zf(1)

        @pl.when(t == Y2 + 5)
        def _():
            send_dz(1, 1)
            send_dz(1, 0)
            send_zf_right()

        @pl.when(t == C2 + 5)
        def _():
            send_dz(0, 1)
            for h in (0, 1):
                dy_s[pl.ds(h * HALF, HALF)] = column(1, h).astype(BF)
                dy(h).start()
            send_dz_right(0)
            send_dz_right(1)

        stage(send_h1, 2)
        stage(send_h4, 4)
        stage(send_x1, 0)

        @pl.when(t == F + 5)
        def _():
            send_zf(0)

        @pl.when(t == F + 6)
        def _():
            send_dz(0, 0)

        pl.when((t >= 6) & (t % 2 == 0))(lambda: grads_in(t - 5))
        pl.when((t >= 7) & (t % 2 == 1))(lambda: grads_down(t - 6))
        return carry

    lax.fori_loop(0, CHUNKS + 5, tick, 0)

    sums = ((sum_gate, out_gate), (sum_up, out_up), (sum_down, out_down))
    stores = [pltpu.make_async_copy(a, b, o_s.at[k]) for k, (a, b) in enumerate(sums)]
    stores[0].start()
    stores[1].start()
    grads_down(CHUNKS - 1)
    stores[2].start()
    def left_all(i, carry):
        for k in (0, 1):
            x1(i, k).wait_send()
            x2(i, k).wait_send()
            h2(i, k).wait_send()
            h3(i, k).wait_send()
        yb(i).wait_send()
        h1(i).wait_send()
        h4(i).wait_send()
        return carry

    lax.fori_loop(0, CHUNKS, left_all, 0)
    for dst in range(1, CHUNKS):
        for h in (0, 1):
            gather(OWN, dst, h, zp).wait_send()
    for h in (0, 1):
        for col in (0, 1):
            zf(col, h).wait_send()
            dz(col, 0, h).wait_send()
            dz(col, 1, h).wait_send()
        for k in range(4):
            dy_right(k, h).wait_send()
        zf_right(h).wait_send()
        dy(h).wait_send()
        dz_right(0, h).wait_send()
        dz_right(1, h).wait_send()

    for h in (0, 1):
        rows = pl.ds(h * HALF, HALF)
        total = both_right(OWN, 0, h)
        dz_right(0, h).wait_recv()
        dz_right(1, h).wait_recv()
        total = total + (dw_r[0, rows].astype(F32) + dw_r[1, rows].astype(F32))
        out_tok[rows, LEFT:] = total.astype(BF)
        total = column(0, h)
        dy(h).wait_recv()
        out_tok[rows, :LEFT] = (total + dy_r[rows].astype(F32)).astype(BF)
    for store in stores:
        store.wait()


def place(*refs):
    ins, outs, by_way, sems = refs[:4], refs[4:8], refs[8:12], refs[12]
    reads, writes = [], []
    for k, (a, b, v) in enumerate(zip(ins, outs, by_way)):
        count = a.shape[0] // PIECES
        for p in range(PIECES):
            rows = pl.ds(p * count, count)
            reads.append(pltpu.make_async_copy(a.at[rows], v.at[rows], sems.at[0, k, p]))
            writes.append(pltpu.make_async_copy(v.at[rows], b.at[rows], sems.at[1, k, p]))
    for copy in reads:
        copy.start()
    for read, write in zip(reads, writes):
        read.wait()
        write.start()
    for copy in writes:
        copy.wait()


def local(tokens, grad_out, keep, count, w_gate, w_up, w_down):
    vmem = pl.BlockSpec(memory_space=pltpu.VMEM)
    anywhere = pl.BlockSpec(memory_space=pl.ANY)
    dma = pltpu.SemaphoreType.DMA
    outs = pl.pallas_call(
        kernel,
        out_shape=(
            jax.ShapeDtypeStruct((ROWS, DM), BF),
            jax.ShapeDtypeStruct((DM, U), F32),
            jax.ShapeDtypeStruct((DM, U), F32),
            jax.ShapeDtypeStruct((U, DM), F32),
        ),
        in_specs=[anywhere, vmem, vmem, pl.BlockSpec(memory_space=pltpu.SMEM)] + [anywhere] * 3,
        out_specs=[vmem] + [anywhere] * 3,
        scratch_shapes=[
            pltpu.VMEM((DM, U), BF),
            pltpu.VMEM((DM, U), BF),
            pltpu.VMEM((U, DM), BF),
            pltpu.VMEM((DM, U), F32),
            pltpu.VMEM((DM, U), F32),
            pltpu.VMEM((U, DM), F32),
            pltpu.VMEM((2, CHUNKS, ROWS, DM), BF),
            pltpu.VMEM((2 * U, DM), BF),
            pltpu.VMEM((DM, U), BF),
            pltpu.VMEM((2, ROWS, U3), F32),
            pltpu.VMEM((CHUNKS, HALF, U3), F32),
            pltpu.VMEM((CHUNKS, 2, 16, U3), BF),
            pltpu.VMEM((CHUNKS, 2, 16, U3), BF),
            pltpu.VMEM((CHUNKS, 2, 32, U3), BF),
            pltpu.VMEM((CHUNKS, 2, 32, U3), BF),
            pltpu.VMEM((CHUNKS, 16, U3), BF),
            pltpu.VMEM((CHUNKS, 16, U3), BF),
            pltpu.VMEM((2, 16, U3), F32),
            pltpu.VMEM((CHUNKS, ROWS, U3), BF),
            pltpu.VMEM((DM, 2 * ROWS), BF),
            pltpu.VMEM((CHUNKS, ROWS, DM), F32),
            pltpu.VMEM((ROWS, LEFT), BF),
            pltpu.VMEM((ROWS, LEFT), BF),
            pltpu.VMEM((2, 2, HALF, LEFT), BF),
            pltpu.VMEM((2, 2, HALF, LEFT), BF),
            pltpu.VMEM((2, 2, ROWS, LEFT), BF),
            pltpu.VMEM((2, 2, ROWS, LEFT), BF),
            pltpu.VMEM((4, ROWS, RIGHT), BF),
            pltpu.VMEM((4, ROWS, RIGHT), BF),
            pltpu.VMEM((2, HALF, RIGHT), BF),
            pltpu.VMEM((2, HALF, RIGHT), BF),
            pltpu.VMEM((2, ROWS, RIGHT), BF),
            pltpu.VMEM((2, ROWS, RIGHT), BF),
            dma((12, CHUNKS)),
            dma((12, CHUNKS)),
            dma((CHUNKS, 2)),
            dma((CHUNKS, 2)),
            dma((7, 4)),
            dma((7, 4)),
            dma((3,)),
            dma((4,)),
        ],
        compiler_params=pltpu.CompilerParams(
            collective_id=0, has_side_effects=True, vmem_limit_bytes=62 * 1024 * 1024
        ),
        cost_estimate=pl.CostEstimate(
            flops=16 * 2048 * DM * U, bytes_accessed=16 << 20, transcendentals=0
        ),
    )(tokens, grad_out, keep, count, w_gate, w_up, w_down)
    return pl.pallas_call(
        place,
        out_shape=tuple(jax.ShapeDtypeStruct(o.shape, o.dtype) for o in outs),
        in_specs=[anywhere] * 4,
        out_specs=[anywhere] * 4,
        scratch_shapes=[pltpu.VMEM(o.shape, o.dtype) for o in outs] + [dma((2, 4, PIECES))],
        compiler_params=pltpu.CompilerParams(vmem_limit_bytes=62 * 1024 * 1024),
    )(*outs)


def solution(mesh):
    placed = (
        P("wide", "mp"),
        P("wide", "mp"),
        P("wide"),
        P(),
        P("mp", "wide"),
        P("mp", "wide"),
        P("wide", "mp"),
    )
    return jax.shard_map(
        local,
        mesh=mesh,
        in_specs=placed,
        out_specs=(P("wide", "mp"), P("mp", "wide"), P("mp", "wide"), P("wide", "mp")),
        check_vma=False,
    )
```

```python
import functools

import jax
import jax.numpy as jnp
from jax import lax
from jax.experimental import pallas as pl
from jax.experimental.pallas import tpu as pltpu
from jax.sharding import PartitionSpec as P

BF = jnp.bfloat16
F32 = jnp.float32
ROWS = 256
HALF = 128
DM = 1024
U = 512
UC, UX, UY = 256, 64, 32
LEFT, RIGHT = 512, 512
CHUNKS = 8
PIECES = 4
OWN, C1, F, YO, Y1, YF, Y2, C2 = range(CHUNKS)
B0, X1P, X1M, X2P, X2M, YB, H1, H2P, H2M, H3P, H3M, H4 = range(12)


def dot(a, b):
    return lax.dot_general(a, b, (((1,), (0,)), ((), ())), preferred_element_type=F32)


def dot_nt(a, b):
    return lax.dot_general(a, b, (((1,), (1,)), ((), ())), preferred_element_type=F32)


def kernel(
    tokens, grad_out, keep, count, in_gate, in_up, in_down,
    out_tok, out_gate, out_up, out_down,
    w_in, w_in_t, w_down, sum_in, sum_down, stage_more, tg, part, b0_r, x1_s, x1_r, x2_s, x2_r,
    yb_s, yb_r, own64, own32, hid,
    to, dy_s, dy_r, zf_s, zf_r, dz_s, dz_r, dv_s, dv_r, zg_s, zg_r, dw_s, dw_r,
    c_ss, c_rs, a_ss, a_rs, d_ss, d_rs, o_s, i_s,
):
    mp, wide = lax.axis_index("mp"), lax.axis_index("wide")
    x, yh, c = mp // 4, (mp // 2) % 2, mp % 2
    core = (mp + 1 - 2 * c, wide)
    xp = ((mp + 4) % 16, wide)
    xm = ((mp + 12) % 16, wide)
    yhp = (mp + 2 - 4 * yh, wide)
    ylp = (mp, wide + 1 - 2 * (wide % 2))
    zp = (mp, (wide + 2) % 8)
    zm = (mp, (wide + 6) % 8)

    def remote(src, dst, ssem, rsem, dev):
        return pltpu.make_async_remote_copy(
            src_ref=src, dst_ref=dst, send_sem=ssem, recv_sem=rsem,
            device_id=dev, device_id_type=pl.DeviceIdType.MESH,
        )

    loads = [
        pltpu.make_async_copy(a, b, i_s.at[k])
        for k, (a, b) in enumerate(
            (
                (tokens, tg.at[0, OWN]),
                (in_gate, w_in.at[:, pl.ds(0, U)]),
                (in_up, w_in.at[:, pl.ds(U, U)]),
                (in_down, w_down),
            )
        )
    ]
    for load in loads:
        load.start()

    barrier = pltpu.get_barrier_semaphore()
    for dev in (core, xp, xm, yhp, ylp, zp, zm):
        pl.semaphore_signal(barrier, inc=1, device_id=dev, device_id_type=pl.DeviceIdType.MESH)

    for r in range(0, ROWS, 128):
        factor = keep[pl.ds(r, 128)].astype(F32) / count[0].astype(F32)
        factor = jnp.broadcast_to(factor[None, :], (128, 128)).T
        for n in range(0, DM, 128):
            block = grad_out[r : r + 128, n : n + 128].astype(F32) * factor
            tg[1, OWN, r : r + 128, n : n + 128] = block.astype(BF)
    loads[0].wait()
    pl.semaphore_wait(barrier, 7)

    def gather(src, dst, h, dev):
        rows = pl.ds(h * HALF, HALF)
        return remote(
            tg.at[:, src, rows], tg.at[:, dst, rows], a_ss.at[dst, h], a_rs.at[dst, h], dev
        )

    def arrived(dst, h):
        gather(OWN, dst, h, zp).wait_recv()

    gather(OWN, C1, 0, zp).start()
    gather(OWN, C1, 1, zm).start()
    gather(OWN, YO, 0, ylp).start()
    gather(OWN, YO, 1, ylp).start()

    for load in loads[1:]:
        load.wait()
    for n in range(0, 2 * U, 256):
        w_in_t[n : n + 256, :] = w_in[:, n : n + 256].T
    sum_in[...] = jnp.zeros_like(sum_in)
    sum_down[...] = jnp.zeros_like(sum_down)

    def b0(i):
        units = pl.ds(pl.multiple_of((1 - c) * UC, UC), UC)
        return remote(part.at[i % 2, :, units], b0_r.at[i], c_ss.at[B0, i], c_rs.at[B0, i], core)

    def x1(i, k):
        return remote(
            x1_s.at[i, k], x1_r.at[i, k], c_ss.at[X1P + k, i], c_rs.at[X1P + k, i], (xp, xm)[k]
        )

    def x2(i, k):
        return remote(
            x2_s.at[i, k], x2_r.at[i, k], c_ss.at[X2P + k, i], c_rs.at[X2P + k, i], (xp, xm)[k]
        )

    def yb(i):
        return remote(yb_s.at[i], yb_r.at[i], c_ss.at[YB, i], c_rs.at[YB, i], yhp)

    def lanes(i, n=1):
        return pl.ds(pl.multiple_of(i * ROWS, ROWS), n * ROWS)

    def same(i, first, n, sem, dev):
        block = hid.at[:, pl.ds(pl.multiple_of(first, UY), n), lanes(i)]
        return remote(block, block, c_ss.at[sem, i], c_rs.at[sem, i], dev)

    mine = c * UC + x * UX
    left = c * UC + ((x + 3) % 4) * UX
    right = c * UC + ((x + 1) % 4) * UX

    def h1(i):
        return same(i, mine + yh * UY, UY, H1, yhp)

    def h2(i, k):
        return same(i, mine, UX, H2P + k, (xp, xm)[k])

    def h3(i, k):
        return same(i, (left, right + UY)[k], UY, H3P + k, (xp, xm)[k])

    def h4(i):
        return same(i, c * UC, UC, H4, core)

    def summed(i, xd, h):
        at = xd * UX + h * UY
        a = part[i % 2, :, pl.ds(pl.multiple_of(c * UC + at, UY), UY), :]
        return a + b0_r[i, :, pl.ds(pl.multiple_of(at, UY), UY), :]

    def partial(i):
        s = i % 2
        for m in (0, 1):
            part[s, m] = dot_nt(w_in_t[m * U : (m + 1) * U, :], tg[0, i])
        part[s, 2] = dot_nt(w_down[...], tg[1, i])
        b0(i).start()

    def send_x1(i):
        b0(i).wait()
        x1_s[i, 0] = summed(i, (x + 2) % 4, 0).astype(BF)
        x1(i, 0).start()
        x1_s[i, 1] = summed(i, (x + 2) % 4, 1).astype(BF)
        x1(i, 1).start()

    def send_x2(i):
        x1(i, 0).wait_recv()
        x2_s[i, 0, :, :UY] = (summed(i, (x + 1) % 4, 0) + x1_r[i, 0].astype(F32)).astype(BF)
        x2_s[i, 0, :, UY:] = summed(i, (x + 1) % 4, 1).astype(BF)
        x2(i, 0).start()
        x1(i, 1).wait_recv()
        x2_s[i, 1, :, :UY] = summed(i, (x + 3) % 4, 0).astype(BF)
        x2_s[i, 1, :, UY:] = (summed(i, (x + 3) % 4, 1) + x1_r[i, 1].astype(F32)).astype(BF)
        x2(i, 1).start()
        own64[i % 2, :, :UY] = summed(i, x, 0)
        own64[i % 2, :, UY:] = summed(i, x, 1)

    def send_yb(i):
        x2(i, 0).wait_recv()
        x2(i, 1).wait_recv()

        def total(h):
            at = pl.ds(pl.multiple_of(h * UY, UY), UY)
            return (
                own64[i % 2, :, at] + x2_r[i, 0, :, at].astype(F32) + x2_r[i, 1, :, at].astype(F32)
            )

        yb_s[i] = total(1 - yh).astype(BF)
        yb(i).start()
        own32[i % 2] = total(yh)

    def send_h1(i):
        yb(i).wait_recv()
        full = own32[i % 2] + yb_r[i].astype(F32)
        gate, up, back = full[0], full[1], full[2]
        sigma = 1.0 / (1.0 + jnp.exp(-gate))
        silu = gate * sigma
        units = pl.ds(pl.multiple_of(mine + yh * UY, UY), UY)
        hid[0, units, lanes(i)] = (silu * up).astype(BF)
        hid[1, units, lanes(i)] = (back * up * sigma * (1.0 + gate * (1.0 - sigma))).astype(BF)
        hid[2, units, lanes(i)] = (back * silu).astype(BF)
        h1(i).start()

    def send_h2(i):
        h1(i).wait_recv()
        h2(i, 0).start()
        h2(i, 1).start()

    def send_h3(i):
        h2(i, 0).wait_recv()
        h3(i, 0).start()
        h2(i, 1).wait_recv()
        h3(i, 1).start()

    def send_h4(i):
        h3(i, 0).wait_recv()
        h3(i, 1).wait_recv()
        h4(i).start()

    def grads_in(g):
        pair = lanes(g - 1, 2)
        for n in range(0, DM, 256):
            tok = tg[0, pl.ds(g - 1, 2), :, n : n + 256].reshape(2 * ROWS, 256)
            for m in (0, 1):
                sum_in[m * U : (m + 1) * U, n : n + 256] += dot(hid[1 + m, :, pair], tok)

    def grads_down(g):
        pair = lanes(g - 1, 2)
        for n in range(0, DM, 256):
            sc = tg[1, pl.ds(g - 1, 2), :, n : n + 256].reshape(2 * ROWS, 256)
            sum_down[:, n : n + 256] += dot(hid[0, :, pair], sc)

    def zf(col, h):
        return remote(
            zf_s.at[col, h], zf_r.at[col, h], d_ss.at[2 * col, h], d_rs.at[2 * col, h], (zm, zp)[h]
        )

    def zf_right(h):
        return remote(zg_s.at[h], zg_r.at[h], d_ss.at[0, 2 + h], d_rs.at[0, 2 + h], (zm, zp)[h])

    def dz(col, k, h):
        sem = 2 * col + 1
        return remote(
            dz_s.at[col, k, h], dz_r.at[col, k, h],
            d_ss.at[sem, 2 * k + h], d_rs.at[sem, 2 * k + h], (zp, zm)[(h + 1 + k) % 2],
        )

    def dz_right(k, h):
        return remote(
            dw_s.at[k, h], dw_r.at[k, h],
            d_ss.at[4, 2 * k + h], d_rs.at[4, 2 * k + h], (zp, zm)[(h + 1 + k) % 2],
        )

    def dy(h):
        return remote(dy_s.at[h], dy_r.at[h], d_ss.at[2, 2 + h], d_rs.at[2, 2 + h], ylp)

    def dy_right(k, h):
        return remote(dv_s.at[k, h], dv_r.at[k, h], d_ss.at[5 + h, k], d_rs.at[5 + h, k], ylp)

    def of_left(j, h):
        return to[j, :LEFT, h * HALF : (h + 1) * HALF]

    def of_right(j, h):
        return to[j, LEFT:, h * HALF : (h + 1) * HALF]

    def send_zf(col):
        for h in (0, 1):
            zf_s[col, h] = of_left((F, YF)[col], h).astype(BF)
            zf(col, h).start()

    def send_dz(col, k):
        for h in (0, 1):
            total = of_left(((C1, C2), (Y1, Y2))[col][k], h)
            if k == 0:
                zf(col, h).wait_recv()
                total = total + zf_r[col, h].astype(F32)
            dz_s[col, k, h] = total.astype(BF)
            dz(col, k, h).start()

    def column(col, h):
        dz(col, 0, h).wait_recv()
        dz(col, 1, h).wait_recv()
        return of_left((OWN, YO)[col], h) + (
            dz_r[col, 0, h].astype(F32) + dz_r[col, 1, h].astype(F32)
        )

    def send_dy():
        for h in (0, 1):
            dy_s[h] = column(1, h).astype(BF)
            dy(h).start()

    def send_dy_right(k):
        for h in (0, 1):
            dv_s[k, h] = of_right((YO, Y1, YF, Y2)[k], h).astype(BF)
            dy_right(k, h).start()

    def both_right(j, k, h):
        dy_right(k, h).wait_recv()
        return of_right(j, h) + dv_r[k, h].astype(F32)

    def send_zf_right():
        for h in (0, 1):
            zg_s[h] = both_right(F, 2, h).astype(BF)
            zf_right(h).start()

    def send_dz_right(k):
        for h in (0, 1):
            total = both_right((C1, C2)[k], 1 + 2 * k, h)
            if k == 0:
                zf_right(h).wait_recv()
                total = total + zg_r[h].astype(F32)
            dw_s[k, h] = total.astype(BF)
            dz_right(k, h).start()

    def term(j):
        h4(j).wait_recv()
        h = hid[1:, :, lanes(j)].reshape(2 * U, ROWS)
        for m in range(0, DM, 512):
            to[j, m : m + 512, :] = dot(w_in[m : m + 512, :], h)

    def arrivals(t):
        @pl.when(t == C1)
        def _():
            arrived(C1, 0)
            gather(C1, F, 0, zp).start()
            arrived(C1, 1)
            gather(C1, F, 1, zm).start()

        @pl.when(t == F)
        def _():
            arrived(YO, 0)
            gather(YO, Y1, 0, zp).start()
            arrived(YO, 1)
            gather(YO, Y1, 1, zm).start()
            arrived(F, 0)
            gather(F, YF, 0, ylp).start()
            arrived(F, 1)

        @pl.when(t == YO)
        def _():
            gather(F, YF, 1, ylp).start()

        for chunk in (Y1, YF, Y2, C2):

            @pl.when(t == chunk)
            def _():
                arrived(chunk, 0)
                arrived(chunk, 1)

    def tick(t, carry):
        def stage(step, lag):
            pl.when((t >= lag) & (t < CHUNKS + lag))(lambda: step(t - lag))

        def at(when, step, *args):
            pl.when(t == when)(lambda: step(*args))

        stage(send_h2, 4)
        arrivals(t)
        stage(partial, 0)

        stage(send_x2, 1)
        stage(send_yb, 2)
        stage(send_h1, 3)
        stage(send_h4, 5)

        @pl.when(t == YO)
        def _():
            gather(YO, Y2, 1, zp).start()
            gather(YO, Y2, 0, zm).start()

        @pl.when(t == Y1)
        def _():
            gather(OWN, C2, 1, zp).start()
            gather(OWN, C2, 0, zm).start()

        pl.when((t >= 7) & (t % 2 == 1))(lambda: grads_in(t - 6))
        pl.when((t >= 8) & (t % 2 == 0))(lambda: grads_down(t - 7))

        stage(send_x1, 0)
        stage(send_h3, 4)
        stage(term, 5)
        for k, chunk in enumerate((YO, Y1, YF, Y2)):
            at(chunk + 5, send_dy_right, k)
        at(F + 5, send_zf, 0)
        at(F + 6, send_dz, 0, 0)
        at(YF + 5, send_zf, 1)
        at(Y2 + 5, send_dz, 1, 1)
        at(Y2 + 5, send_dz, 1, 0)
        at(Y2 + 5, send_zf_right)
        at(C2 + 5, send_dz, 0, 1)
        at(C2 + 5, send_dy)
        at(C2 + 5, send_dz_right, 0)
        at(C2 + 5, send_dz_right, 1)
        return carry

    lax.fori_loop(0, CHUNKS + 5, tick, 0)

    stores = []

    def store(src, dst):
        stores.append(pltpu.make_async_copy(src, dst, o_s.at[len(stores)]))
        stores[-1].start()

    grads_in(CHUNKS - 1)
    blocks = [part.at[k // 3, k % 3] for k in range(6)] + [stage_more.at[0], stage_more.at[1]]
    for first, out in ((0, out_gate), (U, out_up)):
        for u in range(0, U, 256):
            for d in range(0, DM, 512):
                block = blocks[len(stores)]
                block[...] = sum_in[first + u : first + u + 256, d : d + 512].T
                store(block, out.at[pl.ds(d, 512), pl.ds(u, 256)])
    grads_down(CHUNKS - 1)
    store(sum_down, out_down)

    def left_all(i, carry):
        for k in (0, 1):
            x1(i, k).wait_send()
            x2(i, k).wait_send()
            h2(i, k).wait_send()
            h3(i, k).wait_send()
        yb(i).wait_send()
        h1(i).wait_send()
        h4(i).wait_send()
        return carry

    lax.fori_loop(0, CHUNKS, left_all, 0)
    for dst in range(1, CHUNKS):
        for h in (0, 1):
            gather(OWN, dst, h, zp).wait_send()
    for h in (0, 1):
        for col in (0, 1):
            zf(col, h).wait_send()
            dz(col, 0, h).wait_send()
            dz(col, 1, h).wait_send()
        for k in range(4):
            dy_right(k, h).wait_send()
        zf_right(h).wait_send()
        dy(h).wait_send()
        dz_right(0, h).wait_send()
        dz_right(1, h).wait_send()

    for h in (0, 1):
        rows = pl.ds(h * HALF, HALF)
        total = both_right(OWN, 0, h)
        dz_right(0, h).wait_recv()
        dz_right(1, h).wait_recv()
        total = total + (dw_r[0, h].astype(F32) + dw_r[1, h].astype(F32))
        out_tok[rows, LEFT:] = total.T.astype(BF)
        total = column(0, h)
        dy(h).wait_recv()
        out_tok[rows, :LEFT] = (total + dy_r[h].astype(F32)).T.astype(BF)
    for copy in stores:
        copy.wait()


def place(*refs):
    ins, outs, by_way, sems = refs[:4], refs[4:8], refs[8:12], refs[12]
    reads, writes = [], []
    for k, (a, b, v) in enumerate(zip(ins, outs, by_way)):
        count = a.shape[0] // PIECES
        for p in range(PIECES):
            rows = pl.ds(p * count, count)
            reads.append(pltpu.make_async_copy(a.at[rows], v.at[rows], sems.at[0, k, p]))
            writes.append(pltpu.make_async_copy(v.at[rows], b.at[rows], sems.at[1, k, p]))
    for copy in reads:
        copy.start()
    for read, write in zip(reads, writes):
        read.wait()
        write.start()
    for copy in writes:
        copy.wait()


def local(tokens, grad_out, keep, count, w_gate, w_up, w_down):
    vmem = pl.BlockSpec(memory_space=pltpu.VMEM)
    anywhere = pl.BlockSpec(memory_space=pl.ANY)
    dma = pltpu.SemaphoreType.DMA
    outs = pl.pallas_call(
        kernel,
        out_shape=(
            jax.ShapeDtypeStruct((ROWS, DM), BF),
            jax.ShapeDtypeStruct((DM, U), F32),
            jax.ShapeDtypeStruct((DM, U), F32),
            jax.ShapeDtypeStruct((U, DM), F32),
        ),
        in_specs=[anywhere, vmem, vmem, pl.BlockSpec(memory_space=pltpu.SMEM)] + [anywhere] * 3,
        out_specs=[vmem] + [anywhere] * 3,
        scratch_shapes=[
            pltpu.VMEM((DM, 2 * U), BF),
            pltpu.VMEM((2 * U, DM), BF),
            pltpu.VMEM((U, DM), BF),
            pltpu.VMEM((2 * U, DM), F32),
            pltpu.VMEM((U, DM), F32),
            pltpu.VMEM((2, 512, 256), F32),
            pltpu.VMEM((2, CHUNKS, ROWS, DM), BF),
            pltpu.VMEM((2, 3, U, ROWS), F32),
            pltpu.VMEM((CHUNKS, 3, UC, ROWS), F32),
            pltpu.VMEM((CHUNKS, 2, 3, UY, ROWS), BF),
            pltpu.VMEM((CHUNKS, 2, 3, UY, ROWS), BF),
            pltpu.VMEM((CHUNKS, 2, 3, UX, ROWS), BF),
            pltpu.VMEM((CHUNKS, 2, 3, UX, ROWS), BF),
            pltpu.VMEM((CHUNKS, 3, UY, ROWS), BF),
            pltpu.VMEM((CHUNKS, 3, UY, ROWS), BF),
            pltpu.VMEM((2, 3, UX, ROWS), F32),
            pltpu.VMEM((2, 3, UY, ROWS), F32),
            pltpu.VMEM((3, U, CHUNKS * ROWS), BF),
            pltpu.VMEM((CHUNKS, DM, ROWS), F32),
            pltpu.VMEM((2, LEFT, HALF), BF),
            pltpu.VMEM((2, LEFT, HALF), BF),
            pltpu.VMEM((2, 2, LEFT, HALF), BF),
            pltpu.VMEM((2, 2, LEFT, HALF), BF),
            pltpu.VMEM((2, 2, 2, LEFT, HALF), BF),
            pltpu.VMEM((2, 2, 2, LEFT, HALF), BF),
            pltpu.VMEM((4, 2, RIGHT, HALF), BF),
            pltpu.VMEM((4, 2, RIGHT, HALF), BF),
            pltpu.VMEM((2, RIGHT, HALF), BF),
            pltpu.VMEM((2, RIGHT, HALF), BF),
            pltpu.VMEM((2, 2, RIGHT, HALF), BF),
            pltpu.VMEM((2, 2, RIGHT, HALF), BF),
            dma((12, CHUNKS)),
            dma((12, CHUNKS)),
            dma((CHUNKS, 2)),
            dma((CHUNKS, 2)),
            dma((7, 4)),
            dma((7, 4)),
            dma((9,)),
            dma((4,)),
        ],
        compiler_params=pltpu.CompilerParams(
            collective_id=0, has_side_effects=True, vmem_limit_bytes=62 * 1024 * 1024
        ),
        cost_estimate=pl.CostEstimate(
            flops=16 * 2048 * DM * U, bytes_accessed=16 << 20, transcendentals=0
        ),
    )(tokens, grad_out, keep, count, w_gate, w_up, w_down)
    return pl.pallas_call(
        place,
        out_shape=tuple(jax.ShapeDtypeStruct(o.shape, o.dtype) for o in outs),
        in_specs=[anywhere] * 4,
        out_specs=[anywhere] * 4,
        scratch_shapes=[pltpu.VMEM(o.shape, o.dtype) for o in outs] + [dma((2, 4, PIECES))],
        compiler_params=pltpu.CompilerParams(vmem_limit_bytes=62 * 1024 * 1024),
    )(*outs)


def solution(mesh):
    placed = (
        P("wide", "mp"),
        P("wide", "mp"),
        P("wide"),
        P(),
        P("mp", "wide"),
        P("mp", "wide"),
        P("wide", "mp"),
    )
    return jax.shard_map(
        local,
        mesh=mesh,
        in_specs=placed,
        out_specs=(P("wide", "mp"), P("mp", "wide"), P("mp", "wide"), P("wide", "mp")),
        check_vma=False,
    )
```

```python
import functools

import jax
import jax.numpy as jnp
from jax import lax
from jax.experimental import pallas as pl
from jax.experimental.pallas import tpu as pltpu
from jax.sharding import PartitionSpec as P

BF = jnp.bfloat16
F32 = jnp.float32
ROWS = 256
HALF = 128
DM = 1024
U = 512
UC, UX, UY = 256, 64, 32
LEFT, RIGHT = 512, 512
CHUNKS = 8
PIECES = 4
OWN, C1, F, YO, Y1, YF, Y2, C2 = range(CHUNKS)
B0, X1, XE, X2, YB, H1, HE, H2, H3, H4 = 0, 4, 6, 8, 10, 11, 12, 14, 16, 18
MESSAGES = 19


def dot(a, b):
    return lax.dot_general(a, b, (((1,), (0,)), ((), ())), preferred_element_type=F32)


def dot_nt(a, b):
    return lax.dot_general(a, b, (((1,), (1,)), ((), ())), preferred_element_type=F32)


def kernel(
    tokens, grad_out, keep, count, in_gate, in_up, in_down,
    out_tok, out_gate, out_up, out_down,
    w_in, w_in_t, w_down, sum_in, sum_down, stage_more, tg, part, b0_r, x1_s, x1_r, xe_s, xe_r, x2_s, x2_r,
    yb_s, yb_r, own64, own32, hid,
    to, dy_s, dy_r, zf_s, zf_r, dz_s, dz_r, dv_s, dv_r, zg_s, zg_r, dw_s, dw_r,
    c_ss, c_rs, a_ss, a_rs, d_ss, d_rs, o_s, i_s,
):
    mp, wide = lax.axis_index("mp"), lax.axis_index("wide")
    x, yh, c = mp // 4, (mp // 2) % 2, mp % 2
    core = (mp + 1 - 2 * c, wide)
    xp = ((mp + 4) % 16, wide)
    xm = ((mp + 12) % 16, wide)
    yhp = (mp + 2 - 4 * yh, wide)
    ylp = (mp, wide + 1 - 2 * (wide % 2))
    zp = (mp, (wide + 2) % 8)
    zm = (mp, (wide + 6) % 8)

    def remote(src, dst, ssem, rsem, dev):
        return pltpu.make_async_remote_copy(
            src_ref=src, dst_ref=dst, send_sem=ssem, recv_sem=rsem,
            device_id=dev, device_id_type=pl.DeviceIdType.MESH,
        )

    loads = [
        pltpu.make_async_copy(a, b, i_s.at[k])
        for k, (a, b) in enumerate(
            (
                (tokens, tg.at[0, OWN]),
                (in_gate, w_in.at[:, pl.ds(0, U)]),
                (in_up, w_in.at[:, pl.ds(U, U)]),
                (in_down, w_down),
            )
        )
    ]
    for load in loads:
        load.start()

    barrier = pltpu.get_barrier_semaphore()
    for dev in (core, xp, xm, yhp, ylp, zp, zm):
        pl.semaphore_signal(barrier, inc=1, device_id=dev, device_id_type=pl.DeviceIdType.MESH)

    for r in range(0, ROWS, 128):
        factor = keep[pl.ds(r, 128)].astype(F32) / count[0].astype(F32)
        factor = jnp.broadcast_to(factor[None, :], (128, 128)).T
        for n in range(0, DM, 128):
            block = grad_out[r : r + 128, n : n + 128].astype(F32) * factor
            tg[1, OWN, r : r + 128, n : n + 128] = block.astype(BF)
    loads[0].wait()
    pl.semaphore_wait(barrier, 7)

    def gather(src, dst, h, dev):
        rows = pl.ds(h * HALF, HALF)
        return remote(
            tg.at[:, src, rows], tg.at[:, dst, rows], a_ss.at[dst, h], a_rs.at[dst, h], dev
        )

    def arrived(dst, h):
        gather(OWN, dst, h, zp).wait_recv()

    gather(OWN, C1, 0, zp).start()
    gather(OWN, C1, 1, zm).start()
    gather(OWN, YO, 0, ylp).start()
    gather(OWN, YO, 1, ylp).start()

    for load in loads[1:]:
        load.wait()
    for n in range(0, 2 * U, 256):
        w_in_t[n : n + 256, :] = w_in[:, n : n + 256].T
    sum_in[...] = jnp.zeros_like(sum_in)
    sum_down[...] = jnp.zeros_like(sum_down)

    def b0(i, k):
        at = pl.multiple_of(((x + (2, 1, 3, 0)[k]) % 4) * UX, UX)
        src = part.at[i % 2, :, pl.ds(pl.multiple_of((1 - c) * UC + at, UX), UX)]
        return remote(
            src, b0_r.at[i, :, pl.ds(at, UX)], c_ss.at[B0 + k, i], c_rs.at[B0 + k, i], core
        )

    def along_x(i, k, sem, src, dst):
        return remote(
            src.at[i, k], dst.at[i, k], c_ss.at[sem + k, i], c_rs.at[sem + k, i], (xp, xm)[k]
        )

    def x1(i, k):
        return along_x(i, k, X1, x1_s, x1_r)

    def xe(i, k):
        return along_x(i, k, XE, xe_s, xe_r)

    def x2(i, k):
        return along_x(i, k, X2, x2_s, x2_r)

    def yb(i):
        return remote(yb_s.at[i], yb_r.at[i], c_ss.at[YB, i], c_rs.at[YB, i], yhp)

    def lanes(i, n=1):
        return pl.ds(pl.multiple_of(i * ROWS, ROWS), n * ROWS)

    def same(i, first, n, sem, dev):
        block = hid.at[:, pl.ds(pl.multiple_of(first, UY), n), lanes(i)]
        return remote(block, block, c_ss.at[sem, i], c_rs.at[sem, i], dev)

    mine = c * UC + x * UX
    left = c * UC + ((x + 3) % 4) * UX
    right = c * UC + ((x + 1) % 4) * UX

    def h1(i):
        return same(i, mine + yh * UY, UY, H1, yhp)

    def he(i, k):
        return same(i, mine + yh * UY, UY, HE + k, (xp, xm)[k])

    def h2(i, k):
        return same(i, mine + (1 - yh) * UY, UY, H2 + k, (xp, xm)[k])

    def h3(i, k):
        return same(i, (left, right + UY)[k], UY, H3 + k, (xp, xm)[k])

    def h4(i):
        return same(i, c * UC, UC, H4, core)

    def summed(i, xd, h):
        at = xd * UX + h * UY
        a = part[i % 2, :, pl.ds(pl.multiple_of(c * UC + at, UY), UY), :]
        return a + b0_r[i, :, pl.ds(pl.multiple_of(at, UY), UY), :]

    def partial(i):
        s = i % 2
        for m in (0, 1):
            part[s, m] = dot_nt(w_in_t[m * U : (m + 1) * U, :], tg[0, i])
        part[s, 2] = dot_nt(w_down[...], tg[1, i])
        for k in range(4):
            b0(i, k).start()

    def send_x1(i):
        b0(i, 0).wait()
        for k in (0, 1):
            x1_s[i, k] = summed(i, (x + 2) % 4, k).astype(BF)
            x1(i, k).start()
        for k in (0, 1):
            b0(i, 1 + k).wait()
            xe_s[i, k] = summed(i, (x + (1, 3)[k]) % 4, 1 - k).astype(BF)
            xe(i, k).start()

    def send_x2(i):
        for k in (0, 1):
            x1(i, k).wait_recv()
            total = summed(i, (x + (1, 3)[k]) % 4, k) + x1_r[i, k].astype(F32)
            x2_s[i, k] = total.astype(BF)
            x2(i, k).start()
        b0(i, 3).wait()
        for h in (0, 1):
            xe(i, 1 - h).wait_recv()
            own64[i % 2, h] = summed(i, x, h) + xe_r[i, 1 - h].astype(F32)

    def send_yb(i):
        x2(i, 0).wait_recv()
        x2(i, 1).wait_recv()
        yb_s[i] = (own64[i % 2, 1 - yh] + x2_r[i, 1 - yh].astype(F32)).astype(BF)
        yb(i).start()
        own32[i % 2] = own64[i % 2, yh] + x2_r[i, yh].astype(F32)

    def send_h1(i):
        yb(i).wait_recv()
        full = own32[i % 2] + yb_r[i].astype(F32)
        gate, up, back = full[0], full[1], full[2]
        sigma = 1.0 / (1.0 + jnp.exp(-gate))
        silu = gate * sigma
        units = pl.ds(pl.multiple_of(mine + yh * UY, UY), UY)
        hid[0, units, lanes(i)] = (silu * up).astype(BF)
        hid[1, units, lanes(i)] = (back * up * sigma * (1.0 + gate * (1.0 - sigma))).astype(BF)
        hid[2, units, lanes(i)] = (back * silu).astype(BF)
        h1(i).start()
        he(i, 0).start()
        he(i, 1).start()

    def send_h2(i):
        h1(i).wait_recv()
        h2(i, 0).start()
        h2(i, 1).start()

    def send_h3(i):
        for k in (0, 1):
            he(i, k).wait_recv()
            h2(i, k).wait_recv()
            h3(i, k).start()

    def send_h4(i):
        h3(i, 0).wait_recv()
        h3(i, 1).wait_recv()
        h4(i).start()

    def grads_in(g):
        pair = lanes(g - 1, 2)
        for n in range(0, DM, 256):
            tok = tg[0, pl.ds(g - 1, 2), :, n : n + 256].reshape(2 * ROWS, 256)
            for m in (0, 1):
                sum_in[m * U : (m + 1) * U, n : n + 256] += dot(hid[1 + m, :, pair], tok)

    def grads_down(g):
        pair = lanes(g - 1, 2)
        for n in range(0, DM, 256):
            sc = tg[1, pl.ds(g - 1, 2), :, n : n + 256].reshape(2 * ROWS, 256)
            sum_down[:, n : n + 256] += dot(hid[0, :, pair], sc)

    def zf(col, h):
        return remote(
            zf_s.at[col, h], zf_r.at[col, h], d_ss.at[2 * col, h], d_rs.at[2 * col, h], (zm, zp)[h]
        )

    def zf_right(h):
        return remote(zg_s.at[h], zg_r.at[h], d_ss.at[0, 2 + h], d_rs.at[0, 2 + h], (zm, zp)[h])

    def dz(col, k, h):
        sem = 2 * col + 1
        return remote(
            dz_s.at[col, k, h], dz_r.at[col, k, h],
            d_ss.at[sem, 2 * k + h], d_rs.at[sem, 2 * k + h], (zp, zm)[(h + 1 + k) % 2],
        )

    def dz_right(k, h):
        return remote(
            dw_s.at[k, h], dw_r.at[k, h],
            d_ss.at[4, 2 * k + h], d_rs.at[4, 2 * k + h], (zp, zm)[(h + 1 + k) % 2],
        )

    def dy(h):
        return remote(dy_s.at[h], dy_r.at[h], d_ss.at[2, 2 + h], d_rs.at[2, 2 + h], ylp)

    def dy_right(k, h):
        return remote(dv_s.at[k, h], dv_r.at[k, h], d_ss.at[5 + h, k], d_rs.at[5 + h, k], ylp)

    def of_left(j, h):
        return to[j, :LEFT, h * HALF : (h + 1) * HALF]

    def of_right(j, h):
        return to[j, LEFT:, h * HALF : (h + 1) * HALF]

    def send_zf(col):
        for h in (0, 1):
            zf_s[col, h] = of_left((F, YF)[col], h).astype(BF)
            zf(col, h).start()

    def send_dz(col, k):
        for h in (0, 1):
            total = of_left(((C1, C2), (Y1, Y2))[col][k], h)
            if k == 0:
                zf(col, h).wait_recv()
                total = total + zf_r[col, h].astype(F32)
            dz_s[col, k, h] = total.astype(BF)
            dz(col, k, h).start()

    def column(col, h):
        dz(col, 0, h).wait_recv()
        dz(col, 1, h).wait_recv()
        return of_left((OWN, YO)[col], h) + (
            dz_r[col, 0, h].astype(F32) + dz_r[col, 1, h].astype(F32)
        )

    def send_dy():
        for h in (0, 1):
            dy_s[h] = column(1, h).astype(BF)
            dy(h).start()

    def send_dy_right(k):
        for h in (0, 1):
            dv_s[k, h] = of_right((YO, Y1, YF, Y2)[k], h).astype(BF)
            dy_right(k, h).start()

    def both_right(j, k, h):
        dy_right(k, h).wait_recv()
        return of_right(j, h) + dv_r[k, h].astype(F32)

    def send_zf_right():
        for h in (0, 1):
            zg_s[h] = both_right(F, 2, h).astype(BF)
            zf_right(h).start()

    def send_dz_right(k):
        for h in (0, 1):
            total = both_right((C1, C2)[k], 1 + 2 * k, h)
            if k == 0:
                zf_right(h).wait_recv()
                total = total + zg_r[h].astype(F32)
            dw_s[k, h] = total.astype(BF)
            dz_right(k, h).start()

    def term(j):
        h4(j).wait_recv()
        h = hid[1:, :, lanes(j)].reshape(2 * U, ROWS)
        for m in range(0, DM, 512):
            to[j, m : m + 512, :] = dot(w_in[m : m + 512, :], h)

    def arrivals(t):
        @pl.when(t == C1)
        def _():
            arrived(C1, 0)
            gather(C1, F, 0, zp).start()
            arrived(C1, 1)
            gather(C1, F, 1, zm).start()

        @pl.when(t == F)
        def _():
            arrived(YO, 0)
            gather(YO, Y1, 0, zp).start()
            arrived(YO, 1)
            gather(YO, Y1, 1, zm).start()
            arrived(F, 0)
            gather(F, YF, 0, ylp).start()
            arrived(F, 1)

        @pl.when(t == YO)
        def _():
            gather(F, YF, 1, ylp).start()

        for chunk in (Y1, YF, Y2, C2):

            @pl.when(t == chunk)
            def _():
                arrived(chunk, 0)
                arrived(chunk, 1)

    def tick(t, carry):
        def stage(step, lag):
            pl.when((t >= lag) & (t < CHUNKS + lag))(lambda: step(t - lag))

        def at(when, step, *args):
            pl.when(t == when)(lambda: step(*args))

        stage(send_yb, 2)
        stage(send_h3, 4)
        arrivals(t)
        stage(partial, 0)

        stage(send_x2, 1)
        stage(send_h2, 3)
        stage(term, 5)
        for k, chunk in enumerate((YO, Y1, YF, Y2)):
            at(chunk + 5, send_dy_right, k)
        at(F + 5, send_zf, 0)
        at(F + 6, send_dz, 0, 0)
        at(YF + 5, send_zf, 1)
        at(Y2 + 5, send_dz, 1, 1)
        at(Y2 + 5, send_dz, 1, 0)
        at(Y2 + 5, send_zf_right)
        at(C2 + 5, send_dz, 0, 1)
        at(C2 + 5, send_dy)
        at(C2 + 5, send_dz_right, 0)
        at(C2 + 5, send_dz_right, 1)

        @pl.when(t == YO)
        def _():
            gather(YO, Y2, 1, zp).start()
            gather(YO, Y2, 0, zm).start()

        @pl.when(t == Y1)
        def _():
            gather(OWN, C2, 1, zp).start()
            gather(OWN, C2, 0, zm).start()

        stage(send_h1, 2)
        stage(send_h4, 4)
        stage(send_x1, 0)
        pl.when((t >= 6) & (t % 2 == 0))(lambda: grads_in(t - 5))
        pl.when((t >= 7) & (t % 2 == 1))(lambda: grads_down(t - 6))
        return carry

    lax.fori_loop(0, CHUNKS + 5, tick, 0)

    stores = []

    def store(src, dst):
        stores.append(pltpu.make_async_copy(src, dst, o_s.at[len(stores)]))
        stores[-1].start()

    blocks = [part.at[k // 3, k % 3] for k in range(6)] + [stage_more.at[0], stage_more.at[1]]
    for first, out in ((0, out_gate), (U, out_up)):
        for u in range(0, U, 256):
            for d in range(0, DM, 512):
                block = blocks[len(stores)]
                block[...] = sum_in[first + u : first + u + 256, d : d + 512].T
                store(block, out.at[pl.ds(d, 512), pl.ds(u, 256)])
    grads_down(CHUNKS - 1)
    store(sum_down, out_down)

    def left_all(i, carry):
        for k in (0, 1):
            x1(i, k).wait_send()
            xe(i, k).wait_send()
            he(i, k).wait_send()
            x2(i, k).wait_send()
            h2(i, k).wait_send()
            h3(i, k).wait_send()
        yb(i).wait_send()
        h1(i).wait_send()
        h4(i).wait_send()
        return carry

    lax.fori_loop(0, CHUNKS, left_all, 0)
    for dst in range(1, CHUNKS):
        for h in (0, 1):
            gather(OWN, dst, h, zp).wait_send()
    for h in (0, 1):
        for col in (0, 1):
            zf(col, h).wait_send()
            dz(col, 0, h).wait_send()
            dz(col, 1, h).wait_send()
        for k in range(4):
            dy_right(k, h).wait_send()
        zf_right(h).wait_send()
        dy(h).wait_send()
        dz_right(0, h).wait_send()
        dz_right(1, h).wait_send()

    for h in (0, 1):
        rows = pl.ds(h * HALF, HALF)
        total = both_right(OWN, 0, h)
        dz_right(0, h).wait_recv()
        dz_right(1, h).wait_recv()
        total = total + (dw_r[0, h].astype(F32) + dw_r[1, h].astype(F32))
        out_tok[rows, LEFT:] = total.T.astype(BF)
        total = column(0, h)
        dy(h).wait_recv()
        out_tok[rows, :LEFT] = (total + dy_r[h].astype(F32)).T.astype(BF)
    for copy in stores:
        copy.wait()


def place(*refs):
    ins, outs, by_way, sems = refs[:4], refs[4:8], refs[8:12], refs[12]
    reads, writes = [], []
    for k, (a, b, v) in enumerate(zip(ins, outs, by_way)):
        count = a.shape[0] // PIECES
        for p in range(PIECES):
            rows = pl.ds(p * count, count)
            reads.append(pltpu.make_async_copy(a.at[rows], v.at[rows], sems.at[0, k, p]))
            writes.append(pltpu.make_async_copy(v.at[rows], b.at[rows], sems.at[1, k, p]))
    for copy in reads:
        copy.start()
    for read, write in zip(reads, writes):
        read.wait()
        write.start()
    for copy in writes:
        copy.wait()


def local(tokens, grad_out, keep, count, w_gate, w_up, w_down):
    vmem = pl.BlockSpec(memory_space=pltpu.VMEM)
    anywhere = pl.BlockSpec(memory_space=pl.ANY)
    dma = pltpu.SemaphoreType.DMA
    outs = pl.pallas_call(
        kernel,
        out_shape=(
            jax.ShapeDtypeStruct((ROWS, DM), BF),
            jax.ShapeDtypeStruct((DM, U), F32),
            jax.ShapeDtypeStruct((DM, U), F32),
            jax.ShapeDtypeStruct((U, DM), F32),
        ),
        in_specs=[anywhere, vmem, vmem, pl.BlockSpec(memory_space=pltpu.SMEM)] + [anywhere] * 3,
        out_specs=[vmem] + [anywhere] * 3,
        scratch_shapes=[
            pltpu.VMEM((DM, 2 * U), BF),
            pltpu.VMEM((2 * U, DM), BF),
            pltpu.VMEM((U, DM), BF),
            pltpu.VMEM((2 * U, DM), F32),
            pltpu.VMEM((U, DM), F32),
            pltpu.VMEM((2, 512, 256), F32),
            pltpu.VMEM((2, CHUNKS, ROWS, DM), BF),
            pltpu.VMEM((2, 3, U, ROWS), F32),
            pltpu.VMEM((CHUNKS, 3, UC, ROWS), F32),
            pltpu.VMEM((CHUNKS, 2, 3, UY, ROWS), BF),
            pltpu.VMEM((CHUNKS, 2, 3, UY, ROWS), BF),
            pltpu.VMEM((CHUNKS, 2, 3, UY, ROWS), BF),
            pltpu.VMEM((CHUNKS, 2, 3, UY, ROWS), BF),
            pltpu.VMEM((CHUNKS, 2, 3, UY, ROWS), BF),
            pltpu.VMEM((CHUNKS, 2, 3, UY, ROWS), BF),
            pltpu.VMEM((CHUNKS, 3, UY, ROWS), BF),
            pltpu.VMEM((CHUNKS, 3, UY, ROWS), BF),
            pltpu.VMEM((2, 2, 3, UY, ROWS), F32),
            pltpu.VMEM((2, 3, UY, ROWS), F32),
            pltpu.VMEM((3, U, CHUNKS * ROWS), BF),
            pltpu.VMEM((CHUNKS, DM, ROWS), F32),
            pltpu.VMEM((2, LEFT, HALF), BF),
            pltpu.VMEM((2, LEFT, HALF), BF),
            pltpu.VMEM((2, 2, LEFT, HALF), BF),
            pltpu.VMEM((2, 2, LEFT, HALF), BF),
            pltpu.VMEM((2, 2, 2, LEFT, HALF), BF),
            pltpu.VMEM((2, 2, 2, LEFT, HALF), BF),
            pltpu.VMEM((4, 2, RIGHT, HALF), BF),
            pltpu.VMEM((4, 2, RIGHT, HALF), BF),
            pltpu.VMEM((2, RIGHT, HALF), BF),
            pltpu.VMEM((2, RIGHT, HALF), BF),
            pltpu.VMEM((2, 2, RIGHT, HALF), BF),
            pltpu.VMEM((2, 2, RIGHT, HALF), BF),
            dma((MESSAGES, CHUNKS)),
            dma((MESSAGES, CHUNKS)),
            dma((CHUNKS, 2)),
            dma((CHUNKS, 2)),
            dma((7, 4)),
            dma((7, 4)),
            dma((9,)),
            dma((4,)),
        ],
        compiler_params=pltpu.CompilerParams(
            collective_id=0, has_side_effects=True, vmem_limit_bytes=62 * 1024 * 1024
        ),
        cost_estimate=pl.CostEstimate(
            flops=16 * 2048 * DM * U, bytes_accessed=16 << 20, transcendentals=0
        ),
    )(tokens, grad_out, keep, count, w_gate, w_up, w_down)
    return pl.pallas_call(
        place,
        out_shape=tuple(jax.ShapeDtypeStruct(o.shape, o.dtype) for o in outs),
        in_specs=[anywhere] * 4,
        out_specs=[anywhere] * 4,
        scratch_shapes=[pltpu.VMEM(o.shape, o.dtype) for o in outs] + [dma((2, 4, PIECES))],
        compiler_params=pltpu.CompilerParams(vmem_limit_bytes=62 * 1024 * 1024),
    )(*outs)


def solution(mesh):
    placed = (
        P("wide", "mp"),
        P("wide", "mp"),
        P("wide"),
        P(),
        P("mp", "wide"),
        P("mp", "wide"),
        P("wide", "mp"),
    )
    return jax.shard_map(
        local,
        mesh=mesh,
        in_specs=placed,
        out_specs=(P("wide", "mp"), P("mp", "wide"), P("mp", "wide"), P("wide", "mp")),
        check_vma=False,
    )
```

```python
import functools

import jax
import jax.numpy as jnp
from jax import lax
from jax.experimental import pallas as pl
from jax.experimental.pallas import tpu as pltpu
from jax.sharding import PartitionSpec as P

BF = jnp.bfloat16
F32 = jnp.float32
ROWS = 256
HALF = 128
DM = 1024
U = 512
UC, UX, UY = 256, 64, 32
LEFT, RIGHT = 512, 512
CHUNKS = 8
PIECES = 4
OWN, C1, YO, F, Y1, YF, Y2, C2 = range(CHUNKS)
B0, X1, XE, X2, YB, H1, HE, H2, H3, H4 = 0, 4, 6, 8, 10, 11, 12, 14, 16, 18
MESSAGES = 19


def dot(a, b):
    return lax.dot_general(a, b, (((1,), (0,)), ((), ())), preferred_element_type=F32)


def dot_nt(a, b):
    return lax.dot_general(a, b, (((1,), (1,)), ((), ())), preferred_element_type=F32)


def kernel(
    tokens, grad_out, keep, count, in_gate, in_up, in_down,
    out_tok, out_gate, out_up, out_down,
    w_in, w_in_t, w_down, sum_in, sum_down, stage_more, tg, part, b0_r, x1_s, x1_r, xe_s, xe_r, x2_s, x2_r,
    yb_s, yb_r, own64, own32, hid,
    to, dy_s, dy_r, zf_s, zf_r, dz_s, dz_r, dv_s, dv_r, zg_s, zg_r, dw_s, dw_r,
    c_ss, c_rs, a_ss, a_rs, d_ss, d_rs, o_s, i_s,
):
    mp, wide = lax.axis_index("mp"), lax.axis_index("wide")
    x, yh, c = mp // 4, (mp // 2) % 2, mp % 2
    core = (mp + 1 - 2 * c, wide)
    xp = ((mp + 4) % 16, wide)
    xm = ((mp + 12) % 16, wide)
    yhp = (mp + 2 - 4 * yh, wide)
    ylp = (mp, wide + 1 - 2 * (wide % 2))
    zp = (mp, (wide + 2) % 8)
    zm = (mp, (wide + 6) % 8)

    def remote(src, dst, ssem, rsem, dev):
        return pltpu.make_async_remote_copy(
            src_ref=src, dst_ref=dst, send_sem=ssem, recv_sem=rsem,
            device_id=dev, device_id_type=pl.DeviceIdType.MESH,
        )

    loads = [
        pltpu.make_async_copy(a, b, i_s.at[k])
        for k, (a, b) in enumerate(
            (
                (tokens, tg.at[0, OWN]),
                (in_gate, w_in.at[:, pl.ds(0, U)]),
                (in_up, w_in.at[:, pl.ds(U, U)]),
                (in_down, w_down),
            )
        )
    ]
    for load in loads:
        load.start()

    barrier = pltpu.get_barrier_semaphore()
    for dev in (core, xp, xm, yhp, ylp, zp, zm):
        pl.semaphore_signal(barrier, inc=1, device_id=dev, device_id_type=pl.DeviceIdType.MESH)

    for r in range(0, ROWS, 128):
        factor = keep[pl.ds(r, 128)].astype(F32) / count[0].astype(F32)
        factor = jnp.broadcast_to(factor[None, :], (128, 128)).T
        for n in range(0, DM, 128):
            block = grad_out[r : r + 128, n : n + 128].astype(F32) * factor
            tg[1, OWN, r : r + 128, n : n + 128] = block.astype(BF)
    loads[0].wait()
    pl.semaphore_wait(barrier, 7)

    def gather(src, dst, h, dev):
        rows = pl.ds(h * HALF, HALF)
        return remote(
            tg.at[:, src, rows], tg.at[:, dst, rows], a_ss.at[dst, h], a_rs.at[dst, h], dev
        )

    def gather_yf(kind, h):
        rows = pl.ds(h * HALF, HALF)
        return remote(
            tg.at[kind, (Y1, F)[kind], rows], tg.at[kind, YF, rows],
            a_ss.at[(YF, CHUNKS)[kind], h], a_rs.at[(YF, CHUNKS)[kind], h],
            ((zp, zm)[h], ylp)[kind],
        )

    def arrived(dst, h):
        gather(OWN, dst, h, zp).wait_recv()

    gather(OWN, C1, 0, zp).start()
    gather(OWN, C1, 1, zm).start()
    gather(OWN, YO, 0, ylp).start()
    gather(OWN, YO, 1, ylp).start()

    for load in loads[1:]:
        load.wait()
    for n in range(0, 2 * U, 256):
        w_in_t[n : n + 256, :] = w_in[:, n : n + 256].T
    sum_in[...] = jnp.zeros_like(sum_in)
    sum_down[...] = jnp.zeros_like(sum_down)

    def b0(i, k):
        at = pl.multiple_of(((x + (2, 1, 3, 0)[k]) % 4) * UX, UX)
        src = part.at[i % 2, :, pl.ds(pl.multiple_of((1 - c) * UC + at, UX), UX)]
        return remote(
            src, b0_r.at[i, :, pl.ds(at, UX)], c_ss.at[B0 + k, i], c_rs.at[B0 + k, i], core
        )

    def along_x(i, k, sem, src, dst):
        return remote(
            src.at[i, k], dst.at[i, k], c_ss.at[sem + k, i], c_rs.at[sem + k, i], (xp, xm)[k]
        )

    def x1(i, k):
        return along_x(i, k, X1, x1_s, x1_r)

    def xe(i, k):
        return along_x(i, k, XE, xe_s, xe_r)

    def x2(i, k):
        return along_x(i, k, X2, x2_s, x2_r)

    def yb(i):
        return remote(yb_s.at[i], yb_r.at[i], c_ss.at[YB, i], c_rs.at[YB, i], yhp)

    def lanes(i, n=1):
        return pl.ds(pl.multiple_of(i * ROWS, ROWS), n * ROWS)

    def same(i, first, n, sem, dev):
        block = hid.at[:, pl.ds(pl.multiple_of(first, UY), n), lanes(i)]
        return remote(block, block, c_ss.at[sem, i], c_rs.at[sem, i], dev)

    mine = c * UC + x * UX
    left = c * UC + ((x + 3) % 4) * UX
    right = c * UC + ((x + 1) % 4) * UX

    def h1(i):
        return same(i, mine + yh * UY, UY, H1, yhp)

    def he(i, k):
        return same(i, mine + yh * UY, UY, HE + k, (xp, xm)[k])

    def h2(i, k):
        return same(i, mine + (1 - yh) * UY, UY, H2 + k, (xp, xm)[k])

    def h3(i, k):
        return same(i, (left, right + UY)[k], UY, H3 + k, (xp, xm)[k])

    def h4(i):
        return same(i, c * UC, UC, H4, core)

    def summed(i, xd, h):
        at = xd * UX + h * UY
        a = part[i % 2, :, pl.ds(pl.multiple_of(c * UC + at, UY), UY), :]
        return a + b0_r[i, :, pl.ds(pl.multiple_of(at, UY), UY), :]

    def partial(i):
        s = i % 2
        for m in (0, 1):
            part[s, m] = dot_nt(w_in_t[m * U : (m + 1) * U, :], tg[0, i])
        part[s, 2] = dot_nt(w_down[...], tg[1, i])
        for k in range(4):
            b0(i, k).start()

    def send_x1(i):
        b0(i, 0).wait()
        for k in (0, 1):
            x1_s[i, k] = summed(i, (x + 2) % 4, k).astype(BF)
            x1(i, k).start()
        for k in (0, 1):
            b0(i, 1 + k).wait()
            xe_s[i, k] = summed(i, (x + (1, 3)[k]) % 4, 1 - k).astype(BF)
            xe(i, k).start()

    def send_x2(i):
        for k in (0, 1):
            x1(i, k).wait_recv()
            total = summed(i, (x + (1, 3)[k]) % 4, k) + x1_r[i, k].astype(F32)
            x2_s[i, k] = total.astype(BF)
            x2(i, k).start()
        b0(i, 3).wait()
        for h in (0, 1):
            xe(i, 1 - h).wait_recv()
            own64[i % 2, h] = summed(i, x, h) + xe_r[i, 1 - h].astype(F32)

    def send_yb(i):
        x2(i, 0).wait_recv()
        x2(i, 1).wait_recv()
        yb_s[i] = (own64[i % 2, 1 - yh] + x2_r[i, 1 - yh].astype(F32)).astype(BF)
        yb(i).start()
        own32[i % 2] = own64[i % 2, yh] + x2_r[i, yh].astype(F32)

    def send_h1(i):
        yb(i).wait_recv()
        full = own32[i % 2] + yb_r[i].astype(F32)
        gate, up, back = full[0], full[1], full[2]
        sigma = 1.0 / (1.0 + jnp.exp(-gate))
        silu = gate * sigma
        units = pl.ds(pl.multiple_of(mine + yh * UY, UY), UY)
        hid[0, units, lanes(i)] = (silu * up).astype(BF)
        hid[1, units, lanes(i)] = (back * up * sigma * (1.0 + gate * (1.0 - sigma))).astype(BF)
        hid[2, units, lanes(i)] = (back * silu).astype(BF)
        h1(i).start()
        he(i, 0).start()
        he(i, 1).start()

    def send_h2(i):
        h1(i).wait_recv()
        h2(i, 0).start()
        h2(i, 1).start()

    def send_h3(i):
        for k in (0, 1):
            he(i, k).wait_recv()
            h2(i, k).wait_recv()
            h3(i, k).start()

    def send_h4(i):
        h3(i, 0).wait_recv()
        h3(i, 1).wait_recv()
        h4(i).start()

    def grads_in(g):
        pair = lanes(g - 1, 2)
        for n in range(0, DM, 256):
            tok = tg[0, pl.ds(g - 1, 2), :, n : n + 256].reshape(2 * ROWS, 256)
            for m in (0, 1):
                sum_in[m * U : (m + 1) * U, n : n + 256] += dot(hid[1 + m, :, pair], tok)

    def grads_down(g):
        pair = lanes(g - 1, 2)
        for n in range(0, DM, 256):
            sc = tg[1, pl.ds(g - 1, 2), :, n : n + 256].reshape(2 * ROWS, 256)
            sum_down[:, n : n + 256] += dot(hid[0, :, pair], sc)

    def zf(col, h):
        return remote(
            zf_s.at[col, h], zf_r.at[col, h], d_ss.at[2 * col, h], d_rs.at[2 * col, h], (zm, zp)[h]
        )

    def zf_right(h):
        return remote(zg_s.at[h], zg_r.at[h], d_ss.at[0, 2 + h], d_rs.at[0, 2 + h], (zm, zp)[h])

    def dz(col, k, h):
        sem = 2 * col + 1
        return remote(
            dz_s.at[col, k, h], dz_r.at[col, k, h],
            d_ss.at[sem, 2 * k + h], d_rs.at[sem, 2 * k + h], (zp, zm)[(h + 1 + k) % 2],
        )

    def dz_right(k, h):
        return remote(
            dw_s.at[k, h], dw_r.at[k, h],
            d_ss.at[4, 2 * k + h], d_rs.at[4, 2 * k + h], (zp, zm)[(h + 1 + k) % 2],
        )

    def dy(h):
        return remote(dy_s.at[h], dy_r.at[h], d_ss.at[2, 2 + h], d_rs.at[2, 2 + h], ylp)

    def dy_right(k, h):
        return remote(dv_s.at[k, h], dv_r.at[k, h], d_ss.at[5 + h, k], d_rs.at[5 + h, k], ylp)

    def of_left(j, h):
        return to[j, :LEFT, h * HALF : (h + 1) * HALF]

    def of_right(j, h):
        return to[j, LEFT:, h * HALF : (h + 1) * HALF]

    def send_zf(col):
        for h in (0, 1):
            zf_s[col, h] = of_left((F, YF)[col], h).astype(BF)
            zf(col, h).start()

    def send_dz(col, k):
        for h in (0, 1):
            total = of_left(((C1, C2), (Y1, Y2))[col][k], h)
            if k == 0:
                zf(col, h).wait_recv()
                total = total + zf_r[col, h].astype(F32)
            dz_s[col, k, h] = total.astype(BF)
            dz(col, k, h).start()

    def column(col, h):
        dz(col, 0, h).wait_recv()
        dz(col, 1, h).wait_recv()
        return of_left((OWN, YO)[col], h) + (
            dz_r[col, 0, h].astype(F32) + dz_r[col, 1, h].astype(F32)
        )

    def send_dy():
        for h in (0, 1):
            dy_s[h] = column(1, h).astype(BF)
            dy(h).start()

    def send_dy_right(k):
        for h in (0, 1):
            dv_s[k, h] = of_right((YO, Y1, YF, Y2)[k], h).astype(BF)
            dy_right(k, h).start()

    def both_right(j, k, h):
        dy_right(k, h).wait_recv()
        return of_right(j, h) + dv_r[k, h].astype(F32)

    def send_zf_right():
        for h in (0, 1):
            zg_s[h] = both_right(F, 2, h).astype(BF)
            zf_right(h).start()

    def send_dz_right(k):
        for h in (0, 1):
            total = both_right((C1, C2)[k], 1 + 2 * k, h)
            if k == 0:
                zf_right(h).wait_recv()
                total = total + zg_r[h].astype(F32)
            dw_s[k, h] = total.astype(BF)
            dz_right(k, h).start()

    def term(j):
        h4(j).wait_recv()
        h = hid[1:, :, lanes(j)].reshape(2 * U, ROWS)
        for m in range(0, DM, 512):
            to[j, m : m + 512, :] = dot(w_in[m : m + 512, :], h)

    def arrivals(t):
        @pl.when(t == C1)
        def _():
            arrived(C1, 0)
            gather(C1, F, 0, zp).start()
            arrived(C1, 1)
            gather(C1, F, 1, zm).start()

        @pl.when(t == YO)
        def _():
            arrived(YO, 0)
            gather(YO, Y1, 0, zp).start()
            arrived(YO, 1)
            gather(YO, Y1, 1, zm).start()

        @pl.when(t == F)
        def _():
            gather_yf(1, 1).start()

        @pl.when(t == Y1)
        def _():
            for h in (0, 1):
                arrived(Y1, h)
                gather_yf(0, h).start()

        @pl.when(t == YF)
        def _():
            for kind in (0, 1):
                for h in (0, 1):
                    gather_yf(kind, h).wait_recv()

        for chunk in (Y2, C2):

            @pl.when(t == chunk)
            def _():
                arrived(chunk, 0)
                arrived(chunk, 1)

    def tick(t, carry):
        def stage(step, lag):
            pl.when((t >= lag) & (t < CHUNKS + lag))(lambda: step(t - lag))

        def at(when, step, *args):
            pl.when(t == when)(lambda: step(*args))

        stage(send_yb, 2)
        stage(send_h3, 4)
        arrivals(t)
        stage(partial, 0)

        stage(send_x2, 1)
        stage(send_h2, 3)
        stage(term, 5)
        for k, chunk in enumerate((YO, Y1, YF, Y2)):
            at(chunk + 5, send_dy_right, k)
        at(F + 5, send_zf, 0)
        at(F + 6, send_dz, 0, 0)
        at(YF + 5, send_zf, 1)
        at(Y2 + 5, send_dz, 1, 1)
        at(Y2 + 5, send_dz, 1, 0)
        at(Y2 + 5, send_zf_right)
        at(C2 + 5, send_dz, 0, 1)
        at(C2 + 5, send_dy)
        at(C2 + 5, send_dz_right, 0)
        at(C2 + 5, send_dz_right, 1)

        @pl.when(t == YO)
        def _():
            arrived(F, 0)
            arrived(F, 1)
            gather_yf(1, 0).start()

        @pl.when(t == Y1)
        def _():
            gather(YO, Y2, 1, zp).start()
            gather(YO, Y2, 0, zm).start()

        @pl.when(t == YF)
        def _():
            gather(OWN, C2, 1, zp).start()
            gather(OWN, C2, 0, zm).start()

        stage(send_h1, 2)
        stage(send_h4, 4)
        stage(send_x1, 0)
        pl.when((t >= 6) & (t % 2 == 0))(lambda: grads_in(t - 5))
        pl.when((t >= 7) & (t % 2 == 1))(lambda: grads_down(t - 6))
        return carry

    lax.fori_loop(0, CHUNKS + 5, tick, 0)

    stores = []

    def store(src, dst):
        stores.append(pltpu.make_async_copy(src, dst, o_s.at[len(stores)]))
        stores[-1].start()

    blocks = [part.at[k // 3, k % 3] for k in range(6)] + [stage_more.at[0], stage_more.at[1]]
    for first, out in ((0, out_gate), (U, out_up)):
        for u in range(0, U, 256):
            for d in range(0, DM, 512):
                block = blocks[len(stores)]
                block[...] = sum_in[first + u : first + u + 256, d : d + 512].T
                store(block, out.at[pl.ds(d, 512), pl.ds(u, 256)])
    grads_down(CHUNKS - 1)
    store(sum_down, out_down)

    def left_all(i, carry):
        for k in (0, 1):
            x1(i, k).wait_send()
            xe(i, k).wait_send()
            he(i, k).wait_send()
            x2(i, k).wait_send()
            h2(i, k).wait_send()
            h3(i, k).wait_send()
        yb(i).wait_send()
        h1(i).wait_send()
        h4(i).wait_send()
        return carry

    lax.fori_loop(0, CHUNKS, left_all, 0)
    for dst in (C1, YO, F, Y1, Y2, C2):
        for h in (0, 1):
            gather(OWN, dst, h, zp).wait_send()
    for h in (0, 1):
        gather_yf(0, h).wait_send()
        gather_yf(1, h).wait_send()
    for h in (0, 1):
        for col in (0, 1):
            zf(col, h).wait_send()
            dz(col, 0, h).wait_send()
            dz(col, 1, h).wait_send()
        for k in range(4):
            dy_right(k, h).wait_send()
        zf_right(h).wait_send()
        dy(h).wait_send()
        dz_right(0, h).wait_send()
        dz_right(1, h).wait_send()

    for h in (0, 1):
        rows = pl.ds(h * HALF, HALF)
        total = both_right(OWN, 0, h)
        dz_right(0, h).wait_recv()
        dz_right(1, h).wait_recv()
        total = total + (dw_r[0, h].astype(F32) + dw_r[1, h].astype(F32))
        out_tok[rows, LEFT:] = total.T.astype(BF)
        total = column(0, h)
        dy(h).wait_recv()
        out_tok[rows, :LEFT] = (total + dy_r[h].astype(F32)).T.astype(BF)
    for copy in stores:
        copy.wait()


def place(*refs):
    ins, outs, by_way, sems = refs[:4], refs[4:8], refs[8:12], refs[12]
    reads, writes = [], []
    for k, (a, b, v) in enumerate(zip(ins, outs, by_way)):
        count = a.shape[0] // PIECES
        for p in range(PIECES):
            rows = pl.ds(p * count, count)
            reads.append(pltpu.make_async_copy(a.at[rows], v.at[rows], sems.at[0, k, p]))
            writes.append(pltpu.make_async_copy(v.at[rows], b.at[rows], sems.at[1, k, p]))
    for copy in reads:
        copy.start()
    for read, write in zip(reads, writes):
        read.wait()
        write.start()
    for copy in writes:
        copy.wait()


def local(tokens, grad_out, keep, count, w_gate, w_up, w_down):
    vmem = pl.BlockSpec(memory_space=pltpu.VMEM)
    anywhere = pl.BlockSpec(memory_space=pl.ANY)
    dma = pltpu.SemaphoreType.DMA
    outs = pl.pallas_call(
        kernel,
        out_shape=(
            jax.ShapeDtypeStruct((ROWS, DM), BF),
            jax.ShapeDtypeStruct((DM, U), F32),
            jax.ShapeDtypeStruct((DM, U), F32),
            jax.ShapeDtypeStruct((U, DM), F32),
        ),
        in_specs=[anywhere, vmem, vmem, pl.BlockSpec(memory_space=pltpu.SMEM)] + [anywhere] * 3,
        out_specs=[vmem] + [anywhere] * 3,
        scratch_shapes=[
            pltpu.VMEM((DM, 2 * U), BF),
            pltpu.VMEM((2 * U, DM), BF),
            pltpu.VMEM((U, DM), BF),
            pltpu.VMEM((2 * U, DM), F32),
            pltpu.VMEM((U, DM), F32),
            pltpu.VMEM((2, 512, 256), F32),
            pltpu.VMEM((2, CHUNKS, ROWS, DM), BF),
            pltpu.VMEM((2, 3, U, ROWS), F32),
            pltpu.VMEM((CHUNKS, 3, UC, ROWS), F32),
            pltpu.VMEM((CHUNKS, 2, 3, UY, ROWS), BF),
            pltpu.VMEM((CHUNKS, 2, 3, UY, ROWS), BF),
            pltpu.VMEM((CHUNKS, 2, 3, UY, ROWS), BF),
            pltpu.VMEM((CHUNKS, 2, 3, UY, ROWS), BF),
            pltpu.VMEM((CHUNKS, 2, 3, UY, ROWS), BF),
            pltpu.VMEM((CHUNKS, 2, 3, UY, ROWS), BF),
            pltpu.VMEM((CHUNKS, 3, UY, ROWS), BF),
            pltpu.VMEM((CHUNKS, 3, UY, ROWS), BF),
            pltpu.VMEM((2, 2, 3, UY, ROWS), F32),
            pltpu.VMEM((2, 3, UY, ROWS), F32),
            pltpu.VMEM((3, U, CHUNKS * ROWS), BF),
            pltpu.VMEM((CHUNKS, DM, ROWS), F32),
            pltpu.VMEM((2, LEFT, HALF), BF),
            pltpu.VMEM((2, LEFT, HALF), BF),
            pltpu.VMEM((2, 2, LEFT, HALF), BF),
            pltpu.VMEM((2, 2, LEFT, HALF), BF),
            pltpu.VMEM((2, 2, 2, LEFT, HALF), BF),
            pltpu.VMEM((2, 2, 2, LEFT, HALF), BF),
            pltpu.VMEM((4, 2, RIGHT, HALF), BF),
            pltpu.VMEM((4, 2, RIGHT, HALF), BF),
            pltpu.VMEM((2, RIGHT, HALF), BF),
            pltpu.VMEM((2, RIGHT, HALF), BF),
            pltpu.VMEM((2, 2, RIGHT, HALF), BF),
            pltpu.VMEM((2, 2, RIGHT, HALF), BF),
            dma((MESSAGES, CHUNKS)),
            dma((MESSAGES, CHUNKS)),
            dma((CHUNKS + 1, 2)),
            dma((CHUNKS + 1, 2)),
            dma((7, 4)),
            dma((7, 4)),
            dma((9,)),
            dma((4,)),
        ],
        compiler_params=pltpu.CompilerParams(
            collective_id=0, has_side_effects=True, vmem_limit_bytes=62 * 1024 * 1024
        ),
        cost_estimate=pl.CostEstimate(
            flops=16 * 2048 * DM * U, bytes_accessed=16 << 20, transcendentals=0
        ),
    )(tokens, grad_out, keep, count, w_gate, w_up, w_down)
    return pl.pallas_call(
        place,
        out_shape=tuple(jax.ShapeDtypeStruct(o.shape, o.dtype) for o in outs),
        in_specs=[anywhere] * 4,
        out_specs=[anywhere] * 4,
        scratch_shapes=[pltpu.VMEM(o.shape, o.dtype) for o in outs] + [dma((2, 4, PIECES))],
        compiler_params=pltpu.CompilerParams(vmem_limit_bytes=62 * 1024 * 1024),
    )(*outs)


def solution(mesh):
    placed = (
        P("wide", "mp"),
        P("wide", "mp"),
        P("wide"),
        P(),
        P("mp", "wide"),
        P("mp", "wide"),
        P("wide", "mp"),
    )
    return jax.shard_map(
        local,
        mesh=mesh,
        in_specs=placed,
        out_specs=(P("wide", "mp"), P("mp", "wide"), P("mp", "wide"), P("wide", "mp")),
        check_vma=False,
    )
```

```python
import functools

import jax
import jax.numpy as jnp
from jax import lax
from jax.experimental import pallas as pl
from jax.experimental.pallas import tpu as pltpu
from jax.sharding import PartitionSpec as P

BF = jnp.bfloat16
F32 = jnp.float32
ROWS = 256
HALF = 128
DM = 1024
U = 512
UC, UX, UY = 256, 64, 32
LEFT, RIGHT = 512, 512
CHUNKS = 8
PIECES = 4
OWN, C1, YO, F, Y1, YF, Y2, C2 = range(CHUNKS)
B0, X1, XE, X2, YB, H1, HE, H2, H3, H4 = 0, 3, 7, 9, 11, 12, 13, 15, 17, 21
MESSAGES = 24


def dot(a, b):
    return lax.dot_general(a, b, (((1,), (0,)), ((), ())), preferred_element_type=F32)


def dot_nt(a, b):
    return lax.dot_general(a, b, (((1,), (1,)), ((), ())), preferred_element_type=F32)


def kernel(
    tokens, grad_out, keep, count, in_gate, in_up, in_down,
    out_tok, out_gate, out_up, out_down,
    w_in, w_in_t, w_down, sum_in, sum_down, stage_more, tg, part, b0_r, x1_s, x1_r, xe_s, xe_r, x2_s, x2_r,
    yb_s, yb_r, own64, own32, hid,
    to, dy_s, dy_r, zf_s, zf_r, dz_s, dz_r, dv_s, dv_r, zg_s, zg_r, dw_s, dw_r,
    c_ss, c_rs, a_ss, a_rs, d_ss, d_rs, o_s, i_s,
):
    mp, wide = lax.axis_index("mp"), lax.axis_index("wide")
    x, yh, c = mp // 4, (mp // 2) % 2, mp % 2
    core = (mp + 1 - 2 * c, wide)
    xp = ((mp + 4) % 16, wide)
    xm = ((mp + 12) % 16, wide)
    xp_other = ((mp + 4) % 16 + 1 - 2 * c, wide)
    xm_other = ((mp + 12) % 16 + 1 - 2 * c, wide)
    yhp = (mp + 2 - 4 * yh, wide)
    ylp = (mp, wide + 1 - 2 * (wide % 2))
    zp = (mp, (wide + 2) % 8)
    zm = (mp, (wide + 6) % 8)

    def remote(src, dst, ssem, rsem, dev):
        return pltpu.make_async_remote_copy(
            src_ref=src, dst_ref=dst, send_sem=ssem, recv_sem=rsem,
            device_id=dev, device_id_type=pl.DeviceIdType.MESH,
        )

    loads = [
        pltpu.make_async_copy(a, b, i_s.at[k])
        for k, (a, b) in enumerate(
            (
                (tokens, tg.at[0, OWN]),
                (in_gate, w_in.at[:, pl.ds(0, U)]),
                (in_up, w_in.at[:, pl.ds(U, U)]),
                (in_down, w_down),
            )
        )
    ]
    for load in loads:
        load.start()

    barrier = pltpu.get_barrier_semaphore()
    for dev in (core, xp, xm, xp_other, xm_other, yhp, ylp, zp, zm):
        pl.semaphore_signal(barrier, inc=1, device_id=dev, device_id_type=pl.DeviceIdType.MESH)

    for r in range(0, ROWS, 128):
        factor = keep[pl.ds(r, 128)].astype(F32) / count[0].astype(F32)
        factor = jnp.broadcast_to(factor[None, :], (128, 128)).T
        for n in range(0, DM, 128):
            block = grad_out[r : r + 128, n : n + 128].astype(F32) * factor
            tg[1, OWN, r : r + 128, n : n + 128] = block.astype(BF)
    loads[0].wait()
    pl.semaphore_wait(barrier, 9)

    def gather(src, dst, h, dev):
        rows = pl.ds(h * HALF, HALF)
        return remote(
            tg.at[:, src, rows], tg.at[:, dst, rows], a_ss.at[dst, h], a_rs.at[dst, h], dev
        )

    def gather_yf(kind, h):
        rows = pl.ds(h * HALF, HALF)
        return remote(
            tg.at[kind, (Y1, F)[kind], rows], tg.at[kind, YF, rows],
            a_ss.at[(YF, CHUNKS)[kind], h], a_rs.at[(YF, CHUNKS)[kind], h],
            ((zp, zm)[h], ylp)[kind],
        )

    def arrived(dst, h):
        gather(OWN, dst, h, zp).wait_recv()

    gather(OWN, C1, 0, zp).start()
    gather(OWN, C1, 1, zm).start()
    gather(OWN, YO, 0, ylp).start()
    gather(OWN, YO, 1, ylp).start()

    for load in loads[1:]:
        load.wait()
    for n in range(0, 2 * U, 256):
        w_in_t[n : n + 256, :] = w_in[:, n : n + 256].T
    sum_in[...] = jnp.zeros_like(sum_in)
    sum_down[...] = jnp.zeros_like(sum_down)

    def b0(i, k):
        at = pl.multiple_of(((x + (1, 3, 0)[k]) % 4) * UX, UX)
        src = part.at[i % 2, :, pl.ds(pl.multiple_of((1 - c) * UC + at, UX), UX)]
        return remote(
            src, b0_r.at[i, :, pl.ds(at, UX)], c_ss.at[B0 + k, i], c_rs.at[B0 + k, i], core
        )

    def x1(i, k, o):
        sem = X1 + 2 * k + o
        dev = ((xp, xm), (xp_other, xm_other))[o][k]
        return remote(
            x1_s.at[i, k, o], x1_r.at[i, k, o], c_ss.at[sem, i], c_rs.at[sem, i], dev
        )

    def along_x(i, k, sem, src, dst):
        return remote(
            src.at[i, k], dst.at[i, k], c_ss.at[sem + k, i], c_rs.at[sem + k, i], (xp, xm)[k]
        )

    def xe(i, k):
        return along_x(i, k, XE, xe_s, xe_r)

    def x2(i, k):
        return along_x(i, k, X2, x2_s, x2_r)

    def yb(i):
        return remote(yb_s.at[i], yb_r.at[i], c_ss.at[YB, i], c_rs.at[YB, i], yhp)

    def lanes(i, n=1):
        return pl.ds(pl.multiple_of(i * ROWS, ROWS), n * ROWS)

    def same(i, first, n, sem, dev):
        block = hid.at[:, pl.ds(pl.multiple_of(first, UY), n), lanes(i)]
        return remote(block, block, c_ss.at[sem, i], c_rs.at[sem, i], dev)

    mine = c * UC + x * UX
    left = c * UC + ((x + 3) % 4) * UX
    right = c * UC + ((x + 1) % 4) * UX

    def h1(i):
        return same(i, mine + yh * UY, UY, H1, yhp)

    def he(i, k):
        return same(i, mine + yh * UY, UY, HE + k, (xp, xm)[k])

    def h2(i, k):
        return same(i, mine + (1 - yh) * UY, UY, H2 + k, (xp, xm)[k])

    def h3(i, k, o):
        dev = ((xp, xm), (xp_other, xm_other))[o][k]
        return same(i, (left, right + UY)[k], UY, H3 + 2 * k + o, dev)

    def h4(i, k):
        return same(i, (mine, left, right)[k], UX, H4 + k, core)

    def summed(i, xd, h):
        at = xd * UX + h * UY
        a = part[i % 2, :, pl.ds(pl.multiple_of(c * UC + at, UY), UY), :]
        return a + b0_r[i, :, pl.ds(pl.multiple_of(at, UY), UY), :]

    def partial(i):
        s = i % 2
        for m in (0, 1):
            part[s, m] = dot_nt(w_in_t[m * U : (m + 1) * U, :], tg[0, i])
        part[s, 2] = dot_nt(w_down[...], tg[1, i])
        far = ((x + 2) % 4) * UX
        for k in (0, 1):
            for o in (0, 1):
                first = (c + o - 2 * c * o) * UC + far + k * UY
                x1_s[i, k, o] = part[s, :, pl.ds(pl.multiple_of(first, UY), UY), :].astype(BF)
                x1(i, k, o).start()
        for k in range(3):
            b0(i, k).start()

    def send_x2(i):
        for k in (0, 1):
            b0(i, k).wait()
            x1(i, k, 0).wait_recv()
            x1(i, k, 1).wait_recv()
            far = x1_r[i, k, 0].astype(F32) + x1_r[i, k, 1].astype(F32)
            x2_s[i, k] = (summed(i, (x + (1, 3)[k]) % 4, k) + far).astype(BF)
            x2(i, k).start()
            xe_s[i, k] = summed(i, (x + (1, 3)[k]) % 4, 1 - k).astype(BF)
            xe(i, k).start()
        b0(i, 2).wait()
        for h in (0, 1):
            own64[i % 2, h] = summed(i, x, h)

    def send_yb(i):
        for k in (0, 1):
            x2(i, k).wait_recv()
            xe(i, k).wait_recv()

        def total(h):
            return own64[i % 2, h] + (x2_r[i, h].astype(F32) + xe_r[i, 1 - h].astype(F32))

        yb_s[i] = total(1 - yh).astype(BF)
        yb(i).start()
        own32[i % 2] = total(yh)

    def send_h1(i):
        yb(i).wait_recv()
        full = own32[i % 2] + yb_r[i].astype(F32)
        gate, up, back = full[0], full[1], full[2]
        sigma = 1.0 / (1.0 + jnp.exp(-gate))
        silu = gate * sigma
        units = pl.ds(pl.multiple_of(mine + yh * UY, UY), UY)
        hid[0, units, lanes(i)] = (silu * up).astype(BF)
        hid[1, units, lanes(i)] = (back * up * sigma * (1.0 + gate * (1.0 - sigma))).astype(BF)
        hid[2, units, lanes(i)] = (back * silu).astype(BF)
        h1(i).start()
        he(i, 0).start()
        he(i, 1).start()

    def send_h2(i):
        h1(i).wait_recv()
        h2(i, 0).start()
        h2(i, 1).start()

    def send_h3(i):
        for k in (0, 1):
            he(i, k).wait_recv()
            h2(i, k).wait_recv()
            for o in (0, 1):
                h3(i, k, o).start()
        for k in range(3):
            h4(i, k).start()

    def grads_in(g):
        pair = lanes(g - 1, 2)
        for n in range(0, DM, 256):
            tok = tg[0, pl.ds(g - 1, 2), :, n : n + 256].reshape(2 * ROWS, 256)
            for m in (0, 1):
                sum_in[m * U : (m + 1) * U, n : n + 256] += dot(hid[1 + m, :, pair], tok)

    def grads_down(g):
        pair = lanes(g - 1, 2)
        for n in range(0, DM, 256):
            sc = tg[1, pl.ds(g - 1, 2), :, n : n + 256].reshape(2 * ROWS, 256)
            sum_down[:, n : n + 256] += dot(hid[0, :, pair], sc)

    def zf(col, h):
        return remote(
            zf_s.at[col, h], zf_r.at[col, h], d_ss.at[2 * col, h], d_rs.at[2 * col, h], (zm, zp)[h]
        )

    def zf_right(h):
        return remote(zg_s.at[h], zg_r.at[h], d_ss.at[0, 2 + h], d_rs.at[0, 2 + h], (zm, zp)[h])

    def dz(col, k, h):
        sem = 2 * col + 1
        return remote(
            dz_s.at[col, k, h], dz_r.at[col, k, h],
            d_ss.at[sem, 2 * k + h], d_rs.at[sem, 2 * k + h], (zp, zm)[(h + 1 + k) % 2],
        )

    def dz_right(k, h):
        return remote(
            dw_s.at[k, h], dw_r.at[k, h],
            d_ss.at[4, 2 * k + h], d_rs.at[4, 2 * k + h], (zp, zm)[(h + 1 + k) % 2],
        )

    def dy(h):
        return remote(dy_s.at[h], dy_r.at[h], d_ss.at[2, 2 + h], d_rs.at[2, 2 + h], ylp)

    def dy_right(k, h):
        return remote(dv_s.at[k, h], dv_r.at[k, h], d_ss.at[5 + h, k], d_rs.at[5 + h, k], ylp)

    def of_left(j, h):
        return to[j, :LEFT, h * HALF : (h + 1) * HALF]

    def of_right(j, h):
        return to[j, LEFT:, h * HALF : (h + 1) * HALF]

    def send_zf(col):
        for h in (0, 1):
            zf_s[col, h] = of_left((F, YF)[col], h).astype(BF)
            zf(col, h).start()

    def send_dz(col, k):
        for h in (0, 1):
            total = of_left(((C1, C2), (Y1, Y2))[col][k], h)
            if k == 0:
                zf(col, h).wait_recv()
                total = total + zf_r[col, h].astype(F32)
            dz_s[col, k, h] = total.astype(BF)
            dz(col, k, h).start()

    def column(col, h):
        dz(col, 0, h).wait_recv()
        dz(col, 1, h).wait_recv()
        return of_left((OWN, YO)[col], h) + (
            dz_r[col, 0, h].astype(F32) + dz_r[col, 1, h].astype(F32)
        )

    def send_dy():
        for h in (0, 1):
            dy_s[h] = column(1, h).astype(BF)
            dy(h).start()

    def send_dy_right(k):
        for h in (0, 1):
            dv_s[k, h] = of_right((YO, Y1, YF, Y2)[k], h).astype(BF)
            dy_right(k, h).start()

    def both_right(j, k, h):
        dy_right(k, h).wait_recv()
        return of_right(j, h) + dv_r[k, h].astype(F32)

    def send_zf_right():
        for h in (0, 1):
            zg_s[h] = both_right(F, 2, h).astype(BF)
            zf_right(h).start()

    def send_dz_right(k):
        for h in (0, 1):
            total = both_right((C1, C2)[k], 1 + 2 * k, h)
            if k == 0:
                zf_right(h).wait_recv()
                total = total + zg_r[h].astype(F32)
            dw_s[k, h] = total.astype(BF)
            dz_right(k, h).start()

    def term(j):
        for k in range(3):
            h4(j, k).wait_recv()
        for k in (0, 1):
            h3(j, k, 0).wait_recv()
            h3(j, k, 1).wait_recv()
        h = hid[1:, :, lanes(j)].reshape(2 * U, ROWS)
        for m in range(0, DM, 512):
            to[j, m : m + 512, :] = dot(w_in[m : m + 512, :], h)

    def arrivals(t):
        @pl.when(t == C1)
        def _():
            arrived(C1, 0)
            gather(C1, F, 0, zp).start()
            arrived(C1, 1)
            gather(C1, F, 1, zm).start()

        @pl.when(t == YO)
        def _():
            arrived(YO, 0)
            gather(YO, Y1, 0, zp).start()
            arrived(YO, 1)
            gather(YO, Y1, 1, zm).start()

        @pl.when(t == F)
        def _():
            gather_yf(1, 1).start()

        @pl.when(t == Y1)
        def _():
            for h in (0, 1):
                arrived(Y1, h)
                gather_yf(0, h).start()

        @pl.when(t == YF)
        def _():
            for kind in (0, 1):
                for h in (0, 1):
                    gather_yf(kind, h).wait_recv()

        for chunk in (Y2, C2):

            @pl.when(t == chunk)
            def _():
                arrived(chunk, 0)
                arrived(chunk, 1)

    def tick(t, carry):
        def stage(step, lag):
            pl.when((t >= lag) & (t < CHUNKS + lag))(lambda: step(t - lag))

        def at(when, step, *args):
            pl.when(t == when)(lambda: step(*args))

        stage(send_h1, 2)
        stage(term, 4)
        at(YO + 4, send_dy_right, 0)
        at(F + 4, send_zf, 0)
        at(F + 5, send_dz, 0, 0)
        at(Y1 + 5, send_dy_right, 1)
        at(YF + 4, send_dy_right, 2)
        at(YF + 4, send_zf, 1)
        at(Y2 + 4, send_dy_right, 3)
        at(Y2 + 4, send_dz, 1, 1)
        at(Y2 + 4, send_dz, 1, 0)
        at(Y2 + 4, send_zf_right)
        at(C2 + 4, send_dz, 0, 1)
        at(C2 + 4, send_dy)
        at(C2 + 4, send_dz_right, 0)
        at(C2 + 4, send_dz_right, 1)
        arrivals(t)
        stage(partial, 0)

        stage(send_yb, 1)
        stage(send_h3, 3)

        @pl.when(t == YO)
        def _():
            arrived(F, 0)
            arrived(F, 1)
            gather_yf(1, 0).start()

        @pl.when(t == F)
        def _():
            gather(YO, Y2, 1, zp).start()
            gather(YO, Y2, 0, zm).start()

        pl.when((t == 5) | (t == 7))(lambda: grads_in(t - 4))

        stage(send_x2, 0)
        stage(send_h2, 2)

        @pl.when(t == Y1)
        def _():
            gather(OWN, C2, 1, zp).start()
            gather(OWN, C2, 0, zm).start()

        pl.when((t == 6) | (t == 8))(lambda: grads_down(t - 5))
        return carry

    lax.fori_loop(0, CHUNKS + 4, tick, 0)

    stores = []

    def store(src, dst):
        stores.append(pltpu.make_async_copy(src, dst, o_s.at[len(stores)]))
        stores[-1].start()

    grads_in(Y1 + 1)
    grads_in(CHUNKS - 1)
    blocks = [part.at[k // 3, k % 3] for k in range(6)] + [stage_more.at[0], stage_more.at[1]]
    for first, out in ((0, out_gate), (U, out_up)):
        for u in range(0, U, 256):
            for d in range(0, DM, 512):
                block = blocks[len(stores)]
                block[...] = sum_in[first + u : first + u + 256, d : d + 512].T
                store(block, out.at[pl.ds(d, 512), pl.ds(u, 256)])
    grads_down(Y1 + 1)
    grads_down(CHUNKS - 1)
    store(sum_down, out_down)

    def left_all(i, carry):
        for k in (0, 1):
            for o in (0, 1):
                x1(i, k, o).wait_send()
                h3(i, k, o).wait_send()
            xe(i, k).wait_send()
            he(i, k).wait_send()
            x2(i, k).wait_send()
            h2(i, k).wait_send()
        yb(i).wait_send()
        h1(i).wait_send()
        for k in range(3):
            h4(i, k).wait_send()
        return carry

    lax.fori_loop(0, CHUNKS, left_all, 0)
    for dst in (C1, YO, F, Y1, Y2, C2):
        for h in (0, 1):
            gather(OWN, dst, h, zp).wait_send()
    for h in (0, 1):
        gather_yf(0, h).wait_send()
        gather_yf(1, h).wait_send()
    for h in (0, 1):
        for col in (0, 1):
            zf(col, h).wait_send()
            dz(col, 0, h).wait_send()
            dz(col, 1, h).wait_send()
        for k in range(4):
            dy_right(k, h).wait_send()
        zf_right(h).wait_send()
        dy(h).wait_send()
        dz_right(0, h).wait_send()
        dz_right(1, h).wait_send()

    for h in (0, 1):
        rows = pl.ds(h * HALF, HALF)
        total = both_right(OWN, 0, h)
        dz_right(0, h).wait_recv()
        dz_right(1, h).wait_recv()
        total = total + (dw_r[0, h].astype(F32) + dw_r[1, h].astype(F32))
        out_tok[rows, LEFT:] = total.T.astype(BF)
        total = column(0, h)
        dy(h).wait_recv()
        out_tok[rows, :LEFT] = (total + dy_r[h].astype(F32)).T.astype(BF)
    for copy in stores:
        copy.wait()


def place(*refs):
    ins, outs, by_way, sems = refs[:4], refs[4:8], refs[8:12], refs[12]
    reads, writes = [], []
    for k, (a, b, v) in enumerate(zip(ins, outs, by_way)):
        count = a.shape[0] // PIECES
        for p in range(PIECES):
            rows = pl.ds(p * count, count)
            reads.append(pltpu.make_async_copy(a.at[rows], v.at[rows], sems.at[0, k, p]))
            writes.append(pltpu.make_async_copy(v.at[rows], b.at[rows], sems.at[1, k, p]))
    for copy in reads:
        copy.start()
    for read, write in zip(reads, writes):
        read.wait()
        write.start()
    for copy in writes:
        copy.wait()


def local(tokens, grad_out, keep, count, w_gate, w_up, w_down):
    vmem = pl.BlockSpec(memory_space=pltpu.VMEM)
    anywhere = pl.BlockSpec(memory_space=pl.ANY)
    dma = pltpu.SemaphoreType.DMA
    outs = pl.pallas_call(
        kernel,
        out_shape=(
            jax.ShapeDtypeStruct((ROWS, DM), BF),
            jax.ShapeDtypeStruct((DM, U), F32),
            jax.ShapeDtypeStruct((DM, U), F32),
            jax.ShapeDtypeStruct((U, DM), F32),
        ),
        in_specs=[anywhere, vmem, vmem, pl.BlockSpec(memory_space=pltpu.SMEM)] + [anywhere] * 3,
        out_specs=[vmem] + [anywhere] * 3,
        scratch_shapes=[
            pltpu.VMEM((DM, 2 * U), BF),
            pltpu.VMEM((2 * U, DM), BF),
            pltpu.VMEM((U, DM), BF),
            pltpu.VMEM((2 * U, DM), F32),
            pltpu.VMEM((U, DM), F32),
            pltpu.VMEM((2, 512, 256), F32),
            pltpu.VMEM((2, CHUNKS, ROWS, DM), BF),
            pltpu.VMEM((2, 3, U, ROWS), F32),
            pltpu.VMEM((CHUNKS, 3, UC, ROWS), F32),
            pltpu.VMEM((CHUNKS, 2, 2, 3, UY, ROWS), BF),
            pltpu.VMEM((CHUNKS, 2, 2, 3, UY, ROWS), BF),
            pltpu.VMEM((CHUNKS, 2, 3, UY, ROWS), BF),
            pltpu.VMEM((CHUNKS, 2, 3, UY, ROWS), BF),
            pltpu.VMEM((CHUNKS, 2, 3, UY, ROWS), BF),
            pltpu.VMEM((CHUNKS, 2, 3, UY, ROWS), BF),
            pltpu.VMEM((CHUNKS, 3, UY, ROWS), BF),
            pltpu.VMEM((CHUNKS, 3, UY, ROWS), BF),
            pltpu.VMEM((2, 2, 3, UY, ROWS), F32),
            pltpu.VMEM((2, 3, UY, ROWS), F32),
            pltpu.VMEM((3, U, CHUNKS * ROWS), BF),
            pltpu.VMEM((CHUNKS, DM, ROWS), F32),
            pltpu.VMEM((2, LEFT, HALF), BF),
            pltpu.VMEM((2, LEFT, HALF), BF),
            pltpu.VMEM((2, 2, LEFT, HALF), BF),
            pltpu.VMEM((2, 2, LEFT, HALF), BF),
            pltpu.VMEM((2, 2, 2, LEFT, HALF), BF),
            pltpu.VMEM((2, 2, 2, LEFT, HALF), BF),
            pltpu.VMEM((4, 2, RIGHT, HALF), BF),
            pltpu.VMEM((4, 2, RIGHT, HALF), BF),
            pltpu.VMEM((2, RIGHT, HALF), BF),
            pltpu.VMEM((2, RIGHT, HALF), BF),
            pltpu.VMEM((2, 2, RIGHT, HALF), BF),
            pltpu.VMEM((2, 2, RIGHT, HALF), BF),
            dma((MESSAGES, CHUNKS)),
            dma((MESSAGES, CHUNKS)),
            dma((CHUNKS + 1, 2)),
            dma((CHUNKS + 1, 2)),
            dma((7, 4)),
            dma((7, 4)),
            dma((9,)),
            dma((4,)),
        ],
        compiler_params=pltpu.CompilerParams(
            collective_id=0, has_side_effects=True, vmem_limit_bytes=62 * 1024 * 1024
        ),
        cost_estimate=pl.CostEstimate(
            flops=16 * 2048 * DM * U, bytes_accessed=16 << 20, transcendentals=0
        ),
    )(tokens, grad_out, keep, count, w_gate, w_up, w_down)
    return pl.pallas_call(
        place,
        out_shape=tuple(jax.ShapeDtypeStruct(o.shape, o.dtype) for o in outs),
        in_specs=[anywhere] * 4,
        out_specs=[anywhere] * 4,
        scratch_shapes=[pltpu.VMEM(o.shape, o.dtype) for o in outs] + [dma((2, 4, PIECES))],
        compiler_params=pltpu.CompilerParams(vmem_limit_bytes=62 * 1024 * 1024),
    )(*outs)


def solution(mesh):
    placed = (
        P("wide", "mp"),
        P("wide", "mp"),
        P("wide"),
        P(),
        P("mp", "wide"),
        P("mp", "wide"),
        P("wide", "mp"),
    )
    return jax.shard_map(
        local,
        mesh=mesh,
        in_specs=placed,
        out_specs=(P("wide", "mp"), P("mp", "wide"), P("mp", "wide"), P("wide", "mp")),
        check_vma=False,
    )
```

```python
import functools

import jax
import jax.numpy as jnp
from jax import lax
from jax.experimental import pallas as pl
from jax.experimental.pallas import tpu as pltpu
from jax.sharding import PartitionSpec as P

BF = jnp.bfloat16
F32 = jnp.float32
ROWS = 256
HALF = 128
DM = 1024
U = 512
UC, UX, UY = 256, 64, 32
LEFT, RIGHT = 512, 512
CHUNKS = 8
PIECES = 4
OWN, C1, YO, F, Y1, YF, Y2, C2 = range(CHUNKS)
B0, X1, XE, X2, YB, H1, HE, H2, H3, H4 = 0, 3, 7, 9, 11, 12, 13, 15, 17, 21
MESSAGES = 24


def dot(a, b):
    return lax.dot_general(a, b, (((1,), (0,)), ((), ())), preferred_element_type=F32)


def dot_nt(a, b):
    return lax.dot_general(a, b, (((1,), (1,)), ((), ())), preferred_element_type=F32)


def kernel(
    tokens, grad_out, keep, count, in_gate, in_up, in_down,
    out_tok, out_gate, out_up, out_down,
    w_in, w_in_t, w_down, sum_in, sum_down, stage_more, tg, part, b0_r, x1_s, x1_r, xe_s, xe_r, x2_s, x2_r,
    yb_s, yb_r, own64, own32, hid,
    to, dy_s, dy_r, zf_s, zf_r, dz_s, dz_r, dv_s, dv_r, zg_s, zg_r, dw_s, dw_r,
    c_ss, c_rs, a_ss, a_rs, d_ss, d_rs, o_s, i_s,
):
    mp, wide = lax.axis_index("mp"), lax.axis_index("wide")
    x, yh, c = mp // 4, (mp // 2) % 2, mp % 2
    core = (mp + 1 - 2 * c, wide)
    xp = ((mp + 4) % 16, wide)
    xm = ((mp + 12) % 16, wide)
    xp_other = ((mp + 4) % 16 + 1 - 2 * c, wide)
    xm_other = ((mp + 12) % 16 + 1 - 2 * c, wide)
    yhp = (mp + 2 - 4 * yh, wide)
    ylp = (mp, wide + 1 - 2 * (wide % 2))
    zp = (mp, (wide + 2) % 8)
    zm = (mp, (wide + 6) % 8)

    def remote(src, dst, ssem, rsem, dev):
        return pltpu.make_async_remote_copy(
            src_ref=src, dst_ref=dst, send_sem=ssem, recv_sem=rsem,
            device_id=dev, device_id_type=pl.DeviceIdType.MESH,
        )

    loads = [
        pltpu.make_async_copy(a, b, i_s.at[k])
        for k, (a, b) in enumerate(
            (
                (tokens, tg.at[0, OWN]),
                (in_gate, w_in.at[:, pl.ds(0, U)]),
                (in_up, w_in.at[:, pl.ds(U, U)]),
                (in_down, w_down),
            )
        )
    ]
    for load in loads:
        load.start()

    barrier = pltpu.get_barrier_semaphore()
    for dev in (core, xp, xm, xp_other, xm_other, yhp, ylp, zp, zm):
        pl.semaphore_signal(barrier, inc=1, device_id=dev, device_id_type=pl.DeviceIdType.MESH)

    for r in range(0, ROWS, 128):
        factor = keep[pl.ds(r, 128)].astype(F32) / count[0].astype(F32)
        factor = jnp.broadcast_to(factor[None, :], (128, 128)).T
        for n in range(0, DM, 128):
            block = grad_out[r : r + 128, n : n + 128].astype(F32) * factor
            tg[1, OWN, r : r + 128, n : n + 128] = block.astype(BF)
    loads[0].wait()
    pl.semaphore_wait(barrier, 9)

    def gather(src, dst, h, dev):
        rows = pl.ds(h * HALF, HALF)
        return remote(
            tg.at[:, src, rows], tg.at[:, dst, rows], a_ss.at[dst, h], a_rs.at[dst, h], dev
        )

    def gather_yf(kind, h):
        rows = pl.ds(h * HALF, HALF)
        return remote(
            tg.at[kind, (Y1, F)[kind], rows], tg.at[kind, YF, rows],
            a_ss.at[(YF, CHUNKS)[kind], h], a_rs.at[(YF, CHUNKS)[kind], h],
            ((zp, zm)[h], ylp)[kind],
        )

    def arrived(dst, h):
        gather(OWN, dst, h, zp).wait_recv()

    gather(OWN, C1, 0, zp).start()
    gather(OWN, C1, 1, zm).start()
    gather(OWN, YO, 0, ylp).start()
    gather(OWN, YO, 1, ylp).start()

    for load in loads[1:]:
        load.wait()
    for n in range(0, 2 * U, 256):
        w_in_t[n : n + 256, :] = w_in[:, n : n + 256].T
    sum_in[...] = jnp.zeros_like(sum_in)
    sum_down[...] = jnp.zeros_like(sum_down)

    def b0(i, k):
        at = pl.multiple_of(((x + (1, 3, 0)[k]) % 4) * UX, UX)
        src = part.at[i % 2, :, pl.ds(pl.multiple_of((1 - c) * UC + at, UX), UX)]
        return remote(
            src, b0_r.at[i, :, pl.ds(at, UX)], c_ss.at[B0 + k, i], c_rs.at[B0 + k, i], core
        )

    def x1(i, k, o):
        sem = X1 + 2 * k + o
        dev = ((xp, xm), (xp_other, xm_other))[o][k]
        return remote(
            x1_s.at[i, k, o], x1_r.at[i, k, o], c_ss.at[sem, i], c_rs.at[sem, i], dev
        )

    def along_x(i, k, sem, src, dst):
        return remote(
            src.at[i, k], dst.at[i, k], c_ss.at[sem + k, i], c_rs.at[sem + k, i], (xp, xm)[k]
        )

    def xe(i, k):
        return along_x(i, k, XE, xe_s, xe_r)

    def x2(i, k):
        return along_x(i, k, X2, x2_s, x2_r)

    def yb(i):
        return remote(yb_s.at[i], yb_r.at[i], c_ss.at[YB, i], c_rs.at[YB, i], yhp)

    def lanes(i, n=1):
        return pl.ds(pl.multiple_of(i * ROWS, ROWS), n * ROWS)

    def same(i, first, n, sem, dev):
        block = hid.at[:, pl.ds(pl.multiple_of(first, UY), n), lanes(i)]
        return remote(block, block, c_ss.at[sem, i], c_rs.at[sem, i], dev)

    mine = c * UC + x * UX
    left = c * UC + ((x + 3) % 4) * UX
    right = c * UC + ((x + 1) % 4) * UX

    def h1(i):
        return same(i, mine + yh * UY, UY, H1, yhp)

    def he(i, k):
        return same(i, mine + yh * UY, UY, HE + k, (xp, xm)[k])

    def h2(i, k):
        return same(i, mine + (1 - yh) * UY, UY, H2 + k, (xp, xm)[k])

    def h3(i, k, o):
        dev = ((xp, xm), (xp_other, xm_other))[o][k]
        return same(i, (left, right + UY)[k], UY, H3 + 2 * k + o, dev)

    def h4(i, k):
        return same(i, (mine, left, right)[k], UX, H4 + k, core)

    def summed(i, xd, h):
        at = xd * UX + h * UY
        a = part[i % 2, :, pl.ds(pl.multiple_of(c * UC + at, UY), UY), :]
        return a + b0_r[i, :, pl.ds(pl.multiple_of(at, UY), UY), :]

    def partial(i):
        s = i % 2
        for m in (0, 1):
            part[s, m] = dot_nt(w_in_t[m * U : (m + 1) * U, :], tg[0, i])
        part[s, 2] = dot_nt(w_down[...], tg[1, i])
        far = ((x + 2) % 4) * UX
        for k in (0, 1):
            for o in (0, 1):
                first = (c + o - 2 * c * o) * UC + far + k * UY
                x1_s[i, k, o] = part[s, :, pl.ds(pl.multiple_of(first, UY), UY), :].astype(BF)
                x1(i, k, o).start()
        for k in range(3):
            b0(i, k).start()

    def send_x2(i):
        for k in (0, 1):
            b0(i, k).wait()
            x1(i, k, 0).wait_recv()
            x1(i, k, 1).wait_recv()
            far = x1_r[i, k, 0].astype(F32) + x1_r[i, k, 1].astype(F32)
            x2_s[i, k] = (summed(i, (x + (1, 3)[k]) % 4, k) + far).astype(BF)
            x2(i, k).start()
            xe_s[i, k] = summed(i, (x + (1, 3)[k]) % 4, 1 - k).astype(BF)
            xe(i, k).start()
        b0(i, 2).wait()
        for h in (0, 1):
            own64[i % 2, h] = summed(i, x, h)

    def send_yb(i):
        for k in (0, 1):
            x2(i, k).wait_recv()
            xe(i, k).wait_recv()

        def total(h):
            return own64[i % 2, h] + (x2_r[i, h].astype(F32) + xe_r[i, 1 - h].astype(F32))

        yb_s[i] = total(1 - yh).astype(BF)
        yb(i).start()
        own32[i % 2] = total(yh)

    def send_h1(i):
        yb(i).wait_recv()
        full = own32[i % 2] + yb_r[i].astype(F32)
        gate, up, back = full[0], full[1], full[2]
        sigma = 1.0 / (1.0 + jnp.exp(-gate))
        silu = gate * sigma
        units = pl.ds(pl.multiple_of(mine + yh * UY, UY), UY)
        hid[0, units, lanes(i)] = (silu * up).astype(BF)
        hid[1, units, lanes(i)] = (back * up * sigma * (1.0 + gate * (1.0 - sigma))).astype(BF)
        hid[2, units, lanes(i)] = (back * silu).astype(BF)
        h1(i).start()
        he(i, 0).start()
        he(i, 1).start()

    def send_h2(i):
        h1(i).wait_recv()
        h2(i, 0).start()
        h2(i, 1).start()

    def send_h3(i):
        for k in (0, 1):
            he(i, k).wait_recv()
            h2(i, k).wait_recv()
            for o in (0, 1):
                h3(i, k, o).start()
        for k in range(3):
            h4(i, k).start()

    def grads_in(g):
        pair = lanes(g - 1, 2)
        for n in range(0, DM, 256):
            tok = tg[0, pl.ds(g - 1, 2), :, n : n + 256].reshape(2 * ROWS, 256)
            for m in (0, 1):
                sum_in[m * U : (m + 1) * U, n : n + 256] += dot(hid[1 + m, :, pair], tok)

    def grads_down(g):
        pair = lanes(g - 1, 2)
        for n in range(0, DM, 256):
            sc = tg[1, pl.ds(g - 1, 2), :, n : n + 256].reshape(2 * ROWS, 256)
            sum_down[:, n : n + 256] += dot(hid[0, :, pair], sc)

    def zf(col, h):
        return remote(
            zf_s.at[col, h], zf_r.at[col, h], d_ss.at[2 * col, h], d_rs.at[2 * col, h], (zm, zp)[h]
        )

    def zf_right(h):
        return remote(zg_s.at[h], zg_r.at[h], d_ss.at[0, 2 + h], d_rs.at[0, 2 + h], (zm, zp)[h])

    def dz(col, k, h):
        sem = 2 * col + 1
        return remote(
            dz_s.at[col, k, h], dz_r.at[col, k, h],
            d_ss.at[sem, 2 * k + h], d_rs.at[sem, 2 * k + h], (zp, zm)[(h + 1 + k) % 2],
        )

    def dz_right(k, h):
        return remote(
            dw_s.at[k, h], dw_r.at[k, h],
            d_ss.at[4, 2 * k + h], d_rs.at[4, 2 * k + h], (zp, zm)[(h + 1 + k) % 2],
        )

    def dy(h):
        return remote(dy_s.at[h], dy_r.at[h], d_ss.at[2, 2 + h], d_rs.at[2, 2 + h], ylp)

    def dy_right(k, h):
        return remote(dv_s.at[k, h], dv_r.at[k, h], d_ss.at[5 + h, k], d_rs.at[5 + h, k], ylp)

    def of_left(j, h):
        return to[j, :LEFT, h * HALF : (h + 1) * HALF]

    def of_right(j, h):
        return to[j, LEFT:, h * HALF : (h + 1) * HALF]

    def send_zf(col):
        for h in (0, 1):
            zf_s[col, h] = of_left((F, YF)[col], h).astype(BF)
            zf(col, h).start()

    def send_dz(col, k):
        for h in (0, 1):
            total = of_left(((C1, C2), (Y1, Y2))[col][k], h)
            if k == 0:
                zf(col, h).wait_recv()
                total = total + zf_r[col, h].astype(F32)
            dz_s[col, k, h] = total.astype(BF)
            dz(col, k, h).start()

    def column(col, h):
        dz(col, 0, h).wait_recv()
        dz(col, 1, h).wait_recv()
        return of_left((OWN, YO)[col], h) + (
            dz_r[col, 0, h].astype(F32) + dz_r[col, 1, h].astype(F32)
        )

    def send_dy():
        for h in (0, 1):
            dy_s[h] = column(1, h).astype(BF)
            dy(h).start()

    def send_dy_right(k):
        for h in (0, 1):
            dv_s[k, h] = of_right((YO, Y1, YF, Y2)[k], h).astype(BF)
            dy_right(k, h).start()

    def both_right(j, k, h):
        dy_right(k, h).wait_recv()
        return of_right(j, h) + dv_r[k, h].astype(F32)

    def send_zf_right():
        for h in (0, 1):
            zg_s[h] = both_right(F, 2, h).astype(BF)
            zf_right(h).start()

    def send_dz_right(k):
        for h in (0, 1):
            total = both_right((C1, C2)[k], 1 + 2 * k, h)
            if k == 0:
                zf_right(h).wait_recv()
                total = total + zg_r[h].astype(F32)
            dw_s[k, h] = total.astype(BF)
            dz_right(k, h).start()

    def term(j):
        for k in range(3):
            h4(j, k).wait_recv()
        for k in (0, 1):
            h3(j, k, 0).wait_recv()
            h3(j, k, 1).wait_recv()
        h = hid[1:, :, lanes(j)].reshape(2 * U, ROWS)
        for m in range(0, DM, 512):
            to[j, m : m + 512, :] = dot(w_in[m : m + 512, :], h)

    def arrivals(t):
        @pl.when(t == C1)
        def _():
            arrived(C1, 0)
            gather(C1, F, 0, zp).start()
            arrived(C1, 1)
            gather(C1, F, 1, zm).start()

        @pl.when(t == YO)
        def _():
            arrived(YO, 0)
            gather(YO, Y1, 0, zp).start()
            arrived(YO, 1)
            gather(YO, Y1, 1, zm).start()

        @pl.when(t == F)
        def _():
            gather_yf(1, 1).start()

        @pl.when(t == Y1)
        def _():
            for h in (0, 1):
                arrived(Y1, h)
                gather_yf(0, h).start()

        @pl.when(t == YF)
        def _():
            for kind in (0, 1):
                for h in (0, 1):
                    gather_yf(kind, h).wait_recv()

        for chunk in (Y2, C2):

            @pl.when(t == chunk)
            def _():
                arrived(chunk, 0)
                arrived(chunk, 1)

    def tick(t, carry):
        def stage(step, lag):
            pl.when((t >= lag) & (t < CHUNKS + lag))(lambda: step(t - lag))

        def at(when, step, *args):
            pl.when(t == when)(lambda: step(*args))

        stage(send_h1, 2)
        stage(term, 4)
        at(YO + 4, send_dy_right, 0)
        at(F + 4, send_zf, 0)
        at(F + 5, send_dz, 0, 0)
        at(YF + 4, send_dy_right, 2)
        at(YF + 4, send_zf, 1)
        at(Y2 + 4, send_dy_right, 3)
        at(Y2 + 4, send_dz, 1, 1)
        at(Y2 + 4, send_dz, 1, 0)
        at(Y2 + 4, send_zf_right)
        at(C2 + 4, send_dz, 0, 1)
        at(C2 + 4, send_dy)
        at(C2 + 4, send_dz_right, 0)
        at(C2 + 4, send_dz_right, 1)
        arrivals(t)
        stage(partial, 0)

        stage(send_yb, 1)
        stage(send_h3, 3)

        @pl.when(t == YO)
        def _():
            arrived(F, 0)
            arrived(F, 1)
            gather_yf(1, 0).start()

        @pl.when(t == F)
        def _():
            gather(YO, Y2, 1, zp).start()
            gather(YO, Y2, 0, zm).start()

        pl.when((t >= 5) & (t % 2 == 1))(lambda: grads_in(t - 4))

        stage(send_x2, 0)
        stage(send_h2, 2)

        @pl.when(t == Y1)
        def _():
            gather(OWN, C2, 1, zp).start()
            gather(OWN, C2, 0, zm).start()

        at(Y1 + 4, send_dy_right, 1)
        pl.when((t >= 6) & (t % 2 == 0))(lambda: grads_down(t - 5))
        return carry

    lax.fori_loop(0, CHUNKS + 4, tick, 0)

    stores = []

    def store(src, dst):
        stores.append(pltpu.make_async_copy(src, dst, o_s.at[len(stores)]))
        stores[-1].start()

    blocks = [part.at[k // 3, k % 3] for k in range(6)] + [stage_more.at[0], stage_more.at[1]]
    for first, out in ((0, out_gate), (U, out_up)):
        for u in range(0, U, 256):
            for d in range(0, DM, 512):
                block = blocks[len(stores)]
                block[...] = sum_in[first + u : first + u + 256, d : d + 512].T
                store(block, out.at[pl.ds(d, 512), pl.ds(u, 256)])
    grads_down(CHUNKS - 1)
    store(sum_down, out_down)

    def left_all(i, carry):
        for k in (0, 1):
            for o in (0, 1):
                x1(i, k, o).wait_send()
                h3(i, k, o).wait_send()
            xe(i, k).wait_send()
            he(i, k).wait_send()
            x2(i, k).wait_send()
            h2(i, k).wait_send()
        yb(i).wait_send()
        h1(i).wait_send()
        for k in range(3):
            h4(i, k).wait_send()
        return carry

    lax.fori_loop(0, CHUNKS, left_all, 0)
    for dst in (C1, YO, F, Y1, Y2, C2):
        for h in (0, 1):
            gather(OWN, dst, h, zp).wait_send()
    for h in (0, 1):
        gather_yf(0, h).wait_send()
        gather_yf(1, h).wait_send()
    for h in (0, 1):
        for col in (0, 1):
            zf(col, h).wait_send()
            dz(col, 0, h).wait_send()
            dz(col, 1, h).wait_send()
        for k in range(4):
            dy_right(k, h).wait_send()
        zf_right(h).wait_send()
        dy(h).wait_send()
        dz_right(0, h).wait_send()
        dz_right(1, h).wait_send()

    for h in (0, 1):
        rows = pl.ds(h * HALF, HALF)
        total = both_right(OWN, 0, h)
        dz_right(0, h).wait_recv()
        dz_right(1, h).wait_recv()
        total = total + (dw_r[0, h].astype(F32) + dw_r[1, h].astype(F32))
        out_tok[rows, LEFT:] = total.T.astype(BF)
        total = column(0, h)
        dy(h).wait_recv()
        out_tok[rows, :LEFT] = (total + dy_r[h].astype(F32)).T.astype(BF)
    for copy in stores:
        copy.wait()


def place(*refs):
    ins, outs, by_way, sems = refs[:4], refs[4:8], refs[8:12], refs[12]
    reads, writes = [], []
    for k, (a, b, v) in enumerate(zip(ins, outs, by_way)):
        count = a.shape[0] // PIECES
        for p in range(PIECES):
            rows = pl.ds(p * count, count)
            reads.append(pltpu.make_async_copy(a.at[rows], v.at[rows], sems.at[0, k, p]))
            writes.append(pltpu.make_async_copy(v.at[rows], b.at[rows], sems.at[1, k, p]))
    for copy in reads:
        copy.start()
    for read, write in zip(reads, writes):
        read.wait()
        write.start()
    for copy in writes:
        copy.wait()


def local(tokens, grad_out, keep, count, w_gate, w_up, w_down):
    vmem = pl.BlockSpec(memory_space=pltpu.VMEM)
    anywhere = pl.BlockSpec(memory_space=pl.ANY)
    dma = pltpu.SemaphoreType.DMA
    outs = pl.pallas_call(
        kernel,
        out_shape=(
            jax.ShapeDtypeStruct((ROWS, DM), BF),
            jax.ShapeDtypeStruct((DM, U), F32),
            jax.ShapeDtypeStruct((DM, U), F32),
            jax.ShapeDtypeStruct((U, DM), F32),
        ),
        in_specs=[anywhere, vmem, vmem, pl.BlockSpec(memory_space=pltpu.SMEM)] + [anywhere] * 3,
        out_specs=[vmem] + [anywhere] * 3,
        scratch_shapes=[
            pltpu.VMEM((DM, 2 * U), BF),
            pltpu.VMEM((2 * U, DM), BF),
            pltpu.VMEM((U, DM), BF),
            pltpu.VMEM((2 * U, DM), F32),
            pltpu.VMEM((U, DM), F32),
            pltpu.VMEM((2, 512, 256), F32),
            pltpu.VMEM((2, CHUNKS, ROWS, DM), BF),
            pltpu.VMEM((2, 3, U, ROWS), F32),
            pltpu.VMEM((CHUNKS, 3, UC, ROWS), F32),
            pltpu.VMEM((CHUNKS, 2, 2, 3, UY, ROWS), BF),
            pltpu.VMEM((CHUNKS, 2, 2, 3, UY, ROWS), BF),
            pltpu.VMEM((CHUNKS, 2, 3, UY, ROWS), BF),
            pltpu.VMEM((CHUNKS, 2, 3, UY, ROWS), BF),
            pltpu.VMEM((CHUNKS, 2, 3, UY, ROWS), BF),
            pltpu.VMEM((CHUNKS, 2, 3, UY, ROWS), BF),
            pltpu.VMEM((CHUNKS, 3, UY, ROWS), BF),
            pltpu.VMEM((CHUNKS, 3, UY, ROWS), BF),
            pltpu.VMEM((2, 2, 3, UY, ROWS), F32),
            pltpu.VMEM((2, 3, UY, ROWS), F32),
            pltpu.VMEM((3, U, CHUNKS * ROWS), BF),
            pltpu.VMEM((CHUNKS, DM, ROWS), F32),
            pltpu.VMEM((2, LEFT, HALF), BF),
            pltpu.VMEM((2, LEFT, HALF), BF),
            pltpu.VMEM((2, 2, LEFT, HALF), BF),
            pltpu.VMEM((2, 2, LEFT, HALF), BF),
            pltpu.VMEM((2, 2, 2, LEFT, HALF), BF),
            pltpu.VMEM((2, 2, 2, LEFT, HALF), BF),
            pltpu.VMEM((4, 2, RIGHT, HALF), BF),
            pltpu.VMEM((4, 2, RIGHT, HALF), BF),
            pltpu.VMEM((2, RIGHT, HALF), BF),
            pltpu.VMEM((2, RIGHT, HALF), BF),
            pltpu.VMEM((2, 2, RIGHT, HALF), BF),
            pltpu.VMEM((2, 2, RIGHT, HALF), BF),
            dma((MESSAGES, CHUNKS)),
            dma((MESSAGES, CHUNKS)),
            dma((CHUNKS + 1, 2)),
            dma((CHUNKS + 1, 2)),
            dma((7, 4)),
            dma((7, 4)),
            dma((9,)),
            dma((4,)),
        ],
        compiler_params=pltpu.CompilerParams(
            collective_id=0, has_side_effects=True, vmem_limit_bytes=62 * 1024 * 1024
        ),
        cost_estimate=pl.CostEstimate(
            flops=16 * 2048 * DM * U, bytes_accessed=16 << 20, transcendentals=0
        ),
    )(tokens, grad_out, keep, count, w_gate, w_up, w_down)
    return pl.pallas_call(
        place,
        out_shape=tuple(jax.ShapeDtypeStruct(o.shape, o.dtype) for o in outs),
        in_specs=[anywhere] * 4,
        out_specs=[anywhere] * 4,
        scratch_shapes=[pltpu.VMEM(o.shape, o.dtype) for o in outs] + [dma((2, 4, PIECES))],
        compiler_params=pltpu.CompilerParams(vmem_limit_bytes=62 * 1024 * 1024),
    )(*outs)


def solution(mesh):
    placed = (
        P("wide", "mp"),
        P("wide", "mp"),
        P("wide"),
        P(),
        P("mp", "wide"),
        P("mp", "wide"),
        P("wide", "mp"),
    )
    return jax.shard_map(
        local,
        mesh=mesh,
        in_specs=placed,
        out_specs=(P("wide", "mp"), P("mp", "wide"), P("mp", "wide"), P("wide", "mp")),
        check_vma=False,
    )
```

```python
import functools

import jax
import jax.numpy as jnp
from jax import lax
from jax.experimental import pallas as pl
from jax.experimental.pallas import tpu as pltpu
from jax.sharding import PartitionSpec as P

BF = jnp.bfloat16
F32 = jnp.float32
ROWS = 256
HALF = 128
DM = 1024
U = 512
UC, UX, UY = 256, 64, 32
LEFT, RIGHT = 512, 512
CHUNKS = 8
PIECES = 4
OWN, C1, YO, F, Y1, YF, Y2, C2 = range(CHUNKS)
B0, X1, XE, X2, YB, H1, HE, H2, H3, H4 = 0, 3, 7, 9, 11, 12, 13, 15, 17, 21
MESSAGES = 24


def dot(a, b):
    return lax.dot_general(a, b, (((1,), (0,)), ((), ())), preferred_element_type=F32)


def dot_nt(a, b):
    return lax.dot_general(a, b, (((1,), (1,)), ((), ())), preferred_element_type=F32)


def kernel(
    tokens, grad_out, keep, count, in_gate, in_up, in_down,
    out_tok, out_gate, out_up, out_down,
    w_in, w_in_t, w_down, sum_in, sum_down, stage_more, tg, part, b0_r, x1_s, x1_r, xe_s, xe_r, x2_s, x2_r,
    yb_s, yb_r, own64, own32, hid,
    to, dy_s, dy_r, zf_s, zf_r, dz_s, dz_r, dv_s, dv_r, zg_s, zg_r, dw_s, dw_r,
    c_ss, c_rs, a_ss, a_rs, d_ss, d_rs, o_s, i_s,
):
    mp, wide = lax.axis_index("mp"), lax.axis_index("wide")
    x, yh, c = mp // 4, (mp // 2) % 2, mp % 2
    core = (mp + 1 - 2 * c, wide)
    xp = ((mp + 4) % 16, wide)
    xm = ((mp + 12) % 16, wide)
    xp_other = ((mp + 4) % 16 + 1 - 2 * c, wide)
    xm_other = ((mp + 12) % 16 + 1 - 2 * c, wide)
    yhp = (mp + 2 - 4 * yh, wide)
    ylp = (mp, wide + 1 - 2 * (wide % 2))
    zp = (mp, (wide + 2) % 8)
    zm = (mp, (wide + 6) % 8)

    def remote(src, dst, ssem, rsem, dev):
        return pltpu.make_async_remote_copy(
            src_ref=src, dst_ref=dst, send_sem=ssem, recv_sem=rsem,
            device_id=dev, device_id_type=pl.DeviceIdType.MESH,
        )

    loads = [
        pltpu.make_async_copy(a, b, i_s.at[k])
        for k, (a, b) in enumerate(
            (
                (tokens, tg.at[0, OWN]),
                (in_gate, w_in.at[:, pl.ds(0, U)]),
                (in_up, w_in.at[:, pl.ds(U, U)]),
                (in_down, w_down),
            )
        )
    ]
    for load in loads:
        load.start()

    barrier = pltpu.get_barrier_semaphore()
    for dev in (core, xp, xm, xp_other, xm_other, yhp, ylp, zp, zm):
        pl.semaphore_signal(barrier, inc=1, device_id=dev, device_id_type=pl.DeviceIdType.MESH)

    for r in range(0, ROWS, 128):
        factor = keep[pl.ds(r, 128)].astype(F32) / count[0].astype(F32)
        factor = jnp.broadcast_to(factor[None, :], (128, 128)).T
        for n in range(0, DM, 128):
            block = grad_out[r : r + 128, n : n + 128].astype(F32) * factor
            tg[1, OWN, r : r + 128, n : n + 128] = block.astype(BF)
    loads[0].wait()
    pl.semaphore_wait(barrier, 9)

    def gather(src, dst, h, dev):
        rows = pl.ds(h * HALF, HALF)
        return remote(
            tg.at[:, src, rows], tg.at[:, dst, rows], a_ss.at[dst, h], a_rs.at[dst, h], dev
        )

    def gather_yf(kind, h):
        rows = pl.ds(h * HALF, HALF)
        return remote(
            tg.at[kind, (Y1, F)[kind], rows], tg.at[kind, YF, rows],
            a_ss.at[(YF, CHUNKS)[kind], h], a_rs.at[(YF, CHUNKS)[kind], h],
            ((zp, zm)[h], ylp)[kind],
        )

    def arrived(dst, h):
        gather(OWN, dst, h, zp).wait_recv()

    gather(OWN, C1, 0, zp).start()
    gather(OWN, C1, 1, zm).start()
    gather(OWN, YO, 0, ylp).start()
    gather(OWN, YO, 1, ylp).start()

    for load in loads[1:]:
        load.wait()
    for n in range(0, 2 * U, 256):
        w_in_t[n : n + 256, :] = w_in[:, n : n + 256].T
    sum_in[...] = jnp.zeros_like(sum_in)
    sum_down[...] = jnp.zeros_like(sum_down)

    def b0(i, k):
        at = pl.multiple_of(((x + (1, 3, 0)[k]) % 4) * UX, UX)
        src = part.at[i % 2, :, pl.ds(pl.multiple_of((1 - c) * UC + at, UX), UX)]
        return remote(
            src, b0_r.at[i, :, pl.ds(at, UX)], c_ss.at[B0 + k, i], c_rs.at[B0 + k, i], core
        )

    def x1(i, k, o):
        sem = X1 + 2 * k + o
        dev = ((xp, xm), (xp_other, xm_other))[o][k]
        return remote(
            x1_s.at[i, k, o], x1_r.at[i, k, o], c_ss.at[sem, i], c_rs.at[sem, i], dev
        )

    def along_x(i, k, sem, src, dst):
        return remote(
            src.at[i, k], dst.at[i, k], c_ss.at[sem + k, i], c_rs.at[sem + k, i], (xp, xm)[k]
        )

    def xe(i, k):
        return along_x(i, k, XE, xe_s, xe_r)

    def x2(i, k):
        return along_x(i, k, X2, x2_s, x2_r)

    def yb(i):
        return remote(yb_s.at[i], yb_r.at[i], c_ss.at[YB, i], c_rs.at[YB, i], yhp)

    def lanes(i, n=1):
        return pl.ds(pl.multiple_of(i * ROWS, ROWS), n * ROWS)

    def same(i, first, n, sem, dev):
        block = hid.at[:, pl.ds(pl.multiple_of(first, UY), n), lanes(i)]
        return remote(block, block, c_ss.at[sem, i], c_rs.at[sem, i], dev)

    mine = c * UC + x * UX
    left = c * UC + ((x + 3) % 4) * UX
    right = c * UC + ((x + 1) % 4) * UX

    def h1(i):
        return same(i, mine + yh * UY, UY, H1, yhp)

    def he(i, k):
        return same(i, mine + yh * UY, UY, HE + k, (xp, xm)[k])

    def h2(i, k):
        return same(i, mine + (1 - yh) * UY, UY, H2 + k, (xp, xm)[k])

    def h3(i, k, o):
        dev = ((xp, xm), (xp_other, xm_other))[o][k]
        return same(i, (left, right + UY)[k], UY, H3 + 2 * k + o, dev)

    def h4(i, k):
        return same(i, (mine, left, right)[k], UX, H4 + k, core)

    def summed(i, xd, h):
        at = xd * UX + h * UY
        a = part[i % 2, :, pl.ds(pl.multiple_of(c * UC + at, UY), UY), :]
        return a + b0_r[i, :, pl.ds(pl.multiple_of(at, UY), UY), :]

    def partial(i):
        s = i % 2
        for m in (0, 1):
            part[s, m] = dot_nt(w_in_t[m * U : (m + 1) * U, :], tg[0, i])
        part[s, 2] = dot_nt(w_down[...], tg[1, i])
        far = ((x + 2) % 4) * UX
        for k in (0, 1):
            for o in (0, 1):
                first = (c + o - 2 * c * o) * UC + far + k * UY
                x1_s[i, k, o] = part[s, :, pl.ds(pl.multiple_of(first, UY), UY), :].astype(BF)
                x1(i, k, o).start()
        for k in range(3):
            b0(i, k).start()

    def send_x2(i):
        for k in (0, 1):
            b0(i, k).wait()
            x1(i, k, 0).wait_recv()
            x1(i, k, 1).wait_recv()
            far = x1_r[i, k, 0].astype(F32) + x1_r[i, k, 1].astype(F32)
            x2_s[i, k] = (summed(i, (x + (1, 3)[k]) % 4, k) + far).astype(BF)
            x2(i, k).start()
            xe_s[i, k] = summed(i, (x + (1, 3)[k]) % 4, 1 - k).astype(BF)
            xe(i, k).start()
        b0(i, 2).wait()
        for h in (0, 1):
            own64[i % 2, h] = summed(i, x, h)

    def send_yb(i):
        for k in (0, 1):
            x2(i, k).wait_recv()
            xe(i, k).wait_recv()

        def total(h):
            return own64[i % 2, h] + (x2_r[i, h].astype(F32) + xe_r[i, 1 - h].astype(F32))

        yb_s[i] = total(1 - yh).astype(BF)
        yb(i).start()
        own32[i % 2] = total(yh)

    def send_h1(i):
        yb(i).wait_recv()
        full = own32[i % 2] + yb_r[i].astype(F32)
        gate, up, back = full[0], full[1], full[2]
        sigma = 1.0 / (1.0 + jnp.exp(-gate))
        silu = gate * sigma
        units = pl.ds(pl.multiple_of(mine + yh * UY, UY), UY)
        hid[0, units, lanes(i)] = (silu * up).astype(BF)
        hid[1, units, lanes(i)] = (back * up * sigma * (1.0 + gate * (1.0 - sigma))).astype(BF)
        hid[2, units, lanes(i)] = (back * silu).astype(BF)
        h1(i).start()
        he(i, 0).start()
        he(i, 1).start()

    def send_h2(i):
        h1(i).wait_recv()
        h2(i, 0).start()
        h2(i, 1).start()

    def send_h3(i):
        for k in (0, 1):
            he(i, k).wait_recv()
            h2(i, k).wait_recv()
            for o in (0, 1):
                h3(i, k, o).start()
        for k in range(3):
            h4(i, k).start()

    def grads_in(g):
        pair = lanes(g - 1, 2)
        for n in range(0, DM, 256):
            tok = tg[0, pl.ds(g - 1, 2), :, n : n + 256].reshape(2 * ROWS, 256)
            for m in (0, 1):
                sum_in[m * U : (m + 1) * U, n : n + 256] += dot(hid[1 + m, :, pair], tok)

    def grads_down(g):
        pair = lanes(g - 1, 2)
        for n in range(0, DM, 256):
            sc = tg[1, pl.ds(g - 1, 2), :, n : n + 256].reshape(2 * ROWS, 256)
            sum_down[:, n : n + 256] += dot(hid[0, :, pair], sc)

    def zf(col, h):
        return remote(
            zf_s.at[col, h], zf_r.at[col, h], d_ss.at[2 * col, h], d_rs.at[2 * col, h], (zm, zp)[h]
        )

    def zf_right(h):
        return remote(zg_s.at[h], zg_r.at[h], d_ss.at[0, 2 + h], d_rs.at[0, 2 + h], (zm, zp)[h])

    def dz(col, k, h):
        sem = 2 * col + 1
        return remote(
            dz_s.at[col, k, h], dz_r.at[col, k, h],
            d_ss.at[sem, 2 * k + h], d_rs.at[sem, 2 * k + h], (zp, zm)[(h + 1 + k) % 2],
        )

    def dz_right(k, h):
        return remote(
            dw_s.at[k, h], dw_r.at[k, h],
            d_ss.at[4, 2 * k + h], d_rs.at[4, 2 * k + h], (zp, zm)[(h + 1 + k) % 2],
        )

    def dy(h):
        return remote(dy_s.at[h], dy_r.at[h], d_ss.at[2, 2 + h], d_rs.at[2, 2 + h], ylp)

    def dy_right(k, h):
        return remote(dv_s.at[k, h], dv_r.at[k, h], d_ss.at[5 + h, k], d_rs.at[5 + h, k], ylp)

    def of_left(j, h):
        return to[j, :LEFT, h * HALF : (h + 1) * HALF]

    def of_right(j, h):
        return to[j, LEFT:, h * HALF : (h + 1) * HALF]

    def send_zf(col):
        for h in (0, 1):
            zf_s[col, h] = of_left((F, YF)[col], h).astype(BF)
            zf(col, h).start()

    def send_dz(col, k):
        for h in (0, 1):
            total = of_left(((C1, C2), (Y1, Y2))[col][k], h)
            if k == 0:
                zf(col, h).wait_recv()
                total = total + zf_r[col, h].astype(F32)
            dz_s[col, k, h] = total.astype(BF)
            dz(col, k, h).start()

    def column(col, h):
        dz(col, 0, h).wait_recv()
        dz(col, 1, h).wait_recv()
        return of_left((OWN, YO)[col], h) + (
            dz_r[col, 0, h].astype(F32) + dz_r[col, 1, h].astype(F32)
        )

    def send_dy():
        for h in (0, 1):
            dy_s[h] = column(1, h).astype(BF)
            dy(h).start()

    def send_dy_right(k):
        for h in (0, 1):
            dv_s[k, h] = of_right((YO, Y1, YF, Y2)[k], h).astype(BF)
            dy_right(k, h).start()

    def both_right(j, k, h):
        dy_right(k, h).wait_recv()
        return of_right(j, h) + dv_r[k, h].astype(F32)

    def send_zf_right():
        for h in (0, 1):
            zg_s[h] = both_right(F, 2, h).astype(BF)
            zf_right(h).start()

    def send_dz_right(k):
        for h in (0, 1):
            total = both_right((C1, C2)[k], 1 + 2 * k, h)
            if k == 0:
                zf_right(h).wait_recv()
                total = total + zg_r[h].astype(F32)
            dw_s[k, h] = total.astype(BF)
            dz_right(k, h).start()

    def term(j):
        for k in range(3):
            h4(j, k).wait_recv()
        for k in (0, 1):
            h3(j, k, 0).wait_recv()
            h3(j, k, 1).wait_recv()
        h = hid[1:, :, lanes(j)].reshape(2 * U, ROWS)
        for m in range(0, DM, 512):
            to[j, m : m + 512, :] = dot(w_in[m : m + 512, :], h)

    def arrivals(t):
        @pl.when(t == C1)
        def _():
            arrived(C1, 0)
            gather(C1, F, 0, zp).start()
            arrived(C1, 1)
            gather(C1, F, 1, zm).start()

        @pl.when(t == YO)
        def _():
            arrived(YO, 0)
            gather(YO, Y1, 0, zp).start()
            arrived(YO, 1)
            gather(YO, Y1, 1, zm).start()

        @pl.when(t == F)
        def _():
            gather_yf(1, 1).start()

        @pl.when(t == Y1)
        def _():
            for h in (0, 1):
                arrived(Y1, h)
                gather_yf(0, h).start()

        @pl.when(t == YF)
        def _():
            for kind in (0, 1):
                for h in (0, 1):
                    gather_yf(kind, h).wait_recv()

        for chunk in (Y2, C2):

            @pl.when(t == chunk)
            def _():
                arrived(chunk, 0)
                arrived(chunk, 1)

    def tick(t, carry):
        def stage(step, lag):
            pl.when((t >= lag) & (t < CHUNKS + lag))(lambda: step(t - lag))

        def at(when, step, *args):
            pl.when(t == when)(lambda: step(*args))

        stage(send_h1, 2)
        arrivals(t)
        stage(partial, 0)

        stage(send_yb, 1)
        stage(send_h3, 3)
        stage(term, 4)
        at(YO + 4, send_dy_right, 0)
        at(F + 4, send_zf, 0)
        at(F + 5, send_dz, 0, 0)
        at(Y1 + 4, send_dy_right, 1)
        at(YF + 4, send_dy_right, 2)
        at(YF + 4, send_zf, 1)
        at(Y2 + 4, send_dy_right, 3)
        at(Y2 + 4, send_dz, 1, 1)
        at(Y2 + 4, send_dz, 1, 0)
        at(Y2 + 4, send_zf_right)
        at(C2 + 4, send_dz, 0, 1)
        at(C2 + 4, send_dy)
        at(C2 + 4, send_dz_right, 0)
        at(C2 + 4, send_dz_right, 1)

        @pl.when(t == YO)
        def _():
            arrived(F, 0)
            arrived(F, 1)
            gather_yf(1, 0).start()

        @pl.when(t == F)
        def _():
            gather(YO, Y2, 1, zp).start()
            gather(YO, Y2, 0, zm).start()

        stage(send_x2, 0)
        stage(send_h2, 2)

        @pl.when(t == Y1)
        def _():
            gather(OWN, C2, 1, zp).start()
            gather(OWN, C2, 0, zm).start()

        pl.when((t >= 5) & (t % 2 == 1))(lambda: grads_in(t - 4))
        pl.when((t >= 6) & (t % 2 == 0))(lambda: grads_down(t - 5))
        return carry

    lax.fori_loop(0, CHUNKS + 4, tick, 0)

    stores = []

    def store(src, dst):
        stores.append(pltpu.make_async_copy(src, dst, o_s.at[len(stores)]))
        stores[-1].start()

    blocks = [part.at[k // 3, k % 3] for k in range(6)] + [stage_more.at[0], stage_more.at[1]]
    for first, out in ((0, out_gate), (U, out_up)):
        for u in range(0, U, 256):
            for d in range(0, DM, 512):
                block = blocks[len(stores)]
                block[...] = sum_in[first + u : first + u + 256, d : d + 512].T
                store(block, out.at[pl.ds(d, 512), pl.ds(u, 256)])
    grads_down(CHUNKS - 1)
    store(sum_down, out_down)

    def left_all(i, carry):
        for k in (0, 1):
            for o in (0, 1):
                x1(i, k, o).wait_send()
                h3(i, k, o).wait_send()
            xe(i, k).wait_send()
            he(i, k).wait_send()
            x2(i, k).wait_send()
            h2(i, k).wait_send()
        yb(i).wait_send()
        h1(i).wait_send()
        for k in range(3):
            h4(i, k).wait_send()
        return carry

    lax.fori_loop(0, CHUNKS, left_all, 0)
    for dst in (C1, YO, F, Y1, Y2, C2):
        for h in (0, 1):
            gather(OWN, dst, h, zp).wait_send()
    for h in (0, 1):
        gather_yf(0, h).wait_send()
        gather_yf(1, h).wait_send()
    for h in (0, 1):
        for col in (0, 1):
            zf(col, h).wait_send()
            dz(col, 0, h).wait_send()
            dz(col, 1, h).wait_send()
        for k in range(4):
            dy_right(k, h).wait_send()
        zf_right(h).wait_send()
        dy(h).wait_send()
        dz_right(0, h).wait_send()
        dz_right(1, h).wait_send()

    for h in (0, 1):
        rows = pl.ds(h * HALF, HALF)
        total = both_right(OWN, 0, h)
        dz_right(0, h).wait_recv()
        dz_right(1, h).wait_recv()
        total = total + (dw_r[0, h].astype(F32) + dw_r[1, h].astype(F32))
        out_tok[rows, LEFT:] = total.T.astype(BF)
        total = column(0, h)
        dy(h).wait_recv()
        out_tok[rows, :LEFT] = (total + dy_r[h].astype(F32)).T.astype(BF)
    for copy in stores:
        copy.wait()


def place(*refs):
    ins, outs, by_way, sems = refs[:4], refs[4:8], refs[8:12], refs[12]
    reads, writes = [], []
    for k, (a, b, v) in enumerate(zip(ins, outs, by_way)):
        count = a.shape[0] // PIECES
        for p in range(PIECES):
            rows = pl.ds(p * count, count)
            reads.append(pltpu.make_async_copy(a.at[rows], v.at[rows], sems.at[0, k, p]))
            writes.append(pltpu.make_async_copy(v.at[rows], b.at[rows], sems.at[1, k, p]))
    for copy in reads:
        copy.start()
    for read, write in zip(reads, writes):
        read.wait()
        write.start()
    for copy in writes:
        copy.wait()


def local(tokens, grad_out, keep, count, w_gate, w_up, w_down):
    vmem = pl.BlockSpec(memory_space=pltpu.VMEM)
    anywhere = pl.BlockSpec(memory_space=pl.ANY)
    dma = pltpu.SemaphoreType.DMA
    outs = pl.pallas_call(
        kernel,
        out_shape=(
            jax.ShapeDtypeStruct((ROWS, DM), BF),
            jax.ShapeDtypeStruct((DM, U), F32),
            jax.ShapeDtypeStruct((DM, U), F32),
            jax.ShapeDtypeStruct((U, DM), F32),
        ),
        in_specs=[anywhere, vmem, vmem, pl.BlockSpec(memory_space=pltpu.SMEM)] + [anywhere] * 3,
        out_specs=[vmem] + [anywhere] * 3,
        scratch_shapes=[
            pltpu.VMEM((DM, 2 * U), BF),
            pltpu.VMEM((2 * U, DM), BF),
            pltpu.VMEM((U, DM), BF),
            pltpu.VMEM((2 * U, DM), F32),
            pltpu.VMEM((U, DM), F32),
            pltpu.VMEM((2, 512, 256), F32),
            pltpu.VMEM((2, CHUNKS, ROWS, DM), BF),
            pltpu.VMEM((2, 3, U, ROWS), F32),
            pltpu.VMEM((CHUNKS, 3, UC, ROWS), F32),
            pltpu.VMEM((CHUNKS, 2, 2, 3, UY, ROWS), BF),
            pltpu.VMEM((CHUNKS, 2, 2, 3, UY, ROWS), BF),
            pltpu.VMEM((CHUNKS, 2, 3, UY, ROWS), BF),
            pltpu.VMEM((CHUNKS, 2, 3, UY, ROWS), BF),
            pltpu.VMEM((CHUNKS, 2, 3, UY, ROWS), BF),
            pltpu.VMEM((CHUNKS, 2, 3, UY, ROWS), BF),
            pltpu.VMEM((CHUNKS, 3, UY, ROWS), BF),
            pltpu.VMEM((CHUNKS, 3, UY, ROWS), BF),
            pltpu.VMEM((2, 2, 3, UY, ROWS), F32),
            pltpu.VMEM((2, 3, UY, ROWS), F32),
            pltpu.VMEM((3, U, CHUNKS * ROWS), BF),
            pltpu.VMEM((CHUNKS, DM, ROWS), F32),
            pltpu.VMEM((2, LEFT, HALF), BF),
            pltpu.VMEM((2, LEFT, HALF), BF),
            pltpu.VMEM((2, 2, LEFT, HALF), BF),
            pltpu.VMEM((2, 2, LEFT, HALF), BF),
            pltpu.VMEM((2, 2, 2, LEFT, HALF), BF),
            pltpu.VMEM((2, 2, 2, LEFT, HALF), BF),
            pltpu.VMEM((4, 2, RIGHT, HALF), BF),
            pltpu.VMEM((4, 2, RIGHT, HALF), BF),
            pltpu.VMEM((2, RIGHT, HALF), BF),
            pltpu.VMEM((2, RIGHT, HALF), BF),
            pltpu.VMEM((2, 2, RIGHT, HALF), BF),
            pltpu.VMEM((2, 2, RIGHT, HALF), BF),
            dma((MESSAGES, CHUNKS)),
            dma((MESSAGES, CHUNKS)),
            dma((CHUNKS + 1, 2)),
            dma((CHUNKS + 1, 2)),
            dma((7, 4)),
            dma((7, 4)),
            dma((9,)),
            dma((4,)),
        ],
        compiler_params=pltpu.CompilerParams(
            collective_id=0, has_side_effects=True, vmem_limit_bytes=62 * 1024 * 1024
        ),
        cost_estimate=pl.CostEstimate(
            flops=16 * 2048 * DM * U, bytes_accessed=16 << 20, transcendentals=0
        ),
    )(tokens, grad_out, keep, count, w_gate, w_up, w_down)
    return pl.pallas_call(
        place,
        out_shape=tuple(jax.ShapeDtypeStruct(o.shape, o.dtype) for o in outs),
        in_specs=[anywhere] * 4,
        out_specs=[anywhere] * 4,
        scratch_shapes=[pltpu.VMEM(o.shape, o.dtype) for o in outs] + [dma((2, 4, PIECES))],
        compiler_params=pltpu.CompilerParams(vmem_limit_bytes=62 * 1024 * 1024),
    )(*outs)


def solution(mesh):
    placed = (
        P("wide", "mp"),
        P("wide", "mp"),
        P("wide"),
        P(),
        P("mp", "wide"),
        P("mp", "wide"),
        P("wide", "mp"),
    )
    return jax.shard_map(
        local,
        mesh=mesh,
        in_specs=placed,
        out_specs=(P("wide", "mp"), P("mp", "wide"), P("mp", "wide"), P("wide", "mp")),
        check_vma=False,
    )
```

```python
import functools

import jax
import jax.numpy as jnp
from jax import lax
from jax.experimental import pallas as pl
from jax.experimental.pallas import tpu as pltpu
from jax.sharding import PartitionSpec as P

BF = jnp.bfloat16
F32 = jnp.float32
ROWS = 256
HALF = 128
DM = 1024
U = 512
UC, UX, UY = 256, 64, 32
LEFT, RIGHT = 512, 512
CHUNKS = 8
OWN, C1, YO, F, Y1, YF, Y2, C2 = range(CHUNKS)
B0, X1, XE, X2, YB, H1, HE, H2, H3, H4 = 0, 4, 6, 8, 10, 11, 12, 14, 16, 18
MESSAGES = 19


def dot(a, b):
    return lax.dot_general(a, b, (((1,), (0,)), ((), ())), preferred_element_type=F32)


def dot_nt(a, b):
    return lax.dot_general(a, b, (((1,), (1,)), ((), ())), preferred_element_type=F32)


def kernel(
    tokens, grad_out, keep, count, in_gate, in_up, in_down,
    out_tok, out_in, out_down,
    w_in, w_in_t, w_down, sum_in, sum_down, tg, part, b0_r, x1_s, x1_r, xe_s, xe_r, x2_s, x2_r,
    yb_s, yb_r, own64, own32, hid,
    to, dy_s, dy_r, zf_s, zf_r, dz_s, dz_r, dv_s, dv_r, zg_s, zg_r, dw_s, dw_r,
    c_ss, c_rs, a_ss, a_rs, d_ss, d_rs, o_s, i_s,
):
    mp, wide = lax.axis_index("mp"), lax.axis_index("wide")
    x, yh, c = mp // 4, (mp // 2) % 2, mp % 2
    core = (mp + 1 - 2 * c, wide)
    xp = ((mp + 4) % 16, wide)
    xm = ((mp + 12) % 16, wide)
    yhp = (mp + 2 - 4 * yh, wide)
    ylp = (mp, wide + 1 - 2 * (wide % 2))
    zp = (mp, (wide + 2) % 8)
    zm = (mp, (wide + 6) % 8)

    def remote(src, dst, ssem, rsem, dev):
        return pltpu.make_async_remote_copy(
            src_ref=src, dst_ref=dst, send_sem=ssem, recv_sem=rsem,
            device_id=dev, device_id_type=pl.DeviceIdType.MESH,
        )

    loads = [
        pltpu.make_async_copy(a, b, i_s.at[k])
        for k, (a, b) in enumerate(
            (
                (tokens, tg.at[0, OWN]),
                (in_gate, w_in.at[:, pl.ds(0, U)]),
                (in_up, w_in.at[:, pl.ds(U, U)]),
                (in_down, w_down),
            )
        )
    ]
    for load in loads:
        load.start()

    barrier = pltpu.get_barrier_semaphore()
    for dev in (core, xp, xm, yhp, ylp, zp, zm):
        pl.semaphore_signal(barrier, inc=1, device_id=dev, device_id_type=pl.DeviceIdType.MESH)

    for r in range(0, ROWS, 128):
        factor = keep[pl.ds(r, 128)].astype(F32) / count[0].astype(F32)
        factor = jnp.broadcast_to(factor[None, :], (128, 128)).T
        for n in range(0, DM, 128):
            block = grad_out[r : r + 128, n : n + 128].astype(F32) * factor
            tg[1, OWN, r : r + 128, n : n + 128] = block.astype(BF)
    loads[0].wait()
    pl.semaphore_wait(barrier, 7)

    def gather(src, dst, h, dev):
        rows = pl.ds(h * HALF, HALF)
        return remote(
            tg.at[:, src, rows], tg.at[:, dst, rows], a_ss.at[dst, h], a_rs.at[dst, h], dev
        )

    def gather_yf(kind, h):
        rows = pl.ds(h * HALF, HALF)
        return remote(
            tg.at[kind, (Y1, F)[kind], rows], tg.at[kind, YF, rows],
            a_ss.at[(YF, CHUNKS)[kind], h], a_rs.at[(YF, CHUNKS)[kind], h],
            ((zp, zm)[h], ylp)[kind],
        )

    def arrived(dst, h):
        gather(OWN, dst, h, zp).wait_recv()

    gather(OWN, C1, 0, zp).start()
    gather(OWN, C1, 1, zm).start()
    gather(OWN, YO, 0, ylp).start()
    gather(OWN, YO, 1, ylp).start()

    for load in loads[1:]:
        load.wait()
    for n in range(0, 2 * U, 256):
        w_in_t[n : n + 256, :] = w_in[:, n : n + 256].T
    sum_in[...] = jnp.zeros_like(sum_in)
    sum_down[...] = jnp.zeros_like(sum_down)

    def b0(i, k):
        at = pl.multiple_of(((x + (2, 1, 3, 0)[k]) % 4) * UX, UX)
        src = part.at[i % 2, :, pl.ds(pl.multiple_of((1 - c) * UC + at, UX), UX)]
        return remote(
            src, b0_r.at[i, :, pl.ds(at, UX)], c_ss.at[B0 + k, i], c_rs.at[B0 + k, i], core
        )

    def along_x(i, k, sem, src, dst):
        return remote(
            src.at[i, k], dst.at[i, k], c_ss.at[sem + k, i], c_rs.at[sem + k, i], (xp, xm)[k]
        )

    def x1(i, k):
        return along_x(i, k, X1, x1_s, x1_r)

    def xe(i, k):
        return along_x(i, k, XE, xe_s, xe_r)

    def x2(i, k):
        return along_x(i, k, X2, x2_s, x2_r)

    def yb(i):
        return remote(yb_s.at[i], yb_r.at[i], c_ss.at[YB, i], c_rs.at[YB, i], yhp)

    def lanes(i, n=1):
        return pl.ds(pl.multiple_of(i * ROWS, ROWS), n * ROWS)

    def same(i, first, n, sem, dev):
        block = hid.at[:, pl.ds(pl.multiple_of(first, UY), n), lanes(i)]
        return remote(block, block, c_ss.at[sem, i], c_rs.at[sem, i], dev)

    mine = c * UC + x * UX
    left = c * UC + ((x + 3) % 4) * UX
    right = c * UC + ((x + 1) % 4) * UX

    def h1(i):
        return same(i, mine + yh * UY, UY, H1, yhp)

    def he(i, k):
        return same(i, mine + yh * UY, UY, HE + k, (xp, xm)[k])

    def h2(i, k):
        return same(i, mine + (1 - yh) * UY, UY, H2 + k, (xp, xm)[k])

    def h3(i, k):
        return same(i, (left, right + UY)[k], UY, H3 + k, (xp, xm)[k])

    def h4(i):
        return same(i, c * UC, UC, H4, core)

    def summed(i, xd, h):
        at = xd * UX + h * UY
        a = part[i % 2, :, pl.ds(pl.multiple_of(c * UC + at, UY), UY), :]
        return a + b0_r[i, :, pl.ds(pl.multiple_of(at, UY), UY), :]

    def partial(i):
        s = i % 2
        for m in (0, 1):
            part[s, m] = dot_nt(w_in_t[m * U : (m + 1) * U, :], tg[0, i])
        part[s, 2] = dot_nt(w_down[...], tg[1, i])
        for k in range(4):
            b0(i, k).start()

    def send_x1(i):
        b0(i, 0).wait()
        for k in (0, 1):
            x1_s[i, k] = summed(i, (x + 2) % 4, k).astype(BF)
            x1(i, k).start()
        for k in (0, 1):
            b0(i, 1 + k).wait()
            xe_s[i, k] = summed(i, (x + (1, 3)[k]) % 4, 1 - k).astype(BF)
            xe(i, k).start()

    def send_x2(i):
        for k in (0, 1):
            x1(i, k).wait_recv()
            total = summed(i, (x + (1, 3)[k]) % 4, k) + x1_r[i, k].astype(F32)
            x2_s[i, k] = total.astype(BF)
            x2(i, k).start()
        b0(i, 3).wait()
        for h in (0, 1):
            xe(i, 1 - h).wait_recv()
            own64[i % 2, h] = summed(i, x, h) + xe_r[i, 1 - h].astype(F32)

    def send_yb(i):
        x2(i, 0).wait_recv()
        x2(i, 1).wait_recv()
        yb_s[i] = (own64[i % 2, 1 - yh] + x2_r[i, 1 - yh].astype(F32)).astype(BF)
        yb(i).start()
        own32[i % 2] = own64[i % 2, yh] + x2_r[i, yh].astype(F32)

    def send_h1(i):
        yb(i).wait_recv()
        full = own32[i % 2] + yb_r[i].astype(F32)
        gate, up, back = full[0], full[1], full[2]
        sigma = 1.0 / (1.0 + jnp.exp(-gate))
        silu = gate * sigma
        units = pl.ds(pl.multiple_of(mine + yh * UY, UY), UY)
        hid[0, units, lanes(i)] = (silu * up).astype(BF)
        hid[1, units, lanes(i)] = (back * up * sigma * (1.0 + gate * (1.0 - sigma))).astype(BF)
        hid[2, units, lanes(i)] = (back * silu).astype(BF)
        h1(i).start()
        he(i, 0).start()
        he(i, 1).start()

    def send_h2(i):
        h1(i).wait_recv()
        h2(i, 0).start()
        h2(i, 1).start()

    def send_h3(i):
        for k in (0, 1):
            he(i, k).wait_recv()
            h2(i, k).wait_recv()
            h3(i, k).start()

    def send_h4(i):
        h3(i, 0).wait_recv()
        h3(i, 1).wait_recv()
        h4(i).start()

    def grads_in(g):
        pair = lanes(g - 1, 2)
        for n in range(0, DM, 256):
            tok = tg[0, pl.ds(g - 1, 2), :, n : n + 256].reshape(2 * ROWS, 256)
            for m in (0, 1):
                sum_in[m * U : (m + 1) * U, n : n + 256] += dot(hid[1 + m, :, pair], tok)

    def grads_down(g):
        pair = lanes(g - 1, 2)
        for n in range(0, DM, 256):
            sc = tg[1, pl.ds(g - 1, 2), :, n : n + 256].reshape(2 * ROWS, 256)
            sum_down[:, n : n + 256] += dot(hid[0, :, pair], sc)

    def zf(col, h):
        return remote(
            zf_s.at[col, h], zf_r.at[col, h], d_ss.at[2 * col, h], d_rs.at[2 * col, h], (zm, zp)[h]
        )

    def zf_right(h):
        return remote(zg_s.at[h], zg_r.at[h], d_ss.at[0, 2 + h], d_rs.at[0, 2 + h], (zm, zp)[h])

    def dz(col, k, h):
        sem = 2 * col + 1
        return remote(
            dz_s.at[col, k, h], dz_r.at[col, k, h],
            d_ss.at[sem, 2 * k + h], d_rs.at[sem, 2 * k + h], (zp, zm)[(h + 1 + k) % 2],
        )

    def dz_right(k, h):
        return remote(
            dw_s.at[k, h], dw_r.at[k, h],
            d_ss.at[4, 2 * k + h], d_rs.at[4, 2 * k + h], (zp, zm)[(h + 1 + k) % 2],
        )

    def dy(h):
        return remote(dy_s.at[h], dy_r.at[h], d_ss.at[2, 2 + h], d_rs.at[2, 2 + h], ylp)

    def dy_right(k, h):
        return remote(dv_s.at[k, h], dv_r.at[k, h], d_ss.at[5 + h, k], d_rs.at[5 + h, k], ylp)

    def of_left(j, h):
        return to[j, :LEFT, h * HALF : (h + 1) * HALF]

    def of_right(j, h):
        return to[j, LEFT:, h * HALF : (h + 1) * HALF]

    def send_zf(col):
        for h in (0, 1):
            zf_s[col, h] = of_left((F, YF)[col], h).astype(BF)
            zf(col, h).start()

    def send_dz(col, k):
        for h in (0, 1):
            total = of_left(((C1, C2), (Y1, Y2))[col][k], h)
            if k == 0:
                zf(col, h).wait_recv()
                total = total + zf_r[col, h].astype(F32)
            dz_s[col, k, h] = total.astype(BF)
            dz(col, k, h).start()

    def column(col, h):
        dz(col, 0, h).wait_recv()
        dz(col, 1, h).wait_recv()
        return of_left((OWN, YO)[col], h) + (
            dz_r[col, 0, h].astype(F32) + dz_r[col, 1, h].astype(F32)
        )

    def send_dy():
        for h in (0, 1):
            dy_s[h] = column(1, h).astype(BF)
            dy(h).start()

    def send_dy_right(k):
        for h in (0, 1):
            dv_s[k, h] = of_right((YO, Y1, YF, Y2)[k], h).astype(BF)
            dy_right(k, h).start()

    def both_right(j, k, h):
        dy_right(k, h).wait_recv()
        return of_right(j, h) + dv_r[k, h].astype(F32)

    def send_zf_right():
        for h in (0, 1):
            zg_s[h] = both_right(F, 2, h).astype(BF)
            zf_right(h).start()

    def send_dz_right(k):
        for h in (0, 1):
            total = both_right((C1, C2)[k], 1 + 2 * k, h)
            if k == 0:
                zf_right(h).wait_recv()
                total = total + zg_r[h].astype(F32)
            dw_s[k, h] = total.astype(BF)
            dz_right(k, h).start()

    def term(j):
        h4(j).wait_recv()
        h = hid[1:, :, lanes(j)].reshape(2 * U, ROWS)
        for m in range(0, DM, 512):
            to[j, m : m + 512, :] = dot(w_in[m : m + 512, :], h)

    def arrivals(t):
        @pl.when(t == C1)
        def _():
            arrived(C1, 0)
            gather(C1, F, 0, zp).start()
            arrived(C1, 1)
            gather(C1, F, 1, zm).start()

        @pl.when(t == YO)
        def _():
            arrived(YO, 0)
            gather(YO, Y1, 0, zp).start()
            arrived(YO, 1)
            gather(YO, Y1, 1, zm).start()

        @pl.when(t == F)
        def _():
            gather_yf(1, 1).start()

        @pl.when(t == Y1)
        def _():
            for h in (0, 1):
                arrived(Y1, h)
                gather_yf(0, h).start()
            gather(YO, Y2, 1, zp).start()
            gather(YO, Y2, 0, zm).start()

        @pl.when(t == YF)
        def _():
            for kind in (0, 1):
                for h in (0, 1):
                    gather_yf(kind, h).wait_recv()

        for chunk in (Y2, C2):

            @pl.when(t == chunk)
            def _():
                arrived(chunk, 0)
                arrived(chunk, 1)

    def left_all(i):
        for k in (0, 1):
            x1(i, k).wait_send()
            xe(i, k).wait_send()
            he(i, k).wait_send()
            x2(i, k).wait_send()
            h2(i, k).wait_send()
            h3(i, k).wait_send()
        yb(i).wait_send()
        h1(i).wait_send()
        h4(i).wait_send()

    def tick(t, carry):
        def stage(step, lag):
            pl.when((t >= lag) & (t < CHUNKS + lag))(lambda: step(t - lag))

        def at(when, step, *args):
            pl.when(t == when)(lambda: step(*args))

        stage(send_yb, 2)
        stage(send_h3, 4)
        at(YF + 6, send_dz, 1, 0)
        arrivals(t)
        stage(partial, 0)

        stage(send_x2, 1)
        stage(send_h2, 3)
        stage(term, 5)
        for k, chunk in enumerate((YO, Y1, YF, Y2)):
            at(chunk + 5, send_dy_right, k)
        at(F + 5, send_zf, 0)
        at(F + 6, send_dz, 0, 0)
        at(YF + 5, send_zf, 1)
        at(Y2 + 5, send_dz, 1, 1)
        at(Y2 + 5, send_zf_right)
        at(C2 + 5, send_dz, 0, 1)
        at(C2 + 5, send_dy)
        at(C2 + 5, send_dz_right, 0)
        at(C2 + 5, send_dz_right, 1)

        @pl.when(t == YO)
        def _():
            arrived(F, 0)
            arrived(F, 1)
            gather_yf(1, 0).start()

        stage(send_h1, 2)
        stage(send_h4, 4)
        stage(send_x1, 0)

        @pl.when(t == Y1)
        def _():
            gather(OWN, C2, 1, zp).start()
            gather(OWN, C2, 0, zm).start()

        pl.when((t >= 7) & (t < CHUNKS + 5))(lambda: left_all(t - 7))
        pl.when((t >= 6) & (t % 2 == 0))(lambda: grads_in(t - 5))
        pl.when((t >= 7) & (t % 2 == 1))(lambda: grads_down(t - 6))
        return carry

    lax.fori_loop(0, CHUNKS + 5, tick, 0)

    stores = [
        pltpu.make_async_copy(sum_in, out_in, o_s.at[0]),
        pltpu.make_async_copy(sum_down, out_down, o_s.at[1]),
    ]
    stores[0].start()
    grads_down(CHUNKS - 1)
    stores[1].start()

    left_all(CHUNKS - 2)
    left_all(CHUNKS - 1)
    for dst in (C1, YO, F, Y1, Y2, C2):
        for h in (0, 1):
            gather(OWN, dst, h, zp).wait_send()
    for h in (0, 1):
        gather_yf(0, h).wait_send()
        gather_yf(1, h).wait_send()
    for h in (0, 1):
        for col in (0, 1):
            zf(col, h).wait_send()
            dz(col, 0, h).wait_send()
            dz(col, 1, h).wait_send()
        for k in range(4):
            dy_right(k, h).wait_send()
        zf_right(h).wait_send()
        dy(h).wait_send()
        dz_right(0, h).wait_send()
        dz_right(1, h).wait_send()

    for h in (0, 1):
        rows = pl.ds(h * HALF, HALF)
        total = both_right(OWN, 0, h)
        dz_right(0, h).wait_recv()
        dz_right(1, h).wait_recv()
        total = total + (dw_r[0, h].astype(F32) + dw_r[1, h].astype(F32))
        out_tok[rows, LEFT:] = total.T.astype(BF)
        total = column(0, h)
        dy(h).wait_recv()
        out_tok[rows, :LEFT] = (total + dy_r[h].astype(F32)).T.astype(BF)
    for copy in stores:
        copy.wait()


def place(tok, sums, down, out_tok, out_gate, out_up, out_down, v_tok, v_sums, v_down, v_out, sems):
    reads, writes = [], []

    def piece(src, via, dst, by_way=None):
        k = len(reads)
        reads.append(pltpu.make_async_copy(src, via, sems.at[0, k]))
        writes.append(pltpu.make_async_copy(via if by_way is None else by_way, dst, sems.at[1, k]))
        reads[-1].start()

    turns = []
    for o, out in enumerate((out_gate, out_up)):
        for u in range(0, U, 256):
            for d in range(0, DM, 512):
                src = (pl.ds(o * U + u, 256), pl.ds(d, 512))
                dst = (pl.ds(d, 512), pl.ds(u, 256))
                turns.append((src, (o, *dst)))
                piece(sums.at[src], v_sums.at[src], out.at[dst], v_out.at[(o, *dst)])
    for p in range(0, U, 128):
        rows = pl.ds(p, 128)
        piece(down.at[rows], v_down.at[rows], out_down.at[rows])
    piece(tok, v_tok, out_tok)
    for k, (read, write) in enumerate(zip(reads, writes)):
        read.wait()
        if k < len(turns):
            src, dst = turns[k]
            v_out[dst] = v_sums[src].T
        write.start()
    for write in writes:
        write.wait()


def local(tokens, grad_out, keep, count, w_gate, w_up, w_down):
    vmem = pl.BlockSpec(memory_space=pltpu.VMEM)
    anywhere = pl.BlockSpec(memory_space=pl.ANY)
    dma = pltpu.SemaphoreType.DMA
    outs = pl.pallas_call(
        kernel,
        out_shape=(
            jax.ShapeDtypeStruct((ROWS, DM), BF),
            jax.ShapeDtypeStruct((2 * U, DM), F32),
            jax.ShapeDtypeStruct((U, DM), F32),
        ),
        in_specs=[anywhere, vmem, vmem, pl.BlockSpec(memory_space=pltpu.SMEM)] + [anywhere] * 3,
        out_specs=[vmem] + [anywhere] * 2,
        scratch_shapes=[
            pltpu.VMEM((DM, 2 * U), BF),
            pltpu.VMEM((2 * U, DM), BF),
            pltpu.VMEM((U, DM), BF),
            pltpu.VMEM((2 * U, DM), F32),
            pltpu.VMEM((U, DM), F32),
            pltpu.VMEM((2, CHUNKS, ROWS, DM), BF),
            pltpu.VMEM((2, 3, U, ROWS), F32),
            pltpu.VMEM((CHUNKS, 3, UC, ROWS), F32),
            pltpu.VMEM((CHUNKS, 2, 3, UY, ROWS), BF),
            pltpu.VMEM((CHUNKS, 2, 3, UY, ROWS), BF),
            pltpu.VMEM((CHUNKS, 2, 3, UY, ROWS), BF),
            pltpu.VMEM((CHUNKS, 2, 3, UY, ROWS), BF),
            pltpu.VMEM((CHUNKS, 2, 3, UY, ROWS), BF),
            pltpu.VMEM((CHUNKS, 2, 3, UY, ROWS), BF),
            pltpu.VMEM((CHUNKS, 3, UY, ROWS), BF),
            pltpu.VMEM((CHUNKS, 3, UY, ROWS), BF),
            pltpu.VMEM((2, 2, 3, UY, ROWS), F32),
            pltpu.VMEM((2, 3, UY, ROWS), F32),
            pltpu.VMEM((3, U, CHUNKS * ROWS), BF),
            pltpu.VMEM((CHUNKS, DM, ROWS), F32),
            pltpu.VMEM((2, LEFT, HALF), BF),
            pltpu.VMEM((2, LEFT, HALF), BF),
            pltpu.VMEM((2, 2, LEFT, HALF), BF),
            pltpu.VMEM((2, 2, LEFT, HALF), BF),
            pltpu.VMEM((2, 2, 2, LEFT, HALF), BF),
            pltpu.VMEM((2, 2, 2, LEFT, HALF), BF),
            pltpu.VMEM((4, 2, RIGHT, HALF), BF),
            pltpu.VMEM((4, 2, RIGHT, HALF), BF),
            pltpu.VMEM((2, RIGHT, HALF), BF),
            pltpu.VMEM((2, RIGHT, HALF), BF),
            pltpu.VMEM((2, 2, RIGHT, HALF), BF),
            pltpu.VMEM((2, 2, RIGHT, HALF), BF),
            dma((MESSAGES, CHUNKS)),
            dma((MESSAGES, CHUNKS)),
            dma((CHUNKS + 1, 2)),
            dma((CHUNKS + 1, 2)),
            dma((7, 4)),
            dma((7, 4)),
            dma((2,)),
            dma((4,)),
        ],
        compiler_params=pltpu.CompilerParams(
            collective_id=0, has_side_effects=True, vmem_limit_bytes=62 * 1024 * 1024
        ),
        cost_estimate=pl.CostEstimate(
            flops=16 * 2048 * DM * U, bytes_accessed=16 << 20, transcendentals=0
        ),
    )(tokens, grad_out, keep, count, w_gate, w_up, w_down)
    return pl.pallas_call(
        place,
        out_shape=(
            jax.ShapeDtypeStruct((ROWS, DM), BF),
            jax.ShapeDtypeStruct((DM, U), F32),
            jax.ShapeDtypeStruct((DM, U), F32),
            jax.ShapeDtypeStruct((U, DM), F32),
        ),
        in_specs=[anywhere] * 3,
        out_specs=[anywhere] * 4,
        scratch_shapes=[
            pltpu.VMEM((ROWS, DM), BF),
            pltpu.VMEM((2 * U, DM), F32),
            pltpu.VMEM((U, DM), F32),
            pltpu.VMEM((2, DM, U), F32),
            dma((2, 13)),
        ],
        compiler_params=pltpu.CompilerParams(vmem_limit_bytes=62 * 1024 * 1024),
    )(*outs)


def solution(mesh):
    placed = (
        P("wide", "mp"),
        P("wide", "mp"),
        P("wide"),
        P(),
        P("mp", "wide"),
        P("mp", "wide"),
        P("wide", "mp"),
    )
    return jax.shard_map(
        local,
        mesh=mesh,
        in_specs=placed,
        out_specs=(P("wide", "mp"), P("mp", "wide"), P("mp", "wide"), P("wide", "mp")),
        check_vma=False,
    )
```

```python
import functools

import jax
import jax.numpy as jnp
from jax import lax
from jax.experimental import pallas as pl
from jax.experimental.pallas import tpu as pltpu
from jax.sharding import PartitionSpec as P

BF = jnp.bfloat16
F32 = jnp.float32
ROWS = 256
HALF = 128
DM = 1024
U = 512
UC, UX, UY = 256, 64, 32
LEFT, RIGHT = 512, 512
CHUNKS = 8
OWN, C1, YO, F, Y1, YF, Y2, C2 = range(CHUNKS)
B0, X1, XE, X2, YB, H1, HE, H2, H3, H4 = 0, 4, 8, 10, 12, 13, 14, 16, 18, 22
MESSAGES = 25
FAST = YF


def dot(a, b):
    return lax.dot_general(a, b, (((1,), (0,)), ((), ())), preferred_element_type=F32)


def dot_nt(a, b):
    return lax.dot_general(a, b, (((1,), (1,)), ((), ())), preferred_element_type=F32)


def kernel(
    tokens, grad_out, keep, count, in_gate, in_up, in_down,
    out_tok, out_in, out_down,
    w_in, w_in_t, w_down, sum_in, sum_down, tg, part, b0_r, x1_s, x1_r, xe_s, xe_r, x2_s, x2_r,
    yb_s, yb_r, own64, own32, hid,
    to, dy_s, dy_r, zf_s, zf_r, dz_s, dz_r, dv_s, dv_r, zg_s, zg_r, dw_s, dw_r,
    c_ss, c_rs, a_ss, a_rs, d_ss, d_rs, o_s, i_s,
):
    mp, wide = lax.axis_index("mp"), lax.axis_index("wide")
    x, yh, c = mp // 4, (mp // 2) % 2, mp % 2
    core = (mp + 1 - 2 * c, wide)
    xp = ((mp + 4) % 16, wide)
    xm = ((mp + 12) % 16, wide)
    xp_other = ((mp + 4) % 16 + 1 - 2 * c, wide)
    xm_other = ((mp + 12) % 16 + 1 - 2 * c, wide)
    yhp = (mp + 2 - 4 * yh, wide)
    ylp = (mp, wide + 1 - 2 * (wide % 2))
    zp = (mp, (wide + 2) % 8)
    zm = (mp, (wide + 6) % 8)

    def remote(src, dst, ssem, rsem, dev):
        return pltpu.make_async_remote_copy(
            src_ref=src, dst_ref=dst, send_sem=ssem, recv_sem=rsem,
            device_id=dev, device_id_type=pl.DeviceIdType.MESH,
        )

    loads = [
        pltpu.make_async_copy(a, b, i_s.at[k])
        for k, (a, b) in enumerate(
            (
                (tokens, tg.at[0, OWN]),
                (in_gate, w_in.at[:, pl.ds(0, U)]),
                (in_up, w_in.at[:, pl.ds(U, U)]),
                (in_down, w_down),
            )
        )
    ]
    for load in loads:
        load.start()

    barrier = pltpu.get_barrier_semaphore()
    for dev in (core, xp, xm, xp_other, xm_other, yhp, ylp, zp, zm):
        pl.semaphore_signal(barrier, inc=1, device_id=dev, device_id_type=pl.DeviceIdType.MESH)

    for r in range(0, ROWS, 128):
        factor = keep[pl.ds(r, 128)].astype(F32) / count[0].astype(F32)
        factor = jnp.broadcast_to(factor[None, :], (128, 128)).T
        for n in range(0, DM, 128):
            block = grad_out[r : r + 128, n : n + 128].astype(F32) * factor
            tg[1, OWN, r : r + 128, n : n + 128] = block.astype(BF)
    loads[0].wait()
    pl.semaphore_wait(barrier, 9)

    def gather(src, dst, h, dev):
        rows = pl.ds(h * HALF, HALF)
        return remote(
            tg.at[:, src, rows], tg.at[:, dst, rows], a_ss.at[dst, h], a_rs.at[dst, h], dev
        )

    def gather_yf(kind, h):
        rows = pl.ds(h * HALF, HALF)
        return remote(
            tg.at[kind, (Y1, F)[kind], rows], tg.at[kind, YF, rows],
            a_ss.at[(YF, CHUNKS)[kind], h], a_rs.at[(YF, CHUNKS)[kind], h],
            ((zp, zm)[h], ylp)[kind],
        )

    def arrived(dst, h):
        gather(OWN, dst, h, zp).wait_recv()

    gather(OWN, C1, 0, zp).start()
    gather(OWN, C1, 1, zm).start()
    gather(OWN, YO, 0, ylp).start()
    gather(OWN, YO, 1, ylp).start()

    for load in loads[1:]:
        load.wait()
    for n in range(0, 2 * U, 256):
        w_in_t[n : n + 256, :] = w_in[:, n : n + 256].T
    sum_in[...] = jnp.zeros_like(sum_in)
    sum_down[...] = jnp.zeros_like(sum_down)

    def b0(i, k):
        at = pl.multiple_of(((x + (2, 1, 3, 0)[k]) % 4) * UX, UX)
        src = part.at[i % 2, :, pl.ds(pl.multiple_of((1 - c) * UC + at, UX), UX)]
        return remote(
            src, b0_r.at[i, :, pl.ds(at, UX)], c_ss.at[B0 + k, i], c_rs.at[B0 + k, i], core
        )

    def along_x(i, k, sem, src, dst):
        return remote(
            src.at[i, k], dst.at[i, k], c_ss.at[sem + k, i], c_rs.at[sem + k, i], (xp, xm)[k]
        )

    def x1(i, k, o=0):
        sem = X1 + 2 * k + o
        dev = ((xp, xm), (xp_other, xm_other))[o][k]
        return remote(
            x1_s.at[i, k, o], x1_r.at[i, k, o], c_ss.at[sem, i], c_rs.at[sem, i], dev
        )

    def xe(i, k):
        return along_x(i, k, XE, xe_s, xe_r)

    def x2(i, k):
        return along_x(i, k, X2, x2_s, x2_r)

    def yb(i):
        return remote(yb_s.at[i], yb_r.at[i], c_ss.at[YB, i], c_rs.at[YB, i], yhp)

    def lanes(i, n=1):
        return pl.ds(pl.multiple_of(i * ROWS, ROWS), n * ROWS)

    def same(i, first, n, sem, dev):
        block = hid.at[:, pl.ds(pl.multiple_of(first, UY), n), lanes(i)]
        return remote(block, block, c_ss.at[sem, i], c_rs.at[sem, i], dev)

    mine = c * UC + x * UX
    left = c * UC + ((x + 3) % 4) * UX
    right = c * UC + ((x + 1) % 4) * UX

    def h1(i):
        return same(i, mine + yh * UY, UY, H1, yhp)

    def he(i, k):
        return same(i, mine + yh * UY, UY, HE + k, (xp, xm)[k])

    def h2(i, k):
        return same(i, mine + (1 - yh) * UY, UY, H2 + k, (xp, xm)[k])

    def h3(i, k, o=0):
        dev = ((xp, xm), (xp_other, xm_other))[o][k]
        return same(i, (left, right + UY)[k], UY, H3 + 2 * k + o, dev)

    def h4(i):
        return same(i, c * UC, UC, H4, core)

    def h4_fast(i, k):
        return same(i, (mine, left, right)[k], UX, H4 + k, core)

    def summed(i, xd, h):
        at = xd * UX + h * UY
        a = part[i % 2, :, pl.ds(pl.multiple_of(c * UC + at, UY), UY), :]
        return a + b0_r[i, :, pl.ds(pl.multiple_of(at, UY), UY), :]

    def partial(i):
        s = i % 2
        for m in (0, 1):
            part[s, m] = dot_nt(w_in_t[m * U : (m + 1) * U, :], tg[0, i])
        part[s, 2] = dot_nt(w_down[...], tg[1, i])

        @pl.when(i < FAST)
        def _():
            b0(i, 0).start()

        @pl.when(i >= FAST)
        def _():
            far = ((x + 2) % 4) * UX
            for k in (0, 1):
                for o in (0, 1):
                    first = (c + o - 2 * c * o) * UC + far + k * UY
                    mine_far = part[s, :, pl.ds(pl.multiple_of(first, UY), UY), :]
                    x1_s[i, k, o] = mine_far.astype(BF)
                    x1(i, k, o).start()

        for k in (1, 2, 3):
            b0(i, k).start()

    def send_x1(i):
        b0(i, 0).wait()
        for k in (0, 1):
            x1_s[i, k, 0] = summed(i, (x + 2) % 4, k).astype(BF)
            x1(i, k).start()
        for k in (0, 1):
            b0(i, 1 + k).wait()
            xe_s[i, k] = summed(i, (x + (1, 3)[k]) % 4, 1 - k).astype(BF)
            xe(i, k).start()

    def send_x2(i):
        for k in (0, 1):
            x1(i, k).wait_recv()
            total = summed(i, (x + (1, 3)[k]) % 4, k) + x1_r[i, k, 0].astype(F32)
            x2_s[i, k] = total.astype(BF)
            x2(i, k).start()
        b0(i, 3).wait()
        for h in (0, 1):
            xe(i, 1 - h).wait_recv()
            own64[i % 2, h] = summed(i, x, h) + xe_r[i, 1 - h].astype(F32)

    def send_x2_fast(i):
        for k in (0, 1):
            b0(i, 1 + k).wait()
            x1(i, k, 0).wait_recv()
            x1(i, k, 1).wait_recv()
            far = x1_r[i, k, 0].astype(F32) + x1_r[i, k, 1].astype(F32)
            x2_s[i, k] = (summed(i, (x + (1, 3)[k]) % 4, k) + far).astype(BF)
            x2(i, k).start()
            xe_s[i, k] = summed(i, (x + (1, 3)[k]) % 4, 1 - k).astype(BF)
            xe(i, k).start()
        b0(i, 3).wait()
        for h in (0, 1):
            own64[i % 2, h] = summed(i, x, h)

    def send_yb_fast(i):
        for h in (0, 1):
            xe(i, 1 - h).wait_recv()
            own64[i % 2, h] += xe_r[i, 1 - h].astype(F32)
        send_yb(i)

    def send_yb(i):
        x2(i, 0).wait_recv()
        x2(i, 1).wait_recv()
        yb_s[i] = (own64[i % 2, 1 - yh] + x2_r[i, 1 - yh].astype(F32)).astype(BF)
        yb(i).start()
        own32[i % 2] = own64[i % 2, yh] + x2_r[i, yh].astype(F32)

    def send_h1(i):
        yb(i).wait_recv()
        full = own32[i % 2] + yb_r[i].astype(F32)
        gate, up, back = full[0], full[1], full[2]
        sigma = 1.0 / (1.0 + jnp.exp(-gate))
        silu = gate * sigma
        units = pl.ds(pl.multiple_of(mine + yh * UY, UY), UY)
        hid[0, units, lanes(i)] = (silu * up).astype(BF)
        hid[1, units, lanes(i)] = (back * up * sigma * (1.0 + gate * (1.0 - sigma))).astype(BF)
        hid[2, units, lanes(i)] = (back * silu).astype(BF)
        h1(i).start()
        he(i, 0).start()
        he(i, 1).start()

    def send_h2(i):
        h1(i).wait_recv()
        h2(i, 0).start()
        h2(i, 1).start()

    def send_h3(i):
        for k in (0, 1):
            he(i, k).wait_recv()
            h2(i, k).wait_recv()
            h3(i, k).start()

    def send_h3_fast(i):
        for k in (0, 1):
            he(i, k).wait_recv()
            h2(i, k).wait_recv()
            for o in (0, 1):
                h3(i, k, o).start()
        for k in range(3):
            h4_fast(i, k).start()

    def send_h4(i):
        h3(i, 0).wait_recv()
        h3(i, 1).wait_recv()
        h4(i).start()

    def grads_in(g):
        pair = lanes(g - 1, 2)
        for n in range(0, DM, 256):
            tok = tg[0, pl.ds(g - 1, 2), :, n : n + 256].reshape(2 * ROWS, 256)
            for m in (0, 1):
                sum_in[m * U : (m + 1) * U, n : n + 256] += dot(hid[1 + m, :, pair], tok)

    def grads_down(g):
        pair = lanes(g - 1, 2)
        for n in range(0, DM, 256):
            sc = tg[1, pl.ds(g - 1, 2), :, n : n + 256].reshape(2 * ROWS, 256)
            sum_down[:, n : n + 256] += dot(hid[0, :, pair], sc)

    def zf(col, h):
        return remote(
            zf_s.at[col, h], zf_r.at[col, h], d_ss.at[2 * col, h], d_rs.at[2 * col, h], (zm, zp)[h]
        )

    def zf_right(h):
        return remote(zg_s.at[h], zg_r.at[h], d_ss.at[0, 2 + h], d_rs.at[0, 2 + h], (zm, zp)[h])

    def dz(col, k, h):
        sem = 2 * col + 1
        return remote(
            dz_s.at[col, k, h], dz_r.at[col, k, h],
            d_ss.at[sem, 2 * k + h], d_rs.at[sem, 2 * k + h], (zp, zm)[(h + 1 + k) % 2],
        )

    def dz_right(k, h):
        return remote(
            dw_s.at[k, h], dw_r.at[k, h],
            d_ss.at[4, 2 * k + h], d_rs.at[4, 2 * k + h], (zp, zm)[(h + 1 + k) % 2],
        )

    def dy(h):
        return remote(dy_s.at[h], dy_r.at[h], d_ss.at[2, 2 + h], d_rs.at[2, 2 + h], ylp)

    def dy_right(k, h):
        return remote(dv_s.at[k, h], dv_r.at[k, h], d_ss.at[5 + h, k], d_rs.at[5 + h, k], ylp)

    def of_left(j, h):
        return to[j, :LEFT, h * HALF : (h + 1) * HALF]

    def of_right(j, h):
        return to[j, LEFT:, h * HALF : (h + 1) * HALF]

    def send_zf(col):
        for h in (0, 1):
            zf_s[col, h] = of_left((F, YF)[col], h).astype(BF)
            zf(col, h).start()

    def send_dz(col, k):
        for h in (0, 1):
            total = of_left(((C1, C2), (Y1, Y2))[col][k], h)
            if k == 0:
                zf(col, h).wait_recv()
                total = total + zf_r[col, h].astype(F32)
            dz_s[col, k, h] = total.astype(BF)
            dz(col, k, h).start()

    def column(col, h):
        dz(col, 0, h).wait_recv()
        dz(col, 1, h).wait_recv()
        return of_left((OWN, YO)[col], h) + (
            dz_r[col, 0, h].astype(F32) + dz_r[col, 1, h].astype(F32)
        )

    def send_dy():
        for h in (0, 1):
            dy_s[h] = column(1, h).astype(BF)
            dy(h).start()

    def send_dy_right(k):
        for h in (0, 1):
            dv_s[k, h] = of_right((YO, Y1, YF, Y2)[k], h).astype(BF)
            dy_right(k, h).start()

    def both_right(j, k, h):
        dy_right(k, h).wait_recv()
        return of_right(j, h) + dv_r[k, h].astype(F32)

    def send_zf_right():
        for h in (0, 1):
            zg_s[h] = both_right(F, 2, h).astype(BF)
            zf_right(h).start()

    def send_dz_right(k):
        for h in (0, 1):
            total = both_right((C1, C2)[k], 1 + 2 * k, h)
            if k == 0:
                zf_right(h).wait_recv()
                total = total + zg_r[h].astype(F32)
            dw_s[k, h] = total.astype(BF)
            dz_right(k, h).start()

    def term_fast(j):
        for k in range(3):
            h4_fast(j, k).wait_recv()
        for k in (0, 1):
            h3(j, k, 0).wait_recv()
            h3(j, k, 1).wait_recv()
        product(j)

    def term(j):
        h4(j).wait_recv()
        product(j)

    def product(j):
        h = hid[1:, :, lanes(j)].reshape(2 * U, ROWS)
        for m in range(0, DM, 512):
            to[j, m : m + 512, :] = dot(w_in[m : m + 512, :], h)

    def arrivals(t):
        @pl.when(t == C1)
        def _():
            arrived(C1, 0)
            gather(C1, F, 0, zp).start()
            arrived(C1, 1)
            gather(C1, F, 1, zm).start()

        @pl.when(t == YO)
        def _():
            arrived(YO, 0)
            gather(YO, Y1, 0, zp).start()
            arrived(YO, 1)
            gather(YO, Y1, 1, zm).start()

        @pl.when(t == F)
        def _():
            gather_yf(1, 1).start()

        @pl.when(t == Y1)
        def _():
            for h in (0, 1):
                arrived(Y1, h)
                gather_yf(0, h).start()
            gather(YO, Y2, 1, zp).start()
            gather(YO, Y2, 0, zm).start()

        @pl.when(t == YF)
        def _():
            for kind in (0, 1):
                for h in (0, 1):
                    gather_yf(kind, h).wait_recv()

        for chunk in (Y2, C2):

            @pl.when(t == chunk)
            def _():
                arrived(chunk, 0)
                arrived(chunk, 1)

    def left_both(i):
        for k in (0, 1):
            x1(i, k).wait_send()
            xe(i, k).wait_send()
            he(i, k).wait_send()
            x2(i, k).wait_send()
            h2(i, k).wait_send()
            h3(i, k).wait_send()
        yb(i).wait_send()
        h1(i).wait_send()

    def left_all(i):
        left_both(i)
        h4(i).wait_send()

    def left_fast(i):
        left_both(i)
        for k in (0, 1):
            x1(i, k, 1).wait_send()
            h3(i, k, 1).wait_send()
        for k in range(3):
            h4_fast(i, k).wait_send()

    def tick(t, carry):
        def stage(step, lag, first=0, end=CHUNKS):
            pl.when((t >= first + lag) & (t < end + lag))(lambda: step(t - lag))

        def normal(step, lag):
            stage(step, lag, end=FAST)

        def fast(step, lag):
            stage(step, lag, first=FAST)

        def at(when, step, *args):
            pl.when(t == when)(lambda: step(*args))

        normal(send_yb, 2)
        fast(send_h1, 2)
        normal(send_h3, 4)
        at(YF + 5, send_dz, 1, 0)
        fast(term_fast, 4)
        at(YF + 4, send_dy_right, 2)
        at(YF + 4, send_zf, 1)
        at(Y2 + 4, send_dy_right, 3)
        at(Y2 + 4, send_dz, 1, 1)
        at(C2 + 4, send_dz, 0, 1)
        at(C2 + 4, send_dz_right, 0)
        at(C2 + 4, send_dz_right, 1)
        arrivals(t)
        stage(partial, 0)

        normal(send_x2, 1)
        fast(send_yb_fast, 1)
        normal(send_h2, 3)
        fast(send_h3_fast, 3)
        normal(term, 5)
        at(YO + 5, send_dy_right, 0)
        at(F + 5, send_zf, 0)
        at(F + 6, send_dz, 0, 0)
        at(Y1 + 5, send_dy_right, 1)
        at(Y2 + 4, send_zf_right)

        @pl.when(t == YO)
        def _():
            arrived(F, 0)
            arrived(F, 1)
            gather_yf(1, 0).start()

        pl.when((t == 10) | (t == 11))(lambda: grads_in(2 * t - 15))

        normal(send_h1, 2)
        fast(send_x2_fast, 0)
        fast(send_h2, 2)
        normal(send_h4, 4)
        normal(send_x1, 0)
        at(Y2 + 4, send_dy)

        @pl.when(t == Y1)
        def _():
            gather(OWN, C2, 1, zp).start()
            gather(OWN, C2, 0, zm).start()

        normal(left_all, 7)
        pl.when((t == 6) | (t == 8))(lambda: grads_in(t - 5))
        pl.when((t == 7) | (t == 9))(lambda: grads_down(t - 6))
        at(10, grads_down, 5)
        return carry

    lax.fori_loop(0, CHUNKS + 4, tick, 0)

    stores = [
        pltpu.make_async_copy(sum_in, out_in, o_s.at[0]),
        pltpu.make_async_copy(sum_down, out_down, o_s.at[1]),
    ]
    stores[0].start()
    grads_down(CHUNKS - 1)
    stores[1].start()

    for i in range(FAST, CHUNKS):
        left_fast(i)
    for dst in (C1, YO, F, Y1, Y2, C2):
        for h in (0, 1):
            gather(OWN, dst, h, zp).wait_send()
    for h in (0, 1):
        gather_yf(0, h).wait_send()
        gather_yf(1, h).wait_send()
    for h in (0, 1):
        for col in (0, 1):
            zf(col, h).wait_send()
            dz(col, 0, h).wait_send()
            dz(col, 1, h).wait_send()
        for k in range(4):
            dy_right(k, h).wait_send()
        zf_right(h).wait_send()
        dy(h).wait_send()
        dz_right(0, h).wait_send()
        dz_right(1, h).wait_send()

    for h in (0, 1):
        rows = pl.ds(h * HALF, HALF)
        total = both_right(OWN, 0, h)
        dz_right(0, h).wait_recv()
        dz_right(1, h).wait_recv()
        total = total + (dw_r[0, h].astype(F32) + dw_r[1, h].astype(F32))
        out_tok[rows, LEFT:] = total.T.astype(BF)
        total = column(0, h)
        dy(h).wait_recv()
        out_tok[rows, :LEFT] = (total + dy_r[h].astype(F32)).T.astype(BF)
    for copy in stores:
        copy.wait()


def place(tok, sums, down, out_tok, out_gate, out_up, out_down, v_tok, v_sums, v_down, v_out, sems):
    reads, writes = [], []

    def piece(src, via, dst, by_way=None):
        k = len(reads)
        reads.append(pltpu.make_async_copy(src, via, sems.at[0, k]))
        writes.append(pltpu.make_async_copy(via if by_way is None else by_way, dst, sems.at[1, k]))
        reads[-1].start()

    turns = []
    for o, out in enumerate((out_gate, out_up)):
        for u in range(0, U, 256):
            for d in range(0, DM, 512):
                src = (pl.ds(o * U + u, 256), pl.ds(d, 512))
                dst = (pl.ds(d, 512), pl.ds(u, 256))
                turns.append((src, (o, *dst)))
                piece(sums.at[src], v_sums.at[src], out.at[dst], v_out.at[(o, *dst)])
    for p in range(0, U, 128):
        rows = pl.ds(p, 128)
        piece(down.at[rows], v_down.at[rows], out_down.at[rows])
    piece(tok, v_tok, out_tok)
    for k, (read, write) in enumerate(zip(reads, writes)):
        read.wait()
        if k < len(turns):
            src, dst = turns[k]
            v_out[dst] = v_sums[src].T
        write.start()
    for write in writes:
        write.wait()


def local(tokens, grad_out, keep, count, w_gate, w_up, w_down):
    vmem = pl.BlockSpec(memory_space=pltpu.VMEM)
    anywhere = pl.BlockSpec(memory_space=pl.ANY)
    dma = pltpu.SemaphoreType.DMA
    outs = pl.pallas_call(
        kernel,
        out_shape=(
            jax.ShapeDtypeStruct((ROWS, DM), BF),
            jax.ShapeDtypeStruct((2 * U, DM), F32),
            jax.ShapeDtypeStruct((U, DM), F32),
        ),
        in_specs=[anywhere, vmem, vmem, pl.BlockSpec(memory_space=pltpu.SMEM)] + [anywhere] * 3,
        out_specs=[vmem] + [anywhere] * 2,
        scratch_shapes=[
            pltpu.VMEM((DM, 2 * U), BF),
            pltpu.VMEM((2 * U, DM), BF),
            pltpu.VMEM((U, DM), BF),
            pltpu.VMEM((2 * U, DM), F32),
            pltpu.VMEM((U, DM), F32),
            pltpu.VMEM((2, CHUNKS, ROWS, DM), BF),
            pltpu.VMEM((2, 3, U, ROWS), F32),
            pltpu.VMEM((CHUNKS, 3, UC, ROWS), F32),
            pltpu.VMEM((CHUNKS, 2, 2, 3, UY, ROWS), BF),
            pltpu.VMEM((CHUNKS, 2, 2, 3, UY, ROWS), BF),
            pltpu.VMEM((CHUNKS, 2, 3, UY, ROWS), BF),
            pltpu.VMEM((CHUNKS, 2, 3, UY, ROWS), BF),
            pltpu.VMEM((CHUNKS, 2, 3, UY, ROWS), BF),
            pltpu.VMEM((CHUNKS, 2, 3, UY, ROWS), BF),
            pltpu.VMEM((CHUNKS, 3, UY, ROWS), BF),
            pltpu.VMEM((CHUNKS, 3, UY, ROWS), BF),
            pltpu.VMEM((2, 2, 3, UY, ROWS), F32),
            pltpu.VMEM((2, 3, UY, ROWS), F32),
            pltpu.VMEM((3, U, CHUNKS * ROWS), BF),
            pltpu.VMEM((CHUNKS, DM, ROWS), F32),
            pltpu.VMEM((2, LEFT, HALF), BF),
            pltpu.VMEM((2, LEFT, HALF), BF),
            pltpu.VMEM((2, 2, LEFT, HALF), BF),
            pltpu.VMEM((2, 2, LEFT, HALF), BF),
            pltpu.VMEM((2, 2, 2, LEFT, HALF), BF),
            pltpu.VMEM((2, 2, 2, LEFT, HALF), BF),
            pltpu.VMEM((4, 2, RIGHT, HALF), BF),
            pltpu.VMEM((4, 2, RIGHT, HALF), BF),
            pltpu.VMEM((2, RIGHT, HALF), BF),
            pltpu.VMEM((2, RIGHT, HALF), BF),
            pltpu.VMEM((2, 2, RIGHT, HALF), BF),
            pltpu.VMEM((2, 2, RIGHT, HALF), BF),
            dma((MESSAGES, CHUNKS)),
            dma((MESSAGES, CHUNKS)),
            dma((CHUNKS + 1, 2)),
            dma((CHUNKS + 1, 2)),
            dma((7, 4)),
            dma((7, 4)),
            dma((2,)),
            dma((4,)),
        ],
        compiler_params=pltpu.CompilerParams(
            collective_id=0, has_side_effects=True, vmem_limit_bytes=62 * 1024 * 1024
        ),
        cost_estimate=pl.CostEstimate(
            flops=16 * 2048 * DM * U, bytes_accessed=16 << 20, transcendentals=0
        ),
    )(tokens, grad_out, keep, count, w_gate, w_up, w_down)
    return pl.pallas_call(
        place,
        out_shape=(
            jax.ShapeDtypeStruct((ROWS, DM), BF),
            jax.ShapeDtypeStruct((DM, U), F32),
            jax.ShapeDtypeStruct((DM, U), F32),
            jax.ShapeDtypeStruct((U, DM), F32),
        ),
        in_specs=[anywhere] * 3,
        out_specs=[anywhere] * 4,
        scratch_shapes=[
            pltpu.VMEM((ROWS, DM), BF),
            pltpu.VMEM((2 * U, DM), F32),
            pltpu.VMEM((U, DM), F32),
            pltpu.VMEM((2, DM, U), F32),
            dma((2, 13)),
        ],
        compiler_params=pltpu.CompilerParams(vmem_limit_bytes=62 * 1024 * 1024),
    )(*outs)


def solution(mesh):
    placed = (
        P("wide", "mp"),
        P("wide", "mp"),
        P("wide"),
        P(),
        P("mp", "wide"),
        P("mp", "wide"),
        P("wide", "mp"),
    )
    return jax.shard_map(
        local,
        mesh=mesh,
        in_specs=placed,
        out_specs=(P("wide", "mp"), P("mp", "wide"), P("mp", "wide"), P("wide", "mp")),
        check_vma=False,
    )
```

```python
import functools

import jax
import jax.numpy as jnp
from jax import lax
from jax.experimental import pallas as pl
from jax.experimental.pallas import tpu as pltpu
from jax.sharding import PartitionSpec as P

BF = jnp.bfloat16
F32 = jnp.float32
ROWS = 256
HALF = 128
DM = 1024
U = 512
UC, UX, UY = 256, 64, 32
LEFT, RIGHT = 640, 384
CHUNKS = 8
OWN, C1, YO, F, Y1, YF, Y2, C2 = range(CHUNKS)
B0, X1, XE, X2, YB, H1, HE, H2, H3, H4 = 0, 4, 8, 10, 12, 13, 14, 16, 18, 22
MESSAGES = 25
FAST = Y1


def dot(a, b):
    return lax.dot_general(a, b, (((1,), (0,)), ((), ())), preferred_element_type=F32)


def dot_nt(a, b):
    return lax.dot_general(a, b, (((1,), (1,)), ((), ())), preferred_element_type=F32)


def kernel(
    tokens, grad_out, keep, count, in_gate, in_up, in_down,
    out_tok, out_in, out_down,
    w_in, w_in_t, w_down, sum_in, sum_down, tg, part, b0_r, x1_s, x1_r, xe_s, xe_r, x2_s, x2_r,
    yb_s, yb_r, own64, own32, hid,
    to, dy_s, dy_r, zf_s, zf_r, dz_s, dz_r, dv_s, dv_r, zg_s, zg_r, dw_s, dw_r,
    c_ss, c_rs, a_ss, a_rs, d_ss, d_rs, o_s, i_s,
):
    mp, wide = lax.axis_index("mp"), lax.axis_index("wide")
    x, yh, c = mp // 4, (mp // 2) % 2, mp % 2
    core = (mp + 1 - 2 * c, wide)
    xp = ((mp + 4) % 16, wide)
    xm = ((mp + 12) % 16, wide)
    xp_other = ((mp + 4) % 16 + 1 - 2 * c, wide)
    xm_other = ((mp + 12) % 16 + 1 - 2 * c, wide)
    yhp = (mp + 2 - 4 * yh, wide)
    ylp = (mp, wide + 1 - 2 * (wide % 2))
    zp = (mp, (wide + 2) % 8)
    zm = (mp, (wide + 6) % 8)

    def remote(src, dst, ssem, rsem, dev):
        return pltpu.make_async_remote_copy(
            src_ref=src, dst_ref=dst, send_sem=ssem, recv_sem=rsem,
            device_id=dev, device_id_type=pl.DeviceIdType.MESH,
        )

    loads = [
        pltpu.make_async_copy(a, b, i_s.at[k])
        for k, (a, b) in enumerate(
            (
                (tokens, tg.at[0, OWN]),
                (in_gate, w_in.at[:, pl.ds(0, U)]),
                (in_up, w_in.at[:, pl.ds(U, U)]),
                (in_down, w_down),
            )
        )
    ]
    for load in loads:
        load.start()

    barrier = pltpu.get_barrier_semaphore()
    for dev in (core, xp, xm, xp_other, xm_other, yhp, ylp, zp, zm):
        pl.semaphore_signal(barrier, inc=1, device_id=dev, device_id_type=pl.DeviceIdType.MESH)

    for r in range(0, ROWS, 128):
        factor = keep[pl.ds(r, 128)].astype(F32) / count[0].astype(F32)
        factor = jnp.broadcast_to(factor[None, :], (128, 128)).T
        for n in range(0, DM, 128):
            block = grad_out[r : r + 128, n : n + 128].astype(F32) * factor
            tg[1, OWN, r : r + 128, n : n + 128] = block.astype(BF)
    loads[0].wait()
    pl.semaphore_wait(barrier, 9)

    def gather(src, dst, h, dev):
        rows = pl.ds(h * HALF, HALF)
        return remote(
            tg.at[:, src, rows], tg.at[:, dst, rows], a_ss.at[dst, h], a_rs.at[dst, h], dev
        )

    def gather_yf(kind, h):
        rows = pl.ds(h * HALF, HALF)
        return remote(
            tg.at[kind, (Y1, F)[kind], rows], tg.at[kind, YF, rows],
            a_ss.at[(YF, CHUNKS)[kind], h], a_rs.at[(YF, CHUNKS)[kind], h],
            ((zp, zm)[h], ylp)[kind],
        )

    def arrived(dst, h):
        gather(OWN, dst, h, zp).wait_recv()

    gather(OWN, C1, 0, zp).start()
    gather(OWN, C1, 1, zm).start()
    gather(OWN, YO, 0, ylp).start()
    gather(OWN, YO, 1, ylp).start()

    for load in loads[1:]:
        load.wait()
    for n in range(0, 2 * U, 256):
        w_in_t[n : n + 256, :] = w_in[:, n : n + 256].T
    sum_in[...] = jnp.zeros_like(sum_in)
    sum_down[...] = jnp.zeros_like(sum_down)

    def b0(i, k):
        at = pl.multiple_of(((x + (2, 1, 3, 0)[k]) % 4) * UX, UX)
        src = part.at[i % 2, :, pl.ds(pl.multiple_of((1 - c) * UC + at, UX), UX)]
        return remote(
            src, b0_r.at[i, :, pl.ds(at, UX)], c_ss.at[B0 + k, i], c_rs.at[B0 + k, i], core
        )

    def along_x(i, k, sem, src, dst):
        return remote(
            src.at[i, k], dst.at[i, k], c_ss.at[sem + k, i], c_rs.at[sem + k, i], (xp, xm)[k]
        )

    def x1(i, k, o=0):
        sem = X1 + 2 * k + o
        dev = ((xp, xm), (xp_other, xm_other))[o][k]
        return remote(
            x1_s.at[i, k, o], x1_r.at[i, k, o], c_ss.at[sem, i], c_rs.at[sem, i], dev
        )

    def xe(i, k):
        return along_x(i, k, XE, xe_s, xe_r)

    def x2(i, k):
        return along_x(i, k, X2, x2_s, x2_r)

    def yb(i):
        return remote(yb_s.at[i], yb_r.at[i], c_ss.at[YB, i], c_rs.at[YB, i], yhp)

    def lanes(i, n=1):
        return pl.ds(pl.multiple_of(i * ROWS, ROWS), n * ROWS)

    def same(i, first, n, sem, dev):
        block = hid.at[:, pl.ds(pl.multiple_of(first, UY), n), lanes(i)]
        return remote(block, block, c_ss.at[sem, i], c_rs.at[sem, i], dev)

    mine = c * UC + x * UX
    left = c * UC + ((x + 3) % 4) * UX
    right = c * UC + ((x + 1) % 4) * UX

    def h1(i):
        return same(i, mine + yh * UY, UY, H1, yhp)

    def he(i, k):
        return same(i, mine + yh * UY, UY, HE + k, (xp, xm)[k])

    def h2(i, k):
        return same(i, mine + (1 - yh) * UY, UY, H2 + k, (xp, xm)[k])

    def h3(i, k, o=0):
        dev = ((xp, xm), (xp_other, xm_other))[o][k]
        return same(i, (left, right + UY)[k], UY, H3 + 2 * k + o, dev)

    def h4(i):
        return same(i, c * UC, UC, H4, core)

    def h4_fast(i, k):
        return same(i, (mine, left, right)[k], UX, H4 + k, core)

    def summed(i, xd, h):
        at = xd * UX + h * UY
        a = part[i % 2, :, pl.ds(pl.multiple_of(c * UC + at, UY), UY), :]
        return a + b0_r[i, :, pl.ds(pl.multiple_of(at, UY), UY), :]

    def partial(i):
        s = i % 2
        for m in (0, 1):
            part[s, m] = dot_nt(w_in_t[m * U : (m + 1) * U, :], tg[0, i])
        part[s, 2] = dot_nt(w_down[...], tg[1, i])

        @pl.when(i < FAST)
        def _():
            b0(i, 0).start()

        @pl.when(i >= FAST)
        def _():
            far = ((x + 2) % 4) * UX
            for k in (0, 1):
                for o in (0, 1):
                    first = (c + o - 2 * c * o) * UC + far + k * UY
                    mine_far = part[s, :, pl.ds(pl.multiple_of(first, UY), UY), :]
                    x1_s[i, k, o] = mine_far.astype(BF)
                    x1(i, k, o).start()

        for k in (1, 2, 3):
            b0(i, k).start()

    def send_x1(i):
        b0(i, 0).wait()
        for k in (0, 1):
            x1_s[i, k, 0] = summed(i, (x + 2) % 4, k).astype(BF)
            x1(i, k).start()
        for k in (0, 1):
            b0(i, 1 + k).wait()
            xe_s[i, k] = summed(i, (x + (1, 3)[k]) % 4, 1 - k).astype(BF)
            xe(i, k).start()

    def send_x2(i):
        for k in (0, 1):
            x1(i, k).wait_recv()
            total = summed(i, (x + (1, 3)[k]) % 4, k) + x1_r[i, k, 0].astype(F32)
            x2_s[i, k] = total.astype(BF)
            x2(i, k).start()
        b0(i, 3).wait()
        for h in (0, 1):
            xe(i, 1 - h).wait_recv()
            own64[i % 2, h] = summed(i, x, h) + xe_r[i, 1 - h].astype(F32)

    def send_x2_fast(i):
        for k in (0, 1):
            b0(i, 1 + k).wait()
            x1(i, k, 0).wait_recv()
            x1(i, k, 1).wait_recv()
            far = x1_r[i, k, 0].astype(F32) + x1_r[i, k, 1].astype(F32)
            x2_s[i, k] = (summed(i, (x + (1, 3)[k]) % 4, k) + far).astype(BF)
            x2(i, k).start()
            xe_s[i, k] = summed(i, (x + (1, 3)[k]) % 4, 1 - k).astype(BF)
            xe(i, k).start()
        b0(i, 3).wait()
        for h in (0, 1):
            own64[i % 2, h] = summed(i, x, h)

    def send_yb_fast(i):
        for h in (0, 1):
            xe(i, 1 - h).wait_recv()
            own64[i % 2, h] += xe_r[i, 1 - h].astype(F32)
        send_yb(i)

    def send_yb(i):
        x2(i, 0).wait_recv()
        x2(i, 1).wait_recv()
        yb_s[i] = (own64[i % 2, 1 - yh] + x2_r[i, 1 - yh].astype(F32)).astype(BF)
        yb(i).start()
        own32[i % 2] = own64[i % 2, yh] + x2_r[i, yh].astype(F32)

    def send_h1(i):
        yb(i).wait_recv()
        full = own32[i % 2] + yb_r[i].astype(F32)
        gate, up, back = full[0], full[1], full[2]
        sigma = 1.0 / (1.0 + jnp.exp(-gate))
        silu = gate * sigma
        units = pl.ds(pl.multiple_of(mine + yh * UY, UY), UY)
        hid[0, units, lanes(i)] = (silu * up).astype(BF)
        hid[1, units, lanes(i)] = (back * up * sigma * (1.0 + gate * (1.0 - sigma))).astype(BF)
        hid[2, units, lanes(i)] = (back * silu).astype(BF)
        h1(i).start()
        he(i, 0).start()
        he(i, 1).start()

    def send_h2(i):
        h1(i).wait_recv()
        h2(i, 0).start()
        h2(i, 1).start()

    def send_h3(i):
        for k in (0, 1):
            he(i, k).wait_recv()
            h2(i, k).wait_recv()
            h3(i, k).start()

    def send_h3_fast(i):
        for k in (0, 1):
            he(i, k).wait_recv()
            h2(i, k).wait_recv()
            for o in (0, 1):
                h3(i, k, o).start()
        for k in range(3):
            h4_fast(i, k).start()

    def send_h4(i):
        h3(i, 0).wait_recv()
        h3(i, 1).wait_recv()
        h4(i).start()

    def grads_in(g):
        pair = lanes(g - 1, 2)
        for n in range(0, DM, 256):
            tok = tg[0, pl.ds(g - 1, 2), :, n : n + 256].reshape(2 * ROWS, 256)
            for m in (0, 1):
                sum_in[m * U : (m + 1) * U, n : n + 256] += dot(hid[1 + m, :, pair], tok)

    def grads_down(g):
        pair = lanes(g - 1, 2)
        for n in range(0, DM, 256):
            sc = tg[1, pl.ds(g - 1, 2), :, n : n + 256].reshape(2 * ROWS, 256)
            sum_down[:, n : n + 256] += dot(hid[0, :, pair], sc)

    def zf(col, h):
        return remote(
            zf_s.at[col, h], zf_r.at[col, h], d_ss.at[2 * col, h], d_rs.at[2 * col, h], (zm, zp)[h]
        )

    def zf_right(h):
        return remote(zg_s.at[h], zg_r.at[h], d_ss.at[0, 2 + h], d_rs.at[0, 2 + h], (zm, zp)[h])

    def dz(col, k, h):
        sem = 2 * col + 1
        return remote(
            dz_s.at[col, k, h], dz_r.at[col, k, h],
            d_ss.at[sem, 2 * k + h], d_rs.at[sem, 2 * k + h], (zp, zm)[(h + 1 + k) % 2],
        )

    def dz_right(k, h):
        return remote(
            dw_s.at[k, h], dw_r.at[k, h],
            d_ss.at[4, 2 * k + h], d_rs.at[4, 2 * k + h], (zp, zm)[(h + 1 + k) % 2],
        )

    def dy(h):
        return remote(dy_s.at[h], dy_r.at[h], d_ss.at[2, 2 + h], d_rs.at[2, 2 + h], ylp)

    def dy_right(k, h):
        return remote(dv_s.at[k, h], dv_r.at[k, h], d_ss.at[5 + h, k], d_rs.at[5 + h, k], ylp)

    def of_left(j, h):
        return to[j, :LEFT, h * HALF : (h + 1) * HALF]

    def of_right(j, h):
        return to[j, LEFT:, h * HALF : (h + 1) * HALF]

    def send_zf(col):
        for h in (0, 1):
            zf_s[col, h] = of_left((F, YF)[col], h).astype(BF)
            zf(col, h).start()

    def send_dz(col, k):
        for h in (0, 1):
            total = of_left(((C1, C2), (Y1, Y2))[col][k], h)
            if k == 0:
                zf(col, h).wait_recv()
                total = total + zf_r[col, h].astype(F32)
            dz_s[col, k, h] = total.astype(BF)
            dz(col, k, h).start()

    def column(col, h):
        dz(col, 0, h).wait_recv()
        dz(col, 1, h).wait_recv()
        return of_left((OWN, YO)[col], h) + (
            dz_r[col, 0, h].astype(F32) + dz_r[col, 1, h].astype(F32)
        )

    def send_dy():
        for h in (0, 1):
            dy_s[h] = column(1, h).astype(BF)
            dy(h).start()

    def send_dy_right(k):
        for h in (0, 1):
            dv_s[k, h] = of_right((YO, Y1, YF, Y2)[k], h).astype(BF)
            dy_right(k, h).start()

    def both_right(j, k, h):
        dy_right(k, h).wait_recv()
        return of_right(j, h) + dv_r[k, h].astype(F32)

    def send_zf_right():
        for h in (0, 1):
            zg_s[h] = both_right(F, 2, h).astype(BF)
            zf_right(h).start()

    def send_dz_right(k):
        for h in (0, 1):
            total = both_right((C1, C2)[k], 1 + 2 * k, h)
            if k == 0:
                zf_right(h).wait_recv()
                total = total + zg_r[h].astype(F32)
            dw_s[k, h] = total.astype(BF)
            dz_right(k, h).start()

    def term_fast(j):
        for k in range(3):
            h4_fast(j, k).wait_recv()
        for k in (0, 1):
            h3(j, k, 0).wait_recv()
            h3(j, k, 1).wait_recv()
        product(j)

    def term(j):
        h4(j).wait_recv()
        product(j)

    def product(j):
        h = hid[1:, :, lanes(j)].reshape(2 * U, ROWS)
        for m in range(0, DM, 512):
            to[j, m : m + 512, :] = dot(w_in[m : m + 512, :], h)

    def arrivals(t):
        @pl.when(t == C1)
        def _():
            arrived(C1, 0)
            gather(C1, F, 0, zp).start()
            arrived(C1, 1)
            gather(C1, F, 1, zm).start()

        @pl.when(t == YO)
        def _():
            arrived(YO, 0)
            gather(YO, Y1, 0, zp).start()
            arrived(YO, 1)
            gather(YO, Y1, 1, zm).start()

        @pl.when(t == F)
        def _():
            gather_yf(1, 1).start()

        @pl.when(t == Y1)
        def _():
            for h in (0, 1):
                arrived(Y1, h)
                gather_yf(0, h).start()
            gather(YO, Y2, 1, zp).start()
            gather(YO, Y2, 0, zm).start()

        @pl.when(t == YF)
        def _():
            for kind in (0, 1):
                for h in (0, 1):
                    gather_yf(kind, h).wait_recv()

        for chunk in (Y2, C2):

            @pl.when(t == chunk)
            def _():
                arrived(chunk, 0)
                arrived(chunk, 1)

    def left_both(i):
        for k in (0, 1):
            x1(i, k).wait_send()
            xe(i, k).wait_send()
            he(i, k).wait_send()
            x2(i, k).wait_send()
            h2(i, k).wait_send()
            h3(i, k).wait_send()
        yb(i).wait_send()
        h1(i).wait_send()

    def left_all(i):
        left_both(i)
        h4(i).wait_send()

    def left_fast(i):
        left_both(i)
        for k in (0, 1):
            x1(i, k, 1).wait_send()
            h3(i, k, 1).wait_send()
        for k in range(3):
            h4_fast(i, k).wait_send()

    def tick(t, carry):
        def stage(step, lag, first=0, end=CHUNKS):
            pl.when((t >= first + lag) & (t < end + lag))(lambda: step(t - lag))

        def normal(step, lag):
            stage(step, lag, end=FAST)

        def fast(step, lag):
            stage(step, lag, first=FAST)

        def at(when, step, *args):
            pl.when(t == when)(lambda: step(*args))

        normal(send_yb, 2)
        fast(send_h1, 2)
        normal(send_h3, 4)
        fast(term_fast, 4)
        at(Y1 + 4, send_dy_right, 1)
        at(YF + 4, send_dy_right, 2)
        at(YF + 4, send_zf, 1)
        at(Y2 + 4, send_dy_right, 3)
        at(Y2 + 4, send_dz, 1, 1)
        at(C2 + 4, send_dz, 0, 1)
        at(C2 + 4, send_dz_right, 0)
        at(C2 + 4, send_dz_right, 1)
        arrivals(t)
        stage(partial, 0)

        normal(send_x2, 1)
        fast(send_yb_fast, 1)
        normal(send_h2, 3)
        fast(send_h3_fast, 3)
        normal(term, 5)
        at(YO + 5, send_dy_right, 0)
        at(F + 5, send_zf, 0)
        at(F + 6, send_dz, 0, 0)
        at(Y2 + 4, send_zf_right)

        @pl.when(t == YO)
        def _():
            arrived(F, 0)
            arrived(F, 1)
            gather_yf(1, 0).start()

        pl.when((t == 10) | (t == 11))(lambda: grads_in(2 * t - 15))

        normal(send_h1, 2)
        fast(send_x2_fast, 0)
        fast(send_h2, 2)
        normal(send_h4, 4)
        normal(send_x1, 0)
        at(Y2 + 4, send_dy)

        @pl.when(t == Y1)
        def _():
            gather(OWN, C2, 1, zp).start()
            gather(OWN, C2, 0, zm).start()

        normal(left_all, 7)
        pl.when((t == 6) | (t == 8))(lambda: grads_in(t - 5))
        pl.when((t == 7) | (t == 9))(lambda: grads_down(t - 6))
        at(10, grads_down, 5)
        at(YF + 4, send_dz, 1, 0)
        return carry

    lax.fori_loop(0, CHUNKS + 4, tick, 0)

    stores = [
        pltpu.make_async_copy(sum_in, out_in, o_s.at[0]),
        pltpu.make_async_copy(sum_down, out_down, o_s.at[1]),
    ]
    stores[0].start()
    grads_down(CHUNKS - 1)
    stores[1].start()

    for i in range(FAST, CHUNKS):
        left_fast(i)
    for dst in (C1, YO, F, Y1, Y2, C2):
        for h in (0, 1):
            gather(OWN, dst, h, zp).wait_send()
    for h in (0, 1):
        gather_yf(0, h).wait_send()
        gather_yf(1, h).wait_send()
    for h in (0, 1):
        for col in (0, 1):
            zf(col, h).wait_send()
            dz(col, 0, h).wait_send()
            dz(col, 1, h).wait_send()
        for k in range(4):
            dy_right(k, h).wait_send()
        zf_right(h).wait_send()
        dy(h).wait_send()
        dz_right(0, h).wait_send()
        dz_right(1, h).wait_send()

    for h in (0, 1):
        rows = pl.ds(h * HALF, HALF)
        total = both_right(OWN, 0, h)
        dz_right(0, h).wait_recv()
        dz_right(1, h).wait_recv()
        total = total + (dw_r[0, h].astype(F32) + dw_r[1, h].astype(F32))
        out_tok[rows, LEFT:] = total.T.astype(BF)
        total = column(0, h)
        dy(h).wait_recv()
        out_tok[rows, :LEFT] = (total + dy_r[h].astype(F32)).T.astype(BF)
    for copy in stores:
        copy.wait()


def place(tok, sums, down, out_tok, out_gate, out_up, out_down, v_tok, v_sums, v_down, v_out, sems):
    reads, writes = [], []

    def piece(src, via, dst, by_way=None):
        k = len(reads)
        reads.append(pltpu.make_async_copy(src, via, sems.at[0, k]))
        writes.append(pltpu.make_async_copy(via if by_way is None else by_way, dst, sems.at[1, k]))
        reads[-1].start()

    turns = []
    for o, out in enumerate((out_gate, out_up)):
        for u in range(0, U, 256):
            for d in range(0, DM, 512):
                src = (pl.ds(o * U + u, 256), pl.ds(d, 512))
                dst = (pl.ds(d, 512), pl.ds(u, 256))
                turns.append((src, (o, *dst)))
                piece(sums.at[src], v_sums.at[src], out.at[dst], v_out.at[(o, *dst)])
    for p in range(0, U, 128):
        rows = pl.ds(p, 128)
        piece(down.at[rows], v_down.at[rows], out_down.at[rows])
    piece(tok, v_tok, out_tok)
    for k, (read, write) in enumerate(zip(reads, writes)):
        read.wait()
        if k < len(turns):
            src, dst = turns[k]
            v_out[dst] = v_sums[src].T
        write.start()
    for write in writes:
        write.wait()


def local(tokens, grad_out, keep, count, w_gate, w_up, w_down):
    vmem = pl.BlockSpec(memory_space=pltpu.VMEM)
    anywhere = pl.BlockSpec(memory_space=pl.ANY)
    dma = pltpu.SemaphoreType.DMA
    outs = pl.pallas_call(
        kernel,
        out_shape=(
            jax.ShapeDtypeStruct((ROWS, DM), BF),
            jax.ShapeDtypeStruct((2 * U, DM), F32),
            jax.ShapeDtypeStruct((U, DM), F32),
        ),
        in_specs=[anywhere, vmem, vmem, pl.BlockSpec(memory_space=pltpu.SMEM)] + [anywhere] * 3,
        out_specs=[vmem] + [anywhere] * 2,
        scratch_shapes=[
            pltpu.VMEM((DM, 2 * U), BF),
            pltpu.VMEM((2 * U, DM), BF),
            pltpu.VMEM((U, DM), BF),
            pltpu.VMEM((2 * U, DM), F32),
            pltpu.VMEM((U, DM), F32),
            pltpu.VMEM((2, CHUNKS, ROWS, DM), BF),
            pltpu.VMEM((2, 3, U, ROWS), F32),
            pltpu.VMEM((CHUNKS, 3, UC, ROWS), F32),
            pltpu.VMEM((CHUNKS, 2, 2, 3, UY, ROWS), BF),
            pltpu.VMEM((CHUNKS, 2, 2, 3, UY, ROWS), BF),
            pltpu.VMEM((CHUNKS, 2, 3, UY, ROWS), BF),
            pltpu.VMEM((CHUNKS, 2, 3, UY, ROWS), BF),
            pltpu.VMEM((CHUNKS, 2, 3, UY, ROWS), BF),
            pltpu.VMEM((CHUNKS, 2, 3, UY, ROWS), BF),
            pltpu.VMEM((CHUNKS, 3, UY, ROWS), BF),
            pltpu.VMEM((CHUNKS, 3, UY, ROWS), BF),
            pltpu.VMEM((2, 2, 3, UY, ROWS), F32),
            pltpu.VMEM((2, 3, UY, ROWS), F32),
            pltpu.VMEM((3, U, CHUNKS * ROWS), BF),
            pltpu.VMEM((CHUNKS, DM, ROWS), F32),
            pltpu.VMEM((2, LEFT, HALF), BF),
            pltpu.VMEM((2, LEFT, HALF), BF),
            pltpu.VMEM((2, 2, LEFT, HALF), BF),
            pltpu.VMEM((2, 2, LEFT, HALF), BF),
            pltpu.VMEM((2, 2, 2, LEFT, HALF), BF),
            pltpu.VMEM((2, 2, 2, LEFT, HALF), BF),
            pltpu.VMEM((4, 2, RIGHT, HALF), BF),
            pltpu.VMEM((4, 2, RIGHT, HALF), BF),
            pltpu.VMEM((2, RIGHT, HALF), BF),
            pltpu.VMEM((2, RIGHT, HALF), BF),
            pltpu.VMEM((2, 2, RIGHT, HALF), BF),
            pltpu.VMEM((2, 2, RIGHT, HALF), BF),
            dma((MESSAGES, CHUNKS)),
            dma((MESSAGES, CHUNKS)),
            dma((CHUNKS + 1, 2)),
            dma((CHUNKS + 1, 2)),
            dma((7, 4)),
            dma((7, 4)),
            dma((2,)),
            dma((4,)),
        ],
        compiler_params=pltpu.CompilerParams(
            collective_id=0, has_side_effects=True, vmem_limit_bytes=62 * 1024 * 1024
        ),
        cost_estimate=pl.CostEstimate(
            flops=16 * 2048 * DM * U, bytes_accessed=16 << 20, transcendentals=0
        ),
    )(tokens, grad_out, keep, count, w_gate, w_up, w_down)
    return pl.pallas_call(
        place,
        out_shape=(
            jax.ShapeDtypeStruct((ROWS, DM), BF),
            jax.ShapeDtypeStruct((DM, U), F32),
            jax.ShapeDtypeStruct((DM, U), F32),
            jax.ShapeDtypeStruct((U, DM), F32),
        ),
        in_specs=[anywhere] * 3,
        out_specs=[anywhere] * 4,
        scratch_shapes=[
            pltpu.VMEM((ROWS, DM), BF),
            pltpu.VMEM((2 * U, DM), F32),
            pltpu.VMEM((U, DM), F32),
            pltpu.VMEM((2, DM, U), F32),
            dma((2, 13)),
        ],
        compiler_params=pltpu.CompilerParams(vmem_limit_bytes=62 * 1024 * 1024),
    )(*outs)


def solution(mesh):
    placed = (
        P("wide", "mp"),
        P("wide", "mp"),
        P("wide"),
        P(),
        P("mp", "wide"),
        P("mp", "wide"),
        P("wide", "mp"),
    )
    return jax.shard_map(
        local,
        mesh=mesh,
        in_specs=placed,
        out_specs=(P("wide", "mp"), P("mp", "wide"), P("mp", "wide"), P("wide", "mp")),
        check_vma=False,
    )
```

```python
import functools

import jax
import jax.numpy as jnp
from jax import lax
from jax.experimental import pallas as pl
from jax.experimental.pallas import tpu as pltpu
from jax.sharding import PartitionSpec as P

BF = jnp.bfloat16
F32 = jnp.float32
ROWS = 256
HALF = 128
DM = 1024
U = 512
UC, UX, UY = 256, 64, 32
LEFT, RIGHT = 512, 512
CHUNKS = 8
OWN, C1, YO, F, Y1, YF, Y2, C2 = range(CHUNKS)
B0, X1, XE, X2, YB, H1, HE, H2, H3, H4 = 0, 4, 6, 8, 10, 11, 12, 14, 16, 18
MESSAGES = 19


def dot(a, b):
    return lax.dot_general(a, b, (((1,), (0,)), ((), ())), preferred_element_type=F32)


def dot_nt(a, b):
    return lax.dot_general(a, b, (((1,), (1,)), ((), ())), preferred_element_type=F32)


def kernel(
    tokens, in_grad, keep, count, in_gate, in_up, in_down,
    out_tok, out_in, out_down,
    grad_out, last, w_in, w_in_t, w_down, sum_in, sum_down, tg, part, b0_r, x1_s, x1_r, xe_s, xe_r, x2_s, x2_r,
    yb_s, yb_r, own64, own32, hid,
    to, dy_s, dy_r, zf_s, zf_r, dz_s, dz_r, dv_s, dv_r, zg_s, zg_r, dw_s, dw_r,
    c_ss, c_rs, a_ss, a_rs, d_ss, d_rs, o_s, i_s,
):
    mp, wide = lax.axis_index("mp"), lax.axis_index("wide")
    x, yh, c = mp // 4, (mp // 2) % 2, mp % 2
    core = (mp + 1 - 2 * c, wide)
    xp = ((mp + 4) % 16, wide)
    xm = ((mp + 12) % 16, wide)
    yhp = (mp + 2 - 4 * yh, wide)
    ylp = (mp, wide + 1 - 2 * (wide % 2))
    zp = (mp, (wide + 2) % 8)
    zm = (mp, (wide + 6) % 8)

    def remote(src, dst, ssem, rsem, dev):
        return pltpu.make_async_remote_copy(
            src_ref=src, dst_ref=dst, send_sem=ssem, recv_sem=rsem,
            device_id=dev, device_id_type=pl.DeviceIdType.MESH,
        )

    barrier = pltpu.get_barrier_semaphore()
    for dev in (core, xp, xm, yhp, ylp, zp, zm):
        pl.semaphore_signal(barrier, inc=1, device_id=dev, device_id_type=pl.DeviceIdType.MESH)

    loads = [
        pltpu.make_async_copy(a, b, i_s.at[k])
        for k, (a, b) in enumerate(
            (
                (in_grad, grad_out),
                (tokens, tg.at[0, OWN]),
                (in_gate, w_in.at[:, pl.ds(0, U)]),
                (in_up, w_in.at[:, pl.ds(U, U)]),
                (in_down, w_down),
            )
        )
    ]
    for load in loads:
        load.start()
    pl.semaphore_wait(barrier, 7)

    def gather(src, dst, h, dev):
        rows = pl.ds(h * HALF, HALF)
        return remote(
            tg.at[:, src, rows], tg.at[:, dst, rows], a_ss.at[dst, h], a_rs.at[dst, h], dev
        )

    def gather_own(kind, dst, h, dev):
        rows = pl.ds(h * HALF, HALF)
        sem = (dst, CHUNKS + 1 + (dst == YO))[kind]
        return remote(
            (tokens.at[rows], tg.at[1, OWN, rows])[kind], tg.at[kind, dst, rows],
            a_ss.at[sem, h], a_rs.at[sem, h], dev,
        )

    def gather_yf(kind, h):
        rows = pl.ds(h * HALF, HALF)
        return remote(
            tg.at[kind, (Y1, F)[kind], rows], tg.at[kind, YF, rows],
            a_ss.at[(YF, CHUNKS)[kind], h], a_rs.at[(YF, CHUNKS)[kind], h],
            ((zp, zm)[h], ylp)[kind],
        )

    def arrived(dst, h):
        if dst in (C1, YO):
            for kind in (0, 1):
                gather_own(kind, dst, h, zp).wait_recv()
        else:
            gather(OWN, dst, h, zp).wait_recv()

    first = [(C1, 0, zp), (C1, 1, zm), (YO, 0, ylp), (YO, 1, ylp)]
    for to_whom in first:
        gather_own(0, *to_whom).start()
    loads[0].wait()
    for r in range(0, ROWS, 128):
        factor = keep[pl.ds(r, 128)].astype(F32) / count[0].astype(F32)
        factor = jnp.broadcast_to(factor[None, :], (128, 128)).T
        for n in range(0, DM, 128):
            block = grad_out[r : r + 128, n : n + 128].astype(F32) * factor
            tg[1, OWN, r : r + 128, n : n + 128] = block.astype(BF)
    for to_whom in first:
        gather_own(1, *to_whom).start()

    for load in loads[1:]:
        load.wait()
    for n in range(0, 2 * U, 256):
        w_in_t[n : n + 256, :] = w_in[:, n : n + 256].T
    sum_in[...] = jnp.zeros_like(sum_in)
    sum_down[...] = jnp.zeros_like(sum_down)

    def b0(i, k):
        at = pl.multiple_of(((x + (2, 1, 3, 0)[k]) % 4) * UX, UX)
        src = part.at[i % 2, :, pl.ds(pl.multiple_of((1 - c) * UC + at, UX), UX)]
        return remote(
            src, b0_r.at[i, :, pl.ds(at, UX)], c_ss.at[B0 + k, i], c_rs.at[B0 + k, i], core
        )

    def along_x(i, k, sem, src, dst):
        return remote(
            src.at[i, k], dst.at[i, k], c_ss.at[sem + k, i], c_rs.at[sem + k, i], (xp, xm)[k]
        )

    def x1(i, k):
        return along_x(i, k, X1, x1_s, x1_r)

    def xe(i, k):
        return along_x(i, k, XE, xe_s, xe_r)

    def x2(i, k):
        return along_x(i, k, X2, x2_s, x2_r)

    def yb(i):
        return remote(yb_s.at[i], yb_r.at[i], c_ss.at[YB, i], c_rs.at[YB, i], yhp)

    def lanes(i, n=1):
        return pl.ds(pl.multiple_of(i * ROWS, ROWS), n * ROWS)

    def same(i, first, n, sem, dev):
        block = hid.at[:, pl.ds(pl.multiple_of(first, UY), n), lanes(i)]
        return remote(block, block, c_ss.at[sem, i], c_rs.at[sem, i], dev)

    mine = c * UC + x * UX
    left = c * UC + ((x + 3) % 4) * UX
    right = c * UC + ((x + 1) % 4) * UX

    def h1(i):
        return same(i, mine + yh * UY, UY, H1, yhp)

    def he(i, k):
        return same(i, mine + yh * UY, UY, HE + k, (xp, xm)[k])

    def h2(i, k):
        return same(i, mine + (1 - yh) * UY, UY, H2 + k, (xp, xm)[k])

    def h3(i, k):
        return same(i, (left, right + UY)[k], UY, H3 + k, (xp, xm)[k])

    def h4(i):
        return same(i, c * UC, UC, H4, core)

    def summed(i, xd, h):
        at = xd * UX + h * UY
        a = part[i % 2, :, pl.ds(pl.multiple_of(c * UC + at, UY), UY), :]
        return a + b0_r[i, :, pl.ds(pl.multiple_of(at, UY), UY), :]

    def partial(i):
        s = i % 2
        for m in (0, 1):
            part[s, m] = dot_nt(w_in_t[m * U : (m + 1) * U, :], tg[0, i])
        part[s, 2] = dot_nt(w_down[...], tg[1, i])
        for k in range(4):
            b0(i, k).start()

    def send_x1(i):
        b0(i, 0).wait()
        for k in (0, 1):
            x1_s[i, k] = summed(i, (x + 2) % 4, k).astype(BF)
            x1(i, k).start()
        for k in (0, 1):
            b0(i, 1 + k).wait()
            xe_s[i, k] = summed(i, (x + (1, 3)[k]) % 4, 1 - k).astype(BF)
            xe(i, k).start()

    def send_x2(i):
        for k in (0, 1):
            x1(i, k).wait_recv()
            total = summed(i, (x + (1, 3)[k]) % 4, k) + x1_r[i, k].astype(F32)
            x2_s[i, k] = total.astype(BF)
            x2(i, k).start()
        b0(i, 3).wait()
        for h in (0, 1):
            xe(i, 1 - h).wait_recv()
            own64[i % 2, h] = summed(i, x, h) + xe_r[i, 1 - h].astype(F32)

    def send_yb(i):
        x2(i, 0).wait_recv()
        x2(i, 1).wait_recv()
        yb_s[i] = (own64[i % 2, 1 - yh] + x2_r[i, 1 - yh].astype(F32)).astype(BF)
        yb(i).start()
        own32[i % 2] = own64[i % 2, yh] + x2_r[i, yh].astype(F32)

    def send_h1(i):
        yb(i).wait_recv()
        full = own32[i % 2] + yb_r[i].astype(F32)
        gate, up, back = full[0], full[1], full[2]
        sigma = 1.0 / (1.0 + jnp.exp(-gate))
        silu = gate * sigma
        units = pl.ds(pl.multiple_of(mine + yh * UY, UY), UY)
        hid[0, units, lanes(i)] = (silu * up).astype(BF)
        hid[1, units, lanes(i)] = (back * up * sigma * (1.0 + gate * (1.0 - sigma))).astype(BF)
        hid[2, units, lanes(i)] = (back * silu).astype(BF)
        h1(i).start()
        he(i, 0).start()
        he(i, 1).start()

    def send_h2(i):
        h1(i).wait_recv()
        h2(i, 0).start()
        h2(i, 1).start()

    def send_h3(i):
        for k in (0, 1):
            he(i, k).wait_recv()
            h2(i, k).wait_recv()
            h3(i, k).start()

    def send_h4(i):
        h3(i, 0).wait_recv()
        h3(i, 1).wait_recv()
        h4(i).start()

    def grads_in(g):
        pair = lanes(g - 1, 2)
        for n in range(0, DM, 256):
            tok = tg[0, pl.ds(g - 1, 2), :, n : n + 256].reshape(2 * ROWS, 256)
            for m in (0, 1):
                sum_in[m * U : (m + 1) * U, n : n + 256] += dot(hid[1 + m, :, pair], tok)

    def grads_down(g):
        pair = lanes(g - 1, 2)
        for n in range(0, DM, 256):
            sc = tg[1, pl.ds(g - 1, 2), :, n : n + 256].reshape(2 * ROWS, 256)
            sum_down[:, n : n + 256] += dot(hid[0, :, pair], sc)

    def zf(col, h):
        return remote(
            zf_s.at[col, h], zf_r.at[col, h], d_ss.at[2 * col, h], d_rs.at[2 * col, h], (zm, zp)[h]
        )

    def zf_right(h):
        return remote(zg_s.at[h], zg_r.at[h], d_ss.at[0, 2 + h], d_rs.at[0, 2 + h], (zm, zp)[h])

    def dz(col, k, h):
        sem = 2 * col + 1
        return remote(
            dz_s.at[col, k, h], dz_r.at[col, k, h],
            d_ss.at[sem, 2 * k + h], d_rs.at[sem, 2 * k + h], (zp, zm)[(h + 1 + k) % 2],
        )

    def dz_right(k, h):
        return remote(
            dw_s.at[k, h], dw_r.at[k, h],
            d_ss.at[4, 2 * k + h], d_rs.at[4, 2 * k + h], (zp, zm)[(h + 1 + k) % 2],
        )

    def dy(h):
        return remote(dy_s.at[h], dy_r.at[h], d_ss.at[2, 2 + h], d_rs.at[2, 2 + h], ylp)

    def dy_right(k, h):
        return remote(dv_s.at[k, h], dv_r.at[k, h], d_ss.at[5 + h, k], d_rs.at[5 + h, k], ylp)

    def of_left(j, h):
        return to[j, :LEFT, h * HALF : (h + 1) * HALF]

    def of_right(j, h):
        return to[j, LEFT:, h * HALF : (h + 1) * HALF]

    def send_zf(col):
        for h in (0, 1):
            zf_s[col, h] = of_left((F, YF)[col], h).astype(BF)
            zf(col, h).start()

    def send_dz(col, k):
        for h in (0, 1):
            total = of_left(((C1, C2), (Y1, Y2))[col][k], h)
            if k == 0:
                zf(col, h).wait_recv()
                total = total + zf_r[col, h].astype(F32)
            dz_s[col, k, h] = total.astype(BF)
            dz(col, k, h).start()

    def column(col, h):
        dz(col, 0, h).wait_recv()
        dz(col, 1, h).wait_recv()
        return of_left((OWN, YO)[col], h) + (
            dz_r[col, 0, h].astype(F32) + dz_r[col, 1, h].astype(F32)
        )

    def send_dy():
        for h in (0, 1):
            dy_s[h] = column(1, h).astype(BF)
            dy(h).start()

    def send_dy_right(k):
        for h in (0, 1):
            dv_s[k, h] = of_right((YO, Y1, YF, Y2)[k], h).astype(BF)
            dy_right(k, h).start()

    def both_right(j, k, h):
        dy_right(k, h).wait_recv()
        return of_right(j, h) + dv_r[k, h].astype(F32)

    def send_zf_right():
        for h in (0, 1):
            zg_s[h] = both_right(F, 2, h).astype(BF)
            zf_right(h).start()

    def send_dz_right(k):
        for h in (0, 1):
            total = both_right((C1, C2)[k], 1 + 2 * k, h)
            if k == 0:
                zf_right(h).wait_recv()
                total = total + zg_r[h].astype(F32)
            dw_s[k, h] = total.astype(BF)
            dz_right(k, h).start()

    def term(j):
        h4(j).wait_recv()
        h = hid[1:, :, lanes(j)].reshape(2 * U, ROWS)
        for m in range(0, DM, 512):
            to[j, m : m + 512, :] = dot(w_in[m : m + 512, :], h)

    def arrivals(t):
        @pl.when(t == C1)
        def _():
            arrived(C1, 0)
            gather(C1, F, 0, zp).start()
            arrived(C1, 1)
            gather(C1, F, 1, zm).start()

        @pl.when(t == YO)
        def _():
            arrived(YO, 0)
            gather(YO, Y1, 0, zp).start()
            arrived(YO, 1)
            gather(YO, Y1, 1, zm).start()

        @pl.when(t == F)
        def _():
            gather_yf(1, 1).start()

        @pl.when(t == Y1)
        def _():
            for h in (0, 1):
                arrived(Y1, h)
                gather_yf(0, h).start()
            gather(YO, Y2, 1, zp).start()
            gather(YO, Y2, 0, zm).start()

        @pl.when(t == YF)
        def _():
            for kind in (0, 1):
                for h in (0, 1):
                    gather_yf(kind, h).wait_recv()

        for chunk in (Y2, C2):

            @pl.when(t == chunk)
            def _():
                arrived(chunk, 0)
                arrived(chunk, 1)

    def left_all(i):
        for k in (0, 1):
            x1(i, k).wait_send()
            xe(i, k).wait_send()
            he(i, k).wait_send()
            x2(i, k).wait_send()
            h2(i, k).wait_send()
            h3(i, k).wait_send()
        yb(i).wait_send()
        h1(i).wait_send()
        h4(i).wait_send()

    def tick(t, carry):
        def stage(step, lag):
            pl.when((t >= lag) & (t < CHUNKS + lag))(lambda: step(t - lag))

        def at(when, step, *args):
            pl.when(t == when)(lambda: step(*args))

        stage(send_yb, 2)
        stage(send_h3, 4)
        at(YF + 6, send_dz, 1, 0)
        arrivals(t)
        stage(partial, 0)

        stage(send_x2, 1)
        stage(send_h2, 3)
        stage(term, 5)
        for k, chunk in enumerate((YO, Y1, YF, Y2)):
            at(chunk + 5, send_dy_right, k)
        at(F + 5, send_zf, 0)
        at(F + 6, send_dz, 0, 0)
        at(YF + 5, send_zf, 1)
        at(Y2 + 5, send_dz, 1, 1)
        at(Y2 + 5, send_zf_right)
        at(C2 + 5, send_dz, 0, 1)
        at(C2 + 5, send_dy)
        at(C2 + 5, send_dz_right, 0)
        at(C2 + 5, send_dz_right, 1)

        @pl.when(t == YO)
        def _():
            arrived(F, 0)
            arrived(F, 1)
            gather_yf(1, 0).start()

        stage(send_h1, 2)
        stage(send_h4, 4)
        stage(send_x1, 0)

        @pl.when(t == Y1)
        def _():
            gather(OWN, C2, 1, zp).start()
            gather(OWN, C2, 0, zm).start()

        pl.when((t >= 7) & (t < CHUNKS + 5))(lambda: left_all(t - 7))
        pl.when((t >= 6) & (t % 2 == 0))(lambda: grads_in(t - 5))
        pl.when((t >= 7) & (t % 2 == 1))(lambda: grads_down(t - 6))
        return carry

    lax.fori_loop(0, CHUNKS + 5, tick, 0)

    stores = [
        pltpu.make_async_copy(sum_in, out_in, o_s.at[0]),
        pltpu.make_async_copy(sum_down, out_down, o_s.at[1]),
    ]
    stores[0].start()
    grads_down(CHUNKS - 1)
    stores[1].start()

    left_all(CHUNKS - 2)
    left_all(CHUNKS - 1)
    for to_whom in first:
        for kind in (0, 1):
            gather_own(kind, *to_whom).wait_send()
    for dst in (F, Y1, Y2, C2):
        for h in (0, 1):
            gather(OWN, dst, h, zp).wait_send()
    for h in (0, 1):
        gather_yf(0, h).wait_send()
        gather_yf(1, h).wait_send()
    for h in (0, 1):
        for col in (0, 1):
            zf(col, h).wait_send()
            dz(col, 0, h).wait_send()
            dz(col, 1, h).wait_send()
        for k in range(4):
            dy_right(k, h).wait_send()
        zf_right(h).wait_send()
        dy(h).wait_send()
        dz_right(0, h).wait_send()
        dz_right(1, h).wait_send()

    for h in (0, 1):
        rows = pl.ds(h * HALF, HALF)
        total = both_right(OWN, 0, h)
        dz_right(0, h).wait_recv()
        dz_right(1, h).wait_recv()
        total = total + (dw_r[0, h].astype(F32) + dw_r[1, h].astype(F32))
        last[rows, LEFT:] = total.T.astype(BF)
        total = column(0, h)
        dy(h).wait_recv()
        last[rows, :LEFT] = (total + dy_r[h].astype(F32)).T.astype(BF)
        stores.append(pltpu.make_async_copy(last.at[rows], out_tok.at[rows], o_s.at[2 + h]))
        stores[-1].start()
    for copy in stores:
        copy.wait()


def place(tok, sums, down, out_tok, out_gate, out_up, out_down, v_tok, v_sums, v_down, v_out, sems):
    reads, writes = [], []

    def piece(src, via, dst, by_way=None):
        k = len(reads)
        reads.append(pltpu.make_async_copy(src, via, sems.at[0, k]))
        writes.append(pltpu.make_async_copy(via if by_way is None else by_way, dst, sems.at[1, k]))
        reads[-1].start()

    turns = []
    for o, out in enumerate((out_gate, out_up)):
        for u in range(0, U, 256):
            for d in range(0, DM, 512):
                src = (pl.ds(o * U + u, 256), pl.ds(d, 512))
                dst = (pl.ds(d, 512), pl.ds(u, 256))
                turns.append((src, (o, *dst)))
                piece(sums.at[src], v_sums.at[src], out.at[dst], v_out.at[(o, *dst)])
    for p in range(0, U, 128):
        rows = pl.ds(p, 128)
        piece(down.at[rows], v_down.at[rows], out_down.at[rows])
    piece(tok, v_tok, out_tok)
    for k, (read, write) in enumerate(zip(reads, writes)):
        read.wait()
        if k < len(turns):
            src, dst = turns[k]
            v_out[dst] = v_sums[src].T
        write.start()
    for write in writes:
        write.wait()


def local(tokens, grad_out, keep, count, w_gate, w_up, w_down):
    vmem = pl.BlockSpec(memory_space=pltpu.VMEM)
    anywhere = pl.BlockSpec(memory_space=pl.ANY)
    dma = pltpu.SemaphoreType.DMA
    outs = pl.pallas_call(
        kernel,
        out_shape=(
            jax.ShapeDtypeStruct((ROWS, DM), BF),
            jax.ShapeDtypeStruct((2 * U, DM), F32),
            jax.ShapeDtypeStruct((U, DM), F32),
        ),
        in_specs=[anywhere, anywhere, vmem, pl.BlockSpec(memory_space=pltpu.SMEM)] + [anywhere] * 3,
        out_specs=[anywhere] * 3,
        scratch_shapes=[
            pltpu.VMEM((ROWS, DM), BF),
            pltpu.VMEM((ROWS, DM), BF),
            pltpu.VMEM((DM, 2 * U), BF),
            pltpu.VMEM((2 * U, DM), BF),
            pltpu.VMEM((U, DM), BF),
            pltpu.VMEM((2 * U, DM), F32),
            pltpu.VMEM((U, DM), F32),
            pltpu.VMEM((2, CHUNKS, ROWS, DM), BF),
            pltpu.VMEM((2, 3, U, ROWS), F32),
            pltpu.VMEM((CHUNKS, 3, UC, ROWS), F32),
            pltpu.VMEM((CHUNKS, 2, 3, UY, ROWS), BF),
            pltpu.VMEM((CHUNKS, 2, 3, UY, ROWS), BF),
            pltpu.VMEM((CHUNKS, 2, 3, UY, ROWS), BF),
            pltpu.VMEM((CHUNKS, 2, 3, UY, ROWS), BF),
            pltpu.VMEM((CHUNKS, 2, 3, UY, ROWS), BF),
            pltpu.VMEM((CHUNKS, 2, 3, UY, ROWS), BF),
            pltpu.VMEM((CHUNKS, 3, UY, ROWS), BF),
            pltpu.VMEM((CHUNKS, 3, UY, ROWS), BF),
            pltpu.VMEM((2, 2, 3, UY, ROWS), F32),
            pltpu.VMEM((2, 3, UY, ROWS), F32),
            pltpu.VMEM((3, U, CHUNKS * ROWS), BF),
            pltpu.VMEM((CHUNKS, DM, ROWS), F32),
            pltpu.VMEM((2, LEFT, HALF), BF),
            pltpu.VMEM((2, LEFT, HALF), BF),
            pltpu.VMEM((2, 2, LEFT, HALF), BF),
            pltpu.VMEM((2, 2, LEFT, HALF), BF),
            pltpu.VMEM((2, 2, 2, LEFT, HALF), BF),
            pltpu.VMEM((2, 2, 2, LEFT, HALF), BF),
            pltpu.VMEM((4, 2, RIGHT, HALF), BF),
            pltpu.VMEM((4, 2, RIGHT, HALF), BF),
            pltpu.VMEM((2, RIGHT, HALF), BF),
            pltpu.VMEM((2, RIGHT, HALF), BF),
            pltpu.VMEM((2, 2, RIGHT, HALF), BF),
            pltpu.VMEM((2, 2, RIGHT, HALF), BF),
            dma((MESSAGES, CHUNKS)),
            dma((MESSAGES, CHUNKS)),
            dma((CHUNKS + 3, 2)),
            dma((CHUNKS + 3, 2)),
            dma((7, 4)),
            dma((7, 4)),
            dma((4,)),
            dma((5,)),
        ],
        compiler_params=pltpu.CompilerParams(
            collective_id=0, has_side_effects=True, vmem_limit_bytes=62 * 1024 * 1024
        ),
        cost_estimate=pl.CostEstimate(
            flops=16 * 2048 * DM * U, bytes_accessed=16 << 20, transcendentals=0
        ),
    )(tokens, grad_out, keep, count, w_gate, w_up, w_down)
    return pl.pallas_call(
        place,
        out_shape=(
            jax.ShapeDtypeStruct((ROWS, DM), BF),
            jax.ShapeDtypeStruct((DM, U), F32),
            jax.ShapeDtypeStruct((DM, U), F32),
            jax.ShapeDtypeStruct((U, DM), F32),
        ),
        in_specs=[anywhere] * 3,
        out_specs=[anywhere] * 4,
        scratch_shapes=[
            pltpu.VMEM((ROWS, DM), BF),
            pltpu.VMEM((2 * U, DM), F32),
            pltpu.VMEM((U, DM), F32),
            pltpu.VMEM((2, DM, U), F32),
            dma((2, 13)),
        ],
        compiler_params=pltpu.CompilerParams(vmem_limit_bytes=62 * 1024 * 1024),
    )(*outs)


def solution(mesh):
    placed = (
        P("wide", "mp"),
        P("wide", "mp"),
        P("wide"),
        P(),
        P("mp", "wide"),
        P("mp", "wide"),
        P("wide", "mp"),
    )
    return jax.shard_map(
        local,
        mesh=mesh,
        in_specs=placed,
        out_specs=(P("wide", "mp"), P("mp", "wide"), P("mp", "wide"), P("wide", "mp")),
        check_vma=False,
    )
```

```python
import functools

import jax
import jax.numpy as jnp
from jax import lax
from jax.experimental import pallas as pl
from jax.experimental.pallas import tpu as pltpu
from jax.sharding import PartitionSpec as P

BF = jnp.bfloat16
F32 = jnp.float32
ROWS = 256
HALF = 128
DM = 1024
U = 512
UC, UX, UY = 256, 64, 32
LEFT, RIGHT = 512, 512
CHUNKS = 8
OWN, C1, YO, F, Y1, YF, Y2, C2 = range(CHUNKS)
B0, X1, XE, X2, YB, H1, HE, H2, H3, H4 = 0, 4, 6, 8, 10, 11, 12, 14, 16, 18
MESSAGES = 19


def dot(a, b):
    return lax.dot_general(a, b, (((1,), (0,)), ((), ())), preferred_element_type=F32)


def dot_nt(a, b):
    return lax.dot_general(a, b, (((1,), (1,)), ((), ())), preferred_element_type=F32)


def kernel(
    tokens, in_grad, keep, count, in_gate, in_up, in_down,
    out_tok, out_in, out_down,
    grad_out, last, w_in, w_in_t, w_down, sum_in, sum_down, tg, part, b0_r, x1_s, x1_r, xe_s, xe_r, x2_s, x2_r,
    yb_s, yb_r, own64, own32, hid,
    to, dy_s, dy_r, zf_s, zf_r, dz_s, dz_r, dv_s, dv_r, zg_s, zg_r, dw_s, dw_r,
    c_ss, c_rs, a_ss, a_rs, d_ss, d_rs, o_s, i_s,
):
    mp, wide = lax.axis_index("mp"), lax.axis_index("wide")
    x, yh, c = mp // 4, (mp // 2) % 2, mp % 2
    core = (mp + 1 - 2 * c, wide)
    xp = ((mp + 4) % 16, wide)
    xm = ((mp + 12) % 16, wide)
    yhp = (mp + 2 - 4 * yh, wide)
    ylp = (mp, wide + 1 - 2 * (wide % 2))
    zp = (mp, (wide + 2) % 8)
    zm = (mp, (wide + 6) % 8)

    def remote(src, dst, ssem, rsem, dev):
        return pltpu.make_async_remote_copy(
            src_ref=src, dst_ref=dst, send_sem=ssem, recv_sem=rsem,
            device_id=dev, device_id_type=pl.DeviceIdType.MESH,
        )

    barrier = pltpu.get_barrier_semaphore()
    for dev in (core, xp, xm, yhp, ylp, zp, zm):
        pl.semaphore_signal(barrier, inc=1, device_id=dev, device_id_type=pl.DeviceIdType.MESH)

    loads = [
        pltpu.make_async_copy(a, b, i_s.at[k])
        for k, (a, b) in enumerate(
            (
                (in_grad, grad_out),
                (tokens, tg.at[0, OWN]),
                (in_gate, w_in.at[:, pl.ds(0, U)]),
                (in_up, w_in.at[:, pl.ds(U, U)]),
                (in_down, w_down),
            )
        )
    ]
    for load in loads:
        load.start()
    pl.semaphore_wait(barrier, 7)

    def gather(src, dst, h, dev):
        rows = pl.ds(h * HALF, HALF)
        return remote(
            tg.at[:, src, rows], tg.at[:, dst, rows], a_ss.at[dst, h], a_rs.at[dst, h], dev
        )

    def gather_own(kind, dst, h, dev):
        rows = pl.ds(h * HALF, HALF)
        sem = (dst, {C1: CHUNKS + 1, YO: CHUNKS + 2, C2: CHUNKS + 3}[dst])[kind]
        return remote(
            (tokens.at[rows], tg.at[1, OWN, rows])[kind], tg.at[kind, dst, rows],
            a_ss.at[sem, h], a_rs.at[sem, h], dev,
        )

    def gather_yf(kind, h):
        rows = pl.ds(h * HALF, HALF)
        return remote(
            tg.at[kind, (Y1, F)[kind], rows], tg.at[kind, YF, rows],
            a_ss.at[(YF, CHUNKS)[kind], h], a_rs.at[(YF, CHUNKS)[kind], h],
            ((zp, zm)[h], ylp)[kind],
        )

    def arrived(dst, h):
        if dst in (C1, YO, C2):
            for kind in (0, 1):
                gather_own(kind, dst, h, zp).wait_recv()
        else:
            gather(OWN, dst, h, zp).wait_recv()

    first = [(C1, 0, zp), (C1, 1, zm), (YO, 0, ylp), (YO, 1, ylp)]
    later = [(C2, 1, zp), (C2, 0, zm)]
    for to_whom in first:
        gather_own(0, *to_whom).start()
    loads[0].wait()
    for r in range(0, ROWS, 128):
        factor = keep[pl.ds(r, 128)].astype(F32) / count[0].astype(F32)
        factor = jnp.broadcast_to(factor[None, :], (128, 128)).T
        for n in range(0, DM, 128):
            block = grad_out[r : r + 128, n : n + 128].astype(F32) * factor
            tg[1, OWN, r : r + 128, n : n + 128] = block.astype(BF)
    for to_whom in first:
        gather_own(1, *to_whom).start()

    for load in loads[1:]:
        load.wait()
    for n in range(0, 2 * U, 256):
        w_in_t[n : n + 256, :] = w_in[:, n : n + 256].T
    sum_in[...] = jnp.zeros_like(sum_in)
    sum_down[...] = jnp.zeros_like(sum_down)

    def b0(i, k):
        at = pl.multiple_of(((x + (2, 1, 3, 0)[k]) % 4) * UX, UX)
        src = part.at[i % 2, :, pl.ds(pl.multiple_of((1 - c) * UC + at, UX), UX)]
        return remote(
            src, b0_r.at[i, :, pl.ds(at, UX)], c_ss.at[B0 + k, i], c_rs.at[B0 + k, i], core
        )

    def along_x(i, k, sem, src, dst):
        return remote(
            src.at[i, k], dst.at[i, k], c_ss.at[sem + k, i], c_rs.at[sem + k, i], (xp, xm)[k]
        )

    def x1(i, k):
        return along_x(i, k, X1, x1_s, x1_r)

    def xe(i, k):
        return along_x(i, k, XE, xe_s, xe_r)

    def x2(i, k):
        return along_x(i, k, X2, x2_s, x2_r)

    def yb(i):
        return remote(yb_s.at[i], yb_r.at[i], c_ss.at[YB, i], c_rs.at[YB, i], yhp)

    def lanes(i, n=1):
        return pl.ds(pl.multiple_of(i * ROWS, ROWS), n * ROWS)

    def same(i, first, n, sem, dev):
        block = hid.at[:, pl.ds(pl.multiple_of(first, UY), n), lanes(i)]
        return remote(block, block, c_ss.at[sem, i], c_rs.at[sem, i], dev)

    mine = c * UC + x * UX
    left = c * UC + ((x + 3) % 4) * UX
    right = c * UC + ((x + 1) % 4) * UX

    def h1(i):
        return same(i, mine + yh * UY, UY, H1, yhp)

    def he(i, k):
        return same(i, mine + yh * UY, UY, HE + k, (xp, xm)[k])

    def h2(i, k):
        return same(i, mine + (1 - yh) * UY, UY, H2 + k, (xp, xm)[k])

    def h3(i, k):
        return same(i, (left, right + UY)[k], UY, H3 + k, (xp, xm)[k])

    def h4(i):
        return same(i, c * UC, UC, H4, core)

    def summed(i, xd, h):
        at = xd * UX + h * UY
        a = part[i % 2, :, pl.ds(pl.multiple_of(c * UC + at, UY), UY), :]
        return a + b0_r[i, :, pl.ds(pl.multiple_of(at, UY), UY), :]

    def partial(i):
        s = i % 2
        for m in (0, 1):
            part[s, m] = dot_nt(w_in_t[m * U : (m + 1) * U, :], tg[0, i])
        part[s, 2] = dot_nt(w_down[...], tg[1, i])
        for k in range(4):
            b0(i, k).start()

    def send_x1(i):
        b0(i, 0).wait()
        for k in (0, 1):
            x1_s[i, k] = summed(i, (x + 2) % 4, k).astype(BF)
            x1(i, k).start()
        for k in (0, 1):
            b0(i, 1 + k).wait()
            xe_s[i, k] = summed(i, (x + (1, 3)[k]) % 4, 1 - k).astype(BF)
            xe(i, k).start()

    def send_x2(i):
        for k in (0, 1):
            x1(i, k).wait_recv()
            total = summed(i, (x + (1, 3)[k]) % 4, k) + x1_r[i, k].astype(F32)
            x2_s[i, k] = total.astype(BF)
            x2(i, k).start()
        b0(i, 3).wait()
        for h in (0, 1):
            xe(i, 1 - h).wait_recv()
            own64[i % 2, h] = summed(i, x, h) + xe_r[i, 1 - h].astype(F32)

    def send_yb(i):
        x2(i, 0).wait_recv()
        x2(i, 1).wait_recv()
        yb_s[i] = (own64[i % 2, 1 - yh] + x2_r[i, 1 - yh].astype(F32)).astype(BF)
        yb(i).start()
        own32[i % 2] = own64[i % 2, yh] + x2_r[i, yh].astype(F32)

    def send_h1(i):
        yb(i).wait_recv()
        full = own32[i % 2] + yb_r[i].astype(F32)
        gate, up, back = full[0], full[1], full[2]
        sigma = 1.0 / (1.0 + jnp.exp(-gate))
        silu = gate * sigma
        units = pl.ds(pl.multiple_of(mine + yh * UY, UY), UY)
        hid[0, units, lanes(i)] = (silu * up).astype(BF)
        hid[1, units, lanes(i)] = (back * up * sigma * (1.0 + gate * (1.0 - sigma))).astype(BF)
        hid[2, units, lanes(i)] = (back * silu).astype(BF)
        h1(i).start()
        he(i, 0).start()
        he(i, 1).start()

    def send_h2(i):
        h1(i).wait_recv()
        h2(i, 0).start()
        h2(i, 1).start()

    def send_h3(i):
        for k in (0, 1):
            he(i, k).wait_recv()
            h2(i, k).wait_recv()
            h3(i, k).start()

    def send_h4(i):
        h3(i, 0).wait_recv()
        h3(i, 1).wait_recv()
        h4(i).start()

    def grads_in(g):
        pair = lanes(g - 1, 2)
        for n in range(0, DM, 256):
            tok = tg[0, pl.ds(g - 1, 2), :, n : n + 256].reshape(2 * ROWS, 256)
            for m in (0, 1):
                sum_in[m * U : (m + 1) * U, n : n + 256] += dot(hid[1 + m, :, pair], tok)

    def grads_down(g):
        pair = lanes(g - 1, 2)
        for n in range(0, DM, 256):
            sc = tg[1, pl.ds(g - 1, 2), :, n : n + 256].reshape(2 * ROWS, 256)
            sum_down[:, n : n + 256] += dot(hid[0, :, pair], sc)

    def zf(col, h):
        return remote(
            zf_s.at[col, h], zf_r.at[col, h], d_ss.at[2 * col, h], d_rs.at[2 * col, h], (zm, zp)[h]
        )

    def zf_right(h):
        return remote(zg_s.at[h], zg_r.at[h], d_ss.at[0, 2 + h], d_rs.at[0, 2 + h], (zm, zp)[h])

    def dz(col, k, h):
        sem = 2 * col + 1
        return remote(
            dz_s.at[col, k, h], dz_r.at[col, k, h],
            d_ss.at[sem, 2 * k + h], d_rs.at[sem, 2 * k + h], (zp, zm)[(h + 1 + k) % 2],
        )

    def dz_right(k, h):
        return remote(
            dw_s.at[k, h], dw_r.at[k, h],
            d_ss.at[4, 2 * k + h], d_rs.at[4, 2 * k + h], (zp, zm)[(h + 1 + k) % 2],
        )

    def dy(h):
        return remote(dy_s.at[h], dy_r.at[h], d_ss.at[2, 2 + h], d_rs.at[2, 2 + h], ylp)

    def dy_right(k, h):
        return remote(dv_s.at[k, h], dv_r.at[k, h], d_ss.at[5 + h, k], d_rs.at[5 + h, k], ylp)

    def of_left(j, h):
        return to[j, :LEFT, h * HALF : (h + 1) * HALF]

    def of_right(j, h):
        return to[j, LEFT:, h * HALF : (h + 1) * HALF]

    def send_zf(col):
        for h in (0, 1):
            zf_s[col, h] = of_left((F, YF)[col], h).astype(BF)
            zf(col, h).start()

    def send_dz(col, k):
        for h in (0, 1):
            total = of_left(((C1, C2), (Y1, Y2))[col][k], h)
            if k == 0:
                zf(col, h).wait_recv()
                total = total + zf_r[col, h].astype(F32)
            dz_s[col, k, h] = total.astype(BF)
            dz(col, k, h).start()

    def column(col, h):
        dz(col, 0, h).wait_recv()
        dz(col, 1, h).wait_recv()
        return of_left((OWN, YO)[col], h) + (
            dz_r[col, 0, h].astype(F32) + dz_r[col, 1, h].astype(F32)
        )

    def send_dy():
        for h in (0, 1):
            dy_s[h] = column(1, h).astype(BF)
            dy(h).start()

    def send_dy_right(k):
        for h in (0, 1):
            dv_s[k, h] = of_right((YO, Y1, YF, Y2)[k], h).astype(BF)
            dy_right(k, h).start()

    def both_right(j, k, h):
        dy_right(k, h).wait_recv()
        return of_right(j, h) + dv_r[k, h].astype(F32)

    def send_zf_right():
        for h in (0, 1):
            zg_s[h] = both_right(F, 2, h).astype(BF)
            zf_right(h).start()

    def send_dz_right(k):
        for h in (0, 1):
            total = both_right((C1, C2)[k], 1 + 2 * k, h)
            if k == 0:
                zf_right(h).wait_recv()
                total = total + zg_r[h].astype(F32)
            dw_s[k, h] = total.astype(BF)
            dz_right(k, h).start()

    def term(j):
        h4(j).wait_recv()
        h = hid[1:, :, lanes(j)].reshape(2 * U, ROWS)
        for m in range(0, DM, 512):
            to[j, m : m + 512, :] = dot(w_in[m : m + 512, :], h)

    def arrivals(t):
        @pl.when(t == C1)
        def _():
            arrived(C1, 0)
            gather(C1, F, 0, zp).start()
            arrived(C1, 1)
            gather(C1, F, 1, zm).start()

        @pl.when(t == YO)
        def _():
            arrived(YO, 0)
            gather(YO, Y1, 0, zp).start()
            arrived(YO, 1)
            gather(YO, Y1, 1, zm).start()

        @pl.when(t == F)
        def _():
            gather_yf(1, 1).start()
            for to_whom in later:
                gather_own(0, *to_whom).start()

        @pl.when(t == Y1)
        def _():
            for h in (0, 1):
                arrived(Y1, h)
                gather_yf(0, h).start()
            gather(YO, Y2, 1, zp).start()
            gather(YO, Y2, 0, zm).start()

        @pl.when(t == YF)
        def _():
            for kind in (0, 1):
                for h in (0, 1):
                    gather_yf(kind, h).wait_recv()

        for chunk in (Y2, C2):

            @pl.when(t == chunk)
            def _():
                arrived(chunk, 0)
                arrived(chunk, 1)

    def left_all(i):
        for k in (0, 1):
            x1(i, k).wait_send()
            xe(i, k).wait_send()
            he(i, k).wait_send()
            x2(i, k).wait_send()
            h2(i, k).wait_send()
            h3(i, k).wait_send()
        yb(i).wait_send()
        h1(i).wait_send()
        h4(i).wait_send()

    def tick(t, carry):
        def stage(step, lag):
            pl.when((t >= lag) & (t < CHUNKS + lag))(lambda: step(t - lag))

        def at(when, step, *args):
            pl.when(t == when)(lambda: step(*args))

        stage(send_yb, 2)
        stage(send_h3, 4)
        at(YF + 6, send_dz, 1, 0)
        arrivals(t)
        stage(partial, 0)

        stage(send_x2, 1)
        stage(send_h2, 3)
        stage(term, 5)
        for k, chunk in enumerate((YO, Y1, YF, Y2)):
            at(chunk + 5, send_dy_right, k)
        at(F + 5, send_zf, 0)
        at(F + 6, send_dz, 0, 0)
        at(YF + 5, send_zf, 1)
        at(Y2 + 5, send_dz, 1, 1)
        at(Y2 + 5, send_zf_right)
        at(C2 + 5, send_dz, 0, 1)
        at(C2 + 5, send_dy)
        at(C2 + 5, send_dz_right, 0)
        at(C2 + 5, send_dz_right, 1)

        @pl.when(t == YO)
        def _():
            arrived(F, 0)
            arrived(F, 1)
            gather_yf(1, 0).start()

        stage(send_h1, 2)
        stage(send_h4, 4)
        stage(send_x1, 0)

        @pl.when(t == Y1)
        def _():
            for to_whom in later:
                gather_own(1, *to_whom).start()

        pl.when((t >= 7) & (t < CHUNKS + 5))(lambda: left_all(t - 7))
        pl.when((t >= 6) & (t % 2 == 0))(lambda: grads_in(t - 5))
        pl.when((t >= 7) & (t % 2 == 1))(lambda: grads_down(t - 6))
        return carry

    lax.fori_loop(0, CHUNKS + 5, tick, 0)

    stores = [
        pltpu.make_async_copy(sum_in, out_in, o_s.at[0]),
        pltpu.make_async_copy(sum_down, out_down, o_s.at[1]),
    ]
    stores[0].start()
    grads_down(CHUNKS - 1)
    stores[1].start()

    left_all(CHUNKS - 2)
    left_all(CHUNKS - 1)
    for to_whom in first + later:
        for kind in (0, 1):
            gather_own(kind, *to_whom).wait_send()
    for dst in (F, Y1, Y2):
        for h in (0, 1):
            gather(OWN, dst, h, zp).wait_send()
    for h in (0, 1):
        gather_yf(0, h).wait_send()
        gather_yf(1, h).wait_send()
    for h in (0, 1):
        for col in (0, 1):
            zf(col, h).wait_send()
            dz(col, 0, h).wait_send()
            dz(col, 1, h).wait_send()
        for k in range(4):
            dy_right(k, h).wait_send()
        zf_right(h).wait_send()
        dy(h).wait_send()
        dz_right(0, h).wait_send()
        dz_right(1, h).wait_send()

    for h in (0, 1):
        rows = pl.ds(h * HALF, HALF)
        total = both_right(OWN, 0, h)
        dz_right(0, h).wait_recv()
        dz_right(1, h).wait_recv()
        total = total + (dw_r[0, h].astype(F32) + dw_r[1, h].astype(F32))
        last[rows, LEFT:] = total.T.astype(BF)
        total = column(0, h)
        dy(h).wait_recv()
        last[rows, :LEFT] = (total + dy_r[h].astype(F32)).T.astype(BF)
        stores.append(pltpu.make_async_copy(last.at[rows], out_tok.at[rows], o_s.at[2 + h]))
        stores[-1].start()
    for copy in stores:
        copy.wait()


def place(tok, sums, down, out_tok, out_gate, out_up, out_down, v_tok, v_sums, v_down, v_out, sems):
    reads, writes = [], []

    def piece(src, via, dst, by_way=None):
        k = len(reads)
        reads.append(pltpu.make_async_copy(src, via, sems.at[0, k]))
        writes.append(pltpu.make_async_copy(via if by_way is None else by_way, dst, sems.at[1, k]))
        reads[-1].start()

    turns = []
    for o, out in enumerate((out_gate, out_up)):
        for u in range(0, U, 256):
            for d in range(0, DM, 512):
                src = (pl.ds(o * U + u, 256), pl.ds(d, 512))
                dst = (pl.ds(d, 512), pl.ds(u, 256))
                turns.append((src, (o, *dst)))
                piece(sums.at[src], v_sums.at[src], out.at[dst], v_out.at[(o, *dst)])
    for p in range(0, U, 128):
        rows = pl.ds(p, 128)
        piece(down.at[rows], v_down.at[rows], out_down.at[rows])
    piece(tok, v_tok, out_tok)
    for k, (read, write) in enumerate(zip(reads, writes)):
        read.wait()
        if k < len(turns):
            src, dst = turns[k]
            v_out[dst] = v_sums[src].T
        write.start()
    for write in writes:
        write.wait()


def local(tokens, grad_out, keep, count, w_gate, w_up, w_down):
    vmem = pl.BlockSpec(memory_space=pltpu.VMEM)
    anywhere = pl.BlockSpec(memory_space=pl.ANY)
    dma = pltpu.SemaphoreType.DMA
    outs = pl.pallas_call(
        kernel,
        out_shape=(
            jax.ShapeDtypeStruct((ROWS, DM), BF),
            jax.ShapeDtypeStruct((2 * U, DM), F32),
            jax.ShapeDtypeStruct((U, DM), F32),
        ),
        in_specs=[anywhere, anywhere, vmem, pl.BlockSpec(memory_space=pltpu.SMEM)] + [anywhere] * 3,
        out_specs=[anywhere] * 3,
        scratch_shapes=[
            pltpu.VMEM((ROWS, DM), BF),
            pltpu.VMEM((ROWS, DM), BF),
            pltpu.VMEM((DM, 2 * U), BF),
            pltpu.VMEM((2 * U, DM), BF),
            pltpu.VMEM((U, DM), BF),
            pltpu.VMEM((2 * U, DM), F32),
            pltpu.VMEM((U, DM), F32),
            pltpu.VMEM((2, CHUNKS, ROWS, DM), BF),
            pltpu.VMEM((2, 3, U, ROWS), F32),
            pltpu.VMEM((CHUNKS, 3, UC, ROWS), F32),
            pltpu.VMEM((CHUNKS, 2, 3, UY, ROWS), BF),
            pltpu.VMEM((CHUNKS, 2, 3, UY, ROWS), BF),
            pltpu.VMEM((CHUNKS, 2, 3, UY, ROWS), BF),
            pltpu.VMEM((CHUNKS, 2, 3, UY, ROWS), BF),
            pltpu.VMEM((CHUNKS, 2, 3, UY, ROWS), BF),
            pltpu.VMEM((CHUNKS, 2, 3, UY, ROWS), BF),
            pltpu.VMEM((CHUNKS, 3, UY, ROWS), BF),
            pltpu.VMEM((CHUNKS, 3, UY, ROWS), BF),
            pltpu.VMEM((2, 2, 3, UY, ROWS), F32),
            pltpu.VMEM((2, 3, UY, ROWS), F32),
            pltpu.VMEM((3, U, CHUNKS * ROWS), BF),
            pltpu.VMEM((CHUNKS, DM, ROWS), F32),
            pltpu.VMEM((2, LEFT, HALF), BF),
            pltpu.VMEM((2, LEFT, HALF), BF),
            pltpu.VMEM((2, 2, LEFT, HALF), BF),
            pltpu.VMEM((2, 2, LEFT, HALF), BF),
            pltpu.VMEM((2, 2, 2, LEFT, HALF), BF),
            pltpu.VMEM((2, 2, 2, LEFT, HALF), BF),
            pltpu.VMEM((4, 2, RIGHT, HALF), BF),
            pltpu.VMEM((4, 2, RIGHT, HALF), BF),
            pltpu.VMEM((2, RIGHT, HALF), BF),
            pltpu.VMEM((2, RIGHT, HALF), BF),
            pltpu.VMEM((2, 2, RIGHT, HALF), BF),
            pltpu.VMEM((2, 2, RIGHT, HALF), BF),
            dma((MESSAGES, CHUNKS)),
            dma((MESSAGES, CHUNKS)),
            dma((CHUNKS + 4, 2)),
            dma((CHUNKS + 4, 2)),
            dma((7, 4)),
            dma((7, 4)),
            dma((4,)),
            dma((5,)),
        ],
        compiler_params=pltpu.CompilerParams(
            collective_id=0, has_side_effects=True, vmem_limit_bytes=62 * 1024 * 1024
        ),
        cost_estimate=pl.CostEstimate(
            flops=16 * 2048 * DM * U, bytes_accessed=16 << 20, transcendentals=0
        ),
    )(tokens, grad_out, keep, count, w_gate, w_up, w_down)
    return pl.pallas_call(
        place,
        out_shape=(
            jax.ShapeDtypeStruct((ROWS, DM), BF),
            jax.ShapeDtypeStruct((DM, U), F32),
            jax.ShapeDtypeStruct((DM, U), F32),
            jax.ShapeDtypeStruct((U, DM), F32),
        ),
        in_specs=[anywhere] * 3,
        out_specs=[anywhere] * 4,
        scratch_shapes=[
            pltpu.VMEM((ROWS, DM), BF),
            pltpu.VMEM((2 * U, DM), F32),
            pltpu.VMEM((U, DM), F32),
            pltpu.VMEM((2, DM, U), F32),
            dma((2, 13)),
        ],
        compiler_params=pltpu.CompilerParams(vmem_limit_bytes=62 * 1024 * 1024),
    )(*outs)


def solution(mesh):
    placed = (
        P("wide", "mp"),
        P("wide", "mp"),
        P("wide"),
        P(),
        P("mp", "wide"),
        P("mp", "wide"),
        P("wide", "mp"),
    )
    return jax.shard_map(
        local,
        mesh=mesh,
        in_specs=placed,
        out_specs=(P("wide", "mp"), P("mp", "wide"), P("mp", "wide"), P("wide", "mp")),
        check_vma=False,
    )
```

```python
import functools

import jax
import jax.numpy as jnp
from jax import lax
from jax.experimental import pallas as pl
from jax.experimental.pallas import tpu as pltpu
from jax.sharding import PartitionSpec as P

BF = jnp.bfloat16
F32 = jnp.float32
ROWS = 256
HALF = 128
DM = 1024
U = 512
UC, UX, UY = 256, 64, 32
LEFT, RIGHT = 512, 512
CHUNKS = 8
OWN, C1, YO, F, Y1, YF, Y2, C2 = range(CHUNKS)
B0, X1, XE, X2, YB, H1, HE, H2, H3, H4 = 0, 4, 6, 8, 10, 11, 12, 14, 16, 18
MESSAGES = 19


def dot(a, b):
    return lax.dot_general(a, b, (((1,), (0,)), ((), ())), preferred_element_type=F32)


def dot_nt(a, b):
    return lax.dot_general(a, b, (((1,), (1,)), ((), ())), preferred_element_type=F32)


def kernel(
    tokens, in_grad, keep, count, in_gate, in_up, in_down,
    out_tok, out_in, out_down,
    grad_out, last, w_in, w_in_t, w_down, sum_in, sum_down, tg, part, b0_r, x1_s, x1_r, xe_s, xe_r, x2_s, x2_r,
    yb_s, yb_r, own64, own32, hid,
    to, dy_s, dy_r, zf_s, zf_r, dz_s, dz_r, dv_s, dv_r, zg_s, zg_r, dw_s, dw_r,
    c_ss, c_rs, a_ss, a_rs, d_ss, d_rs, o_s, i_s,
):
    mp, wide = lax.axis_index("mp"), lax.axis_index("wide")
    x, yh, c = mp // 4, (mp // 2) % 2, mp % 2
    core = (mp + 1 - 2 * c, wide)
    xp = ((mp + 4) % 16, wide)
    xm = ((mp + 12) % 16, wide)
    yhp = (mp + 2 - 4 * yh, wide)
    ylp = (mp, wide + 1 - 2 * (wide % 2))
    zp = (mp, (wide + 2) % 8)
    zm = (mp, (wide + 6) % 8)

    def remote(src, dst, ssem, rsem, dev):
        return pltpu.make_async_remote_copy(
            src_ref=src, dst_ref=dst, send_sem=ssem, recv_sem=rsem,
            device_id=dev, device_id_type=pl.DeviceIdType.MESH,
        )

    barrier = pltpu.get_barrier_semaphore()
    for dev in (core, xp, xm, yhp, ylp, zp, zm):
        pl.semaphore_signal(barrier, inc=1, device_id=dev, device_id_type=pl.DeviceIdType.MESH)

    loads = [
        pltpu.make_async_copy(a, b, i_s.at[k])
        for k, (a, b) in enumerate(
            (
                (in_grad, grad_out),
                (tokens, tg.at[0, OWN]),
                (in_gate, w_in.at[:, pl.ds(0, U)]),
                (in_up, w_in.at[:, pl.ds(U, U)]),
                (in_down, w_down),
            )
        )
    ]
    for load in loads:
        load.start()
    pl.semaphore_wait(barrier, 7)

    def gather(src, dst, h, dev):
        rows = pl.ds(h * HALF, HALF)
        return remote(
            tg.at[:, src, rows], tg.at[:, dst, rows], a_ss.at[dst, h], a_rs.at[dst, h], dev
        )

    def gather_own(kind, dst, h, dev):
        rows = pl.ds(h * HALF, HALF)
        sem = (dst, CHUNKS + 1 + (dst == YO))[kind]
        return remote(
            (tokens.at[rows], tg.at[1, OWN, rows])[kind], tg.at[kind, dst, rows],
            a_ss.at[sem, h], a_rs.at[sem, h], dev,
        )

    def gather_yf(kind, h):
        rows = pl.ds(h * HALF, HALF)
        return remote(
            tg.at[kind, (Y1, F)[kind], rows], tg.at[kind, YF, rows],
            a_ss.at[(YF, CHUNKS)[kind], h], a_rs.at[(YF, CHUNKS)[kind], h],
            ((zp, zm)[h], ylp)[kind],
        )

    def gather_y1(kind, h):
        rows = pl.ds(h * HALF, HALF)
        sem = (Y1, CHUNKS + 3)[kind]
        return remote(
            tg.at[kind, YO, rows], tg.at[kind, Y1, rows], a_ss.at[sem, h], a_rs.at[sem, h],
            (zp, zm)[h],
        )

    def arrived(dst, h):
        if dst in (C1, YO):
            for kind in (0, 1):
                gather_own(kind, dst, h, zp).wait_recv()
        else:
            gather(OWN, dst, h, zp).wait_recv()

    first = [(C1, 0, zp), (C1, 1, zm), (YO, 0, ylp), (YO, 1, ylp)]
    for to_whom in first:
        gather_own(0, *to_whom).start()
    loads[0].wait()
    for r in range(0, ROWS, 128):
        factor = keep[pl.ds(r, 128)].astype(F32) / count[0].astype(F32)
        factor = jnp.broadcast_to(factor[None, :], (128, 128)).T
        for n in range(0, DM, 128):
            block = grad_out[r : r + 128, n : n + 128].astype(F32) * factor
            tg[1, OWN, r : r + 128, n : n + 128] = block.astype(BF)
    for to_whom in first:
        gather_own(1, *to_whom).start()

    for load in loads[1:]:
        load.wait()
    for n in range(0, 2 * U, 256):
        w_in_t[n : n + 256, :] = w_in[:, n : n + 256].T
    sum_in[...] = jnp.zeros_like(sum_in)
    sum_down[...] = jnp.zeros_like(sum_down)

    def b0(i, k):
        at = pl.multiple_of(((x + (2, 1, 3, 0)[k]) % 4) * UX, UX)
        src = part.at[i % 2, :, pl.ds(pl.multiple_of((1 - c) * UC + at, UX), UX)]
        return remote(
            src, b0_r.at[i, :, pl.ds(at, UX)], c_ss.at[B0 + k, i], c_rs.at[B0 + k, i], core
        )

    def along_x(i, k, sem, src, dst):
        return remote(
            src.at[i, k], dst.at[i, k], c_ss.at[sem + k, i], c_rs.at[sem + k, i], (xp, xm)[k]
        )

    def x1(i, k):
        return along_x(i, k, X1, x1_s, x1_r)

    def xe(i, k):
        return along_x(i, k, XE, xe_s, xe_r)

    def x2(i, k):
        return along_x(i, k, X2, x2_s, x2_r)

    def yb(i):
        return remote(yb_s.at[i], yb_r.at[i], c_ss.at[YB, i], c_rs.at[YB, i], yhp)

    def lanes(i, n=1):
        return pl.ds(pl.multiple_of(i * ROWS, ROWS), n * ROWS)

    def same(i, first, n, sem, dev):
        block = hid.at[:, pl.ds(pl.multiple_of(first, UY), n), lanes(i)]
        return remote(block, block, c_ss.at[sem, i], c_rs.at[sem, i], dev)

    mine = c * UC + x * UX
    left = c * UC + ((x + 3) % 4) * UX
    right = c * UC + ((x + 1) % 4) * UX

    def h1(i):
        return same(i, mine + yh * UY, UY, H1, yhp)

    def he(i, k):
        return same(i, mine + yh * UY, UY, HE + k, (xp, xm)[k])

    def h2(i, k):
        return same(i, mine + (1 - yh) * UY, UY, H2 + k, (xp, xm)[k])

    def h3(i, k):
        return same(i, (left, right + UY)[k], UY, H3 + k, (xp, xm)[k])

    def h4(i):
        return same(i, c * UC, UC, H4, core)

    def summed(i, xd, h):
        at = xd * UX + h * UY
        a = part[i % 2, :, pl.ds(pl.multiple_of(c * UC + at, UY), UY), :]
        return a + b0_r[i, :, pl.ds(pl.multiple_of(at, UY), UY), :]

    def partial(i):
        s = i % 2
        for m in (0, 1):
            part[s, m] = dot_nt(w_in_t[m * U : (m + 1) * U, :], tg[0, i])
        part[s, 2] = dot_nt(w_down[...], tg[1, i])
        for k in range(4):
            b0(i, k).start()

    def send_x1(i):
        b0(i, 0).wait()
        for k in (0, 1):
            x1_s[i, k] = summed(i, (x + 2) % 4, k).astype(BF)
            x1(i, k).start()
        for k in (0, 1):
            b0(i, 1 + k).wait()
            xe_s[i, k] = summed(i, (x + (1, 3)[k]) % 4, 1 - k).astype(BF)
            xe(i, k).start()

    def send_x2(i):
        for k in (0, 1):
            x1(i, k).wait_recv()
            total = summed(i, (x + (1, 3)[k]) % 4, k) + x1_r[i, k].astype(F32)
            x2_s[i, k] = total.astype(BF)
            x2(i, k).start()
        b0(i, 3).wait()
        for h in (0, 1):
            xe(i, 1 - h).wait_recv()
            own64[i % 2, h] = summed(i, x, h) + xe_r[i, 1 - h].astype(F32)

    def send_yb(i):
        x2(i, 0).wait_recv()
        x2(i, 1).wait_recv()
        yb_s[i] = (own64[i % 2, 1 - yh] + x2_r[i, 1 - yh].astype(F32)).astype(BF)
        yb(i).start()
        own32[i % 2] = own64[i % 2, yh] + x2_r[i, yh].astype(F32)

    def send_h1(i):
        yb(i).wait_recv()
        full = own32[i % 2] + yb_r[i].astype(F32)
        gate, up, back = full[0], full[1], full[2]
        sigma = 1.0 / (1.0 + jnp.exp(-gate))
        silu = gate * sigma
        units = pl.ds(pl.multiple_of(mine + yh * UY, UY), UY)
        hid[0, units, lanes(i)] = (silu * up).astype(BF)
        hid[1, units, lanes(i)] = (back * up * sigma * (1.0 + gate * (1.0 - sigma))).astype(BF)
        hid[2, units, lanes(i)] = (back * silu).astype(BF)
        h1(i).start()
        he(i, 0).start()
        he(i, 1).start()

    def send_h2(i):
        h1(i).wait_recv()
        h2(i, 0).start()
        h2(i, 1).start()

    def send_h3(i):
        for k in (0, 1):
            he(i, k).wait_recv()
            h2(i, k).wait_recv()
            h3(i, k).start()

    def send_h4(i):
        h3(i, 0).wait_recv()
        h3(i, 1).wait_recv()
        h4(i).start()

    def grads_in(g):
        pair = lanes(g - 1, 2)
        for n in range(0, DM, 256):
            tok = tg[0, pl.ds(g - 1, 2), :, n : n + 256].reshape(2 * ROWS, 256)
            for m in (0, 1):
                sum_in[m * U : (m + 1) * U, n : n + 256] += dot(hid[1 + m, :, pair], tok)

    def grads_down(g):
        pair = lanes(g - 1, 2)
        for n in range(0, DM, 256):
            sc = tg[1, pl.ds(g - 1, 2), :, n : n + 256].reshape(2 * ROWS, 256)
            sum_down[:, n : n + 256] += dot(hid[0, :, pair], sc)

    def zf(col, h):
        return remote(
            zf_s.at[col, h], zf_r.at[col, h], d_ss.at[2 * col, h], d_rs.at[2 * col, h], (zm, zp)[h]
        )

    def zf_right(h):
        return remote(zg_s.at[h], zg_r.at[h], d_ss.at[0, 2 + h], d_rs.at[0, 2 + h], (zm, zp)[h])

    def dz(col, k, h):
        sem = 2 * col + 1
        return remote(
            dz_s.at[col, k, h], dz_r.at[col, k, h],
            d_ss.at[sem, 2 * k + h], d_rs.at[sem, 2 * k + h], (zp, zm)[(h + 1 + k) % 2],
        )

    def dz_right(k, h):
        return remote(
            dw_s.at[k, h], dw_r.at[k, h],
            d_ss.at[4, 2 * k + h], d_rs.at[4, 2 * k + h], (zp, zm)[(h + 1 + k) % 2],
        )

    def dy(h):
        return remote(dy_s.at[h], dy_r.at[h], d_ss.at[2, 2 + h], d_rs.at[2, 2 + h], ylp)

    def dy_right(k, h):
        return remote(dv_s.at[k, h], dv_r.at[k, h], d_ss.at[5 + h, k], d_rs.at[5 + h, k], ylp)

    def of_left(j, h):
        return to[j, :LEFT, h * HALF : (h + 1) * HALF]

    def of_right(j, h):
        return to[j, LEFT:, h * HALF : (h + 1) * HALF]

    def send_zf(col):
        for h in (0, 1):
            zf_s[col, h] = of_left((F, YF)[col], h).astype(BF)
            zf(col, h).start()

    def send_dz(col, k):
        for h in (0, 1):
            total = of_left(((C1, C2), (Y1, Y2))[col][k], h)
            if k == 0:
                zf(col, h).wait_recv()
                total = total + zf_r[col, h].astype(F32)
            dz_s[col, k, h] = total.astype(BF)
            dz(col, k, h).start()

    def column(col, h):
        dz(col, 0, h).wait_recv()
        dz(col, 1, h).wait_recv()
        return of_left((OWN, YO)[col], h) + (
            dz_r[col, 0, h].astype(F32) + dz_r[col, 1, h].astype(F32)
        )

    def send_dy():
        for h in (0, 1):
            dy_s[h] = column(1, h).astype(BF)
            dy(h).start()

    def send_dy_right(k):
        for h in (0, 1):
            dv_s[k, h] = of_right((YO, Y1, YF, Y2)[k], h).astype(BF)
            dy_right(k, h).start()

    def both_right(j, k, h):
        dy_right(k, h).wait_recv()
        return of_right(j, h) + dv_r[k, h].astype(F32)

    def send_zf_right():
        for h in (0, 1):
            zg_s[h] = both_right(F, 2, h).astype(BF)
            zf_right(h).start()

    def send_dz_right(k):
        for h in (0, 1):
            total = both_right((C1, C2)[k], 1 + 2 * k, h)
            if k == 0:
                zf_right(h).wait_recv()
                total = total + zg_r[h].astype(F32)
            dw_s[k, h] = total.astype(BF)
            dz_right(k, h).start()

    def term(j):
        h4(j).wait_recv()
        h = hid[1:, :, lanes(j)].reshape(2 * U, ROWS)
        for m in range(0, DM, 512):
            to[j, m : m + 512, :] = dot(w_in[m : m + 512, :], h)

    def arrivals(t):
        @pl.when(t == C1)
        def _():
            arrived(C1, 0)
            gather(C1, F, 0, zp).start()
            arrived(C1, 1)
            gather(C1, F, 1, zm).start()

        @pl.when(t == YO)
        def _():
            for h in (0, 1):
                arrived(YO, h)
                gather_y1(0, h).start()
            gather_y1(1, 0).start()
            gather_y1(1, 1).start()
            for h in (0, 1):
                arrived(F, h)
                gather_yf(1, h).start()

        @pl.when(t == F)
        def _():
            for h in (0, 1):
                gather_y1(0, h).wait_recv()
                gather_yf(0, h).start()

        @pl.when(t == Y1)
        def _():
            gather_y1(1, 0).wait_recv()
            gather_y1(1, 1).wait_recv()
            gather(YO, Y2, 1, zp).start()
            gather(YO, Y2, 0, zm).start()

        @pl.when(t == YF)
        def _():
            for kind in (0, 1):
                for h in (0, 1):
                    gather_yf(kind, h).wait_recv()

        for chunk in (Y2, C2):

            @pl.when(t == chunk)
            def _():
                arrived(chunk, 0)
                arrived(chunk, 1)

    def left_all(i):
        for k in (0, 1):
            x1(i, k).wait_send()
            xe(i, k).wait_send()
            he(i, k).wait_send()
            x2(i, k).wait_send()
            h2(i, k).wait_send()
            h3(i, k).wait_send()
        yb(i).wait_send()
        h1(i).wait_send()
        h4(i).wait_send()

    def tick(t, carry):
        def stage(step, lag):
            pl.when((t >= lag) & (t < CHUNKS + lag))(lambda: step(t - lag))

        def at(when, step, *args):
            pl.when(t == when)(lambda: step(*args))

        stage(send_yb, 2)
        stage(send_h3, 4)
        at(YF + 6, send_dz, 1, 0)
        arrivals(t)
        stage(partial, 0)

        stage(send_x2, 1)
        stage(send_h2, 3)
        stage(term, 5)
        for k, chunk in enumerate((YO, Y1, YF, Y2)):
            at(chunk + 5, send_dy_right, k)
        at(F + 5, send_zf, 0)
        at(F + 6, send_dz, 0, 0)
        at(YF + 5, send_zf, 1)
        at(Y2 + 5, send_dz, 1, 1)
        at(Y2 + 5, send_zf_right)
        at(C2 + 5, send_dz, 0, 1)
        at(C2 + 5, send_dy)
        at(C2 + 5, send_dz_right, 0)
        at(C2 + 5, send_dz_right, 1)

        stage(send_h1, 2)
        stage(send_h4, 4)
        stage(send_x1, 0)

        @pl.when(t == Y1)
        def _():
            gather(OWN, C2, 1, zp).start()
            gather(OWN, C2, 0, zm).start()

        pl.when((t >= 7) & (t < CHUNKS + 5))(lambda: left_all(t - 7))
        pl.when((t >= 6) & (t % 2 == 0))(lambda: grads_in(t - 5))
        pl.when((t >= 7) & (t % 2 == 1))(lambda: grads_down(t - 6))
        return carry

    lax.fori_loop(0, CHUNKS + 5, tick, 0)

    stores = [
        pltpu.make_async_copy(sum_in, out_in, o_s.at[0]),
        pltpu.make_async_copy(sum_down, out_down, o_s.at[1]),
    ]
    stores[0].start()
    grads_down(CHUNKS - 1)
    stores[1].start()

    left_all(CHUNKS - 2)
    left_all(CHUNKS - 1)
    for to_whom in first:
        for kind in (0, 1):
            gather_own(kind, *to_whom).wait_send()
    for dst in (F, Y2, C2):
        for h in (0, 1):
            gather(OWN, dst, h, zp).wait_send()
    for h in (0, 1):
        gather_y1(0, h).wait_send()
        gather_y1(1, h).wait_send()
        gather_yf(0, h).wait_send()
        gather_yf(1, h).wait_send()
    for h in (0, 1):
        for col in (0, 1):
            zf(col, h).wait_send()
            dz(col, 0, h).wait_send()
            dz(col, 1, h).wait_send()
        for k in range(4):
            dy_right(k, h).wait_send()
        zf_right(h).wait_send()
        dy(h).wait_send()
        dz_right(0, h).wait_send()
        dz_right(1, h).wait_send()

    for h in (0, 1):
        rows = pl.ds(h * HALF, HALF)
        total = both_right(OWN, 0, h)
        dz_right(0, h).wait_recv()
        dz_right(1, h).wait_recv()
        total = total + (dw_r[0, h].astype(F32) + dw_r[1, h].astype(F32))
        last[rows, LEFT:] = total.T.astype(BF)
        total = column(0, h)
        dy(h).wait_recv()
        last[rows, :LEFT] = (total + dy_r[h].astype(F32)).T.astype(BF)
        stores.append(pltpu.make_async_copy(last.at[rows], out_tok.at[rows], o_s.at[2 + h]))
        stores[-1].start()
    for copy in stores:
        copy.wait()


def place(tok, sums, down, out_tok, out_gate, out_up, out_down, v_tok, v_sums, v_down, v_out, sems):
    reads, writes = [], []

    def piece(src, via, dst, by_way=None):
        k = len(reads)
        reads.append(pltpu.make_async_copy(src, via, sems.at[0, k]))
        writes.append(pltpu.make_async_copy(via if by_way is None else by_way, dst, sems.at[1, k]))
        reads[-1].start()

    turns = []
    for o, out in enumerate((out_gate, out_up)):
        for u in range(0, U, 256):
            for d in range(0, DM, 512):
                src = (pl.ds(o * U + u, 256), pl.ds(d, 512))
                dst = (pl.ds(d, 512), pl.ds(u, 256))
                turns.append((src, (o, *dst)))
                piece(sums.at[src], v_sums.at[src], out.at[dst], v_out.at[(o, *dst)])
    for p in range(0, U, 128):
        rows = pl.ds(p, 128)
        piece(down.at[rows], v_down.at[rows], out_down.at[rows])
    piece(tok, v_tok, out_tok)
    for k, (read, write) in enumerate(zip(reads, writes)):
        read.wait()
        if k < len(turns):
            src, dst = turns[k]
            v_out[dst] = v_sums[src].T
        write.start()
    for write in writes:
        write.wait()


def local(tokens, grad_out, keep, count, w_gate, w_up, w_down):
    vmem = pl.BlockSpec(memory_space=pltpu.VMEM)
    anywhere = pl.BlockSpec(memory_space=pl.ANY)
    dma = pltpu.SemaphoreType.DMA
    outs = pl.pallas_call(
        kernel,
        out_shape=(
            jax.ShapeDtypeStruct((ROWS, DM), BF),
            jax.ShapeDtypeStruct((2 * U, DM), F32),
            jax.ShapeDtypeStruct((U, DM), F32),
        ),
        in_specs=[anywhere, anywhere, vmem, pl.BlockSpec(memory_space=pltpu.SMEM)] + [anywhere] * 3,
        out_specs=[anywhere] * 3,
        scratch_shapes=[
            pltpu.VMEM((ROWS, DM), BF),
            pltpu.VMEM((ROWS, DM), BF),
            pltpu.VMEM((DM, 2 * U), BF),
            pltpu.VMEM((2 * U, DM), BF),
            pltpu.VMEM((U, DM), BF),
            pltpu.VMEM((2 * U, DM), F32),
            pltpu.VMEM((U, DM), F32),
            pltpu.VMEM((2, CHUNKS, ROWS, DM), BF),
            pltpu.VMEM((2, 3, U, ROWS), F32),
            pltpu.VMEM((CHUNKS, 3, UC, ROWS), F32),
            pltpu.VMEM((CHUNKS, 2, 3, UY, ROWS), BF),
            pltpu.VMEM((CHUNKS, 2, 3, UY, ROWS), BF),
            pltpu.VMEM((CHUNKS, 2, 3, UY, ROWS), BF),
            pltpu.VMEM((CHUNKS, 2, 3, UY, ROWS), BF),
            pltpu.VMEM((CHUNKS, 2, 3, UY, ROWS), BF),
            pltpu.VMEM((CHUNKS, 2, 3, UY, ROWS), BF),
            pltpu.VMEM((CHUNKS, 3, UY, ROWS), BF),
            pltpu.VMEM((CHUNKS, 3, UY, ROWS), BF),
            pltpu.VMEM((2, 2, 3, UY, ROWS), F32),
            pltpu.VMEM((2, 3, UY, ROWS), F32),
            pltpu.VMEM((3, U, CHUNKS * ROWS), BF),
            pltpu.VMEM((CHUNKS, DM, ROWS), F32),
            pltpu.VMEM((2, LEFT, HALF), BF),
            pltpu.VMEM((2, LEFT, HALF), BF),
            pltpu.VMEM((2, 2, LEFT, HALF), BF),
            pltpu.VMEM((2, 2, LEFT, HALF), BF),
            pltpu.VMEM((2, 2, 2, LEFT, HALF), BF),
            pltpu.VMEM((2, 2, 2, LEFT, HALF), BF),
            pltpu.VMEM((4, 2, RIGHT, HALF), BF),
            pltpu.VMEM((4, 2, RIGHT, HALF), BF),
            pltpu.VMEM((2, RIGHT, HALF), BF),
            pltpu.VMEM((2, RIGHT, HALF), BF),
            pltpu.VMEM((2, 2, RIGHT, HALF), BF),
            pltpu.VMEM((2, 2, RIGHT, HALF), BF),
            dma((MESSAGES, CHUNKS)),
            dma((MESSAGES, CHUNKS)),
            dma((CHUNKS + 4, 2)),
            dma((CHUNKS + 4, 2)),
            dma((7, 4)),
            dma((7, 4)),
            dma((4,)),
            dma((5,)),
        ],
        compiler_params=pltpu.CompilerParams(
            collective_id=0, has_side_effects=True, vmem_limit_bytes=62 * 1024 * 1024
        ),
        cost_estimate=pl.CostEstimate(
            flops=16 * 2048 * DM * U, bytes_accessed=16 << 20, transcendentals=0
        ),
    )(tokens, grad_out, keep, count, w_gate, w_up, w_down)
    return pl.pallas_call(
        place,
        out_shape=(
            jax.ShapeDtypeStruct((ROWS, DM), BF),
            jax.ShapeDtypeStruct((DM, U), F32),
            jax.ShapeDtypeStruct((DM, U), F32),
            jax.ShapeDtypeStruct((U, DM), F32),
        ),
        in_specs=[anywhere] * 3,
        out_specs=[anywhere] * 4,
        scratch_shapes=[
            pltpu.VMEM((ROWS, DM), BF),
            pltpu.VMEM((2 * U, DM), F32),
            pltpu.VMEM((U, DM), F32),
            pltpu.VMEM((2, DM, U), F32),
            dma((2, 13)),
        ],
        compiler_params=pltpu.CompilerParams(vmem_limit_bytes=62 * 1024 * 1024),
    )(*outs)


def solution(mesh):
    placed = (
        P("wide", "mp"),
        P("wide", "mp"),
        P("wide"),
        P(),
        P("mp", "wide"),
        P("mp", "wide"),
        P("wide", "mp"),
    )
    return jax.shard_map(
        local,
        mesh=mesh,
        in_specs=placed,
        out_specs=(P("wide", "mp"), P("mp", "wide"), P("mp", "wide"), P("wide", "mp")),
        check_vma=False,
    )
```

```python
import functools

import jax
import jax.numpy as jnp
from jax import lax
from jax.experimental import pallas as pl
from jax.experimental.pallas import tpu as pltpu
from jax.sharding import PartitionSpec as P

BF = jnp.bfloat16
F32 = jnp.float32
ROWS = 256
HALF = 128
DM = 1024
U = 512
UC, UX, UY = 256, 64, 32
LEFT, RIGHT = 512, 512
CHUNKS = 8
OWN, C1, YO, F, Y1, YF, Y2, C2 = range(CHUNKS)
B0, X1, XE, X2, YB, H1, HE, H2, H3, H4 = 0, 4, 6, 8, 10, 11, 12, 14, 16, 18
MESSAGES = 19


def dot(a, b):
    return lax.dot_general(a, b, (((1,), (0,)), ((), ())), preferred_element_type=F32)


def dot_nt(a, b):
    return lax.dot_general(a, b, (((1,), (1,)), ((), ())), preferred_element_type=F32)


def kernel(
    tokens, in_grad, keep, count, in_gate, in_up, in_down,
    out_tok, out_in, out_down,
    grad_out, last, w_in, w_in_t, w_down, sum_in, sum_down, tg, part, b0_r, x1_s, x1_r, xe_s, xe_r, x2_s, x2_r,
    yb_s, yb_r, own64, own32, hid,
    to, dy_s, dy_r, zf_s, zf_r, dz_s, dz_r, dv_s, dv_r, zg_s, zg_r, dw_s, dw_r,
    c_ss, c_rs, a_ss, a_rs, d_ss, d_rs, o_s, i_s,
):
    mp, wide = lax.axis_index("mp"), lax.axis_index("wide")
    x, yh, c = mp // 4, (mp // 2) % 2, mp % 2
    core = (mp + 1 - 2 * c, wide)
    xp = ((mp + 4) % 16, wide)
    xm = ((mp + 12) % 16, wide)
    yhp = (mp + 2 - 4 * yh, wide)
    ylp = (mp, wide + 1 - 2 * (wide % 2))
    zp = (mp, (wide + 2) % 8)
    zm = (mp, (wide + 6) % 8)

    def remote(src, dst, ssem, rsem, dev):
        return pltpu.make_async_remote_copy(
            src_ref=src, dst_ref=dst, send_sem=ssem, recv_sem=rsem,
            device_id=dev, device_id_type=pl.DeviceIdType.MESH,
        )

    barrier = pltpu.get_barrier_semaphore()
    for dev in (core, xp, xm, yhp, ylp, zp, zm):
        pl.semaphore_signal(barrier, inc=1, device_id=dev, device_id_type=pl.DeviceIdType.MESH)

    loads = [
        pltpu.make_async_copy(a, b, i_s.at[k])
        for k, (a, b) in enumerate(
            (
                (in_grad, grad_out),
                (tokens, tg.at[0, OWN]),
                (in_gate, w_in.at[:, pl.ds(0, U)]),
                (in_up, w_in.at[:, pl.ds(U, U)]),
                (in_down, w_down),
            )
        )
    ]
    for load in loads:
        load.start()
    pl.semaphore_wait(barrier, 7)

    def gather(src, dst, h, dev):
        rows = pl.ds(h * HALF, HALF)
        return remote(
            tg.at[:, src, rows], tg.at[:, dst, rows], a_ss.at[dst, h], a_rs.at[dst, h], dev
        )

    def gather_own(kind, dst, h, dev):
        rows = pl.ds(h * HALF, HALF)
        sem = (dst, CHUNKS + 1 + (dst == YO))[kind]
        return remote(
            (tokens.at[rows], tg.at[1, OWN, rows])[kind], tg.at[kind, dst, rows],
            a_ss.at[sem, h], a_rs.at[sem, h], dev,
        )

    def gather_yf(kind, h):
        rows = pl.ds(h * HALF, HALF)
        return remote(
            tg.at[kind, (Y1, F)[kind], rows], tg.at[kind, YF, rows],
            a_ss.at[(YF, CHUNKS)[kind], h], a_rs.at[(YF, CHUNKS)[kind], h],
            ((zp, zm)[h], ylp)[kind],
        )

    def gather_y1(kind, h):
        rows = pl.ds(h * HALF, HALF)
        sem = (Y1, CHUNKS + 3)[kind]
        return remote(
            tg.at[kind, YO, rows], tg.at[kind, Y1, rows], a_ss.at[sem, h], a_rs.at[sem, h],
            (zp, zm)[h],
        )

    def arrived(dst, h):
        if dst in (C1, YO):
            for kind in (0, 1):
                gather_own(kind, dst, h, zp).wait_recv()
        else:
            gather(OWN, dst, h, zp).wait_recv()

    first = [(C1, 0, zp), (C1, 1, zm), (YO, 0, ylp), (YO, 1, ylp)]
    for to_whom in first:
        gather_own(0, *to_whom).start()
    loads[0].wait()
    for r in range(0, ROWS, 128):
        factor = keep[pl.ds(r, 128)].astype(F32) / count[0].astype(F32)
        factor = jnp.broadcast_to(factor[None, :], (128, 128)).T
        for n in range(0, DM, 128):
            block = grad_out[r : r + 128, n : n + 128].astype(F32) * factor
            tg[1, OWN, r : r + 128, n : n + 128] = block.astype(BF)
    for to_whom in first:
        gather_own(1, *to_whom).start()

    for load in loads[1:]:
        load.wait()
    for n in range(0, 2 * U, 256):
        w_in_t[n : n + 256, :] = w_in[:, n : n + 256].T
    sum_in[...] = jnp.zeros_like(sum_in)
    sum_down[...] = jnp.zeros_like(sum_down)

    def b0(i, k):
        at = pl.multiple_of(((x + (2, 1, 3, 0)[k]) % 4) * UX, UX)
        src = part.at[i % 2, :, pl.ds(pl.multiple_of((1 - c) * UC + at, UX), UX)]
        return remote(
            src, b0_r.at[i, :, pl.ds(at, UX)], c_ss.at[B0 + k, i], c_rs.at[B0 + k, i], core
        )

    def along_x(i, k, sem, src, dst):
        return remote(
            src.at[i, k], dst.at[i, k], c_ss.at[sem + k, i], c_rs.at[sem + k, i], (xp, xm)[k]
        )

    def x1(i, k):
        return along_x(i, k, X1, x1_s, x1_r)

    def xe(i, k):
        return along_x(i, k, XE, xe_s, xe_r)

    def x2(i, k):
        return along_x(i, k, X2, x2_s, x2_r)

    def yb(i):
        return remote(yb_s.at[i], yb_r.at[i], c_ss.at[YB, i], c_rs.at[YB, i], yhp)

    def lanes(i, n=1):
        return pl.ds(pl.multiple_of(i * ROWS, ROWS), n * ROWS)

    def same(i, first, n, sem, dev):
        block = hid.at[:, pl.ds(pl.multiple_of(first, UY), n), lanes(i)]
        return remote(block, block, c_ss.at[sem, i], c_rs.at[sem, i], dev)

    mine = c * UC + x * UX
    left = c * UC + ((x + 3) % 4) * UX
    right = c * UC + ((x + 1) % 4) * UX

    def h1(i):
        return same(i, mine + yh * UY, UY, H1, yhp)

    def he(i, k):
        return same(i, mine + yh * UY, UY, HE + k, (xp, xm)[k])

    def h2(i, k):
        return same(i, mine + (1 - yh) * UY, UY, H2 + k, (xp, xm)[k])

    def h3(i, k):
        return same(i, (left, right + UY)[k], UY, H3 + k, (xp, xm)[k])

    def h4(i):
        return same(i, c * UC, UC, H4, core)

    def summed(i, xd, h):
        at = xd * UX + h * UY
        a = part[i % 2, :, pl.ds(pl.multiple_of(c * UC + at, UY), UY), :]
        return a + b0_r[i, :, pl.ds(pl.multiple_of(at, UY), UY), :]

    def partial(i):
        s = i % 2
        for m in (0, 1):
            part[s, m] = dot_nt(w_in_t[m * U : (m + 1) * U, :], tg[0, i])
        part[s, 2] = dot_nt(w_down[...], tg[1, i])
        for k in range(4):
            b0(i, k).start()

    def send_x1(i):
        b0(i, 0).wait()
        for k in (0, 1):
            x1_s[i, k] = summed(i, (x + 2) % 4, k).astype(BF)
            x1(i, k).start()
        for k in (0, 1):
            b0(i, 1 + k).wait()
            xe_s[i, k] = summed(i, (x + (1, 3)[k]) % 4, 1 - k).astype(BF)
            xe(i, k).start()

    def send_x2(i):
        for k in (0, 1):
            x1(i, k).wait_recv()
            total = summed(i, (x + (1, 3)[k]) % 4, k) + x1_r[i, k].astype(F32)
            x2_s[i, k] = total.astype(BF)
            x2(i, k).start()
        b0(i, 3).wait()
        for h in (0, 1):
            xe(i, 1 - h).wait_recv()
            own64[i % 2, h] = summed(i, x, h) + xe_r[i, 1 - h].astype(F32)

    def send_yb(i):
        x2(i, 0).wait_recv()
        x2(i, 1).wait_recv()
        yb_s[i] = (own64[i % 2, 1 - yh] + x2_r[i, 1 - yh].astype(F32)).astype(BF)
        yb(i).start()
        own32[i % 2] = own64[i % 2, yh] + x2_r[i, yh].astype(F32)

    def send_h1(i):
        yb(i).wait_recv()
        full = own32[i % 2] + yb_r[i].astype(F32)
        gate, up, back = full[0], full[1], full[2]
        sigma = 1.0 / (1.0 + jnp.exp(-gate))
        silu = gate * sigma
        units = pl.ds(pl.multiple_of(mine + yh * UY, UY), UY)
        hid[0, units, lanes(i)] = (silu * up).astype(BF)
        hid[1, units, lanes(i)] = (back * up * sigma * (1.0 + gate * (1.0 - sigma))).astype(BF)
        hid[2, units, lanes(i)] = (back * silu).astype(BF)
        h1(i).start()
        he(i, 0).start()
        he(i, 1).start()

    def send_h2(i):
        h1(i).wait_recv()
        h2(i, 0).start()
        h2(i, 1).start()

    def send_h3(i):
        for k in (0, 1):
            he(i, k).wait_recv()
            h2(i, k).wait_recv()
            h3(i, k).start()

    def send_h4(i):
        h3(i, 0).wait_recv()
        h3(i, 1).wait_recv()
        h4(i).start()

    def grads_in(g):
        pair = lanes(g - 1, 2)
        for n in range(0, DM, 256):
            tok = tg[0, pl.ds(g - 1, 2), :, n : n + 256].reshape(2 * ROWS, 256)
            for m in (0, 1):
                sum_in[m * U : (m + 1) * U, n : n + 256] += dot(hid[1 + m, :, pair], tok)

    def grads_down(g):
        pair = lanes(g - 1, 2)
        for n in range(0, DM, 256):
            sc = tg[1, pl.ds(g - 1, 2), :, n : n + 256].reshape(2 * ROWS, 256)
            sum_down[:, n : n + 256] += dot(hid[0, :, pair], sc)

    def zf(col, h):
        return remote(
            zf_s.at[col, h], zf_r.at[col, h], d_ss.at[2 * col, h], d_rs.at[2 * col, h], (zm, zp)[h]
        )

    def zf_right(h):
        return remote(zg_s.at[h], zg_r.at[h], d_ss.at[0, 2 + h], d_rs.at[0, 2 + h], (zm, zp)[h])

    def dz(col, k, h):
        sem = 2 * col + 1
        return remote(
            dz_s.at[col, k, h], dz_r.at[col, k, h],
            d_ss.at[sem, 2 * k + h], d_rs.at[sem, 2 * k + h], (zp, zm)[(h + 1 + k) % 2],
        )

    def dz_right(k, h):
        return remote(
            dw_s.at[k, h], dw_r.at[k, h],
            d_ss.at[4, 2 * k + h], d_rs.at[4, 2 * k + h], (zp, zm)[(h + 1 + k) % 2],
        )

    def dy(h):
        return remote(dy_s.at[h], dy_r.at[h], d_ss.at[2, 2 + h], d_rs.at[2, 2 + h], ylp)

    def dy_right(k, h):
        return remote(dv_s.at[k, h], dv_r.at[k, h], d_ss.at[5 + h, k], d_rs.at[5 + h, k], ylp)

    def of_left(j, h):
        return to[j, :LEFT, h * HALF : (h + 1) * HALF]

    def of_right(j, h):
        return to[j, LEFT:, h * HALF : (h + 1) * HALF]

    def send_zf(col):
        for h in (0, 1):
            zf_s[col, h] = of_left((F, YF)[col], h).astype(BF)
            zf(col, h).start()

    def send_dz(col, k):
        for h in (0, 1):
            total = of_left(((C1, C2), (Y1, Y2))[col][k], h)
            if k == 0:
                zf(col, h).wait_recv()
                total = total + zf_r[col, h].astype(F32)
            dz_s[col, k, h] = total.astype(BF)
            dz(col, k, h).start()

    def column(col, h):
        dz(col, 0, h).wait_recv()
        dz(col, 1, h).wait_recv()
        return of_left((OWN, YO)[col], h) + (
            dz_r[col, 0, h].astype(F32) + dz_r[col, 1, h].astype(F32)
        )

    def send_dy():
        for h in (0, 1):
            dy_s[h] = column(1, h).astype(BF)
            dy(h).start()

    def send_dy_right(k):
        for h in (0, 1):
            dv_s[k, h] = of_right((YO, Y1, YF, Y2)[k], h).astype(BF)
            dy_right(k, h).start()

    def both_right(j, k, h):
        dy_right(k, h).wait_recv()
        return of_right(j, h) + dv_r[k, h].astype(F32)

    def send_zf_right():
        for h in (0, 1):
            zg_s[h] = both_right(F, 2, h).astype(BF)
            zf_right(h).start()

    def send_dz_right(k):
        for h in (0, 1):
            total = both_right((C1, C2)[k], 1 + 2 * k, h)
            if k == 0:
                zf_right(h).wait_recv()
                total = total + zg_r[h].astype(F32)
            dw_s[k, h] = total.astype(BF)
            dz_right(k, h).start()

    def term(j):
        h4(j).wait_recv()
        h = hid[1:, :, lanes(j)].reshape(2 * U, ROWS)
        for m in range(0, DM, 512):
            to[j, m : m + 512, :] = dot(w_in[m : m + 512, :], h)

    def arrivals(t):
        @pl.when(t == C1)
        def _():
            arrived(C1, 0)
            gather(C1, F, 0, zp).start()
            arrived(C1, 1)
            gather(C1, F, 1, zm).start()

        @pl.when(t == YO)
        def _():
            for h in (0, 1):
                arrived(YO, h)
                gather_y1(0, h).start()
            gather_y1(1, 0).start()
            gather_y1(1, 1).start()
            for h in (0, 1):
                arrived(F, h)
                gather_yf(1, h).start()

        @pl.when(t == F)
        def _():
            for h in (0, 1):
                gather_y1(0, h).wait_recv()
                gather_yf(0, h).start()

        @pl.when(t == Y1)
        def _():
            gather_y1(1, 0).wait_recv()
            gather_y1(1, 1).wait_recv()
            gather(YO, Y2, 1, zp).start()
            gather(YO, Y2, 0, zm).start()

        @pl.when(t == YF)
        def _():
            for kind in (0, 1):
                for h in (0, 1):
                    gather_yf(kind, h).wait_recv()

        @pl.when(t == Y2)
        def _():
            arrived(Y2, 0)
            arrived(Y2, 1)

    def left_all(i):
        for k in (0, 1):
            x1(i, k).wait_send()
            xe(i, k).wait_send()
            he(i, k).wait_send()
            x2(i, k).wait_send()
            h2(i, k).wait_send()
            h3(i, k).wait_send()
        yb(i).wait_send()
        h1(i).wait_send()
        h4(i).wait_send()

    def tick(t, carry):
        def stage(step, lag):
            pl.when((t >= lag) & (t < C2 + lag))(lambda: step(t - lag))

        def at(when, step, *args):
            pl.when(t == when)(lambda: step(*args))

        def late(step, lag):
            at(C2 + lag, step, C2)

        stage(send_yb, 2)
        stage(send_h3, 4)
        late(send_x2, 2)
        late(send_h2, 4)
        at(YF + 6, send_dz, 1, 0)
        late(term, 6)
        at(C2 + 6, send_dz, 0, 1)
        at(C2 + 6, send_dz_right, 1)
        arrivals(t)
        stage(partial, 0)

        stage(send_x2, 1)
        stage(send_h2, 3)
        late(send_x1, 1)
        late(send_h1, 3)
        late(send_h4, 5)
        stage(term, 5)
        for k, chunk in enumerate((YO, Y1, YF, Y2)):
            at(chunk + 5, send_dy_right, k)
        at(F + 5, send_zf, 0)
        at(F + 6, send_dz, 0, 0)
        at(YF + 5, send_zf, 1)
        at(Y2 + 5, send_dz, 1, 1)
        at(Y2 + 5, send_zf_right)
        at(Y2 + 6, send_dy)
        at(Y2 + 6, send_dz_right, 0)

        stage(send_h1, 2)
        stage(send_h4, 4)
        stage(send_x1, 0)
        late(send_yb, 2)
        late(send_h3, 4)

        @pl.when(t == Y1)
        def _():
            gather(OWN, C2, 1, zp).start()
            gather(OWN, C2, 0, zm).start()

        pl.when((t >= 7) & (t < C2 + 7))(lambda: left_all(t - 7))
        pl.when((t == 6) | (t == 8) | (t == 10))(lambda: grads_in(t - 5))
        pl.when((t == 7) | (t == 9) | (t == 11))(lambda: grads_down(t - 6))
        at(C2 + 6, grads_in, C2)

        @pl.when(t == C2)
        def _():
            arrived(C2, 0)
            arrived(C2, 1)
            partial(C2)

        return carry

    lax.fori_loop(0, CHUNKS + 6, tick, 0)

    stores = [
        pltpu.make_async_copy(sum_in, out_in, o_s.at[0]),
        pltpu.make_async_copy(sum_down, out_down, o_s.at[1]),
    ]
    stores[0].start()
    grads_down(CHUNKS - 1)
    stores[1].start()

    left_all(C2)
    for to_whom in first:
        for kind in (0, 1):
            gather_own(kind, *to_whom).wait_send()
    for dst in (F, Y2, C2):
        for h in (0, 1):
            gather(OWN, dst, h, zp).wait_send()
    for h in (0, 1):
        gather_y1(0, h).wait_send()
        gather_y1(1, h).wait_send()
        gather_yf(0, h).wait_send()
        gather_yf(1, h).wait_send()
    for h in (0, 1):
        for col in (0, 1):
            zf(col, h).wait_send()
            dz(col, 0, h).wait_send()
            dz(col, 1, h).wait_send()
        for k in range(4):
            dy_right(k, h).wait_send()
        zf_right(h).wait_send()
        dy(h).wait_send()
        dz_right(0, h).wait_send()
        dz_right(1, h).wait_send()

    for h in (0, 1):
        rows = pl.ds(h * HALF, HALF)
        total = both_right(OWN, 0, h)
        dz_right(0, h).wait_recv()
        dz_right(1, h).wait_recv()
        total = total + (dw_r[0, h].astype(F32) + dw_r[1, h].astype(F32))
        last[rows, LEFT:] = total.T.astype(BF)
        total = column(0, h)
        dy(h).wait_recv()
        last[rows, :LEFT] = (total + dy_r[h].astype(F32)).T.astype(BF)
        stores.append(pltpu.make_async_copy(last.at[rows], out_tok.at[rows], o_s.at[2 + h]))
        stores[-1].start()
    for copy in stores:
        copy.wait()


def place(tok, sums, down, out_tok, out_gate, out_up, out_down, v_tok, v_sums, v_down, v_out, sems):
    reads, writes = [], []

    def piece(src, via, dst, by_way=None):
        k = len(reads)
        reads.append(pltpu.make_async_copy(src, via, sems.at[0, k]))
        writes.append(pltpu.make_async_copy(via if by_way is None else by_way, dst, sems.at[1, k]))
        reads[-1].start()

    turns = []
    for o, out in enumerate((out_gate, out_up)):
        for u in range(0, U, 256):
            for d in range(0, DM, 512):
                src = (pl.ds(o * U + u, 256), pl.ds(d, 512))
                dst = (pl.ds(d, 512), pl.ds(u, 256))
                turns.append((src, (o, *dst)))
                piece(sums.at[src], v_sums.at[src], out.at[dst], v_out.at[(o, *dst)])
    for p in range(0, U, 128):
        rows = pl.ds(p, 128)
        piece(down.at[rows], v_down.at[rows], out_down.at[rows])
    piece(tok, v_tok, out_tok)
    for k, (read, write) in enumerate(zip(reads, writes)):
        read.wait()
        if k < len(turns):
            src, dst = turns[k]
            v_out[dst] = v_sums[src].T
        write.start()
    for write in writes:
        write.wait()


def local(tokens, grad_out, keep, count, w_gate, w_up, w_down):
    vmem = pl.BlockSpec(memory_space=pltpu.VMEM)
    anywhere = pl.BlockSpec(memory_space=pl.ANY)
    dma = pltpu.SemaphoreType.DMA
    outs = pl.pallas_call(
        kernel,
        out_shape=(
            jax.ShapeDtypeStruct((ROWS, DM), BF),
            jax.ShapeDtypeStruct((2 * U, DM), F32),
            jax.ShapeDtypeStruct((U, DM), F32),
        ),
        in_specs=[anywhere, anywhere, vmem, pl.BlockSpec(memory_space=pltpu.SMEM)] + [anywhere] * 3,
        out_specs=[anywhere] * 3,
        scratch_shapes=[
            pltpu.VMEM((ROWS, DM), BF),
            pltpu.VMEM((ROWS, DM), BF),
            pltpu.VMEM((DM, 2 * U), BF),
            pltpu.VMEM((2 * U, DM), BF),
            pltpu.VMEM((U, DM), BF),
            pltpu.VMEM((2 * U, DM), F32),
            pltpu.VMEM((U, DM), F32),
            pltpu.VMEM((2, CHUNKS, ROWS, DM), BF),
            pltpu.VMEM((2, 3, U, ROWS), F32),
            pltpu.VMEM((CHUNKS, 3, UC, ROWS), F32),
            pltpu.VMEM((CHUNKS, 2, 3, UY, ROWS), BF),
            pltpu.VMEM((CHUNKS, 2, 3, UY, ROWS), BF),
            pltpu.VMEM((CHUNKS, 2, 3, UY, ROWS), BF),
            pltpu.VMEM((CHUNKS, 2, 3, UY, ROWS), BF),
            pltpu.VMEM((CHUNKS, 2, 3, UY, ROWS), BF),
            pltpu.VMEM((CHUNKS, 2, 3, UY, ROWS), BF),
            pltpu.VMEM((CHUNKS, 3, UY, ROWS), BF),
            pltpu.VMEM((CHUNKS, 3, UY, ROWS), BF),
            pltpu.VMEM((2, 2, 3, UY, ROWS), F32),
            pltpu.VMEM((2, 3, UY, ROWS), F32),
            pltpu.VMEM((3, U, CHUNKS * ROWS), BF),
            pltpu.VMEM((CHUNKS, DM, ROWS), F32),
            pltpu.VMEM((2, LEFT, HALF), BF),
            pltpu.VMEM((2, LEFT, HALF), BF),
            pltpu.VMEM((2, 2, LEFT, HALF), BF),
            pltpu.VMEM((2, 2, LEFT, HALF), BF),
            pltpu.VMEM((2, 2, 2, LEFT, HALF), BF),
            pltpu.VMEM((2, 2, 2, LEFT, HALF), BF),
            pltpu.VMEM((4, 2, RIGHT, HALF), BF),
            pltpu.VMEM((4, 2, RIGHT, HALF), BF),
            pltpu.VMEM((2, RIGHT, HALF), BF),
            pltpu.VMEM((2, RIGHT, HALF), BF),
            pltpu.VMEM((2, 2, RIGHT, HALF), BF),
            pltpu.VMEM((2, 2, RIGHT, HALF), BF),
            dma((MESSAGES, CHUNKS)),
            dma((MESSAGES, CHUNKS)),
            dma((CHUNKS + 4, 2)),
            dma((CHUNKS + 4, 2)),
            dma((7, 4)),
            dma((7, 4)),
            dma((4,)),
            dma((5,)),
        ],
        compiler_params=pltpu.CompilerParams(
            collective_id=0, has_side_effects=True, vmem_limit_bytes=62 * 1024 * 1024
        ),
        cost_estimate=pl.CostEstimate(
            flops=16 * 2048 * DM * U, bytes_accessed=16 << 20, transcendentals=0
        ),
    )(tokens, grad_out, keep, count, w_gate, w_up, w_down)
    return pl.pallas_call(
        place,
        out_shape=(
            jax.ShapeDtypeStruct((ROWS, DM), BF),
            jax.ShapeDtypeStruct((DM, U), F32),
            jax.ShapeDtypeStruct((DM, U), F32),
            jax.ShapeDtypeStruct((U, DM), F32),
        ),
        in_specs=[anywhere] * 3,
        out_specs=[anywhere] * 4,
        scratch_shapes=[
            pltpu.VMEM((ROWS, DM), BF),
            pltpu.VMEM((2 * U, DM), F32),
            pltpu.VMEM((U, DM), F32),
            pltpu.VMEM((2, DM, U), F32),
            dma((2, 13)),
        ],
        compiler_params=pltpu.CompilerParams(vmem_limit_bytes=62 * 1024 * 1024),
    )(*outs)


def solution(mesh):
    placed = (
        P("wide", "mp"),
        P("wide", "mp"),
        P("wide"),
        P(),
        P("mp", "wide"),
        P("mp", "wide"),
        P("wide", "mp"),
    )
    return jax.shard_map(
        local,
        mesh=mesh,
        in_specs=placed,
        out_specs=(P("wide", "mp"), P("mp", "wide"), P("mp", "wide"), P("wide", "mp")),
        check_vma=False,
    )
```

```python
import functools

import jax
import jax.numpy as jnp
from jax import lax
from jax.experimental import pallas as pl
from jax.experimental.pallas import tpu as pltpu
from jax.sharding import PartitionSpec as P

BF = jnp.bfloat16
F32 = jnp.float32
ROWS = 256
HALF = 128
DM = 1024
U = 512
UC, UX, UY = 256, 64, 32
LEFT, RIGHT = 512, 512
CHUNKS = 8
OWN, C1, YO, F, Y1, YF, Y2, C2 = range(CHUNKS)
B0, X1, XE, X2, YB, H1, HE, H2, H3, H4 = 0, 4, 6, 8, 10, 11, 12, 14, 16, 18
MESSAGES = 19


def dot(a, b):
    return lax.dot_general(a, b, (((1,), (0,)), ((), ())), preferred_element_type=F32)


def dot_nt(a, b):
    return lax.dot_general(a, b, (((1,), (1,)), ((), ())), preferred_element_type=F32)


def kernel(
    tokens, in_grad, keep, count, in_gate, in_up, in_down,
    out_tok, out_in, out_down,
    grad_out, last, w_in, w_in_t, w_down, sum_in, sum_down, tg, part, b0_r, x1_s, x1_r, xe_s, xe_r, x2_s, x2_r,
    yb_s, yb_r, own64, own32, hid,
    to, dy_s, dy_r, zf_s, zf_r, dz_s, dz_r, dv_s, dv_r, zg_s, zg_r, dw_s, dw_r,
    c_ss, c_rs, a_ss, a_rs, d_ss, d_rs, o_s, i_s,
):
    mp, wide = lax.axis_index("mp"), lax.axis_index("wide")
    x, yh, c = mp // 4, (mp // 2) % 2, mp % 2
    core = (mp + 1 - 2 * c, wide)
    xp = ((mp + 4) % 16, wide)
    xm = ((mp + 12) % 16, wide)
    yhp = (mp + 2 - 4 * yh, wide)
    ylp = (mp, wide + 1 - 2 * (wide % 2))
    zp = (mp, (wide + 2) % 8)
    zm = (mp, (wide + 6) % 8)

    def remote(src, dst, ssem, rsem, dev):
        return pltpu.make_async_remote_copy(
            src_ref=src, dst_ref=dst, send_sem=ssem, recv_sem=rsem,
            device_id=dev, device_id_type=pl.DeviceIdType.MESH,
        )

    barrier = pltpu.get_barrier_semaphore()
    for dev in (core, xp, xm, yhp, ylp, zp, zm):
        pl.semaphore_signal(barrier, inc=1, device_id=dev, device_id_type=pl.DeviceIdType.MESH)

    loads = [
        pltpu.make_async_copy(a, b, i_s.at[k])
        for k, (a, b) in enumerate(
            (
                (in_grad, grad_out),
                (tokens, tg.at[0, OWN]),
                (in_gate, w_in.at[:, pl.ds(0, U)]),
                (in_up, w_in.at[:, pl.ds(U, U)]),
                (in_down, w_down),
            )
        )
    ]
    for load in loads:
        load.start()
    pl.semaphore_wait(barrier, 7)

    def gather(src, dst, h, dev):
        rows = pl.ds(h * HALF, HALF)
        return remote(
            tg.at[:, src, rows], tg.at[:, dst, rows], a_ss.at[dst, h], a_rs.at[dst, h], dev
        )

    def gather_own(kind, dst, h, dev):
        rows = pl.ds(h * HALF, HALF)
        sem = (dst, CHUNKS + 1 + (dst == YO))[kind]
        return remote(
            (tokens.at[rows], tg.at[1, OWN, rows])[kind], tg.at[kind, dst, rows],
            a_ss.at[sem, h], a_rs.at[sem, h], dev,
        )

    def gather_yf(kind, h):
        rows = pl.ds(h * HALF, HALF)
        return remote(
            tg.at[kind, (Y1, F)[kind], rows], tg.at[kind, YF, rows],
            a_ss.at[(YF, CHUNKS)[kind], h], a_rs.at[(YF, CHUNKS)[kind], h],
            ((zp, zm)[h], ylp)[kind],
        )

    def gather_y1(kind, h):
        rows = pl.ds(h * HALF, HALF)
        sem = (Y1, CHUNKS + 3)[kind]
        return remote(
            tg.at[kind, YO, rows], tg.at[kind, Y1, rows], a_ss.at[sem, h], a_rs.at[sem, h],
            (zp, zm)[h],
        )

    def gather_f(kind, h):
        rows = pl.ds(h * HALF, HALF)
        sem = (F, CHUNKS + 4)[kind]
        return remote(
            tg.at[kind, C1, rows], tg.at[kind, F, rows], a_ss.at[sem, h], a_rs.at[sem, h],
            (zp, zm)[h],
        )

    def arrived(dst, h):
        gather(OWN, dst, h, zp).wait_recv()

    first = [(C1, 0, zp), (C1, 1, zm), (YO, 0, ylp), (YO, 1, ylp)]
    for to_whom in first:
        gather_own(0, *to_whom).start()
    loads[0].wait()
    for r in range(0, ROWS, 128):
        factor = keep[pl.ds(r, 128)].astype(F32) / count[0].astype(F32)
        factor = jnp.broadcast_to(factor[None, :], (128, 128)).T
        for n in range(0, DM, 128):
            block = grad_out[r : r + 128, n : n + 128].astype(F32) * factor
            tg[1, OWN, r : r + 128, n : n + 128] = block.astype(BF)
    for to_whom in first:
        gather_own(1, *to_whom).start()

    for load in loads[1:]:
        load.wait()
    for n in range(0, 2 * U, 256):
        w_in_t[n : n + 256, :] = w_in[:, n : n + 256].T
    sum_in[...] = jnp.zeros_like(sum_in)
    sum_down[...] = jnp.zeros_like(sum_down)

    def b0(i, k):
        at = pl.multiple_of(((x + (2, 1, 3, 0)[k]) % 4) * UX, UX)
        src = part.at[i % 2, :, pl.ds(pl.multiple_of((1 - c) * UC + at, UX), UX)]
        return remote(
            src, b0_r.at[i, :, pl.ds(at, UX)], c_ss.at[B0 + k, i], c_rs.at[B0 + k, i], core
        )

    def along_x(i, k, sem, src, dst):
        return remote(
            src.at[i, k], dst.at[i, k], c_ss.at[sem + k, i], c_rs.at[sem + k, i], (xp, xm)[k]
        )

    def x1(i, k):
        return along_x(i, k, X1, x1_s, x1_r)

    def xe(i, k):
        return along_x(i, k, XE, xe_s, xe_r)

    def x2(i, k):
        return along_x(i, k, X2, x2_s, x2_r)

    def yb(i):
        return remote(yb_s.at[i], yb_r.at[i], c_ss.at[YB, i], c_rs.at[YB, i], yhp)

    def lanes(i, n=1):
        return pl.ds(pl.multiple_of(i * ROWS, ROWS), n * ROWS)

    def same(i, first, n, sem, dev):
        block = hid.at[:, pl.ds(pl.multiple_of(first, UY), n), lanes(i)]
        return remote(block, block, c_ss.at[sem, i], c_rs.at[sem, i], dev)

    mine = c * UC + x * UX
    left = c * UC + ((x + 3) % 4) * UX
    right = c * UC + ((x + 1) % 4) * UX

    def h1(i):
        return same(i, mine + yh * UY, UY, H1, yhp)

    def he(i, k):
        return same(i, mine + yh * UY, UY, HE + k, (xp, xm)[k])

    def h2(i, k):
        return same(i, mine + (1 - yh) * UY, UY, H2 + k, (xp, xm)[k])

    def h3(i, k):
        return same(i, (left, right + UY)[k], UY, H3 + k, (xp, xm)[k])

    def h4(i):
        return same(i, c * UC, UC, H4, core)

    def summed(i, xd, h):
        at = xd * UX + h * UY
        a = part[i % 2, :, pl.ds(pl.multiple_of(c * UC + at, UY), UY), :]
        return a + b0_r[i, :, pl.ds(pl.multiple_of(at, UY), UY), :]

    def partial(i):
        s = i % 2
        for m in (0, 1):
            part[s, m] = dot_nt(w_in_t[m * U : (m + 1) * U, :], tg[0, i])
        part[s, 2] = dot_nt(w_down[...], tg[1, i])
        for k in range(4):
            b0(i, k).start()

    def send_x1(i):
        b0(i, 0).wait()
        for k in (0, 1):
            x1_s[i, k] = summed(i, (x + 2) % 4, k).astype(BF)
            x1(i, k).start()
        for k in (0, 1):
            b0(i, 1 + k).wait()
            xe_s[i, k] = summed(i, (x + (1, 3)[k]) % 4, 1 - k).astype(BF)
            xe(i, k).start()

    def send_x2(i):
        for k in (0, 1):
            x1(i, k).wait_recv()
            total = summed(i, (x + (1, 3)[k]) % 4, k) + x1_r[i, k].astype(F32)
            x2_s[i, k] = total.astype(BF)
            x2(i, k).start()
        b0(i, 3).wait()
        for h in (0, 1):
            xe(i, 1 - h).wait_recv()
            own64[i % 2, h] = summed(i, x, h) + xe_r[i, 1 - h].astype(F32)

    def send_yb(i):
        x2(i, 0).wait_recv()
        x2(i, 1).wait_recv()
        yb_s[i] = (own64[i % 2, 1 - yh] + x2_r[i, 1 - yh].astype(F32)).astype(BF)
        yb(i).start()
        own32[i % 2] = own64[i % 2, yh] + x2_r[i, yh].astype(F32)

    def send_h1(i):
        yb(i).wait_recv()
        full = own32[i % 2] + yb_r[i].astype(F32)
        gate, up, back = full[0], full[1], full[2]
        sigma = 1.0 / (1.0 + jnp.exp(-gate))
        silu = gate * sigma
        units = pl.ds(pl.multiple_of(mine + yh * UY, UY), UY)
        hid[0, units, lanes(i)] = (silu * up).astype(BF)
        hid[1, units, lanes(i)] = (back * up * sigma * (1.0 + gate * (1.0 - sigma))).astype(BF)
        hid[2, units, lanes(i)] = (back * silu).astype(BF)
        h1(i).start()
        he(i, 0).start()
        he(i, 1).start()

    def send_h2(i):
        h1(i).wait_recv()
        h2(i, 0).start()
        h2(i, 1).start()

    def send_h3(i):
        for k in (0, 1):
            he(i, k).wait_recv()
            h2(i, k).wait_recv()
            h3(i, k).start()

    def send_h4(i):
        h3(i, 0).wait_recv()
        h3(i, 1).wait_recv()
        h4(i).start()

    def grads_in(g):
        pair = lanes(g - 1, 2)
        for n in range(0, DM, 256):
            tok = tg[0, pl.ds(g - 1, 2), :, n : n + 256].reshape(2 * ROWS, 256)
            for m in (0, 1):
                sum_in[m * U : (m + 1) * U, n : n + 256] += dot(hid[1 + m, :, pair], tok)

    def grads_down(g):
        pair = lanes(g - 1, 2)
        for n in range(0, DM, 256):
            sc = tg[1, pl.ds(g - 1, 2), :, n : n + 256].reshape(2 * ROWS, 256)
            sum_down[:, n : n + 256] += dot(hid[0, :, pair], sc)

    def zf(col, h):
        return remote(
            zf_s.at[col, h], zf_r.at[col, h], d_ss.at[2 * col, h], d_rs.at[2 * col, h], (zm, zp)[h]
        )

    def zf_right(h):
        return remote(zg_s.at[h], zg_r.at[h], d_ss.at[0, 2 + h], d_rs.at[0, 2 + h], (zm, zp)[h])

    def dz(col, k, h):
        sem = 2 * col + 1
        return remote(
            dz_s.at[col, k, h], dz_r.at[col, k, h],
            d_ss.at[sem, 2 * k + h], d_rs.at[sem, 2 * k + h], (zp, zm)[(h + 1 + k) % 2],
        )

    def dz_right(k, h):
        return remote(
            dw_s.at[k, h], dw_r.at[k, h],
            d_ss.at[4, 2 * k + h], d_rs.at[4, 2 * k + h], (zp, zm)[(h + 1 + k) % 2],
        )

    def dy(h):
        return remote(dy_s.at[h], dy_r.at[h], d_ss.at[2, 2 + h], d_rs.at[2, 2 + h], ylp)

    def dy_right(k, h):
        return remote(dv_s.at[k, h], dv_r.at[k, h], d_ss.at[5 + h, k], d_rs.at[5 + h, k], ylp)

    def of_left(j, h):
        return to[j, :LEFT, h * HALF : (h + 1) * HALF]

    def of_right(j, h):
        return to[j, LEFT:, h * HALF : (h + 1) * HALF]

    def send_zf(col):
        for h in (0, 1):
            zf_s[col, h] = of_left((F, YF)[col], h).astype(BF)
            zf(col, h).start()

    def send_dz(col, k):
        for h in (0, 1):
            total = of_left(((C1, C2), (Y1, Y2))[col][k], h)
            if k == 0:
                zf(col, h).wait_recv()
                total = total + zf_r[col, h].astype(F32)
            dz_s[col, k, h] = total.astype(BF)
            dz(col, k, h).start()

    def column(col, h):
        dz(col, 0, h).wait_recv()
        dz(col, 1, h).wait_recv()
        return of_left((OWN, YO)[col], h) + (
            dz_r[col, 0, h].astype(F32) + dz_r[col, 1, h].astype(F32)
        )

    def send_dy():
        for h in (0, 1):
            dy_s[h] = column(1, h).astype(BF)
            dy(h).start()

    def send_dy_right(k):
        for h in (0, 1):
            dv_s[k, h] = of_right((YO, Y1, YF, Y2)[k], h).astype(BF)
            dy_right(k, h).start()

    def both_right(j, k, h):
        dy_right(k, h).wait_recv()
        return of_right(j, h) + dv_r[k, h].astype(F32)

    def send_zf_right():
        for h in (0, 1):
            zg_s[h] = both_right(F, 2, h).astype(BF)
            zf_right(h).start()

    def send_dz_right(k):
        for h in (0, 1):
            total = both_right((C1, C2)[k], 1 + 2 * k, h)
            if k == 0:
                zf_right(h).wait_recv()
                total = total + zg_r[h].astype(F32)
            dw_s[k, h] = total.astype(BF)
            dz_right(k, h).start()

    def term(j):
        h4(j).wait_recv()
        h = hid[1:, :, lanes(j)].reshape(2 * U, ROWS)
        for m in range(0, DM, 512):
            to[j, m : m + 512, :] = dot(w_in[m : m + 512, :], h)

    def arrivals(t):
        @pl.when(t == C1)
        def _():
            for h in (0, 1):
                gather_own(1, C1, h, zp).wait_recv()
                gather_f(1, h).start()

        @pl.when(t == YO)
        def _():
            for h in (0, 1):
                gather_own(1, YO, h, ylp).wait_recv()
                gather_y1(1, h).start()
            for h in (0, 1):
                gather_f(0, h).wait_recv()
                gather_f(1, h).wait_recv()
                gather_yf(1, h).start()

        @pl.when(t == F)
        def _():
            for h in (0, 1):
                gather_y1(0, h).wait_recv()
                gather_yf(0, h).start()

        @pl.when(t == Y1)
        def _():
            gather_y1(1, 0).wait_recv()
            gather_y1(1, 1).wait_recv()
            gather(YO, Y2, 1, zp).start()
            gather(YO, Y2, 0, zm).start()

        @pl.when(t == YF)
        def _():
            for kind in (0, 1):
                for h in (0, 1):
                    gather_yf(kind, h).wait_recv()

        for chunk in (Y2, C2):

            @pl.when(t == chunk)
            def _():
                arrived(chunk, 0)
                arrived(chunk, 1)

    def left_all(i):
        for k in (0, 1):
            x1(i, k).wait_send()
            xe(i, k).wait_send()
            he(i, k).wait_send()
            x2(i, k).wait_send()
            h2(i, k).wait_send()
            h3(i, k).wait_send()
        yb(i).wait_send()
        h1(i).wait_send()
        h4(i).wait_send()

    def tick(t, carry):
        def stage(step, lag):
            pl.when((t >= lag) & (t < CHUNKS + lag))(lambda: step(t - lag))

        def at(when, step, *args):
            pl.when(t == when)(lambda: step(*args))

        stage(send_yb, 2)
        stage(send_h3, 4)
        at(YF + 6, send_dz, 1, 0)
        arrivals(t)
        stage(partial, 0)

        stage(send_x2, 1)
        stage(send_h2, 3)
        stage(term, 5)
        for k, chunk in enumerate((YO, Y1, YF, Y2)):
            at(chunk + 5, send_dy_right, k)
        at(F + 5, send_zf, 0)
        at(F + 6, send_dz, 0, 0)
        at(YF + 5, send_zf, 1)
        at(Y2 + 5, send_dz, 1, 1)
        at(Y2 + 5, send_zf_right)
        at(C2 + 5, send_dz, 0, 1)
        at(C2 + 5, send_dy)
        at(C2 + 5, send_dz_right, 0)
        at(C2 + 5, send_dz_right, 1)

        stage(send_h1, 2)
        stage(send_h4, 4)
        stage(send_x1, 0)

        @pl.when(t == OWN)
        def _():
            for h in (0, 1):
                gather_own(0, C1, h, zp).wait_recv()
                gather_f(0, h).start()

        @pl.when(t == C1)
        def _():
            for h in (0, 1):
                gather_own(0, YO, h, ylp).wait_recv()
                gather_y1(0, h).start()

        @pl.when(t == Y1)
        def _():
            gather(OWN, C2, 1, zp).start()
            gather(OWN, C2, 0, zm).start()

        pl.when((t >= 7) & (t < CHUNKS + 5))(lambda: left_all(t - 7))
        pl.when((t >= 6) & (t % 2 == 0))(lambda: grads_in(t - 5))
        pl.when((t >= 7) & (t % 2 == 1))(lambda: grads_down(t - 6))
        return carry

    lax.fori_loop(0, CHUNKS + 5, tick, 0)

    stores = [
        pltpu.make_async_copy(sum_in, out_in, o_s.at[0]),
        pltpu.make_async_copy(sum_down, out_down, o_s.at[1]),
    ]
    stores[0].start()
    grads_down(CHUNKS - 1)
    stores[1].start()

    left_all(CHUNKS - 2)
    left_all(CHUNKS - 1)
    for to_whom in first:
        for kind in (0, 1):
            gather_own(kind, *to_whom).wait_send()
    for dst in (Y2, C2):
        for h in (0, 1):
            gather(OWN, dst, h, zp).wait_send()
    for h in (0, 1):
        gather_f(0, h).wait_send()
        gather_f(1, h).wait_send()
        gather_y1(0, h).wait_send()
        gather_y1(1, h).wait_send()
        gather_yf(0, h).wait_send()
        gather_yf(1, h).wait_send()
    for h in (0, 1):
        for col in (0, 1):
            zf(col, h).wait_send()
            dz(col, 0, h).wait_send()
            dz(col, 1, h).wait_send()
        for k in range(4):
            dy_right(k, h).wait_send()
        zf_right(h).wait_send()
        dy(h).wait_send()
        dz_right(0, h).wait_send()
        dz_right(1, h).wait_send()

    for h in (0, 1):
        rows = pl.ds(h * HALF, HALF)
        total = both_right(OWN, 0, h)
        dz_right(0, h).wait_recv()
        dz_right(1, h).wait_recv()
        total = total + (dw_r[0, h].astype(F32) + dw_r[1, h].astype(F32))
        last[rows, LEFT:] = total.T.astype(BF)
        total = column(0, h)
        dy(h).wait_recv()
        last[rows, :LEFT] = (total + dy_r[h].astype(F32)).T.astype(BF)
        stores.append(pltpu.make_async_copy(last.at[rows], out_tok.at[rows], o_s.at[2 + h]))
        stores[-1].start()
    for copy in stores:
        copy.wait()


def place(tok, sums, down, out_tok, out_gate, out_up, out_down, v_tok, v_sums, v_down, v_out, sems):
    reads, writes = [], []

    def piece(src, via, dst, by_way=None):
        k = len(reads)
        reads.append(pltpu.make_async_copy(src, via, sems.at[0, k]))
        writes.append(pltpu.make_async_copy(via if by_way is None else by_way, dst, sems.at[1, k]))
        reads[-1].start()

    turns = []
    for o, out in enumerate((out_gate, out_up)):
        for u in range(0, U, 256):
            for d in range(0, DM, 512):
                src = (pl.ds(o * U + u, 256), pl.ds(d, 512))
                dst = (pl.ds(d, 512), pl.ds(u, 256))
                turns.append((src, (o, *dst)))
                piece(sums.at[src], v_sums.at[src], out.at[dst], v_out.at[(o, *dst)])
    for p in range(0, U, 128):
        rows = pl.ds(p, 128)
        piece(down.at[rows], v_down.at[rows], out_down.at[rows])
    piece(tok, v_tok, out_tok)
    for k, (read, write) in enumerate(zip(reads, writes)):
        read.wait()
        if k < len(turns):
            src, dst = turns[k]
            v_out[dst] = v_sums[src].T
        write.start()
    for write in writes:
        write.wait()


def local(tokens, grad_out, keep, count, w_gate, w_up, w_down):
    vmem = pl.BlockSpec(memory_space=pltpu.VMEM)
    anywhere = pl.BlockSpec(memory_space=pl.ANY)
    dma = pltpu.SemaphoreType.DMA
    outs = pl.pallas_call(
        kernel,
        out_shape=(
            jax.ShapeDtypeStruct((ROWS, DM), BF),
            jax.ShapeDtypeStruct((2 * U, DM), F32),
            jax.ShapeDtypeStruct((U, DM), F32),
        ),
        in_specs=[anywhere, anywhere, vmem, pl.BlockSpec(memory_space=pltpu.SMEM)] + [anywhere] * 3,
        out_specs=[anywhere] * 3,
        scratch_shapes=[
            pltpu.VMEM((ROWS, DM), BF),
            pltpu.VMEM((ROWS, DM), BF),
            pltpu.VMEM((DM, 2 * U), BF),
            pltpu.VMEM((2 * U, DM), BF),
            pltpu.VMEM((U, DM), BF),
            pltpu.VMEM((2 * U, DM), F32),
            pltpu.VMEM((U, DM), F32),
            pltpu.VMEM((2, CHUNKS, ROWS, DM), BF),
            pltpu.VMEM((2, 3, U, ROWS), F32),
            pltpu.VMEM((CHUNKS, 3, UC, ROWS), F32),
            pltpu.VMEM((CHUNKS, 2, 3, UY, ROWS), BF),
            pltpu.VMEM((CHUNKS, 2, 3, UY, ROWS), BF),
            pltpu.VMEM((CHUNKS, 2, 3, UY, ROWS), BF),
            pltpu.VMEM((CHUNKS, 2, 3, UY, ROWS), BF),
            pltpu.VMEM((CHUNKS, 2, 3, UY, ROWS), BF),
            pltpu.VMEM((CHUNKS, 2, 3, UY, ROWS), BF),
            pltpu.VMEM((CHUNKS, 3, UY, ROWS), BF),
            pltpu.VMEM((CHUNKS, 3, UY, ROWS), BF),
            pltpu.VMEM((2, 2, 3, UY, ROWS), F32),
            pltpu.VMEM((2, 3, UY, ROWS), F32),
            pltpu.VMEM((3, U, CHUNKS * ROWS), BF),
            pltpu.VMEM((CHUNKS, DM, ROWS), F32),
            pltpu.VMEM((2, LEFT, HALF), BF),
            pltpu.VMEM((2, LEFT, HALF), BF),
            pltpu.VMEM((2, 2, LEFT, HALF), BF),
            pltpu.VMEM((2, 2, LEFT, HALF), BF),
            pltpu.VMEM((2, 2, 2, LEFT, HALF), BF),
            pltpu.VMEM((2, 2, 2, LEFT, HALF), BF),
            pltpu.VMEM((4, 2, RIGHT, HALF), BF),
            pltpu.VMEM((4, 2, RIGHT, HALF), BF),
            pltpu.VMEM((2, RIGHT, HALF), BF),
            pltpu.VMEM((2, RIGHT, HALF), BF),
            pltpu.VMEM((2, 2, RIGHT, HALF), BF),
            pltpu.VMEM((2, 2, RIGHT, HALF), BF),
            dma((MESSAGES, CHUNKS)),
            dma((MESSAGES, CHUNKS)),
            dma((CHUNKS + 5, 2)),
            dma((CHUNKS + 5, 2)),
            dma((7, 4)),
            dma((7, 4)),
            dma((4,)),
            dma((5,)),
        ],
        compiler_params=pltpu.CompilerParams(
            collective_id=0, has_side_effects=True, vmem_limit_bytes=62 * 1024 * 1024
        ),
        cost_estimate=pl.CostEstimate(
            flops=16 * 2048 * DM * U, bytes_accessed=16 << 20, transcendentals=0
        ),
    )(tokens, grad_out, keep, count, w_gate, w_up, w_down)
    return pl.pallas_call(
        place,
        out_shape=(
            jax.ShapeDtypeStruct((ROWS, DM), BF),
            jax.ShapeDtypeStruct((DM, U), F32),
            jax.ShapeDtypeStruct((DM, U), F32),
            jax.ShapeDtypeStruct((U, DM), F32),
        ),
        in_specs=[anywhere] * 3,
        out_specs=[anywhere] * 4,
        scratch_shapes=[
            pltpu.VMEM((ROWS, DM), BF),
            pltpu.VMEM((2 * U, DM), F32),
            pltpu.VMEM((U, DM), F32),
            pltpu.VMEM((2, DM, U), F32),
            dma((2, 13)),
        ],
        compiler_params=pltpu.CompilerParams(vmem_limit_bytes=62 * 1024 * 1024),
    )(*outs)


def solution(mesh):
    placed = (
        P("wide", "mp"),
        P("wide", "mp"),
        P("wide"),
        P(),
        P("mp", "wide"),
        P("mp", "wide"),
        P("wide", "mp"),
    )
    return jax.shard_map(
        local,
        mesh=mesh,
        in_specs=placed,
        out_specs=(P("wide", "mp"), P("mp", "wide"), P("mp", "wide"), P("wide", "mp")),
        check_vma=False,
    )
```

```python
import functools

import jax
import jax.numpy as jnp
from jax import lax
from jax.experimental import pallas as pl
from jax.experimental.pallas import tpu as pltpu
from jax.sharding import PartitionSpec as P

BF = jnp.bfloat16
F32 = jnp.float32
ROWS = 256
HALF = 128
DM = 1024
U = 512
UC, UX, UY = 256, 64, 32
LEFT, RIGHT = 512, 512
CHUNKS = 8
OWN, C1, YO, F, Y1, YF, Y2, C2 = range(CHUNKS)
B0, X1, XE, X2, YB, H1, HE, H2, H3, H4 = 0, 4, 6, 8, 10, 11, 12, 14, 16, 18
MESSAGES = 19


def dot(a, b):
    return lax.dot_general(a, b, (((1,), (0,)), ((), ())), preferred_element_type=F32)


def dot_nt(a, b):
    return lax.dot_general(a, b, (((1,), (1,)), ((), ())), preferred_element_type=F32)


def kernel(
    tokens, in_grad, keep, count, in_gate, in_up, in_down,
    out_tok, out_in, out_down,
    grad_out, last, w_in, w_in_t, w_down, sum_in, sum_down, tg, part, b0_r, x1_s, x1_r, xe_s, xe_r, x2_s, x2_r,
    yb_s, yb_r, own64, own32, hid,
    to, dy_s, dy_r, zf_s, zf_r, dz_s, dz_r, dv_s, dv_r, zg_s, zg_r, dw_s, dw_r,
    c_ss, c_rs, a_ss, a_rs, d_ss, d_rs, o_s, i_s,
):
    mp, wide = lax.axis_index("mp"), lax.axis_index("wide")
    x, yh, c = mp // 4, (mp // 2) % 2, mp % 2
    core = (mp + 1 - 2 * c, wide)
    xp = ((mp + 4) % 16, wide)
    xm = ((mp + 12) % 16, wide)
    yhp = (mp + 2 - 4 * yh, wide)
    ylp = (mp, wide + 1 - 2 * (wide % 2))
    zp = (mp, (wide + 2) % 8)
    zm = (mp, (wide + 6) % 8)

    def remote(src, dst, ssem, rsem, dev):
        return pltpu.make_async_remote_copy(
            src_ref=src, dst_ref=dst, send_sem=ssem, recv_sem=rsem,
            device_id=dev, device_id_type=pl.DeviceIdType.MESH,
        )

    barrier = pltpu.get_barrier_semaphore()
    for dev in (core, xp, xm, yhp, ylp, zp, zm):
        pl.semaphore_signal(barrier, inc=1, device_id=dev, device_id_type=pl.DeviceIdType.MESH)

    loads = [
        pltpu.make_async_copy(a, b, i_s.at[k])
        for k, (a, b) in enumerate(
            (
                (in_grad, grad_out),
                (tokens, tg.at[0, OWN]),
                (in_gate, w_in.at[:, pl.ds(0, U)]),
                (in_up, w_in.at[:, pl.ds(U, U)]),
                (in_down, w_down),
            )
        )
    ]
    for load in loads:
        load.start()
    pl.semaphore_wait(barrier, 7)

    def gather(src, dst, h, dev):
        rows = pl.ds(h * HALF, HALF)
        return remote(
            tg.at[:, src, rows], tg.at[:, dst, rows], a_ss.at[dst, h], a_rs.at[dst, h], dev
        )

    def gather_own(kind, dst, h, dev):
        rows = pl.ds(h * HALF, HALF)
        sem = (dst, CHUNKS + 1 + (dst == YO))[kind]
        return remote(
            (tokens.at[rows], tg.at[1, OWN, rows])[kind], tg.at[kind, dst, rows],
            a_ss.at[sem, h], a_rs.at[sem, h], dev,
        )

    def gather_yf(kind, h):
        rows = pl.ds(h * HALF, HALF)
        return remote(
            tg.at[kind, (Y1, F)[kind], rows], tg.at[kind, YF, rows],
            a_ss.at[(YF, CHUNKS)[kind], h], a_rs.at[(YF, CHUNKS)[kind], h],
            ((zp, zm)[h], ylp)[kind],
        )

    def gather_y1(kind, h):
        rows = pl.ds(h * HALF, HALF)
        sem = (Y1, CHUNKS + 3)[kind]
        return remote(
            tg.at[kind, YO, rows], tg.at[kind, Y1, rows], a_ss.at[sem, h], a_rs.at[sem, h],
            (zp, zm)[h],
        )

    def gather_f(kind, h):
        rows = pl.ds(h * HALF, HALF)
        sem = (F, CHUNKS + 4)[kind]
        return remote(
            tg.at[kind, C1, rows], tg.at[kind, F, rows], a_ss.at[sem, h], a_rs.at[sem, h],
            (zp, zm)[h],
        )

    def arrived(dst, h):
        gather(OWN, dst, h, zp).wait_recv()

    first = [(C1, 0, zp), (C1, 1, zm), (YO, 0, ylp), (YO, 1, ylp)]
    for to_whom in first:
        gather_own(0, *to_whom).start()
    loads[0].wait()
    for r in range(0, ROWS, 128):
        factor = keep[pl.ds(r, 128)].astype(F32) / count[0].astype(F32)
        factor = jnp.broadcast_to(factor[None, :], (128, 128)).T
        for n in range(0, DM, 128):
            block = grad_out[r : r + 128, n : n + 128].astype(F32) * factor
            tg[1, OWN, r : r + 128, n : n + 128] = block.astype(BF)
    for to_whom in first:
        gather_own(1, *to_whom).start()

    for load in loads[1:]:
        load.wait()
    for n in range(0, 2 * U, 256):
        w_in_t[n : n + 256, :] = w_in[:, n : n + 256].T
    sum_in[...] = jnp.zeros_like(sum_in)
    sum_down[...] = jnp.zeros_like(sum_down)

    def b0(i, k):
        at = pl.multiple_of(((x + (2, 1, 3, 0)[k]) % 4) * UX, UX)
        src = part.at[i % 2, :, pl.ds(pl.multiple_of((1 - c) * UC + at, UX), UX)]
        return remote(
            src, b0_r.at[i, :, pl.ds(at, UX)], c_ss.at[B0 + k, i], c_rs.at[B0 + k, i], core
        )

    def along_x(i, k, sem, src, dst):
        return remote(
            src.at[i, k], dst.at[i, k], c_ss.at[sem + k, i], c_rs.at[sem + k, i], (xp, xm)[k]
        )

    def x1(i, k):
        return along_x(i, k, X1, x1_s, x1_r)

    def xe(i, k):
        return along_x(i, k, XE, xe_s, xe_r)

    def x2(i, k):
        return along_x(i, k, X2, x2_s, x2_r)

    def yb(i):
        return remote(yb_s.at[i], yb_r.at[i], c_ss.at[YB, i], c_rs.at[YB, i], yhp)

    def lanes(i, n=1):
        return pl.ds(pl.multiple_of(i * ROWS, ROWS), n * ROWS)

    def same(i, first, n, sem, dev):
        block = hid.at[:, pl.ds(pl.multiple_of(first, UY), n), lanes(i)]
        return remote(block, block, c_ss.at[sem, i], c_rs.at[sem, i], dev)

    mine = c * UC + x * UX
    left = c * UC + ((x + 3) % 4) * UX
    right = c * UC + ((x + 1) % 4) * UX

    def h1(i):
        return same(i, mine + yh * UY, UY, H1, yhp)

    def he(i, k):
        return same(i, mine + yh * UY, UY, HE + k, (xp, xm)[k])

    def h2(i, k):
        return same(i, mine + (1 - yh) * UY, UY, H2 + k, (xp, xm)[k])

    def h3(i, k):
        return same(i, (left, right + UY)[k], UY, H3 + k, (xp, xm)[k])

    def h4(i):
        return same(i, c * UC, UC, H4, core)

    def summed(i, xd, h):
        at = xd * UX + h * UY
        a = part[i % 2, :, pl.ds(pl.multiple_of(c * UC + at, UY), UY), :]
        return a + b0_r[i, :, pl.ds(pl.multiple_of(at, UY), UY), :]

    def partial(i):
        s = i % 2
        for m in (0, 1):
            part[s, m] = dot_nt(w_in_t[m * U : (m + 1) * U, :], tg[0, i])
        part[s, 2] = dot_nt(w_down[...], tg[1, i])
        for k in range(4):
            b0(i, k).start()

    def send_x1(i):
        b0(i, 0).wait()
        for k in (0, 1):
            x1_s[i, k] = summed(i, (x + 2) % 4, k).astype(BF)
            x1(i, k).start()
        for k in (0, 1):
            b0(i, 1 + k).wait()
            xe_s[i, k] = summed(i, (x + (1, 3)[k]) % 4, 1 - k).astype(BF)
            xe(i, k).start()

    def send_x2(i):
        for k in (0, 1):
            x1(i, k).wait_recv()
            total = summed(i, (x + (1, 3)[k]) % 4, k) + x1_r[i, k].astype(F32)
            x2_s[i, k] = total.astype(BF)
            x2(i, k).start()
        b0(i, 3).wait()
        for h in (0, 1):
            xe(i, 1 - h).wait_recv()
            own64[i % 2, h] = summed(i, x, h) + xe_r[i, 1 - h].astype(F32)

    def send_yb(i):
        x2(i, 0).wait_recv()
        x2(i, 1).wait_recv()
        yb_s[i] = (own64[i % 2, 1 - yh] + x2_r[i, 1 - yh].astype(F32)).astype(BF)
        yb(i).start()
        own32[i % 2] = own64[i % 2, yh] + x2_r[i, yh].astype(F32)

    def send_h1(i):
        yb(i).wait_recv()
        full = own32[i % 2] + yb_r[i].astype(F32)
        gate, up, back = full[0], full[1], full[2]
        sigma = 1.0 / (1.0 + jnp.exp(-gate))
        silu = gate * sigma
        units = pl.ds(pl.multiple_of(mine + yh * UY, UY), UY)
        hid[0, units, lanes(i)] = (silu * up).astype(BF)
        hid[1, units, lanes(i)] = (back * up * sigma * (1.0 + gate * (1.0 - sigma))).astype(BF)
        hid[2, units, lanes(i)] = (back * silu).astype(BF)
        h1(i).start()
        he(i, 0).start()
        he(i, 1).start()

    def send_h2(i):
        h1(i).wait_recv()
        h2(i, 0).start()
        h2(i, 1).start()

    def send_h3(i):
        for k in (0, 1):
            he(i, k).wait_recv()
            h2(i, k).wait_recv()
            h3(i, k).start()

    def send_h4(i):
        h3(i, 0).wait_recv()
        h3(i, 1).wait_recv()
        h4(i).start()

    def grads_in(g):
        pair = lanes(g - 1, 2)
        for n in range(0, DM, 256):
            tok = tg[0, pl.ds(g - 1, 2), :, n : n + 256].reshape(2 * ROWS, 256)
            for m in (0, 1):
                sum_in[m * U : (m + 1) * U, n : n + 256] += dot(hid[1 + m, :, pair], tok)

    def grads_down(g):
        pair = lanes(g - 1, 2)
        for n in range(0, DM, 256):
            sc = tg[1, pl.ds(g - 1, 2), :, n : n + 256].reshape(2 * ROWS, 256)
            sum_down[:, n : n + 256] += dot(hid[0, :, pair], sc)

    def zf(col, h):
        return remote(
            zf_s.at[col, h], zf_r.at[col, h], d_ss.at[2 * col, h], d_rs.at[2 * col, h], (zm, zp)[h]
        )

    def zf_right(h):
        return remote(zg_s.at[h], zg_r.at[h], d_ss.at[0, 2 + h], d_rs.at[0, 2 + h], (zm, zp)[h])

    def dz(col, k, h):
        sem = 2 * col + 1
        return remote(
            dz_s.at[col, k, h], dz_r.at[col, k, h],
            d_ss.at[sem, 2 * k + h], d_rs.at[sem, 2 * k + h], (zp, zm)[(h + 1 + k) % 2],
        )

    def dz_right(k, h):
        return remote(
            dw_s.at[k, h], dw_r.at[k, h],
            d_ss.at[4, 2 * k + h], d_rs.at[4, 2 * k + h], (zp, zm)[(h + 1 + k) % 2],
        )

    def dy(h):
        return remote(dy_s.at[h], dy_r.at[h], d_ss.at[2, 2 + h], d_rs.at[2, 2 + h], ylp)

    def dy_right(k, h):
        return remote(dv_s.at[k, h], dv_r.at[k, h], d_ss.at[5 + h, k], d_rs.at[5 + h, k], ylp)

    def of_left(j, h):
        return to[j, :LEFT, h * HALF : (h + 1) * HALF]

    def of_right(j, h):
        return to[j, LEFT:, h * HALF : (h + 1) * HALF]

    def send_zf(col):
        for h in (0, 1):
            zf_s[col, h] = of_left((F, YF)[col], h).astype(BF)
            zf(col, h).start()

    def send_dz(col, k):
        for h in (0, 1):
            total = of_left(((C1, C2), (Y1, Y2))[col][k], h)
            if k == 0:
                zf(col, h).wait_recv()
                total = total + zf_r[col, h].astype(F32)
            dz_s[col, k, h] = total.astype(BF)
            dz(col, k, h).start()

    def column(col, h):
        dz(col, 0, h).wait_recv()
        dz(col, 1, h).wait_recv()
        return of_left((OWN, YO)[col], h) + (
            dz_r[col, 0, h].astype(F32) + dz_r[col, 1, h].astype(F32)
        )

    def send_dy():
        for h in (0, 1):
            dy_s[h] = column(1, h).astype(BF)
            dy(h).start()

    def send_dy_right(k):
        for h in (0, 1):
            dv_s[k, h] = of_right((YO, Y1, YF, Y2)[k], h).astype(BF)
            dy_right(k, h).start()

    def both_right(j, k, h):
        dy_right(k, h).wait_recv()
        return of_right(j, h) + dv_r[k, h].astype(F32)

    def send_zf_right():
        for h in (0, 1):
            zg_s[h] = both_right(F, 2, h).astype(BF)
            zf_right(h).start()

    def send_dz_right(k):
        for h in (0, 1):
            total = both_right((C1, C2)[k], 1 + 2 * k, h)
            if k == 0:
                zf_right(h).wait_recv()
                total = total + zg_r[h].astype(F32)
            dw_s[k, h] = total.astype(BF)
            dz_right(k, h).start()

    def term(j):
        h4(j).wait_recv()
        h = hid[1:, :, lanes(j)].reshape(2 * U, ROWS)
        for m in range(0, DM, 512):
            to[j, m : m + 512, :] = dot(w_in[m : m + 512, :], h)

    def arrivals(t):
        @pl.when(t == C1)
        def _():
            for h in (0, 1):
                gather_own(1, C1, h, zp).wait_recv()
                gather_f(1, h).start()

        @pl.when(t == YO)
        def _():
            for h in (0, 1):
                gather_own(1, YO, h, ylp).wait_recv()
                gather_y1(1, h).start()
            for h in (0, 1):
                gather_f(0, h).wait_recv()
                gather_f(1, h).wait_recv()
                gather_yf(1, h).start()

        @pl.when(t == F)
        def _():
            for h in (0, 1):
                gather_y1(0, h).wait_recv()
                gather_yf(0, h).start()

        @pl.when(t == Y1)
        def _():
            gather_y1(1, 0).wait_recv()
            gather_y1(1, 1).wait_recv()
            gather(YO, Y2, 1, zp).start()
            gather(YO, Y2, 0, zm).start()

        @pl.when(t == YF)
        def _():
            for kind in (0, 1):
                for h in (0, 1):
                    gather_yf(kind, h).wait_recv()

        for chunk in (Y2, C2):

            @pl.when(t == chunk)
            def _():
                arrived(chunk, 0)
                arrived(chunk, 1)

    def left_all(i):
        for k in (0, 1):
            x1(i, k).wait_send()
            xe(i, k).wait_send()
            he(i, k).wait_send()
            x2(i, k).wait_send()
            h2(i, k).wait_send()
            h3(i, k).wait_send()
        yb(i).wait_send()
        h1(i).wait_send()
        h4(i).wait_send()

    def tick(t, carry):
        def stage(step, lag):
            pl.when((t >= lag) & (t < CHUNKS + lag))(lambda: step(t - lag))

        def at(when, step, *args):
            pl.when(t == when)(lambda: step(*args))

        stage(send_yb, 2)
        stage(send_h3, 4)
        at(YF + 6, send_dz, 1, 0)
        arrivals(t)
        stage(partial, 0)

        stage(send_x2, 1)
        stage(send_h2, 3)
        at(C2 + 5, send_dy)
        stage(term, 5)
        for k, chunk in enumerate((YO, Y1, YF, Y2)):
            at(chunk + 5, send_dy_right, k)
        at(F + 5, send_zf, 0)
        at(F + 6, send_dz, 0, 0)
        at(YF + 5, send_zf, 1)
        at(Y2 + 5, send_dz, 1, 1)
        at(Y2 + 5, send_zf_right)
        at(C2 + 5, send_dz, 0, 1)
        at(C2 + 5, send_dz_right, 0)
        at(C2 + 5, send_dz_right, 1)

        stage(send_h1, 2)
        stage(send_h4, 4)
        stage(send_x1, 0)

        @pl.when(t == OWN)
        def _():
            for h in (0, 1):
                gather_own(0, C1, h, zp).wait_recv()
                gather_f(0, h).start()

        @pl.when(t == C1)
        def _():
            for h in (0, 1):
                gather_own(0, YO, h, ylp).wait_recv()
                gather_y1(0, h).start()

        @pl.when(t == Y1)
        def _():
            gather(OWN, C2, 1, zp).start()
            gather(OWN, C2, 0, zm).start()

        pl.when((t >= 7) & (t < CHUNKS + 5))(lambda: left_all(t - 7))
        pl.when((t >= 6) & (t % 2 == 0))(lambda: grads_in(t - 5))
        pl.when((t >= 7) & (t % 2 == 1))(lambda: grads_down(t - 6))
        return carry

    lax.fori_loop(0, CHUNKS + 5, tick, 0)

    stores = [
        pltpu.make_async_copy(sum_in, out_in, o_s.at[0]),
        pltpu.make_async_copy(sum_down, out_down, o_s.at[1]),
    ]
    stores[0].start()
    grads_down(CHUNKS - 1)
    stores[1].start()

    left_all(CHUNKS - 2)
    left_all(CHUNKS - 1)
    for to_whom in first:
        for kind in (0, 1):
            gather_own(kind, *to_whom).wait_send()
    for dst in (Y2, C2):
        for h in (0, 1):
            gather(OWN, dst, h, zp).wait_send()
    for h in (0, 1):
        gather_f(0, h).wait_send()
        gather_f(1, h).wait_send()
        gather_y1(0, h).wait_send()
        gather_y1(1, h).wait_send()
        gather_yf(0, h).wait_send()
        gather_yf(1, h).wait_send()
    for h in (0, 1):
        for col in (0, 1):
            zf(col, h).wait_send()
            dz(col, 0, h).wait_send()
            dz(col, 1, h).wait_send()
        for k in range(4):
            dy_right(k, h).wait_send()
        zf_right(h).wait_send()
        dy(h).wait_send()
        dz_right(0, h).wait_send()
        dz_right(1, h).wait_send()

    for h in (0, 1):
        rows = pl.ds(h * HALF, HALF)
        total = both_right(OWN, 0, h)
        dz_right(0, h).wait_recv()
        dz_right(1, h).wait_recv()
        total = total + (dw_r[0, h].astype(F32) + dw_r[1, h].astype(F32))
        last[rows, LEFT:] = total.T.astype(BF)
        total = column(0, h)
        dy(h).wait_recv()
        last[rows, :LEFT] = (total + dy_r[h].astype(F32)).T.astype(BF)
        stores.append(pltpu.make_async_copy(last.at[rows], out_tok.at[rows], o_s.at[2 + h]))
        stores[-1].start()
    for copy in stores:
        copy.wait()


def place(tok, sums, down, out_tok, out_gate, out_up, out_down, v_tok, v_sums, v_down, v_out, sems):
    reads, writes = [], []

    def piece(src, via, dst, by_way=None):
        k = len(reads)
        reads.append(pltpu.make_async_copy(src, via, sems.at[0, k]))
        writes.append(pltpu.make_async_copy(via if by_way is None else by_way, dst, sems.at[1, k]))
        reads[-1].start()

    turns = []
    for o, out in enumerate((out_gate, out_up)):
        for u in range(0, U, 256):
            for d in range(0, DM, 512):
                src = (pl.ds(o * U + u, 256), pl.ds(d, 512))
                dst = (pl.ds(d, 512), pl.ds(u, 256))
                turns.append((src, (o, *dst)))
                piece(sums.at[src], v_sums.at[src], out.at[dst], v_out.at[(o, *dst)])
    for p in range(0, U, 128):
        rows = pl.ds(p, 128)
        piece(down.at[rows], v_down.at[rows], out_down.at[rows])
    piece(tok, v_tok, out_tok)
    for k, (read, write) in enumerate(zip(reads, writes)):
        read.wait()
        if k < len(turns):
            src, dst = turns[k]
            v_out[dst] = v_sums[src].T
        write.start()
    for write in writes:
        write.wait()


def local(tokens, grad_out, keep, count, w_gate, w_up, w_down):
    vmem = pl.BlockSpec(memory_space=pltpu.VMEM)
    anywhere = pl.BlockSpec(memory_space=pl.ANY)
    dma = pltpu.SemaphoreType.DMA
    outs = pl.pallas_call(
        kernel,
        out_shape=(
            jax.ShapeDtypeStruct((ROWS, DM), BF),
            jax.ShapeDtypeStruct((2 * U, DM), F32),
            jax.ShapeDtypeStruct((U, DM), F32),
        ),
        in_specs=[anywhere, anywhere, vmem, pl.BlockSpec(memory_space=pltpu.SMEM)] + [anywhere] * 3,
        out_specs=[anywhere] * 3,
        scratch_shapes=[
            pltpu.VMEM((ROWS, DM), BF),
            pltpu.VMEM((ROWS, DM), BF),
            pltpu.VMEM((DM, 2 * U), BF),
            pltpu.VMEM((2 * U, DM), BF),
            pltpu.VMEM((U, DM), BF),
            pltpu.VMEM((2 * U, DM), F32),
            pltpu.VMEM((U, DM), F32),
            pltpu.VMEM((2, CHUNKS, ROWS, DM), BF),
            pltpu.VMEM((2, 3, U, ROWS), F32),
            pltpu.VMEM((CHUNKS, 3, UC, ROWS), F32),
            pltpu.VMEM((CHUNKS, 2, 3, UY, ROWS), BF),
            pltpu.VMEM((CHUNKS, 2, 3, UY, ROWS), BF),
            pltpu.VMEM((CHUNKS, 2, 3, UY, ROWS), BF),
            pltpu.VMEM((CHUNKS, 2, 3, UY, ROWS), BF),
            pltpu.VMEM((CHUNKS, 2, 3, UY, ROWS), BF),
            pltpu.VMEM((CHUNKS, 2, 3, UY, ROWS), BF),
            pltpu.VMEM((CHUNKS, 3, UY, ROWS), BF),
            pltpu.VMEM((CHUNKS, 3, UY, ROWS), BF),
            pltpu.VMEM((2, 2, 3, UY, ROWS), F32),
            pltpu.VMEM((2, 3, UY, ROWS), F32),
            pltpu.VMEM((3, U, CHUNKS * ROWS), BF),
            pltpu.VMEM((CHUNKS, DM, ROWS), F32),
            pltpu.VMEM((2, LEFT, HALF), BF),
            pltpu.VMEM((2, LEFT, HALF), BF),
            pltpu.VMEM((2, 2, LEFT, HALF), BF),
            pltpu.VMEM((2, 2, LEFT, HALF), BF),
            pltpu.VMEM((2, 2, 2, LEFT, HALF), BF),
            pltpu.VMEM((2, 2, 2, LEFT, HALF), BF),
            pltpu.VMEM((4, 2, RIGHT, HALF), BF),
            pltpu.VMEM((4, 2, RIGHT, HALF), BF),
            pltpu.VMEM((2, RIGHT, HALF), BF),
            pltpu.VMEM((2, RIGHT, HALF), BF),
            pltpu.VMEM((2, 2, RIGHT, HALF), BF),
            pltpu.VMEM((2, 2, RIGHT, HALF), BF),
            dma((MESSAGES, CHUNKS)),
            dma((MESSAGES, CHUNKS)),
            dma((CHUNKS + 5, 2)),
            dma((CHUNKS + 5, 2)),
            dma((7, 4)),
            dma((7, 4)),
            dma((4,)),
            dma((5,)),
        ],
        compiler_params=pltpu.CompilerParams(
            collective_id=0, has_side_effects=True, vmem_limit_bytes=62 * 1024 * 1024
        ),
        cost_estimate=pl.CostEstimate(
            flops=16 * 2048 * DM * U, bytes_accessed=16 << 20, transcendentals=0
        ),
    )(tokens, grad_out, keep, count, w_gate, w_up, w_down)
    return pl.pallas_call(
        place,
        out_shape=(
            jax.ShapeDtypeStruct((ROWS, DM), BF),
            jax.ShapeDtypeStruct((DM, U), F32),
            jax.ShapeDtypeStruct((DM, U), F32),
            jax.ShapeDtypeStruct((U, DM), F32),
        ),
        in_specs=[anywhere] * 3,
        out_specs=[anywhere] * 4,
        scratch_shapes=[
            pltpu.VMEM((ROWS, DM), BF),
            pltpu.VMEM((2 * U, DM), F32),
            pltpu.VMEM((U, DM), F32),
            pltpu.VMEM((2, DM, U), F32),
            dma((2, 13)),
        ],
        compiler_params=pltpu.CompilerParams(vmem_limit_bytes=62 * 1024 * 1024),
    )(*outs)


def solution(mesh):
    placed = (
        P("wide", "mp"),
        P("wide", "mp"),
        P("wide"),
        P(),
        P("mp", "wide"),
        P("mp", "wide"),
        P("wide", "mp"),
    )
    return jax.shard_map(
        local,
        mesh=mesh,
        in_specs=placed,
        out_specs=(P("wide", "mp"), P("mp", "wide"), P("mp", "wide"), P("wide", "mp")),
        check_vma=False,
    )
```
